32 devices in a mesh: section: 2 (over x), dp: 2 (over core), seq: 8 (over z, y).
Axes of the slice: x: 2, y: 2, z: 4, core: 2. Of those that a mesh axis runs over, the one named last changes fastest.
Arguments:
- inputs: bfloat16 [8, 2, 1024, 768], P('dp', None, 'seq'), may hold values from -6 to 6
- cotangent: bfloat16 [8, 2, 1024, 768], P('dp', None, 'seq'), may hold values from -6 to 6
- qkv_weight: float32 [2, 768, 2304], P('section', 'seq'), may hold values from -0.21875 to 0.21875
- out_weight: float32 [2, 768, 768], P('section', 'seq'), may hold values from -0.875 to 0.875
- up_weight: float32 [2, 768, 3072], P('section', 'seq'), may hold values from -0.21875 to 0.21875
- down_weight: float32 [2, 3072, 768], P('section', 'seq'), may hold values from -0.109375 to 0.109375
- map_weight: float32 [2, 1536, 64], P('section', 'seq'), may hold values from -1.5 to 1.5
- biases: float32 [2, 8448], P('section', 'seq'), may hold values from -1.2 to 1.2
- gains: float32 [2, 1536], P('section', 'seq'), may hold values from 0.5 to 1.5
Outputs:
- layer_out: bfloat16 [2, 8, 2, 1024, 768], P('section', 'dp', None, 'seq')
- input_grads: bfloat16 [2, 8, 2, 1024, 768], P('section', 'dp', None, 'seq')
- qkv_grad: float32 [2, 768, 2304], P('section', 'seq')
- out_grad: float32 [2, 768, 768], P('section', 'seq')
- up_grad: float32 [2, 768, 3072], P('section', 'seq')
- down_grad: float32 [2, 3072, 768], P('section', 'seq')
- map_grad: float32 [2, 1536, 64], P('section', 'seq')
- bias_grad: float32 [2, 8448], P('section', 'seq')
- gain_grad: float32 [2, 1536], P('section', 'seq')
The draws below stay inside these ranges and needn't reach their ends.
All inputs are finite; a program needn't handle non-finite values.
Results may differ from the reference program's by a relative error of at most 0.015.
The reference program's roundings to bfloat16 on the way count: a program that leaves them out, or rounds other values in their place, can miss the bound.
Values may be sent and summed in bfloat16 or wider, within the bound.
A program may use at most 512 MiB of HBM per device.

```python
import jax
import jax.numpy as jnp
from jax import lax

D = 768
FF = 3072
H = 12
HEAD = 64
BLOCK = 64
MICRO = 2
SEQS = 8
MBL = 1024
LENGTH = 2048


def level_of(own_key, extent, shards, smallest, top_value):
    gain = 1.0
    for position, parts in shards:
        heights = jax.random.uniform(jax.random.fold_in(jax.random.fold_in(own_key, 6), position), (parts,), jnp.float32, smallest / len(shards), top_value / len(shards))
        gain = gain * jnp.repeat(jnp.exp(heights), extent[position] // parts).reshape((-1,) + (1,) * (len(extent) - 1 - position))
    return gain


def noise(key, shape, scale, bound, split=(), kind=jnp.bfloat16):
    result = jax.random.normal(key, shape, jnp.float32) * scale
    if len(split) > 0:
        result = level_of(key, shape, split, -0.22, 0.18) * result
    return jnp.clip(result, min=-bound, max=bound).astype(kind)


def setup_inputs(seed: int = 0) -> dict:
    splits = jax.random.split(jax.random.key(seed), 10)
    return {
        "inputs": noise(splits[0], (SEQS, MICRO, MBL, D), 1.0, 6.0, ((0, 2), (2, 8))),
        "cotangent": noise(splits[1], (SEQS, MICRO, MBL, D), 1.0, 6.0, ((0, 2), (2, 8))),
        "qkv_weight": noise(splits[2], (2, D, 3 * D), D ** -0.5, 0.21875, ((0, 2), (1, 8)), jnp.float32),
        "out_weight": noise(splits[3], (2, D, D), (D // 16) ** -0.5, 0.875, ((0, 2), (1, 8)), jnp.float32),
        "up_weight": noise(splits[4], (2, D, FF), D ** -0.5, 0.21875, ((0, 2), (1, 8)), jnp.float32),
        "down_weight": noise(splits[5], (2, FF, D), FF ** -0.5, 0.109375, ((0, 2), (1, 8)), jnp.float32),
        "map_weight": noise(splits[6], (2, 2 * H * HEAD, HEAD), (HEAD // 4) ** -0.5, 1.5, ((0, 2), (1, 8)), jnp.float32),
        "biases": noise(splits[7], (2, 7 * D + FF), 0.2, 1.2, ((0, 2), (1, 8)), jnp.float32),
        "gains": jnp.clip(1.0 + 0.1 * jax.random.normal(splits[8], (2, 2 * D), jnp.float32), 0.5, 1.5),
    }


MAXIMUM_ACCURACY = lax.Precision.HIGHEST
NORM_EPSILON = 1e-05

@jax.custom_vjp
def low(v):
    return lax.optimization_barrier(v.astype(jnp.bfloat16)).astype(jnp.float32)

@jax.custom_vjp
def low_back(v):
    return v

def low_keep(v):
    return (low(v), None)

def low_pass(kept, grad):
    return (grad,)

def back_keep(v):
    return (v, None)

def back_low(kept, grad):
    return (low(grad),)
low.defvjp(low_keep, low_pass)
low_back.defvjp(back_keep, back_low)

def normalize(values, gain_vector, shift_vector):
    average = lax.optimization_barrier(jnp.mean(values, -1, keepdims=True))
    centred = values - average
    spread = lax.optimization_barrier(jnp.mean(centred * centred, -1, keepdims=True))
    return centred * lax.rsqrt(spread + NORM_EPSILON) * gain_vector + shift_vector

def features(logits):
    return jnp.concatenate([jax.nn.softmax(logits, -1), jax.nn.softmax(-logits, -1)], -1)

def product(left_side, right_side):
    return jnp.dot(left_side, right_side, precision=MAXIMUM_ACCURACY)

def attend(query_map, key_map, value_rows):
    length = query_map.shape[0]
    blocks = length // BLOCK
    causal_order = jnp.tril(jnp.ones((BLOCK, BLOCK), jnp.float32))
    query_blocks = query_map.reshape(blocks, BLOCK, H, 2 * HEAD)
    key_blocks = key_map.reshape(blocks, BLOCK, H, 2 * HEAD)
    value_blocks = value_rows.reshape(blocks, BLOCK, H, HEAD)

    @jax.checkpoint
    def one_block(carry, pieces):
        prefix_state_sum, totals = carry
        query_block_rows, key_block_rows, value_block_rows = pieces
        score_matrix = jnp.einsum('tep,cep->etc', query_block_rows, key_block_rows, precision=MAXIMUM_ACCURACY) * causal_order
        numerator = jnp.einsum('hqk,khe->qhe', score_matrix, value_block_rows, precision=MAXIMUM_ACCURACY)
        numerator = numerator + jnp.einsum('qhf,hfe->qhe', query_block_rows, prefix_state_sum, precision=MAXIMUM_ACCURACY)
        denominator = lax.optimization_barrier(jnp.sum(score_matrix, -1)).T + jnp.einsum('qhf,hf->qh', query_block_rows, totals, precision=MAXIMUM_ACCURACY)
        mixture = numerator / denominator[:, :, None]
        prefix_state_sum = prefix_state_sum + jnp.einsum('rng,rna->nga', key_block_rows, value_block_rows, precision=MAXIMUM_ACCURACY)
        totals = totals + lax.optimization_barrier(jnp.sum(key_block_rows, 0))
        return ((prefix_state_sum, totals), mixture)
    start_pair = (jnp.zeros((H, 2 * HEAD, HEAD), jnp.float32), jnp.zeros((H, 2 * HEAD), jnp.float32))
    _, mixture = lax.scan(one_block, start_pair, (query_blocks, key_blocks, value_blocks))
    return mixture.reshape(length, H, HEAD)

def hedgehog_layer(tokens, weights):
    qkv_weight, out_weight, up_weight, down_weight, map_weight, biases, gains = [low(param_array) for param_array in weights]
    length = tokens.shape[0]
    shift_one = biases[:D]
    qkv_bias = biases[D:4 * D]
    out_bias = biases[4 * D:5 * D]
    shift_two = biases[5 * D:6 * D]
    up_bias = biases[6 * D:6 * D + FF]
    down_bias = biases[6 * D + FF:]
    gain_one = gains[:D]
    gain_two = gains[D:]
    normed = low(normalize(tokens, gain_one, shift_one))
    projected = low_back(low(product(normed, qkv_weight) + qkv_bias))
    query_rows = projected[:, :D].reshape(length, H, HEAD)
    key_rows = projected[:, D:2 * D].reshape(length, H, HEAD)
    value_rows = projected[:, 2 * D:].reshape(length, H, HEAD)
    feature_maps = map_weight.reshape(2, H, HEAD, HEAD)
    query_map = low(features(jnp.einsum('lhe,hef->lhf', query_rows, feature_maps[0], precision=MAXIMUM_ACCURACY)))
    key_map = low(features(jnp.einsum('lhe,hef->lhf', key_rows, feature_maps[1], precision=MAXIMUM_ACCURACY)))
    mixture = attend(query_map, key_map, value_rows)
    branch = low_back(product(low(mixture.reshape(length, D)), out_weight))
    residual = tokens + branch + out_bias
    normed_two = low(normalize(residual, gain_two, shift_two))
    before_act = low_back(product(normed_two, up_weight) + up_bias)
    hidden = low(jax.nn.gelu(before_act, approximate=True))
    return residual + low_back(product(hidden, down_weight)) + down_bias

def lower_layer(tokens, weights):
    return low(hedgehog_layer(tokens, weights))

def reference(inputs, cotangent, qkv_weight, out_weight, up_weight, down_weight, map_weight, biases, gains):
    params = (qkv_weight, out_weight, up_weight, down_weight, map_weight, biases, gains)
    first_layer = tuple((param_array[0] for param_array in params))
    second_layer = tuple((param_array[1] for param_array in params))
    sequences = inputs.astype(jnp.float32).reshape(SEQS, LENGTH, D)
    cotangents = cotangent.astype(jnp.float32).reshape(SEQS, LENGTH, D)

    def one_sequence(running, pair_given):
        tokens, upstream = pair_given
        middle, first_back = jax.vjp(lower_layer, tokens, first_layer)
        top_out, second_back = jax.vjp(hedgehog_layer, middle, second_layer)
        middle_raw, second_grads = second_back(upstream)
        middle_grad = low(middle_raw)
        token_grad, first_grads = first_back(middle_grad)
        running = tuple((previous + jnp.stack([first_term, second_term]) for previous, first_term, second_term in zip(running, first_grads, second_grads)))
        return (running, (middle, top_out, token_grad, middle_grad))
    start_sums = tuple((jnp.zeros(param_array.shape, jnp.float32) for param_array in params))
    totals, (middle, top_out, token_grad, middle_grad) = lax.scan(one_sequence, start_sums, (sequences, cotangents))
    whole_shape = (SEQS, MICRO, MBL, D)
    layer_out = jnp.stack([middle.reshape(whole_shape), top_out.reshape(whole_shape)]).astype(jnp.bfloat16)
    input_grads = jnp.stack([token_grad.reshape(whole_shape), middle_grad.reshape(whole_shape)]).astype(jnp.bfloat16)
    return (layer_out, input_grads, totals[0], totals[1], totals[2], totals[3], totals[4], totals[5], totals[6])
```

```python
import functools

import jax
import jax.numpy as jnp
from jax import lax
from jax.experimental import pallas as pl
from jax.experimental.pallas import tpu as pltpu
from jax.sharding import PartitionSpec as P

D = 768
FF = 3072
H = 12
HEAD = 64
CH = 128
PAIRS = H // 2
QB = 2 * H * HEAD
STATE_ROWS = D + 16
EPS = 1e-05
TILE = 256
AXES = ("section", "dp", "seq")
f32 = jnp.float32
bf16 = jnp.bfloat16

VMEM = pl.BlockSpec(memory_space=pltpu.VMEM)
SMEM = pl.BlockSpec(memory_space=pltpu.SMEM)
ANY = pl.BlockSpec(memory_space=pl.ANY)


def nn(a, b):
    return lax.dot_general(a, b, (((1,), (0,)), ((), ())), preferred_element_type=f32)


def nt(a, b):
    return lax.dot_general(a, b, (((1,), (1,)), ((), ())), preferred_element_type=f32)


def tn(a, b):
    return lax.dot_general(a, b, (((0,), (0,)), ((), ())), preferred_element_type=f32)


def loop(count, body):
    lax.fori_loop(0, count, lambda i, c: (body(i), c)[1], 0)


def span(i, size):
    return pl.ds(pl.multiple_of(i * size, size), size)


class Weight:
    def __init__(self, arrays, layer, col=0, width=None):
        self.arrays = list(arrays)
        self.layer = layer
        self.col = col
        self.width = width

    def issue(self, refs, dst, sem, place):
        if len(self.arrays) == 1:
            pltpu.make_async_copy(refs[0], dst, sem).start()
            return
        x, d, z, y = (place[i] for i in range(4))
        nz, r = self.arrays[0].shape[:2]
        c = self.width
        for lay in range(2):

            @pl.when(x == (self.layer if lay == 0 else 1 - self.layer))
            def _():
                for yy in range(2):
                    for cc in range(2):
                        src = refs[lay * 4 + yy * 2 + cc]
                        half = jnp.where(d == 0, cc, 1 - cc)
                        ypos = jnp.where(y == 0, yy, 1 - yy)
                        for o in range(nz):
                            row = (lax.rem(z - o + nz, nz) * 2 + ypos) * r
                            pltpu.make_async_copy(
                                src.at[o, :, pl.ds(self.col, c)],
                                dst.at[
                                    pl.ds(pl.multiple_of(row, r), r),
                                    pl.ds(pl.multiple_of(half * c, c), c),
                                ],
                                sem,
                            ).start()


def finish(dst, sem):
    pltpu.make_async_copy(dst, dst, sem).wait()


def call(kernel, outs, scratch, specs, args, flops, out_specs=None, vmem=60):
    if out_specs is None:
        out_specs = [VMEM] * len(outs)
    moved = sum(a.size * a.dtype.itemsize for a in args if a.ndim > 0)
    moved += sum(o.size * o.dtype.itemsize for o in outs)
    return pl.pallas_call(
        kernel,
        out_shape=outs,
        in_specs=specs,
        out_specs=out_specs,
        scratch_shapes=scratch,
        compiler_params=pltpu.CompilerParams(vmem_limit_bytes=vmem * 1024 * 1024),
        cost_estimate=pl.CostEstimate(flops=flops, bytes_accessed=moved, transcendentals=0),
    )(*args)


def shape(dims, kind):
    return jax.ShapeDtypeStruct(dims, kind)


def standardize(u):
    cen = u - jnp.mean(u, -1, keepdims=True)
    rstd = lax.rsqrt(jnp.mean(cen * cen, -1, keepdims=True) + EPS)
    return cen * rstd, rstd


def lanes(rows):
    return lax.broadcasted_iota(jnp.int32, (rows, CH), 1)


def half_sums(t, low):
    s1 = jnp.sum(jnp.where(low, t, 0.0), -1, keepdims=True)
    s2 = jnp.sum(jnp.where(low, 0.0, t), -1, keepdims=True)
    return jnp.where(low, s1, s2)


def half_softmax(l, low):
    m1 = jnp.max(jnp.where(low, l, -jnp.inf), -1, keepdims=True)
    m2 = jnp.max(jnp.where(low, -jnp.inf, l), -1, keepdims=True)
    p = jnp.exp(l - jnp.where(low, m1, m2))
    return p / half_sums(p, low)


def project_kernel(w, nw, place, u, gain, shift, bias, bd, *rest):
    refs, (a, qkv, ph, st, wv, sem) = rest[:nw], rest[nw:]
    w.issue(refs, wv, sem, place)
    t = u.shape[0]

    def norm(i):
        xh, _ = standardize(u[span(i, CH), :].astype(f32))
        a[span(i, CH), :] = (xh * gain[...] + shift[...]).astype(bf16)

    loop(t // CH, norm)
    finish(wv, sem)

    def column(j):
        cols = span(j, TILE)
        qkv[:, cols] = (nn(a[...], wv[:, cols]) + bias[:, cols]).astype(bf16)

    loop(3 * D // TILE, column)
    low = lanes(CH) < HEAD

    def pair(p):
        def rows(i):
            lg = nn(qkv[span(i, CH), span(p, CH)], bd[p])
            for hh in range(2):
                ph[span(i, CH), span(2 * p + hh, CH)] = half_softmax(
                    lg[:, hh * CH : (hh + 1) * CH], low
                ).astype(bf16)

        loop(t // CH, rows)

    loop(2 * PAIRS, pair)

    def state(p):
        v = qkv[:, pl.ds(pl.multiple_of(2 * D + p * CH, CH), CH)]
        for hh in range(2):
            k = ph[:, pl.ds(pl.multiple_of((H + 2 * p + hh) * CH, CH), CH)]
            full = tn(v, k)
            st[span(2 * p + hh, HEAD), :] = full[hh * HEAD : (hh + 1) * HEAD]
            st[pl.ds(D + 2 * p + hh, 1), :] = jnp.sum(k.astype(f32), 0, keepdims=True)

    loop(PAIRS, state)
    st[D + H :, :] = jnp.zeros((STATE_ROWS - D - H, CH), f32)


def project(layer, place, u, vecs, bd, w):
    t = u.shape[0]
    return call(
        functools.partial(project_kernel, w, len(w.arrays)),
        [
            shape((t, D), bf16),
            shape((t, 3 * D), bf16),
            shape((t, 2 * QB), bf16),
            shape((STATE_ROWS, CH), f32),
        ],
        [pltpu.VMEM((D, 3 * D), bf16), pltpu.SemaphoreType.DMA],
        [SMEM] + [VMEM] * 5 + [ANY] * len(w.arrays),
        [place, u, vecs["gain1"], vecs["shift1"], vecs["qkv_bias"], bd] + w.arrays,
        2 * t * D * 3 * D,
    )


def sum_states(dst, parts):
    dst[...] = functools.reduce(jnp.add, [part[...] for part in parts])


def mix_kernel(ws, ns, np_, place, qkv, ph, u, outb, gain, shift, upb, downb, *rest):
    wo, wu, wd = ws
    no, nu, nd = ns
    parts, rest = rest[:np_], rest[np_:]
    ro, ru, rd = rest[:no], rest[no : no + nu], rest[no + nu : no + nu + nd]
    o, inv, ob, r, n2, hid, gp, res, wov, wuv, wdv, s0, sems = rest[no + nu + nd :]
    wo.issue(ro, wov, sems.at[0], place)
    wu.issue(ru, wuv, sems.at[1], place)
    wd.issue(rd, wdv, sems.at[2], place)
    t = u.shape[0]
    sum_states(s0, parts)
    low = lanes(CH) < HEAD
    tril = lax.broadcasted_iota(jnp.int32, (CH, CH), 0) >= lanes(CH)

    def pair(p):
        cols = span(p, CH)
        s = s0[cols, :]
        tot = [s0[pl.ds(D + 2 * p + hh, 1), :] for hh in range(2)]
        for c in range(t // CH):
            rows = pl.ds(c * CH, CH)
            v = qkv[rows, pl.ds(pl.multiple_of(2 * D + p * CH, CH), CH)]
            sl = s.astype(bf16)
            got = []
            new = []
            for hh in range(2):
                q = ph[rows, span(2 * p + hh, CH)]
                k = ph[rows, pl.ds(pl.multiple_of((H + 2 * p + hh) * CH, CH), CH)]
                score = jnp.where(tril, nt(q, k), 0.0)
                num = nn(score.astype(bf16), v) + nt(q, sl)
                den = jnp.sum(score + q.astype(f32) * tot[hh], -1, keepdims=True)
                rec = 1.0 / den
                got.append((num * rec, rec))
                new.append(tn(v, k)[hh * HEAD : (hh + 1) * HEAD])
                tot[hh] = tot[hh] + jnp.sum(k.astype(f32), 0, keepdims=True)
            s = s + jnp.concatenate(new, 0)
            both = jnp.where(low, got[0][0], got[1][0])
            o[rows, cols] = both
            ob[rows, cols] = both.astype(bf16)
            inv[rows, cols] = jnp.where(low, got[0][1], got[1][1])

    loop(PAIRS, pair)
    finish(wov, sems.at[0])

    def out_col(j):
        cols = span(j, TILE)
        r[:, cols] = u[:, cols].astype(f32) + nn(ob[...], wov[:, cols]) + outb[:, cols]

    loop(D // TILE, out_col)

    def norm(i):
        xh, _ = standardize(r[span(i, CH), :])
        n2[span(i, CH), :] = (xh * gain[...] + shift[...]).astype(bf16)

    loop(t // CH, norm)
    finish(wuv, sems.at[1])

    def up_col(j):
        cols = span(j, TILE)
        zt = nn(n2[...], wuv[:, cols]) + upb[:, cols]
        z2 = zt * zt
        th = jnp.tanh(GELU_C * zt * (1.0 + GELU_A * z2))
        half = 0.5 * (1.0 + th)
        hid[:, cols] = (zt * half).astype(bf16)
        gp[:, cols] = half + 0.5 * zt * (1.0 - th * th) * (GELU_C * (1.0 + 3.0 * GELU_A * z2))

    loop(FF // TILE, up_col)
    finish(wdv, sems.at[2])

    def down_col(j):
        cols = span(j, TILE)
        res[:, cols] = (r[:, cols] + nn(hid[...], wdv[:, cols]) + downb[:, cols]).astype(bf16)

    loop(D // TILE, down_col)


GELU_C = 0.7978845608028654
GELU_A = 0.044715


def mix(layer, place, qkv, ph, u, vecs, parts, wo, wu, wd):
    t = u.shape[0]
    ws = (wo, wu, wd)
    ns = tuple(len(w.arrays) for w in ws)
    return call(
        functools.partial(mix_kernel, ws, ns, len(parts)),
        [
            shape((t, D), f32),
            shape((t, D), f32),
            shape((t, D), bf16),
            shape((t, D), f32),
            shape((t, D), bf16),
            shape((t, FF), bf16),
            shape((t, FF), f32),
            shape((t, D), bf16),
        ],
        [
            pltpu.VMEM((D, D), bf16),
            pltpu.VMEM((D, FF), bf16),
            pltpu.VMEM((FF, D), bf16),
            pltpu.VMEM((STATE_ROWS, CH), f32),
            pltpu.SemaphoreType.DMA((3,)),
        ],
        [SMEM] + [VMEM] * (8 + len(parts)) + [ANY] * sum(ns),
        [place, qkv, ph, u, vecs["out_bias"], vecs["gain2"], vecs["shift2"], vecs["up_bias"]]
        + [vecs["down_bias"]]
        + list(parts)
        + wo.arrays
        + wu.arrays
        + wd.arrays,
        2 * t * D * (D + 2 * FF) + 6 * t * H * CH * CH,
    )


def back_mlp_kernel(ws, ns, place, g, gp, r, o, inv, ph, gain, *rest):
    wo, wu, wd = ws
    no, nu, nd = ns
    ro, ru, rd = rest[:no], rest[no : no + nu], rest[no + nu : no + nu + nd]
    dz, dr, drb, gs, es, dst, s_dz, s_g, s_dr, s_sh, s_gn, wov, wuv, wdv, tmp, sems = rest[
        no + nu + nd :
    ]
    wd.issue(rd, wdv, sems.at[2], place)
    wu.issue(ru, wuv, sems.at[1], place)
    wo.issue(ro, wov, sems.at[0], place)
    t = g.shape[0]
    finish(wdv, sems.at[2])

    def hid_col(j):
        cols = span(j, TILE)
        part = (nt(g[...], wdv[cols, :]) * gp[:, cols]).astype(bf16)
        dz[:, cols] = part
        s_dz[:, cols] = jnp.sum(part.astype(f32), 0, keepdims=True)

    loop(FF // TILE, hid_col)
    finish(wuv, sems.at[1])

    def n2_col(j):
        cols = span(j, TILE)
        tmp[:, cols] = nt(dz[...], wuv[cols, :])

    loop(D // TILE, n2_col)
    for ref in (s_g, s_dr, s_sh, s_gn):
        ref[...] = jnp.zeros(ref.shape, f32)

    def norm(i):
        rows = span(i, CH)
        xh, rstd = standardize(r[rows, :])
        dn = tmp[rows, :]
        s_sh[...] += jnp.sum(dn, 0, keepdims=True)
        s_gn[...] += jnp.sum(dn * xh, 0, keepdims=True)
        dx = dn * gain[...]
        back = rstd * (
            dx - jnp.mean(dx, -1, keepdims=True) - xh * jnp.mean(dx * xh, -1, keepdims=True)
        )
        up = g[rows, :].astype(f32)
        total = up + back
        s_g[...] += jnp.sum(up, 0, keepdims=True)
        s_dr[...] += jnp.sum(total, 0, keepdims=True)
        dr[rows, :] = total
        drb[rows, :] = total.astype(bf16)

    loop(t // CH, norm)
    finish(wov, sems.at[0])

    def do_col(j):
        cols = span(j, TILE)
        gs[:, cols] = (nt(drb[...], wov[cols, :]) * inv[:, cols]).astype(bf16)

    loop(D // TILE, do_col)
    lane = lanes(t)
    low = lane < HEAD

    def pair(p):
        cols = span(p, CH)
        gv = gs[:, cols]
        prod = gv.astype(f32) * o[:, cols]
        e0 = -jnp.sum(jnp.where(low, prod, 0.0), -1, keepdims=True)
        e1 = -jnp.sum(jnp.where(low, 0.0, prod), -1, keepdims=True)
        swapped = jnp.where(low, e1, e0)
        es[:, cols] = swapped
        for hh in range(2):
            ge = with_error(gv, swapped, lane, hh)
            full = tn(ge, ph[:, span(2 * p + hh, CH)])
            dst[span(2 * p + hh, HEAD), :] = full[hh * HEAD : (hh + 1) * HEAD]
            at = HEAD * (1 - hh)
            dst[pl.ds(D + 2 * p + hh, 1), :] = full[at : at + 1] + full[at + 1 : at + 2]

    loop(PAIRS, pair)
    dst[D + H :, :] = jnp.zeros((STATE_ROWS - D - H, CH), f32)


def with_error(gv, swapped, lane, hh):
    first = HEAD * (1 - hh)
    hi = swapped.astype(bf16)
    lo = (swapped - hi.astype(f32)).astype(bf16)
    own = (lane < HEAD) if hh == 0 else (lane >= HEAD)
    zero = jnp.zeros_like(gv)
    spare = jnp.where(lane == first + 1, lo, jnp.where((lane == first) | (lane == first + 2), hi, zero))
    return jnp.where(own, gv, spare)


def with_ones(v, lane, hh):
    first = HEAD * (1 - hh)
    own = (lane < HEAD) if hh == 0 else (lane >= HEAD)
    spare = jnp.where((lane == first) | (lane == first + 1), jnp.ones_like(v), jnp.zeros_like(v))
    return jnp.where(own, v, spare)


def with_totals(s, tot, row, hh, again):
    first = HEAD * (1 - hh)
    hi = tot.astype(bf16).astype(f32)
    lo = tot - hi
    own = (row < HEAD) if hh == 0 else (row >= HEAD)
    if again:
        spare = jnp.where(
            (row == first) | (row == first + 1), hi, jnp.where(row == first + 2, lo, 0.0)
        )
    else:
        spare = jnp.where(row == first, hi, jnp.where(row == first + 1, lo, 0.0))
    return jnp.where(own, s, spare).astype(bf16)


def back_mlp(layer, place, g, gp, r, o, inv, ph, vecs, wo, wu, wd):
    t = g.shape[0]
    ws = (wo, wu, wd)
    ns = tuple(len(w.arrays) for w in ws)
    return call(
        functools.partial(back_mlp_kernel, ws, ns),
        [
            shape((t, FF), bf16),
            shape((t, D), f32),
            shape((t, D), bf16),
            shape((t, D), bf16),
            shape((t, D), f32),
            shape((STATE_ROWS, CH), f32),
            shape((1, FF), f32),
            shape((1, D), f32),
            shape((1, D), f32),
            shape((1, D), f32),
            shape((1, D), f32),
        ],
        [
            pltpu.VMEM((D, D), bf16),
            pltpu.VMEM((D, FF), bf16),
            pltpu.VMEM((FF, D), bf16),
            pltpu.VMEM((t, D), f32),
            pltpu.SemaphoreType.DMA((3,)),
        ],
        [SMEM] + [VMEM] * 7 + [ANY] * sum(ns),
        [place, g, gp, r, o, inv, ph, vecs["gain2"]] + wo.arrays + wu.arrays + wd.arrays,
        2 * t * D * (D + 2 * FF),
    )


def back_mix_kernel(w, nw, nf, nb, place, qkv, ph, gs, es, u, dr, gain, bd, *rest):
    firsts, lasts, rest = rest[:nf], rest[nf : nf + nb], rest[nf + nb :]
    refs, rest = rest[:nw], rest[nw:]
    dqkv, du, mg, s_q, s_sh, s_gn, wv, s0, s1, tmp, sem = rest
    w.issue(refs, wv, sem, place)
    t = u.shape[0]
    nc = t // CH
    sum_states(s0, firsts)
    sum_states(s1, lasts)
    lane = lanes(CH)
    low = lane < HEAD
    row = lax.broadcasted_iota(jnp.int32, (CH, CH), 0)
    tril = row >= lane
    triu = row <= lane

    def pair(p):
        cols = span(p, CH)
        vcols = pl.ds(pl.multiple_of(2 * D + p * CH, CH), CH)
        kcols = pl.ds(pl.multiple_of(D + p * CH, CH), CH)
        before = []
        s = s0[cols, :]
        tot = [s0[pl.ds(D + 2 * p + hh, 1), :] for hh in range(2)]
        for c in range(nc):
            rows = pl.ds(c * CH, CH)
            before.append([with_totals(s, tot[hh], row, hh, True) for hh in range(2)])
            if c < nc - 1:
                v = qkv[rows, vcols]
                new = []
                for hh in range(2):
                    k = ph[rows, pl.ds(pl.multiple_of((H + 2 * p + hh) * CH, CH), CH)]
                    new.append(tn(v, k)[hh * HEAD : (hh + 1) * HEAD])
                    tot[hh] = tot[hh] + jnp.sum(k.astype(f32), 0, keepdims=True)
                s = s + jnp.concatenate(new, 0)
        ds = s1[cols, :]
        dtot = [s1[pl.ds(D + 2 * p + hh, 1), :] for hh in range(2)]
        acc_q = jnp.zeros((CH, 2 * CH), f32)
        acc_k = jnp.zeros((CH, 2 * CH), f32)
        sums = [jnp.zeros((1, CH), f32) for _ in range(3)]
        for c in reversed(range(nc)):
            rows = pl.ds(c * CH, CH)
            v = qkv[rows, vcols]
            gv = gs[rows, cols]
            ev = es[rows, cols]
            dsl = ds.astype(bf16)
            dl_q, dl_k, dv, new = [], [], [], []
            for hh in range(2):
                q = ph[rows, span(2 * p + hh, CH)]
                k = ph[rows, pl.ds(pl.multiple_of((H + 2 * p + hh) * CH, CH), CH)]
                ge = with_error(gv, ev, lane, hh)
                v1 = with_ones(v, lane, hh)
                after = with_totals(ds, dtot[hh], row, hh, False)
                da = jnp.where(tril, nt(ge, v1), 0.0).astype(bf16)
                dat = jnp.where(triu, nt(v1, ge), 0.0).astype(bf16)
                at = jnp.where(triu, nt(k, q), 0.0).astype(bf16)
                dq = nn(da, k) + nn(ge, before[c][hh])
                dk = nn(dat, q) + nn(v1, after)
                dv.append(nn(at, gv) + nt(k, dsl))
                for p_, d_, to in ((q, dq, dl_q), (k, dk, dl_k)):
                    pf = p_.astype(f32)
                    to.append((pf * (d_ - half_sums(pf * d_, low))).astype(bf16))
                full = tn(ge, q)
                new.append(full[hh * HEAD : (hh + 1) * HEAD])
                first = HEAD * (1 - hh)
                dtot[hh] = dtot[hh] + full[first : first + 1] + full[first + 1 : first + 2]
            ds = ds + jnp.concatenate(new, 0)
            dl_q = jnp.concatenate(dl_q, 1)
            dl_k = jnp.concatenate(dl_k, 1)
            acc_q = acc_q + tn(qkv[rows, cols], dl_q)
            acc_k = acc_k + tn(qkv[rows, kcols], dl_k)
            parts = (
                (cols, nt(dl_q, bd[p])),
                (kcols, nt(dl_k, bd[PAIRS + p])),
                (vcols, jnp.where(low, dv[0], dv[1])),
            )
            for i, (where, val) in enumerate(parts):
                val = val.astype(bf16)
                dqkv[rows, where] = val
                sums[i] = sums[i] + jnp.sum(val.astype(f32), 0, keepdims=True)
        for where, val in zip((cols, kcols, vcols), sums):
            s_q[:, where] = val
        for which, acc in enumerate((acc_q, acc_k)):
            for hh in range(2):
                blk = acc[hh * HEAD : (hh + 1) * HEAD, hh * CH : (hh + 1) * CH]
                mg[which * H + 2 * p + hh] = blk - pltpu.roll(blk, HEAD, 1)

    loop(PAIRS, pair)
    finish(wv, sem)

    def n1_col(j):
        cols = span(j, TILE)
        tmp[:, cols] = nt(dqkv[...], wv[cols, :])

    loop(D // TILE, n1_col)
    s_sh[...] = jnp.zeros(s_sh.shape, f32)
    s_gn[...] = jnp.zeros(s_gn.shape, f32)

    def norm(i):
        rows = span(i, CH)
        xh, rstd = standardize(u[rows, :].astype(f32))
        dn = tmp[rows, :]
        s_sh[...] += jnp.sum(dn, 0, keepdims=True)
        s_gn[...] += jnp.sum(dn * xh, 0, keepdims=True)
        dx = dn * gain[...]
        back = rstd * (
            dx - jnp.mean(dx, -1, keepdims=True) - xh * jnp.mean(dx * xh, -1, keepdims=True)
        )
        du[rows, :] = (dr[rows, :] + back).astype(bf16)

    loop(nc, norm)


def back_mix(layer, place, qkv, ph, gs, es, u, dr, vecs, bd, firsts, lasts, w):
    t = u.shape[0]
    nw = len(w.arrays)
    return call(
        functools.partial(back_mix_kernel, w, nw, len(firsts), len(lasts)),
        [
            shape((t, 3 * D), bf16),
            shape((t, D), bf16),
            shape((2 * H, HEAD, CH), f32),
            shape((1, 3 * D), f32),
            shape((1, D), f32),
            shape((1, D), f32),
        ],
        [
            pltpu.VMEM((D, 3 * D), bf16),
            pltpu.VMEM((STATE_ROWS, CH), f32),
            pltpu.VMEM((STATE_ROWS, CH), f32),
            pltpu.VMEM((t, D), f32),
            pltpu.SemaphoreType.DMA,
        ],
        [SMEM] + [VMEM] * (8 + len(firsts) + len(lasts)) + [ANY] * nw,
        [place, qkv, ph, gs, es, u, dr, vecs["gain1"], bd]
        + list(firsts)
        + list(lasts)
        + w.arrays,
        2 * t * D * 3 * D + 14 * t * H * CH * CH,
    )


def grad_tiles(lhs, rhs, place, other, width, put):
    d = place[1]
    base = jnp.where(d == 0, other, 1 - other) * width
    rows = lhs.shape[1]
    step = D if rows == D else 512
    tile = width if rows != D else (384 if width % 384 == 0 else 128)
    for i in range(rows // step):
        for j in range(width // tile):
            cols = pl.ds(pl.multiple_of(base + j * tile, CH), tile)
            put(pl.ds(i * step, step), pl.ds(j * tile, tile), tn(lhs[:, i * step : (i + 1) * step], rhs[:, cols]))


def grad_send_kernel(place, lhs, rhs, out):
    def put(rows, cols, val):
        out[rows, cols] = val.astype(bf16)

    grad_tiles(lhs, rhs, place, 1, out.shape[1], put)


def grad_send(place, lhs, rhs):
    rows, cols = lhs.shape[1], rhs.shape[1] // 2
    return call(
        grad_send_kernel,
        [shape((rows, cols), bf16)],
        [],
        [SMEM, VMEM, VMEM],
        [place, lhs, rhs],
        2 * lhs.shape[0] * rows * cols,
    )[0]


def grad_keep_kernel(place, lhs, rhs, got, keep, send, buf, sem):
    def put(rows, cols, val):
        buf[rows, cols] = (val + got[rows, cols].astype(f32)).astype(bf16)

    grad_tiles(lhs, rhs, place, 0, buf.shape[1], put)
    nz, r = keep.shape[:2]
    y = place[3]
    copies = []
    for i in range(nz):
        for out, yy in ((send, 1 - y), (keep, y)):
            row = pl.multiple_of((i * 2 + yy) * r, r)
            copies.append(pltpu.make_async_copy(buf.at[pl.ds(row, r), :], out.at[i], sem))
    for copy in copies:
        copy.start()
    finish(buf, sem)


def grad_keep(place, lhs, rhs, got, nz):
    rows, cols = got.shape
    half = shape((nz, rows // nz // 2, cols), bf16)
    return call(
        grad_keep_kernel,
        [half, half],
        [pltpu.VMEM((rows, cols), bf16), pltpu.SemaphoreType.DMA],
        [SMEM, VMEM, VMEM, VMEM],
        [place, lhs, rhs, got],
        2 * lhs.shape[0] * rows * cols,
        [ANY, ANY],
    )


def shards(inputs, cotangent, *weights):
    n = lax.axis_size("seq")
    nz = n // 2
    group = n // 4
    x, d, j = (lax.axis_index(a) for a in AXES)
    z, y = j // 2, j % 2
    i_seq, jj = j // group, j % group
    place = jnp.stack([x, d, z, y]).astype(jnp.int32)
    t = 4 * CH

    def move(value, rule):
        pairs = []
        for xx in range(2):
            for dd in range(2):
                for k in range(n):
                    to = rule(xx, dd, k)
                    if to is not None:
                        pairs.append(((xx * 2 + dd) * n + k, (to[0] * 2 + to[1]) * n + to[2]))
        return lax.ppermute(value, AXES, pairs)

    def swap_x(value):
        return move(value, lambda xx, dd, k: (1 - xx, dd, k))

    def swap_d(value):
        return move(value, lambda xx, dd, k: (xx, 1 - dd, k))

    def swap_y(value):
        return move(value, lambda xx, dd, k: (xx, dd, k ^ 1))

    def shift_z(value, o):
        return move(value, lambda xx, dd, k: (xx, dd, (k + 2 * o) % n))

    def spread(own, y_last):
        zs = jnp.stack([own] + [shift_z(own, o) for o in range(1, nz)])
        ys = swap_y(zs)
        xs = swap_x(zs)
        xys = swap_y(xs) if y_last else swap_x(ys)
        return zs, ys, xs, xys

    def halved(w):
        width = w.shape[1] // 2
        return lax.dynamic_slice_in_dim(w, d * width, width, 1).astype(bf16)

    def with_cores(arrays):
        return [piece for a in arrays for piece in (a, swap_d(a))]

    qkv_w, out_w, up_w, down_w, map_w, bias_w, gain_w = (w[0] for w in weights)
    rows = [w.shape[0] for w in (qkv_w, out_w, up_w, down_w, map_w, bias_w, gain_w)]
    whole = rows[0] % 16 != 0

    def collect(source):
        mine = lax.dynamic_index_in_dim(source, x, 1, False)
        got = []
        for s in range(4):
            part = lax.dynamic_index_in_dim(mine, (j + s) % 4, 0, False)
            got.append(move(part, lambda xx, dd, k, s=s: (xx, dd, ((k + s) % 4) * group + k // 4)))
        ring = jnp.stack(got[::-1] + got[::-1])
        return lax.dynamic_slice_in_dim(ring, 3 - i_seq, 4, 0).reshape(t, D)

    small = jnp.concatenate([map_w.reshape(-1), bias_w, gain_w]).astype(bf16)
    unit = small.shape[0]
    padded = -(-unit // 2048) * 2048
    small = jnp.pad(small, (0, padded - unit)).reshape(-1, CH)
    zs, ys, xs, xys = spread(small, False)
    tokens = collect(inputs)

    def in_order(a, b):
        both = jnp.stack([a, b], 1)
        both = jnp.where(y == 0, both, both[:, ::-1])
        both = both[::-1]
        both = lax.dynamic_slice_in_dim(jnp.concatenate([both, both]), nz - 1 - z, nz, 0)
        return both.reshape(n, padded)[:, :unit]

    near, far = in_order(zs, ys), in_order(xs, xys)
    smalls = (jnp.where(x == 0, near, far), jnp.where(x == 0, far, near))

    if whole:
        everything = [
            lax.all_gather(
                lax.all_gather(w.astype(bf16), "seq", axis=0, tiled=True), "section", axis=0
            )
            for w in (qkv_w, out_w, up_w, down_w)
        ]

        def weight_set(layer):
            return [Weight([w[layer]], layer) for w in everything]

    else:
        g_qkv = with_cores(spread(halved(qkv_w), True))
        g_mid = with_cores(
            spread(jnp.concatenate([halved(out_w), halved(up_w)], 1), False)
        )
        g_down = with_cores(spread(halved(down_w), True))

        def weight_set(layer):
            return [
                Weight(g_qkv, layer, 0, 3 * D // 2),
                Weight(g_mid, layer, 0, D // 2),
                Weight(g_mid, layer, D // 2, FF // 2),
                Weight(g_down, layer, 0, D // 2),
            ]

    sets = [weight_set(0), weight_set(1)]

    def unpack(flat):
        m, b, g = rows[4] * HEAD, rows[5], rows[6]
        maps = flat[:, :m].reshape(2 * H, HEAD, HEAD)
        vec = flat[:, m : m + b].reshape(1, -1).astype(f32)
        gains = flat[:, m + b : m + b + g].reshape(1, -1).astype(f32)
        signed = jnp.concatenate([maps, -maps], -1).reshape(2 * PAIRS, 2, HEAD, CH)
        zero = jnp.zeros_like(signed[:, 0])
        bd = jnp.concatenate(
            [
                jnp.concatenate([signed[:, 0], zero], -1),
                jnp.concatenate([zero, signed[:, 1]], -1),
            ],
            1,
        )
        names = ("shift1", "qkv_bias", "out_bias", "shift2", "up_bias", "down_bias")
        sizes = (D, 3 * D, D, D, FF, D)
        vecs, at = {}, 0
        for name, size in zip(names, sizes):
            vecs[name] = vec[:, at : at + size]
            at += size
        vecs["gain1"], vecs["gain2"] = gains[:, :D], gains[:, D:]
        return vecs, bd

    params = [unpack(flat) for flat in smalls]

    members = 2 * group

    def others(value, sign):
        def rule(o):
            def to(xx, dd, k):
                place_ = xx * group + k % group + sign * o
                if not 0 <= place_ < members:
                    return None
                return (place_ // group, dd, (k // group) * group + place_ % group)

            return to

        return [move(value, rule(o)) for o in range(1, members)]

    u = tokens
    kept = []
    for layer in range(2):
        vecs, bd = params[layer]
        wq, wo, wu, wd = sets[layer]
        a, qkv, ph, st = project(layer, place, u, vecs, bd, wq)
        firsts = others(st, 1)
        o, inv, ob, r, n2, hid, gp, res = mix(layer, place, qkv, ph, u, vecs, firsts, wo, wu, wd)
        kept.append((u, a, qkv, ph, firsts, o, inv, ob, r, n2, hid, gp, res))
        u = res

    def reduce_grad(lhs, rhs, layer):
        send = grad_send(place, lhs, rhs)
        keep, send = grad_keep(place, lhs, rhs, swap_d(send), 1 if whole else nz)
        if whole:
            both = jnp.stack([keep[0], send[0]])
            both = jnp.where(y == 0, both, both[::-1]).reshape(nz, 2, -1, keep.shape[-1])
            keep = jnp.where(y == 0, both[:, 0], both[:, 1])
            send = jnp.where(y == 0, both[:, 1], both[:, 0])
        return after_core(keep, send, layer)

    def after_core(keep, send, layer):
        kind = keep.dtype
        part = (keep.astype(f32) + swap_y(send).astype(f32)).astype(kind)
        total = lax.dynamic_index_in_dim(part, z, 0, False).astype(f32)
        for o in range(1, nz):
            piece = lax.dynamic_index_in_dim(part, (z + o) % nz, 0, False)
            total = total + shift_z(piece, o).astype(f32)
        got = move(
            total.astype(kind), lambda xx, dd, k: (layer, dd, k) if xx == 1 - layer else None
        )
        return total + got.astype(f32)

    def joined(part):
        other = swap_d(part)
        return jnp.where(
            d == 0,
            jnp.concatenate([part, other], 1),
            jnp.concatenate([other, part], 1),
        )

    g = collect(cotangent)
    results = [None, None]
    input_grads = [None, None]
    for layer in (1, 0):
        vecs, bd = params[layer]
        wq, wo, wu, wd = sets[layer]
        u, a, qkv, ph, firsts, o, inv, ob, r, n2, hid, gp, res = kept[layer]
        dz, dr, drb, gs, es, dst, s_dz, s_g, s_dr, s_sh2, s_gn2 = back_mlp(
            layer, place, g, gp, r, o, inv, ph, vecs, wo, wu, wd
        )
        lasts = others(dst, -1)
        g_down = reduce_grad(hid, g, layer)
        g_up = reduce_grad(n2, dz, layer)
        g_out = reduce_grad(ob, drb, layer)
        dqkv, du, mg, s_q, s_sh1, s_gn1 = back_mix(
            layer, place, qkv, ph, gs, es, u, dr, vecs, bd, firsts, lasts, wq
        )
        g_qkv_ = reduce_grad(a, dqkv, layer)
        bias = jnp.concatenate([s_sh1, s_q, s_dr, s_sh2, s_dz, s_g], 1).reshape(n, -1)
        gain = jnp.concatenate([s_gn1, s_gn2], 1).reshape(n, -1)
        flat = jnp.concatenate([mg[:, :, :HEAD].reshape(n, -1), bias, gain], 1)
        flat = jnp.pad(flat, ((0, 0), (0, padded - unit))).reshape(nz, 2, -1, CH)
        flat = flat + swap_d(flat)
        pair = jnp.where(y == 0, flat, flat[:, ::-1])
        small_grad = after_core(pair[:, 0], pair[:, 1], layer)
        results[layer] = (g_qkv_, g_out, g_up, g_down, small_grad)
        input_grads[layer] = du
        g = du

    def deliver(pair):
        own = jnp.where(x == 0, pair[0], pair[1]).reshape(4, CH, D)
        other = jnp.where(x == 0, pair[1], pair[0]).reshape(4, CH, D)
        halves = []
        for flip, source in enumerate((own, other)):
            got = []
            for s in range(4):
                part = lax.dynamic_index_in_dim(source, (i_seq + s) % 4, 0, False)

                def rule(xx, dd, k, s=s, flip=flip):
                    return (xx ^ flip, dd, (k % group) * 4 + (k // group + s) % 4)

                got.append(move(part, rule))
            ring = jnp.stack(got[::-1] + got[::-1])
            halves.append(lax.dynamic_slice_in_dim(ring, 3 - j % 4, 4, 0))
        micro = [jnp.where(x == 0, halves[0], halves[1]), jnp.where(x == 0, halves[1], halves[0])]
        return jnp.stack(micro, 1)[None]

    layer_out = deliver((kept[0][-1], kept[1][-1]))
    grads_out = deliver(input_grads)
    final = [jnp.where(x == 0, p, q) for p, q in zip(results[0], results[1])]
    mats = [joined(m)[None] for m in final[:4]]
    flat = final[4].reshape(1, -1)
    m, b = rows[4] * HEAD, rows[5]
    return (
        layer_out,
        grads_out,
        mats[0],
        mats[1],
        mats[2],
        mats[3],
        flat[:, :m].reshape(1, rows[4], HEAD),
        flat[:, m : m + b],
        flat[:, m + b : unit],
    )


def solution(mesh):
    tokens = P("dp", None, "seq", None)
    matrix = P("section", "seq", None)
    vector = P("section", "seq")
    stacked = P("section", "dp", None, "seq", None)
    return jax.shard_map(
        shards,
        mesh=mesh,
        in_specs=(tokens, tokens) + (matrix,) * 5 + (vector,) * 2,
        out_specs=(stacked, stacked) + (matrix,) * 5 + (vector,) * 2,
        check_vma=False,
    )
```

```python
import functools
from typing import Any, NamedTuple

import jax
import jax.numpy as jnp
from jax import lax
from jax.experimental import pallas as pl
from jax.experimental.pallas import tpu as pltpu
from jax.sharding import PartitionSpec as P


D = 768
FF = 3072
H = 12
HEAD = 64
BLOCK = 64


MAXIMUM_ACCURACY = lax.Precision.HIGHEST
NORM_EPSILON = 1e-05


def carried_in(part, axis, combine, identity, reverse):
    count = lax.axis_size(axis)
    place = lax.axis_index(axis)
    ahead = count - 1 - place if reverse else place
    gathered = jax.tree.map(lambda a: lax.all_gather(a, axis), part)
    state = jax.tree.map(lambda a, e: jnp.zeros_like(a) + jnp.asarray(e, a.dtype), part, identity)

    def one(lap, state):
        source = count - 1 - lap if reverse else lap
        return combine(
            state, jax.tree.map(lambda a: lax.dynamic_index_in_dim(a, source, 0, False), gathered)
        )

    return lax.fori_loop(0, ahead, one, state)


def shifted(value, axis, steps):
    count = lax.axis_size(axis)
    leading, last = (max(0, -steps), min(count, count - steps))
    return lax.ppermute(value, axis, [(source, source + steps) for source in range(leading, last)])


def normalize(values, gain_vector, shift_vector):
    average = jnp.mean(values, -1, keepdims=True)
    centred = values - average
    spread = jnp.mean(centred * centred, -1, keepdims=True)
    return centred * lax.rsqrt(spread + NORM_EPSILON) * gain_vector + shift_vector


def features(logits):
    return jnp.concatenate([jax.nn.softmax(logits, -1), jax.nn.softmax(-logits, -1)], -1)


def gelu_tanh(values):
    return jax.nn.gelu(values, approximate=True)


def adding(earlier, later_part):
    return jax.tree.map(jnp.add, earlier, later_part)


def across_rows(left_side, right_side):
    return lax.dot_general(
        left_side, right_side, (((0,), (0,)), ((), ())), preferred_element_type=jnp.float32
    )


def against_rows(left_side, right_side):
    return lax.dot_general(
        left_side, right_side, (((1,), (1,)), ((), ())), preferred_element_type=jnp.float32
    )


def precise(pattern, left_side, right_side):
    return jnp.einsum(pattern, left_side, right_side, precision=MAXIMUM_ACCURACY)


def causal_mask():
    places = lax.broadcasted_iota(jnp.int32, (BLOCK, BLOCK), 0)
    others = lax.broadcasted_iota(jnp.int32, (BLOCK, BLOCK), 1)
    return (others <= places).astype(jnp.float32)


def in_blocks(source_array, batch_rows):
    return source_array.reshape((batch_rows, -1, BLOCK) + source_array.shape[1:])


def prepare(gathered):
    qkv_full, out_full, up_full, down_full, map_full, bias_full, gain_full = [
        piece_array[0] for piece_array in gathered
    ]
    feature_maps = map_full.reshape(2, H, HEAD, HEAD)
    vectors = bias_full.astype(jnp.float32)
    scales = gain_full.astype(jnp.float32)
    pieces = (
        vectors[:D],
        vectors[D : 4 * D],
        vectors[4 * D : 5 * D],
        vectors[5 * D : 6 * D],
        vectors[6 * D : 6 * D + FF],
        vectors[6 * D + FF :],
        scales[:D],
        scales[D:],
    )
    return (qkv_full, out_full, up_full, down_full, feature_maps, pieces)


def block_sums(query_map, key_map, value_rows, batch_rows):
    query_blocks = in_blocks(query_map, batch_rows)
    key_blocks = in_blocks(key_map, batch_rows)
    value_blocks = in_blocks(value_rows, batch_rows).astype(jnp.float32)
    query_wide = query_blocks.astype(jnp.float32)
    key_wide = key_blocks.astype(jnp.float32)
    score_matrix = (
        jnp.einsum(
            "bcqhf,bckhf->bchqk", query_blocks, key_blocks, preferred_element_type=jnp.float32
        )
        * causal_mask()
    )
    block_state = precise("bckhf,bckhe->bchfe", key_wide, value_blocks)
    block_total = jnp.sum(key_wide, 2)
    return (query_wide, key_wide, value_blocks, score_matrix, block_state, block_total)


def attend(query_map, key_map, value_rows, initial, batch_rows):
    query_wide, key_wide, value_blocks, score_matrix, block_state, block_total = block_sums(
        query_map, key_map, value_rows, batch_rows
    )
    state_sum = jnp.sum(block_state, 1)
    total_sum = jnp.sum(block_total, 1)
    identity = (jnp.zeros_like(state_sum), jnp.zeros_like(total_sum))
    earlier = carried_in((state_sum, total_sum), "seq", adding, identity, False)
    overall = lax.psum((state_sum, total_sum), "seq")
    start_state = initial[0] + earlier[0]
    start_total = initial[1] + earlier[1]
    block_before = start_state[:, None] + jnp.cumsum(block_state, 1) - block_state
    total_before = start_total[:, None] + jnp.cumsum(block_total, 1) - block_total
    numerator = precise("bchqk,bckhe->bcqhe", score_matrix, value_blocks) + precise(
        "bcqhf,bchfe->bcqhe", query_wide, block_before
    )
    denominator = jnp.swapaxes(jnp.sum(score_matrix, -1), 2, 3) + precise(
        "bcqhf,bchf->bcqh", query_wide, total_before
    )
    mixture = numerator / denominator[..., None]
    handed = (initial[0] + overall[0], initial[1] + overall[1])
    return (mixture.reshape(value_rows.shape), denominator, (start_state, start_total), handed)


def attend_back(
    mixture_grad, query_map, key_map, value_rows, mixture, denominator, starts, future, batch_rows
):
    query_wide, key_wide, value_blocks, score_matrix, block_state, block_total = block_sums(
        query_map, key_map, value_rows, batch_rows
    )
    block_before = starts[0][:, None] + jnp.cumsum(block_state, 1) - block_state
    total_before = starts[1][:, None] + jnp.cumsum(block_total, 1) - block_total
    scaled = in_blocks(mixture_grad, batch_rows) / denominator[..., None]
    denominator_grad = -jnp.sum(scaled * in_blocks(mixture, batch_rows), -1)
    score_grad = (
        precise("bcqhe,bckhe->bchqk", scaled, value_blocks)
        + jnp.swapaxes(denominator_grad, 2, 3)[..., None]
    ) * causal_mask()
    query_grad = precise("bchqk,bckhf->bcqhf", score_grad, key_wide) + precise(
        "bcqhe,bchfe->bcqhf", scaled, block_before
    )
    query_grad = query_grad + denominator_grad[..., None] * total_before[:, :, None]
    state_grad = precise("bcqhf,bcqhe->bchfe", query_wide, scaled)
    total_grad = precise("bcqhf,bcqh->bchf", query_wide, denominator_grad)
    state_sum = jnp.sum(state_grad, 1)
    total_sum = jnp.sum(total_grad, 1)
    identity = (jnp.zeros_like(state_sum), jnp.zeros_like(total_sum))
    later_sums = carried_in((state_sum, total_sum), "seq", adding, identity, True)
    overall = lax.psum((state_sum, total_sum), "seq")
    ahead_state = future[0] + later_sums[0]
    ahead_total = future[1] + later_sums[1]
    rest_state = ahead_state[:, None] + state_sum[:, None] - jnp.cumsum(state_grad, 1)
    rest_total = ahead_total[:, None] + total_sum[:, None] - jnp.cumsum(total_grad, 1)
    key_grad = precise("bchqk,bcqhf->bckhf", score_grad, query_wide) + precise(
        "bckhe,bchfe->bckhf", value_blocks, rest_state
    )
    key_grad = key_grad + rest_total[:, :, None]
    value_grad = precise("bchqk,bcqhe->bckhe", score_matrix, scaled) + precise(
        "bckhf,bchfe->bckhe", key_wide, rest_state
    )
    return (
        query_grad.reshape(query_map.shape),
        key_grad.reshape(key_map.shape),
        value_grad.reshape(value_rows.shape),
        overall,
    )


def forward(tokens, params, initial):
    qkv_full, out_full, up_full, down_full, feature_maps, pieces = params
    shift_one, qkv_bias, out_bias, shift_two, up_bias, down_bias, gain_one, gain_two = pieces
    batch_rows = tokens.shape[0]
    flattened = tokens.reshape(-1, D)
    row_count = flattened.shape[0]
    normed = normalize(flattened, gain_one, shift_one).astype(jnp.bfloat16)
    projected = (jnp.dot(normed, qkv_full, preferred_element_type=jnp.float32) + qkv_bias).astype(
        jnp.bfloat16
    )
    query_rows = projected[:, :D].reshape(row_count, H, HEAD)
    key_rows = projected[:, D : 2 * D].reshape(row_count, H, HEAD)
    value_rows = projected[:, 2 * D :].reshape(row_count, H, HEAD)
    query_logits = jnp.einsum(
        "rhe,hef->rhf", query_rows, feature_maps[0], preferred_element_type=jnp.float32
    )
    key_logits = jnp.einsum(
        "rhe,hef->rhf", key_rows, feature_maps[1], preferred_element_type=jnp.float32
    )
    query_map = features(query_logits).astype(jnp.bfloat16)
    key_map = features(key_logits).astype(jnp.bfloat16)
    mixture, denominator, starts, handed = attend(
        query_map, key_map, value_rows, initial, batch_rows
    )
    mixture_low = mixture.reshape(row_count, D).astype(jnp.bfloat16)
    residual = (
        flattened + jnp.dot(mixture_low, out_full, preferred_element_type=jnp.float32) + out_bias
    )
    normed_two = normalize(residual, gain_two, shift_two).astype(jnp.bfloat16)
    before_act = jnp.dot(normed_two, up_full, preferred_element_type=jnp.float32) + up_bias
    hidden = gelu_tanh(before_act).astype(jnp.bfloat16)
    result = residual + jnp.dot(hidden, down_full, preferred_element_type=jnp.float32) + down_bias
    kept_values = (
        flattened,
        normed,
        projected,
        query_logits,
        key_logits,
        query_map,
        key_map,
        mixture,
        denominator,
        starts,
        residual,
        normed_two,
        before_act,
        hidden,
    )
    return (result.reshape(tokens.shape), handed, kept_values)


def backward(upstream, params, kept_values, future):
    qkv_full, out_full, up_full, down_full, feature_maps, pieces = params
    shift_one, qkv_bias, out_bias, shift_two, up_bias, down_bias, gain_one, gain_two = pieces
    (
        flattened,
        normed,
        projected,
        query_logits,
        key_logits,
        query_map,
        key_map,
        mixture,
        denominator,
        starts,
        residual,
        normed_two,
        before_act,
        hidden,
    ) = kept_values
    batch_rows = upstream.shape[0]
    row_count = flattened.shape[0]
    out_grad = upstream.reshape(row_count, D)
    down_bias_grad = jnp.sum(out_grad, 0)
    out_low = out_grad.astype(jnp.bfloat16)
    down_weight_grad = across_rows(hidden, out_low)
    hidden_grad = against_rows(out_low, down_full)
    _, gelu_back = jax.vjp(gelu_tanh, before_act)
    before_grad = gelu_back(hidden_grad)[0].astype(jnp.bfloat16)
    up_bias_grad = jnp.sum(before_grad.astype(jnp.float32), 0)
    up_weight_grad = across_rows(normed_two, before_grad)
    normed_two_grad = against_rows(before_grad, up_full)
    _, norm_back_two = jax.vjp(normalize, residual, gain_two, shift_two)
    residual_part, gain_two_grad, shift_two_grad = norm_back_two(normed_two_grad)
    residual_grad = out_grad + residual_part
    out_bias_grad = jnp.sum(residual_grad, 0)
    residual_low = residual_grad.astype(jnp.bfloat16)
    mixture_low = mixture.reshape(row_count, D).astype(jnp.bfloat16)
    out_weight_grad = across_rows(mixture_low, residual_low)
    mixture_grad = against_rows(residual_low, out_full).reshape(row_count, H, HEAD)
    query_rows = projected[:, :D].reshape(row_count, H, HEAD)
    key_rows = projected[:, D : 2 * D].reshape(row_count, H, HEAD)
    value_rows = projected[:, 2 * D :].reshape(row_count, H, HEAD)
    query_map_grad, key_map_grad, value_grad, handed = attend_back(
        mixture_grad,
        query_map,
        key_map,
        value_rows,
        mixture,
        denominator,
        starts,
        future,
        batch_rows,
    )
    _, query_back = jax.vjp(features, query_logits)
    query_logit_grad = query_back(query_map_grad)[0]
    _, key_back = jax.vjp(features, key_logits)
    key_logit_grad = key_back(key_map_grad)[0]
    maps_wide = feature_maps.astype(jnp.float32)
    query_grad = precise("rhf,hef->rhe", query_logit_grad, maps_wide[0])
    key_grad = precise("rhf,hef->rhe", key_logit_grad, maps_wide[1])
    map_weight_grad = jnp.stack(
        [
            precise("rhe,rhf->hef", query_rows.astype(jnp.float32), query_logit_grad),
            precise("rhe,rhf->hef", key_rows.astype(jnp.float32), key_logit_grad),
        ]
    ).reshape(2 * H * HEAD, HEAD)
    projected_grad = jnp.concatenate(
        [
            query_grad.reshape(row_count, D),
            key_grad.reshape(row_count, D),
            value_grad.reshape(row_count, D),
        ],
        1,
    ).astype(jnp.bfloat16)
    qkv_bias_grad = jnp.sum(projected_grad.astype(jnp.float32), 0)
    qkv_weight_grad = across_rows(normed, projected_grad)
    normed_grad = against_rows(projected_grad, qkv_full)
    _, norm_back_one = jax.vjp(normalize, flattened, gain_one, shift_one)
    input_part, gain_one_grad, shift_one_grad = norm_back_one(normed_grad)
    input_grad = residual_grad + input_part
    bias_grad = jnp.concatenate(
        [shift_one_grad, qkv_bias_grad, out_bias_grad, shift_two_grad, up_bias_grad, down_bias_grad]
    )
    gain_grad = jnp.concatenate([gain_one_grad, gain_two_grad])
    layer_grads = (
        qkv_weight_grad,
        out_weight_grad,
        up_weight_grad,
        down_weight_grad,
        map_weight_grad,
        bias_grad,
        gain_grad,
    )
    return (input_grad.reshape(upstream.shape), handed, layer_grads)


def reduce_grads(full_grads):
    g_qkv, g_out, g_up, g_down, g_map, g_bias, g_gain = full_grads
    s_qkv, s_out, s_up, s_down, s_map, s_bias, s_gain = (
        lax.psum_scatter(g_qkv, "seq", scatter_dimension=1, tiled=True),
        lax.psum_scatter(g_out, "seq", scatter_dimension=1, tiled=True),
        lax.psum_scatter(g_up, "seq", scatter_dimension=1, tiled=True),
        lax.psum_scatter(g_down, "seq", scatter_dimension=1, tiled=True),
        lax.psum_scatter(g_map, "seq", scatter_dimension=1, tiled=True),
        lax.psum_scatter(g_bias, "seq", scatter_dimension=1, tiled=True),
        lax.psum_scatter(g_gain, "seq", scatter_dimension=1, tiled=True),
    )
    return lax.psum((s_qkv, s_out, s_up, s_down, s_map, s_bias, s_gain), "dp")


def plain_shards(
    inputs, cotangent, qkv_weight, out_weight, up_weight, down_weight, map_weight, biases, gains
):
    section_index = lax.axis_index("section")
    batch_rows = inputs.shape[0]
    micro_count = inputs.shape[1]
    gathered = (
        lax.all_gather(qkv_weight.astype(jnp.bfloat16), "seq", axis=1, tiled=True),
        lax.all_gather(out_weight.astype(jnp.bfloat16), "seq", axis=1, tiled=True),
        lax.all_gather(up_weight.astype(jnp.bfloat16), "seq", axis=1, tiled=True),
        lax.all_gather(down_weight.astype(jnp.bfloat16), "seq", axis=1, tiled=True),
        lax.all_gather(map_weight.astype(jnp.bfloat16), "seq", axis=1, tiled=True),
        lax.all_gather(biases.astype(jnp.bfloat16), "seq", axis=1, tiled=True),
        lax.all_gather(gains.astype(jnp.bfloat16), "seq", axis=1, tiled=True),
    )
    params = prepare(gathered)
    empty_state = (
        jnp.zeros((batch_rows, H, 2 * HEAD, HEAD), jnp.float32),
        jnp.zeros((batch_rows, H, 2 * HEAD), jnp.float32),
    )
    blank_rows = jnp.zeros(inputs.shape[:1] + inputs.shape[2:], jnp.bfloat16)
    moments = jnp.arange(micro_count + 1, dtype=jnp.int32)

    def forward_moment(carry, moment):
        handed, arriving = carry
        own_tokens = lax.dynamic_index_in_dim(
            inputs, jnp.minimum(moment, micro_count - 1), 1, False
        )
        source = jnp.where(section_index == 0, own_tokens, arriving).astype(jnp.float32)
        carried = moment - section_index >= 1
        initial = (jnp.where(carried, handed[0], 0.0), jnp.where(carried, handed[1], 0.0))
        result, handed_next, kept_values = forward(source, params, initial)
        outgoing = result.astype(jnp.bfloat16)
        arriving_next = shifted(outgoing, "section", 1)
        return ((handed_next, arriving_next), (outgoing, kept_values))

    _, (result_stack, kept_stack) = lax.scan(forward_moment, (empty_state, blank_rows), moments)
    regathered = (
        lax.all_gather(qkv_weight.astype(jnp.bfloat16), "seq", axis=1, tiled=True),
        lax.all_gather(out_weight.astype(jnp.bfloat16), "seq", axis=1, tiled=True),
        lax.all_gather(up_weight.astype(jnp.bfloat16), "seq", axis=1, tiled=True),
        lax.all_gather(down_weight.astype(jnp.bfloat16), "seq", axis=1, tiled=True),
        lax.all_gather(map_weight.astype(jnp.bfloat16), "seq", axis=1, tiled=True),
        lax.all_gather(biases.astype(jnp.bfloat16), "seq", axis=1, tiled=True),
        lax.all_gather(gains.astype(jnp.bfloat16), "seq", axis=1, tiled=True),
    )
    back_params = prepare(regathered)
    zero_grads = (
        jnp.zeros((D, 3 * D), jnp.float32),
        jnp.zeros((D, D), jnp.float32),
        jnp.zeros((D, FF), jnp.float32),
        jnp.zeros((FF, D), jnp.float32),
        jnp.zeros((2 * H * HEAD, HEAD), jnp.float32),
        jnp.zeros((7 * D + FF,), jnp.float32),
        jnp.zeros((2 * D,), jnp.float32),
    )

    def backward_moment(carry, pieces):
        future, returning, grad_sums = carry
        slot, kept_values = pieces
        chosen = slot - section_index
        own_grad = lax.dynamic_index_in_dim(cotangent, jnp.maximum(slot - 1, 0), 1, False)
        live = (chosen >= 0) & (chosen < micro_count)
        upstream = jnp.where(section_index == 1, own_grad, returning).astype(jnp.float32)
        upstream = jnp.where(live, upstream, 0.0)
        later_micro = live & (chosen < micro_count - 1)
        ahead_part = (
            jnp.where(later_micro, future[0], 0.0),
            jnp.where(later_micro, future[1], 0.0),
        )
        input_grad, future_next, layer_grads = backward(
            upstream, back_params, kept_values, ahead_part
        )
        outgoing = input_grad.astype(jnp.bfloat16)
        grad_sums = tuple((previous + current for previous, current in zip(grad_sums, layer_grads)))
        returning_next = shifted(outgoing, "section", -1)
        return ((future_next, returning_next, grad_sums), outgoing)

    (_, _, grad_sums), grad_stack = lax.scan(
        backward_moment, (empty_state, blank_rows, zero_grads), (moments, kept_stack), reverse=True
    )
    layer_out = jnp.stack(
        [
            lax.dynamic_index_in_dim(result_stack, micro_index + section_index, 0, False)
            for micro_index in range(micro_count)
        ],
        1,
    )
    input_grads = jnp.stack(
        [
            lax.dynamic_index_in_dim(grad_stack, micro_index + section_index, 0, False)
            for micro_index in range(micro_count)
        ],
        1,
    )
    full_grads = tuple((grad_array[None] for grad_array in grad_sums))
    reduced = reduce_grads(full_grads)
    return (
        layer_out[None],
        input_grads[None],
        reduced[0],
        reduced[1],
        reduced[2],
        reduced[3],
        reduced[4],
        reduced[5],
        reduced[6],
    )


CH = 128
PAIRS = H // 2
QB = 2 * H * HEAD
STATE_ROWS = D + 16
EPS = 1e-05
TILE = 256
AXES = ("section", "dp", "seq")
MESH = pl.DeviceIdType.MESH
f32 = jnp.float32
bf16 = jnp.bfloat16
GELU_C = 0.7978845608028654
GELU_A = 0.044715
SMALL_ROWS = 208
VEC_ROWS = 72
GAIN_ROWS = 16
SHIFT1, QKV_BIAS, OUT_BIAS, SHIFT2, UP_BIAS, DOWN_BIAS = 0, 6, 24, 30, 36, 60


class Kept(NamedTuple):
    a: Any
    qkv: Any
    ph: Any
    o: Any
    inv: Any
    ob: Any
    r: Any
    n2: Any
    hid: Any
    gp: Any
    res: Any
    pre: Any


class ForwardRefs(NamedTuple):
    tokens: Any
    cot: Any
    small: Any
    wq: Any
    wo: Any
    wu: Any
    wd: Any
    gq: Any
    go: Any
    gu: Any
    gd: Any
    lay: Any
    gv: Any
    bd: Any
    tok_out: Any
    cot_out: Any


class ForwardScratch(NamedTuple):
    tok: Any
    sm: Any
    vec: Any
    st: Any
    got: Any
    vq: Any
    vo: Any
    vu: Any
    vd: Any
    g_send: Any
    g_recv: Any
    g_local: Any
    c_send: Any
    c_recv: Any
    s_send: Any
    s_recv: Any
    d_send: Any
    d_recv: Any
    w_sem: Any
    o_sem: Any
    m_sem: Any


class Weights(NamedTuple):
    q: Any
    o: Any
    u: Any
    d: Any = None


VMEM = pl.BlockSpec(memory_space=pltpu.VMEM)
SMEM = pl.BlockSpec(memory_space=pltpu.SMEM)
ANY = pl.BlockSpec(memory_space=pl.ANY)


def nn(a, b):
    return lax.dot_general(a, b, (((1,), (0,)), ((), ())), preferred_element_type=f32)


def nt(a, b):
    return lax.dot_general(a, b, (((1,), (1,)), ((), ())), preferred_element_type=f32)


def tn(a, b):
    return lax.dot_general(a, b, (((0,), (0,)), ((), ())), preferred_element_type=f32)


def loop(count, body, events=None):
    events = events or {}

    def step(i, c):
        body(i)
        for at, event in events.items():

            @pl.when(i == at)
            def _():
                event()

        return c

    lax.fori_loop(0, count, step, 0)


def span(i, size):
    return pl.ds(pl.multiple_of(i * size, size), size)


def wide(ref, layer, row, count):
    return jnp.concatenate([ref[layer, pl.ds(row + i, 1), :] for i in range(count)], 1)


def finish(dst, sem):
    pltpu.make_async_copy(dst, dst, sem).wait()


def shape(dims, kind):
    return jax.ShapeDtypeStruct(dims, kind)


def call(kernel, outs, scratch, specs, args, flops, out_specs=None, vmem=60, cid=None):
    if out_specs is None:
        out_specs = [VMEM] * len(outs)
    moved = sum(a.size * a.dtype.itemsize for a in args if a.ndim > 0)
    moved += sum(o.size * o.dtype.itemsize for o in outs)
    params = dict(vmem_limit_bytes=vmem * 1024 * 1024)
    if cid is not None:
        params.update(collective_id=cid, has_side_effects=True)
    return pl.pallas_call(
        kernel,
        out_shape=outs,
        in_specs=specs,
        out_specs=out_specs,
        scratch_shapes=scratch,
        compiler_params=pltpu.CompilerParams(**params),
        cost_estimate=pl.CostEstimate(flops=flops, bytes_accessed=moved, transcendentals=0),
    )(*args)


def standardize(u):
    cen = u - jnp.mean(u, -1, keepdims=True)
    rstd = lax.rsqrt(jnp.mean(cen * cen, -1, keepdims=True) + EPS)
    return cen * rstd, rstd


def lanes(rows):
    return lax.broadcasted_iota(jnp.int32, (rows, CH), 1)


def half_sums(t, low):
    s1 = jnp.sum(jnp.where(low, t, 0.0), -1, keepdims=True)
    s2 = jnp.sum(jnp.where(low, 0.0, t), -1, keepdims=True)
    return jnp.where(low, s1, s2)


def half_softmax(l, low):
    m1 = jnp.max(jnp.where(low, l, -jnp.inf), -1, keepdims=True)
    m2 = jnp.max(jnp.where(low, -jnp.inf, l), -1, keepdims=True)
    p = jnp.exp(l - jnp.where(low, m1, m2))
    return p / half_sums(p, low)


class Place:
    def __init__(self, n):
        self.n, self.nz, self.group = n, n // 2, n // 4
        self.x = lax.axis_index("section")
        self.d = lax.axis_index("dp")
        self.j = lax.axis_index("seq")
        self.z, self.y = lax.div(self.j, 2), lax.rem(self.j, 2)
        self.i = lax.div(self.j, self.group)
        self.jj = lax.rem(self.j, self.group)
        self.r = self.x * self.group + self.jj

    def at(self, x=None, d=None, z=None, y=None, j=None):
        x = self.x if x is None else x
        d = self.d if d is None else d
        if j is None:
            j = (self.z if z is None else z) * 2 + (self.y if y is None else y)
        return (x, d, j)

    def zpos(self, o):
        return lax.rem(self.z + o + self.nz, self.nz)

    def meet(self):
        barrier = pltpu.get_barrier_semaphore()
        for dx in range(2):
            for o in range(self.n):
                if dx == 0 and o == 0:
                    continue
                other = (
                    lax.rem(self.x + dx, 2),
                    self.d,
                    lax.rem(self.j + o, self.n),
                )
                pl.semaphore_signal(barrier, inc=1, device_id=other, device_id_type=MESH)
        pl.semaphore_signal(
            barrier, inc=1, device_id=(self.x, 1 - self.d, self.j), device_id_type=MESH
        )
        pl.semaphore_wait(barrier, 2 * self.n)


def remote(src, dst, send, recv, to):
    return pltpu.make_async_remote_copy(
        src_ref=src, dst_ref=dst, send_sem=send, recv_sem=recv, device_id=to, device_id_type=MESH
    )


class Gather:
    def __init__(self, place, src, buf, send, recv, local, y_last, halves=True):
        self.p, self.src, self.buf = place, src, buf
        self.send, self.recv, self.local = send, recv, local
        self.y_last, self.halves = y_last, halves
        self.width = src.shape[1]
        self.sent = []

    def columns(self):
        if not self.halves:
            return slice(None)
        return pl.ds(pl.multiple_of(self.p.d * self.width, CH), self.width)

    def shard(self, x, z, y):
        return self.buf.at[x, z, y, :, self.columns()]

    def column(self, x, y):
        return self.buf.at[x, :, y, :, self.columns()]

    def go(self, src, dst, slot, to):
        remote(src, dst, self.send.at[slot], self.recv.at[slot], to).start()
        self.sent.append(slot)

    def got(self, ref, slot):
        finish(ref, self.recv.at[slot])

    def start(self):
        p = self.p
        own = self.shard(p.x, p.z, p.y)
        pltpu.make_async_copy(self.src, own, self.local).start()
        for o in range(1, p.nz):
            self.go(self.src, own, o - 1, p.at(z=p.zpos(o)))

    def first(self, o):
        p = self.p
        zi = p.zpos(-o)
        here = self.shard(p.x, zi, p.y)
        src = self.src if o == 0 else here
        if o > 0:
            self.got(here, o - 1)
        self.go(src, here, 3 + o, p.at(y=1 - p.y))
        self.go(src, here, 7 + o, p.at(x=1 - p.x))

    def second(self, o):
        p = self.p
        zi = p.zpos(-o)
        if self.y_last:
            here = self.shard(1 - p.x, zi, p.y)
            self.got(here, 7 + o)
            self.go(here, here, 11 + o, p.at(y=1 - p.y))
        else:
            here = self.shard(p.x, zi, 1 - p.y)
            self.got(here, 3 + o)
            self.go(here, here, 11 + o, p.at(x=1 - p.x))

    def core(self, q):
        p = self.p
        x = p.x if q < 2 else 1 - p.x
        y = p.y if q % 2 == 0 else 1 - p.y
        if q == 0:
            own = self.shard(p.x, p.z, p.y)
            finish(own, self.local)
        elif q == 3 or q == (1 if self.y_last else 2):
            base = 11 if q == 3 else (3 if self.y_last else 7)
            for o in range(p.nz):
                self.got(self.shard(x, p.zpos(-o), y), base + o)
        if self.halves:
            part = self.column(x, y)
            self.go(part, part, 15 + q, p.at(d=1 - p.d))

    def done(self):
        p = self.p
        if self.halves:
            for q in range(4):
                x = p.x if q < 2 else 1 - p.x
                y = p.y if q % 2 == 0 else 1 - p.y
                other = pl.ds(pl.multiple_of((1 - p.d) * self.width, CH), self.width)
                self.got(self.buf.at[x, :, y, :, other], 15 + q)

    def close(self):
        p = self.p
        for slot in self.sent:
            ref = self.column(p.x, p.y) if slot >= 15 else self.shard(p.x, p.z, p.y)
            finish(ref, self.send.at[slot])


def forward_kernel(n, *refs):
    ref = ForwardRefs(*refs[:16])
    saved = [Kept(*refs[16:28]), Kept(*refs[28:40])]
    v = Kept(*refs[40:52])
    own = ForwardScratch(*refs[52:])
    p = Place(n)
    nz, group = p.nz, p.group
    t = v.a.shape[0]
    nc = t // CH
    p.meet()

    def gather(k, src, buf, y_last, halves=True):
        return Gather(
            p, src, buf, own.g_send.at[k], own.g_recv.at[k], own.g_local.at[k], y_last, halves
        )

    gs = gather(0, ref.small, own.sm, False, False)
    gq = gather(1, ref.wq, ref.gq, True)
    go = gather(2, ref.wo, ref.go, False)
    gu = gather(3, ref.wu, ref.gu, False)
    gd = gather(4, ref.wd, ref.gd, True)
    gathers = (gs, gq, go, gu, gd)

    def collect(which, s):
        i = lax.rem(p.j + s, 4)
        to = i * group + lax.div(p.j, 4)
        slot = lax.rem(p.j, 4)
        src = (ref.cot if which else ref.tokens).at[i, p.x]
        dst = (ref.cot_out if which else own.tok).at[span(slot, CH), :]
        send, recv = own.c_send.at[which], own.c_recv.at[which]
        copy = remote(src, dst, send.at[s], recv.at[slot], p.at(j=to))

        @pl.when(to != p.j)
        def _():
            copy.start()

        @pl.when(to == p.j)
        def _():
            pltpu.make_async_copy(src, dst, recv.at[slot]).start()

        def close():
            @pl.when(to != p.j)
            def _():
                copy.wait_send()

        return close

    gs.start()
    gs.first(0)
    gq.start()
    gq.first(0)
    closing = [collect(0, s) for s in range(4)]
    for o in range(1, nz):
        gs.first(o)
        gq.first(o)
    go.start()
    gu.start()
    go.first(0)
    gu.first(0)
    for o in range(nz):
        gs.second(o)
    for o in range(nz):
        gq.second(o)
    for q in range(4):
        gs.core(q)
    for q in range(3):
        gq.core(q)

    vec, gv, bd, sm = own.vec, ref.gv, ref.bd, own.sm
    vec[...] = jnp.zeros(vec.shape, f32)
    gv[...] = jnp.zeros(gv.shape, f32)
    bd[...] = jnp.zeros(bd.shape, bf16)
    for layer in range(2):
        for k in range(n):
            part = sm[layer, k // 2, k % 2, 0:16, :].astype(f32)
            row, grow = (33 * k) // 4, (3 * k) // 2
            vec[layer, row : row + 9, :] += part[0:9]
            gv[layer, grow : grow + 2, :] += part[9:11]
        for head in range(2 * H):
            k, at, odd = head // 3, 16 + (head % 3) * HEAD, head % 2
            bd[layer, head // 2, odd * HEAD : (odd + 1) * HEAD, odd * CH : (odd + 1) * CH] = sm[
                layer, k // 2, k % 2, at : at + HEAD, :
            ]

    for k in range(4):
        finish(own.tok.at[pl.ds(k * CH, CH), :], own.c_recv.at[0, k])

    def load(g, dst, layer, k):
        pltpu.make_async_copy(g.buf.at[layer], dst, own.w_sem.at[k]).start()

    def loaded(dst, k):
        finish(dst, own.w_sem.at[k])

    pending = [[], []]

    def save(layer, *sources):
        for src in sources:
            k = [src is x for x in v].index(True)
            if src is v.res:
                src = src.at[layer]
            copy = pltpu.make_async_copy(src, saved[layer][k], own.o_sem.at[layer, k])
            copy.start()
            pending[layer].append(copy)

    flat = Weights(
        own.vq.reshape(D, 3 * D),
        own.vo.reshape(D, D),
        own.vu.reshape(D, FF),
        own.vd.reshape(FF, D),
    )
    low = lanes(CH) < HEAD
    tril = lax.broadcasted_iota(jnp.int32, (CH, CH), 0) >= lanes(CH)

    def norm_rows(layer, src, dst, which, shift):
        gain = wide(gv, layer, which * 6, 6)
        bias = wide(vec, layer, shift, 6)

        def body(i):
            xh, _ = standardize(src[span(i, CH), :].astype(f32))
            dst[span(i, CH), :] = (xh * gain + bias).astype(bf16)

        loop(nc, body)

    def bias_cols(layer, at, j):
        return wide(vec, layer, at + 2 * j, 2)

    def project(layer, u, events):
        a, qkv, ph, st = v.a, v.qkv, v.ph, own.st
        if layer == 1:
            for copy in pending[0]:
                copy.wait()
        norm_rows(layer, u, a, 0, SHIFT1)
        loaded(own.vq, 0)
        save(layer, v.a)

        def column(j):
            cols = span(j, TILE)
            qkv[:, cols] = (
                nn(a[...], flat.q[:, cols]) + bias_cols(layer, QKV_BIAS, j)
            ).astype(bf16)

        loop(3 * D // TILE, column, events[0])
        save(layer, v.qkv)

        def pair(k):
            def rows(i):
                lg = nn(qkv[span(i, CH), span(k, CH)], bd[layer, k])
                for hh in range(2):
                    ph[span(i, CH), span(2 * k + hh, CH)] = half_softmax(
                        lg[:, hh * CH : (hh + 1) * CH], low
                    ).astype(bf16)

            loop(nc, rows)

        loop(2 * PAIRS, pair, events[1])
        save(layer, v.ph)

        def state(k):
            val = qkv[:, pl.ds(pl.multiple_of(2 * D + k * CH, CH), CH)]
            for hh in range(2):
                key = ph[:, pl.ds(pl.multiple_of((H + 2 * k + hh) * CH, CH), CH)]
                full = tn(val, key)
                st[layer, span(2 * k + hh, HEAD), :] = full[hh * HEAD : (hh + 1) * HEAD]
                st[layer, pl.ds(D + 2 * k + hh, 1), :] = jnp.sum(
                    key.astype(f32), 0, keepdims=True
                )

        loop(PAIRS, state)
        st[layer, D + H :, :] = jnp.zeros((STATE_ROWS - D - H, CH), f32)
        send_states(layer, st, 1)

    members = 2 * group

    def state_to(o, sign):
        other = p.r + sign * o
        return (lax.div(other, group), p.d, p.i * group + lax.rem(other, group))

    def send_states(layer, st, sign):
        for o in range(1, members):
            ok = (p.r + o < members) if sign > 0 else (p.r - o >= 0)

            @pl.when(ok)
            def _():
                remote(
                    st.at[layer],
                    own.got.at[layer, o - 1],
                    own.s_send.at[layer, o - 1],
                    own.s_recv.at[layer, o - 1],
                    state_to(o, sign),
                ).start()

    def take_states(layer, sign):
        pre = v.pre
        pre[...] = jnp.zeros(pre.shape, f32)
        for o in range(1, members):
            ok = (p.r - o >= 0) if sign > 0 else (p.r + o < members)

            @pl.when(ok)
            def _():
                finish(own.got.at[layer, o - 1], own.s_recv.at[layer, o - 1])
                pre[...] += own.got[layer, o - 1]

    def close_states(layer, sign):
        for o in range(1, members):
            ok = (p.r + o < members) if sign > 0 else (p.r - o >= 0)

            @pl.when(ok)
            def _():
                finish(own.st.at[layer], own.s_send.at[layer, o - 1])

    def mix(layer, u, events):
        qkv, ph, o_, inv, ob = v.qkv, v.ph, v.o, v.inv, v.ob
        r, n2, hid, gp = v.r, v.n2, v.hid, v.gp
        res = v.res.at[layer]
        take_states(layer, 1)
        save(layer, v.pre)
        s0 = v.pre

        def pair(k):
            cols = span(k, CH)
            s = s0[cols, :]
            tot = [s0[pl.ds(D + 2 * k + hh, 1), :] for hh in range(2)]
            for c in range(nc):
                rows = pl.ds(c * CH, CH)
                val = qkv[rows, pl.ds(pl.multiple_of(2 * D + k * CH, CH), CH)]
                sl = s.astype(bf16)
                done = []
                new = []
                for hh in range(2):
                    qh = ph[rows, span(2 * k + hh, CH)]
                    kh = ph[rows, pl.ds(pl.multiple_of((H + 2 * k + hh) * CH, CH), CH)]
                    score = jnp.where(tril, nt(qh, kh), 0.0)
                    num = nn(score.astype(bf16), val) + nt(qh, sl)
                    den = jnp.sum(score + qh.astype(f32) * tot[hh], -1, keepdims=True)
                    rec = 1.0 / den
                    done.append((num * rec, rec))
                    new.append(tn(val, kh)[hh * HEAD : (hh + 1) * HEAD])
                    tot[hh] = tot[hh] + jnp.sum(kh.astype(f32), 0, keepdims=True)
                s = s + jnp.concatenate(new, 0)
                both = jnp.where(low, done[0][0], done[1][0])
                o_[rows, cols] = both
                ob[rows, cols] = both.astype(bf16)
                inv[rows, cols] = jnp.where(low, done[0][1], done[1][1])

        loop(PAIRS, pair, events[0])
        save(layer, v.o, v.inv, v.ob)
        events[1]()
        loaded(own.vo, 1)

        def out_col(j):
            cols = span(j, TILE)
            r[:, cols] = (
                u[:, cols].astype(f32)
                + nn(ob[...], flat.o[:, cols])
                + bias_cols(layer, OUT_BIAS, j)
            )

        loop(D // TILE, out_col)
        norm_rows(layer, r, n2, 1, SHIFT2)
        save(layer, v.r, v.n2)
        events[2]()
        loaded(own.vu, 2)

        def up_col(j):
            cols = span(j, TILE)
            zt = nn(n2[...], flat.u[:, cols]) + bias_cols(layer, UP_BIAS, j)
            z2 = zt * zt
            th = jnp.tanh(GELU_C * zt * (1.0 + GELU_A * z2))
            half = 0.5 * (1.0 + th)
            hid[:, cols] = (zt * half).astype(bf16)
            gp[:, cols] = (
                half + 0.5 * zt * (1.0 - th * th) * (GELU_C * (1.0 + 3.0 * GELU_A * z2))
            ).astype(bf16)

        loop(FF // TILE, up_col, events[3])
        save(layer, v.hid, v.gp)
        events[4]()
        loaded(own.vd, 3)

        def down_col(j):
            cols = span(j, TILE)
            res[:, cols] = (
                r[:, cols] + nn(hid[...], flat.d[:, cols]) + bias_cols(layer, DOWN_BIAS, j)
            ).astype(bf16)

        loop(D // TILE, down_col)
        save(layer, v.res)
        for k in range(4):
            to = p.jj * 4 + k
            src = res.at[pl.ds(k * CH, CH), :]
            dst = ref.lay.at[0, p.i, p.x]
            slot = p.i * 2 + p.x
            mine = (to == p.j) & (p.x == layer)
            copy = remote(
                src, dst, own.d_send.at[layer, k], own.d_recv.at[slot], p.at(x=layer, j=to)
            )

            @pl.when(jnp.logical_not(mine))
            def _():
                copy.start()

            @pl.when(mine)
            def _():
                pltpu.make_async_copy(src, dst, own.d_recv.at[slot]).start()

            def close(copy=copy, mine=mine):
                @pl.when(jnp.logical_not(mine))
                def _():
                    copy.wait_send()

            closing.append(close)

    def run(*steps):
        def go_():
            for step in steps:
                step()

        return go_

    def each(count, fn, first=0):
        return [functools.partial(fn, o) for o in range(first, count)]

    nothing = run()
    gq.core(3)
    gq.done()
    load(gq, own.vq, 0, 0)
    tok_out = pltpu.make_async_copy(own.tok, ref.tok_out, own.m_sem)
    tok_out.start()
    project(
        0,
        own.tok,
        [
            {
                1: run(*each(nz, go.first, 1)),
                3: run(functools.partial(gu.first, 1)),
                5: run(functools.partial(gu.first, 2)),
                7: run(functools.partial(gu.first, 3), gd.start, functools.partial(gd.first, 0)),
            },
            {
                1: run(*each(nz, go.second)),
                3: run(*each(2, gu.second)),
                5: run(functools.partial(gu.second, 2), *each(3, go.core)),
                7: run(functools.partial(gu.second, 3), functools.partial(gd.first, 1)),
                9: run(*each(3, gu.core), functools.partial(gd.first, 2)),
                11: run(functools.partial(gd.first, 3)),
            },
        ],
    )
    mix(
        0,
        own.tok,
        [
            {
                1: run(functools.partial(go.core, 3), *each(2, gd.second)),
                3: run(*each(nz, gd.second, 2)),
            },
            run(go.done, functools.partial(load, go, own.vo, 0, 1), *each(3, gd.core)),
            run(
                functools.partial(gu.core, 3), gu.done, functools.partial(load, gu, own.vu, 0, 2)
            ),
            {},
            run(
                functools.partial(gd.core, 3),
                gd.done,
                functools.partial(load, gd, own.vd, 0, 3),
                functools.partial(load, gq, own.vq, 1, 0),
                functools.partial(load, go, own.vo, 1, 1),
                functools.partial(load, gu, own.vu, 1, 2),
            ),
        ],
    )
    closing.extend([collect(1, s) for s in range(4)])
    project(1, v.res.at[0], [{}, {0: functools.partial(load, gd, own.vd, 1, 3)}])
    mix(1, v.res.at[0], [{}, nothing, nothing, {}, nothing])

    for g in gathers:
        g.close()
    for close in closing:
        close()
    for k in range(4):
        finish(ref.cot_out.at[pl.ds(k * CH, CH), :], own.c_recv.at[1, k])
    for layer in range(2):
        close_states(layer, 1)

        @pl.when(p.x == layer)
        def _():
            for slot in range(8):
                finish(ref.lay.at[0, slot // 2, slot % 2], own.d_recv.at[slot])

    tok_out.wait()
    for copy in pending[1]:
        copy.wait()


def forward_pass(n, tokens, cotangent, small, wq, wo, wu, wd):
    t = 4 * CH
    nz = n // 2
    full = [
        shape((2, nz, 2, w.shape[0], 2 * w.shape[1]), bf16) for w in (wq, wo, wu, wd)
    ]
    kept = [
        shape((t, D), bf16),
        shape((t, 3 * D), bf16),
        shape((t, 2 * QB), bf16),
        shape((t, D), f32),
        shape((t, D), f32),
        shape((t, D), bf16),
        shape((t, D), f32),
        shape((t, D), bf16),
        shape((t, FF), bf16),
        shape((t, FF), bf16),
        shape((t, D), bf16),
        shape((STATE_ROWS, CH), f32),
    ]
    outs = full + [shape((1, 4, 2, CH, D), bf16)]
    outs += [shape((2, GAIN_ROWS, CH), f32), shape((2, 2 * PAIRS, CH, 2 * CH), bf16)]
    outs += [shape((t, D), bf16)] * 2 + kept * 2
    specs = [ANY] * 5 + [VMEM] * 2 + [ANY] * (len(outs) - 7)
    scratch = [pltpu.VMEM(k.shape, k.dtype) for k in kept]
    scratch[10] = pltpu.VMEM((2, t, D), bf16)
    scratch += [
        pltpu.VMEM((t, D), bf16),
        pltpu.VMEM((2, nz, 2, SMALL_ROWS, CH), bf16),
        pltpu.VMEM((2, VEC_ROWS, CH), f32),
        pltpu.VMEM((2, STATE_ROWS, CH), f32),
        pltpu.VMEM((2, n // 2 - 1, STATE_ROWS, CH), f32),
    ]
    scratch += [pltpu.VMEM(w.shape[1:], bf16) for w in full]
    dma = pltpu.SemaphoreType.DMA
    scratch += [dma((5, 19)), dma((5, 19)), dma((5,)), dma((2, 4)), dma((2, 4))]
    scratch += [dma((2, n // 2 - 1)), dma((2, n // 2 - 1)), dma((2, 4)), dma((8,)), dma((4,))]
    scratch += [dma((2, 12)), dma]
    got = call(
        functools.partial(forward_kernel, n),
        outs,
        scratch,
        [ANY] * 7,
        [tokens, cotangent, small, wq, wo, wu, wd],
        4 * t * D * (4 * D + 2 * FF),
        specs,
        cid=0,
    )
    layers = [Kept(*got[9:21]), Kept(*got[21:33])]
    return got[:4], got[4], got[5], got[6], got[7], got[8], layers


def with_error(gv, swapped, lane, hh):
    first = HEAD * (1 - hh)
    hi = swapped.astype(bf16)
    lo = (swapped - hi.astype(f32)).astype(bf16)
    own = (lane < HEAD) if hh == 0 else (lane >= HEAD)
    spare = jnp.where(
        lane == first + 1,
        lo,
        jnp.where((lane == first) | (lane == first + 2), hi, jnp.zeros_like(gv)),
    )
    return jnp.where(own, gv, spare)


def with_ones(v, lane, hh):
    first = HEAD * (1 - hh)
    own = (lane < HEAD) if hh == 0 else (lane >= HEAD)
    spare = jnp.where((lane == first) | (lane == first + 1), jnp.ones_like(v), jnp.zeros_like(v))
    return jnp.where(own, v, spare)


def with_totals(s, tot, row, hh, again):
    first = HEAD * (1 - hh)
    hi = tot.astype(bf16).astype(f32)
    lo = tot - hi
    own = (row < HEAD) if hh == 0 else (row >= HEAD)
    if again:
        spare = jnp.where(
            (row == first) | (row == first + 1), hi, jnp.where(row == first + 2, lo, 0.0)
        )
    else:
        spare = jnp.where(row == first, hi, jnp.where(row == first + 1, lo, 0.0))
    return jnp.where(own, s, spare).astype(bf16)


def put_rows(ref, layer, row, val):
    for i in range(val.shape[1] // CH):
        ref[layer, pl.ds(row + i, 1), :] = val[:, i * CH : (i + 1) * CH]


class Reduce:
    def __init__(self, place, layer, buf, temp, land, out, fin, send, recv, local, last):
        self.p, self.layer, self.buf, self.temp = place, layer, buf, temp
        self.land_d, self.land_y, self.land_z, self.land_x = land
        self.out, self.fin, self.local, self.last = out, fin, local, last
        self.send, self.recv = send, recv
        self.r, self.c = buf.shape[2], buf.shape[3]

    def go(self, src, dst, slot, to):
        remote(src, dst, self.send.at[slot], self.recv.at[slot], to).start()

    def fetch(self, src, dst):
        copy = pltpu.make_async_copy(src, dst, self.local)
        copy.start()
        copy.wait()

    def send_core(self):
        self.go(self.buf, self.land_d, 0, self.p.at(d=1 - self.p.d))

    def got_core(self):
        finish(self.buf, self.send.at[0])
        finish(self.land_d, self.recv.at[0])

    def send_y(self):
        p = self.p
        self.go(self.buf.at[:, 1 - p.y], self.land_y, 1, p.at(y=1 - p.y))

    def step_y(self):
        p = self.p
        finish(self.land_y, self.recv.at[1])
        self.fetch(self.land_y, self.temp)
        for i in range(1, p.nz + 1):
            zi = p.zpos(i)
            self.buf[zi, p.y] = (
                self.buf[zi, p.y].astype(f32) + self.temp[zi].astype(f32)
            ).astype(bf16)
            if i < p.nz:
                self.go(self.buf.at[zi, p.y], self.land_z.at[i - 1], 1 + i, p.at(z=zi))

    def step_z(self):
        p = self.p
        for i in range(1, p.nz):
            finish(self.land_z.at[i - 1], self.recv.at[1 + i])
        self.fetch(self.land_z, self.temp.at[pl.ds(0, p.nz - 1)])
        total = self.buf[p.z, p.y].astype(f32)
        for i in range(p.nz - 1):
            total = total + self.temp[i].astype(f32)

        @pl.when(p.x == self.layer)
        def _():
            self.fin[...] = total

        @pl.when(p.x != self.layer)
        def _():
            self.buf[p.z, p.y] = total.astype(bf16)
            self.go(self.buf.at[p.z, p.y], self.land_x, 5, p.at(x=1 - p.x))

    def half(self):
        return pl.ds(pl.multiple_of(self.p.d * self.c, CH), self.c)

    def other(self):
        return pl.ds(pl.multiple_of((1 - self.p.d) * self.c, CH), self.c)

    def step_x(self):
        p = self.p

        @pl.when(p.x == self.layer)
        def _():
            finish(self.land_x, self.recv.at[5])
            self.fetch(self.land_x, self.temp.at[0])
            self.fin[...] += self.temp[0].astype(f32)
            own = self.out.at[:, self.half()]
            self.go(self.fin, own, 6, p.at(d=1 - p.d))
            pltpu.make_async_copy(self.fin, own, self.last).start()

    def close(self):
        p = self.p
        finish(self.buf.at[:, 0], self.send.at[1])
        for i in range(1, p.nz):
            finish(self.buf.at[0, 0], self.send.at[1 + i])

        @pl.when(p.x != self.layer)
        def _():
            finish(self.buf.at[0, 0], self.send.at[5])

    def end(self):
        @pl.when(self.p.x == self.layer)
        def _():
            finish(self.fin, self.send.at[6])
            finish(self.out.at[:, self.other()], self.recv.at[6])
            finish(self.fin, self.last)


class SmallReduce:
    def __init__(self, place, layer, buf, land, out, send, recv):
        self.p, self.layer, self.buf, self.out = place, layer, buf, out
        self.land_d, self.land_y, self.land_z, self.land_x = land
        self.send, self.recv = send, recv

    def go(self, src, dst, slot, to):
        remote(src, dst, self.send.at[slot], self.recv.at[slot], to).start()

    def send_core(self):
        self.go(self.buf, self.land_d, 0, self.p.at(d=1 - self.p.d))

    def step_d(self):
        p = self.p
        finish(self.buf, self.send.at[0])
        finish(self.land_d, self.recv.at[0])
        self.buf[...] += self.land_d[...]
        self.go(self.buf.at[:, 1 - p.y], self.land_y, 1, p.at(y=1 - p.y))

    def step_y(self):
        p = self.p
        finish(self.land_y, self.recv.at[1])
        for i in range(1, p.nz + 1):
            zi = p.zpos(i)
            self.buf[zi, p.y] += self.land_y[zi]
            if i < p.nz:
                self.go(self.buf.at[zi, p.y], self.land_z.at[i - 1], 1 + i, p.at(z=zi))

    def step_z(self):
        p = self.p
        for i in range(1, p.nz):
            finish(self.land_z.at[i - 1], self.recv.at[1 + i])
        total = self.buf[p.z, p.y]
        for i in range(p.nz - 1):
            total = total + self.land_z[i]
        self.buf[p.z, p.y] = total

        @pl.when(p.x != self.layer)
        def _():
            self.go(self.buf.at[p.z, p.y], self.land_x, 5, p.at(x=1 - p.x))

    def step_x(self):
        p = self.p

        @pl.when(p.x == self.layer)
        def _():
            finish(self.land_x, self.recv.at[5])
            self.out[...] = self.buf[p.z, p.y] + self.land_x[...]

    def close(self):
        p = self.p
        finish(self.buf.at[:, 0], self.send.at[1])
        for i in range(1, p.nz):
            finish(self.buf.at[0, 0], self.send.at[1 + i])

        @pl.when(p.x != self.layer)
        def _():
            finish(self.buf.at[0, 0], self.send.at[5])


SMALL_OUT = 112


class Loaded(NamedTuple):
    gp: Any
    r: Any
    o: Any
    inv: Any
    ph: Any
    qkv: Any
    n2: Any
    ob: Any
    a: Any
    u: Any
    pre: Any


class BackwardRefs(NamedTuple):
    cot: Any
    gv: Any
    bd: Any
    wq: Any
    wo: Any
    wu: Any
    wd: Any


class BackwardScratch(NamedTuple):
    g: Any
    drb: Any
    gs: Any
    tmp: Any
    acc: Any
    st: Any
    got: Any
    mg: Any
    vr: Any
    gr: Any
    hidr: Any
    wdr: Any
    vq: Any
    vo: Any
    vu: Any
    bq: Any
    bo: Any
    bu: Any
    bd_: Any
    tmp96: Any
    tmpd: Any
    fq: Any
    fo: Any
    fu: Any
    fd: Any
    ty96: Any
    tyd: Any
    sb: Any
    sd: Any
    sy: Any
    sz: Any
    sx: Any
    r_send: Any
    r_recv: Any
    r_local: Any
    q_send: Any
    q_recv: Any
    s_send: Any
    s_recv: Any
    d_send: Any
    d_recv: Any
    w_sem: Any
    l_sem: Any
    h_sem: Any
    t_sem: Any
    k_sem: Any


Q, O, U, DN = range(4)


def backward_kernel(n, *refs):
    ref = BackwardRefs(*refs[:7])
    source = [Loaded(*refs[7:18]), Loaded(*refs[18:29])]
    hidden = refs[29:31]
    gin, small_out = refs[31], refs[36]
    wgrads = refs[32:36]
    lands = refs[37:69]
    v = Loaded(*refs[69:80])
    own = BackwardScratch(*refs[80:])
    p = Place(n)
    nz, group = p.nz, p.group
    t = own.drb.shape[0]
    nc = t // CH
    members = 2 * group
    gains, gbuf, tmp, acc = ref.gv, own.g, own.tmp, own.acc
    vr, gr, mg = own.vr, own.gr, own.mg
    flat = Weights(own.vq.reshape(D, 3 * D), own.vo.reshape(D, D), own.vu.reshape(D, FF))
    stored = (own.vq, own.vo, own.vu)
    lane_t = lanes(t)
    lane = lanes(CH)
    low = lane < HEAD
    row = lax.broadcasted_iota(jnp.int32, (CH, CH), 0)
    tril, triu = row >= lane, row <= lane

    def load(layer, *wanted):
        for dst in wanted:
            k = [dst is x for x in v].index(True)
            pltpu.make_async_copy(source[layer][k], dst, own.l_sem.at[k]).start()

    def loaded(*wanted):
        for dst in wanted:
            k = [dst is x for x in v].index(True)
            finish(dst, own.l_sem.at[k])

    def load_w(layer, k):
        w = (ref.wq, ref.wo, ref.wu)[k]
        pltpu.make_async_copy(w.at[layer], stored[k], own.w_sem.at[k]).start()

    def loaded_w(k):
        finish(stored[k], own.w_sem.at[k])

    def load_wd(layer, k):
        pltpu.make_async_copy(
            ref.wd.at[layer, k // 2, k % 2], own.wdr.at[k % 3], own.k_sem.at[k % 3]
        ).start()

    pltpu.make_async_copy(ref.cot, gbuf.at[0], own.t_sem.at[4]).start()
    for k in range(3):
        load_wd(1, k)
    load(1, v.gp)
    load_w(1, U)
    load(1, v.r, v.o, v.inv, v.ph)
    load_w(1, O)
    load_w(1, Q)
    load(1, v.qkv, v.n2, v.ob, v.a, v.u, v.pre)
    p.meet()
    finish(gbuf.at[0], own.t_sem.at[4])

    width = (3 * D // 2, D // 2, FF // 2, D // 2)
    bufs = (own.bq, own.bo, own.bu, own.bd_)
    fins = (own.fq, own.fo, own.fu, own.fd)
    reduces = []
    for layer in range(2):
        line = []
        for m in (Q, O, U, DN):
            at = (layer * 4 + m) * 4
            line.append(
                Reduce(
                    p,
                    layer,
                    bufs[m],
                    own.tyd if m == DN else own.ty96.at[:, :, pl.ds(0, width[m])],
                    lands[at : at + 4],
                    wgrads[m],
                    fins[m],
                    own.r_send.at[layer, m],
                    own.r_recv.at[layer, m],
                    own.r_local.at[m],
                    own.r_local.at[4 + m],
                )
            )
        reduces.append(line)
    smalls = [
        SmallReduce(
            p,
            layer,
            own.sb.at[layer],
            [land.at[layer] for land in (own.sd, own.sy, own.sz, own.sx)],
            small_out,
            own.q_send.at[layer],
            own.q_recv.at[layer],
        )
        for layer in range(2)
    ]

    def states_ok(o, taking):
        return (p.r + o < members) if taking else (p.r - o >= 0)

    def send_states(layer):
        for o in range(1, members):
            other = p.r - o

            @pl.when(states_ok(o, False))
            def _():
                remote(
                    own.st.at[layer],
                    own.got.at[layer, o - 1],
                    own.s_send.at[layer, o - 1],
                    own.s_recv.at[layer, o - 1],
                    (lax.div(other, group), p.d, p.i * group + lax.rem(other, group)),
                ).start()

    def take_states(layer):
        acc0 = own.got.at[layer, 0]
        for o in range(1, members):

            @pl.when(states_ok(o, True))
            def _():
                finish(own.got.at[layer, o - 1], own.s_recv.at[layer, o - 1])
                if o > 1:
                    acc0[...] += own.got[layer, o - 1]

            if o == 1:

                @pl.when(jnp.logical_not(states_ok(o, True)))
                def _():
                    acc0[...] = jnp.zeros(acc0.shape, f32)

        return acc0

    def close_states(layer):
        for o in range(1, members):

            @pl.when(states_ok(o, False))
            def _():
                finish(own.st.at[layer], own.s_send.at[layer, o - 1])

    def norm_back(x_ref, which, layer, body):
        gain = wide(gains, layer, which * 6, 6)
        acc[...] = jnp.zeros(acc.shape, f32)

        def step(i):
            rows = span(i, CH)
            xh, rstd = standardize(x_ref[rows, :].astype(f32))
            dn = tmp[rows, :]
            acc[0:1, :] += jnp.sum(dn, 0, keepdims=True)
            acc[1:2, :] += jnp.sum(dn * xh, 0, keepdims=True)
            dx = dn * gain
            body(
                rows,
                rstd
                * (dx - jnp.mean(dx, -1, keepdims=True) - xh * jnp.mean(dx * xh, -1, keepdims=True)),
            )

        loop(nc, step)
        put_rows(vr, layer, SHIFT2 if which else SHIFT1, acc[0:1, :])
        put_rows(gr, layer, which * 6, acc[1:2, :])

    def mlp_back(layer, g, events):
        gp, r, o_, inv, ph = v.gp, v.r, v.o, v.inv, v.ph
        drb, gs, st = own.drb, own.gs, own.st
        loaded(v.gp)
        for k in range(2 * nz):
            finish(own.wdr.at[k % 3], own.k_sem.at[k % 3])
            cols = pl.ds(k * FF // n, FF // n)
            part = (nt(g[...], own.wdr[k % 3]) * gp[:, cols]).astype(bf16)
            gp[:, cols] = part
            put_rows(
                vr, layer, UP_BIAS + 3 * k, jnp.sum(part.astype(f32), 0, keepdims=True)
            )
            if k + 3 < 2 * nz:
                load_wd(layer, k + 3)
            if k in events:
                events[k]()
        loaded_w(U)

        def n2_col(j):
            cols = span(j, TILE)
            tmp[:, cols] = nt(gp[...], flat.u[cols, :])

        loop(D // TILE, n2_col)
        loaded(v.r)

        def body(rows, back):
            up = g[rows, :].astype(f32)
            total = up + back
            acc[2:3, :] += jnp.sum(up, 0, keepdims=True)
            acc[3:4, :] += jnp.sum(total, 0, keepdims=True)
            r[rows, :] = total
            drb[rows, :] = total.astype(bf16)

        norm_back(r, 1, layer, body)
        put_rows(vr, layer, DOWN_BIAS, acc[2:3, :])
        put_rows(vr, layer, OUT_BIAS, acc[3:4, :])
        loaded_w(O)
        loaded(v.inv, v.o, v.ph)

        def do_col(j):
            cols = span(j, TILE)
            gs[:, cols] = (nt(drb[...], flat.o[cols, :]) * inv[:, cols]).astype(bf16)

        loop(D // TILE, do_col)
        low_t = lane_t < HEAD

        def pair(k):
            cols = span(k, CH)
            gv = gs[:, cols]
            prod = gv.astype(f32) * o_[:, cols]
            e0 = -jnp.sum(jnp.where(low_t, prod, 0.0), -1, keepdims=True)
            e1 = -jnp.sum(jnp.where(low_t, 0.0, prod), -1, keepdims=True)
            swapped = jnp.where(low_t, e1, e0)
            inv[:, cols] = swapped
            for hh in range(2):
                ge = with_error(gv, swapped, lane_t, hh)
                full = tn(ge, ph[:, span(2 * k + hh, CH)])
                st[layer, span(2 * k + hh, HEAD), :] = full[hh * HEAD : (hh + 1) * HEAD]
                at = HEAD * (1 - hh)
                st[layer, pl.ds(D + 2 * k + hh, 1), :] = full[at : at + 1] + full[at + 1 : at + 2]

        loop(PAIRS, pair)
        st[layer, D + H :, :] = jnp.zeros((STATE_ROWS - D - H, CH), f32)
        send_states(layer)

    def weight_grad(layer, m, keep):
        red = reduces[layer][m]
        buf, c = red.buf, red.c
        base = (p.d if keep else 1 - p.d) * c
        if keep:
            red.got_core()
        elif layer == 0:
            reduces[1][m].close()
        if m == DN:
            rhs = gbuf[1 - layer, :, pl.ds(pl.multiple_of(base, CH), c)]

            def fetch(k):
                pltpu.make_async_copy(
                    hidden[layer].at[:, pl.ds(k * FF // n, FF // n)],
                    own.hidr.at[k % 3],
                    own.h_sem.at[k % 3],
                ).start()
                if keep:
                    pltpu.make_async_copy(
                        red.land_d.at[k // 2, k % 2], own.tmpd.at[k % 3], own.t_sem.at[k % 3]
                    ).start()

            for k in range(3):
                fetch(k)
            for k in range(2 * nz):
                finish(own.hidr.at[k % 3], own.h_sem.at[k % 3])
                val = tn(own.hidr[k % 3], rhs)
                if keep:
                    finish(own.tmpd.at[k % 3], own.t_sem.at[k % 3])
                    val = val + own.tmpd[k % 3].astype(f32)
                buf[k // 2, k % 2] = val.astype(bf16)
                if k + 3 < 2 * nz:
                    fetch(k + 3)
        else:
            lhs = (v.a, v.ob, v.n2)[m]
            rhs = (v.qkv, own.drb, v.gp)[m]
            step = 384
            count = c // step

            def fetch(k):
                pltpu.make_async_copy(
                    red.land_d.at[:, :, :, pl.ds(k * step, step)],
                    own.tmp96.at[k % 2],
                    own.t_sem.at[k % 2],
                ).start()

            if keep:
                for k in range(min(2, count)):
                    fetch(k)
            for k in range(count):
                val = tn(lhs[...], rhs[:, pl.ds(pl.multiple_of(base + k * step, CH), step)])
                if keep:
                    finish(own.tmp96.at[k % 2], own.t_sem.at[k % 2])
                for zi in range(nz):
                    for yi in range(2):
                        at = (zi * 2 + yi) * red.r
                        part = val[at : at + red.r]
                        if keep:
                            part = part + own.tmp96[k % 2, zi, yi].astype(f32)
                        buf[zi, yi, :, pl.ds(k * step, step)] = part.astype(bf16)
                if keep and k + 2 < count:
                    fetch(k + 2)
        if keep:
            red.send_y()
        else:
            red.send_core()

    def mix_back(layer, events):
        qkv, ph, gs, es = v.qkv, v.ph, own.gs, v.inv
        bd = ref.bd.at[layer]
        s1 = take_states(layer)
        loaded(v.qkv, v.pre)
        s0 = v.pre

        def pair(k):
            cols = span(k, CH)
            vcols = pl.ds(pl.multiple_of(2 * D + k * CH, CH), CH)
            kcols = pl.ds(pl.multiple_of(D + k * CH, CH), CH)

            def keys(rows, hh):
                return ph[rows, pl.ds(pl.multiple_of((H + 2 * k + hh) * CH, CH), CH)]

            before = []
            s = s0[cols, :]
            tot = [s0[pl.ds(D + 2 * k + hh, 1), :] for hh in range(2)]
            for c in range(nc):
                rows = pl.ds(c * CH, CH)
                before.append([with_totals(s, tot[hh], row, hh, True) for hh in range(2)])
                if c < nc - 1:
                    val = qkv[rows, vcols]
                    new = []
                    for hh in range(2):
                        kh = keys(rows, hh)
                        new.append(tn(val, kh)[hh * HEAD : (hh + 1) * HEAD])
                        tot[hh] = tot[hh] + jnp.sum(kh.astype(f32), 0, keepdims=True)
                    s = s + jnp.concatenate(new, 0)
            ds = s1[cols, :]
            dtot = [s1[pl.ds(D + 2 * k + hh, 1), :] for hh in range(2)]
            acc_q = jnp.zeros((CH, 2 * CH), f32)
            acc_k = jnp.zeros((CH, 2 * CH), f32)
            sums = [jnp.zeros((1, CH), f32) for _ in range(3)]
            for c in reversed(range(nc)):
                rows = pl.ds(c * CH, CH)
                val = qkv[rows, vcols]
                gv = gs[rows, cols]
                ev = es[rows, cols]
                dsl = ds.astype(bf16)
                dl_q, dl_k, dv, new = [], [], [], []
                for hh in range(2):
                    qh = ph[rows, span(2 * k + hh, CH)]
                    kh = keys(rows, hh)
                    ge = with_error(gv, ev, lane, hh)
                    v1 = with_ones(val, lane, hh)
                    after = with_totals(ds, dtot[hh], row, hh, False)
                    da = jnp.where(tril, nt(ge, v1), 0.0).astype(bf16)
                    dat = jnp.where(triu, nt(v1, ge), 0.0).astype(bf16)
                    at = jnp.where(triu, nt(kh, qh), 0.0).astype(bf16)
                    dq = nn(da, kh) + nn(ge, before[c][hh])
                    dk = nn(dat, qh) + nn(v1, after)
                    dv.append(nn(at, gv) + nt(kh, dsl))
                    for p_, d_, to in ((qh, dq, dl_q), (kh, dk, dl_k)):
                        pf = p_.astype(f32)
                        to.append((pf * (d_ - half_sums(pf * d_, low))).astype(bf16))
                    full = tn(ge, qh)
                    new.append(full[hh * HEAD : (hh + 1) * HEAD])
                    first = HEAD * (1 - hh)
                    dtot[hh] = dtot[hh] + full[first : first + 1] + full[first + 1 : first + 2]
                ds = ds + jnp.concatenate(new, 0)
                dl_q = jnp.concatenate(dl_q, 1)
                dl_k = jnp.concatenate(dl_k, 1)
                acc_q = acc_q + tn(qkv[rows, cols], dl_q)
                acc_k = acc_k + tn(qkv[rows, kcols], dl_k)
                parts = (
                    (cols, nt(dl_q, bd[k])),
                    (kcols, nt(dl_k, bd[PAIRS + k])),
                    (vcols, jnp.where(low, dv[0], dv[1])),
                )
                for i, (where, new_) in enumerate(parts):
                    new_ = new_.astype(bf16)
                    qkv[rows, where] = new_
                    sums[i] = sums[i] + jnp.sum(new_.astype(f32), 0, keepdims=True)
            for i in range(3):
                vr[layer, pl.ds(QKV_BIAS + i * PAIRS + k, 1), :] = sums[i]
            for which, total in enumerate((acc_q, acc_k)):
                for hh in range(2):
                    blk = total[hh * HEAD : (hh + 1) * HEAD, hh * CH : (hh + 1) * CH]
                    mg[which * H + 2 * k + hh] = blk - pltpu.roll(blk, HEAD, 1)

        loop(PAIRS, pair, events)
        loaded_w(Q)

        def n1_col(j):
            cols = span(j, TILE)
            tmp[:, cols] = nt(qkv[...], flat.q[cols, :])

        loop(D // TILE, n1_col)
        loaded(v.u)
        du = gbuf.at[layer]

        def body(rows, back):
            du[rows, :] = (v.r[rows, :] + back).astype(bf16)

        norm_back(v.u, 0, layer, body)

    closing = []

    def deliver(layer):
        for k in range(4):
            to = p.jj * 4 + k
            src = gbuf.at[layer, pl.ds(k * CH, CH), :]
            dst = gin.at[0, p.i, p.x]
            slot = p.i * 2 + p.x
            mine = (to == p.j) & (p.x == layer)
            copy = remote(
                src, dst, own.d_send.at[layer, k], own.d_recv.at[slot], p.at(x=layer, j=to)
            )

            @pl.when(jnp.logical_not(mine))
            def _():
                copy.start()

            @pl.when(mine)
            def _():
                pltpu.make_async_copy(src, dst, own.d_recv.at[slot]).start()

            def close(copy=copy, mine=mine):
                @pl.when(jnp.logical_not(mine))
                def _():
                    copy.wait_send()

            closing.append(close)

    def pack_small(layer):
        sb = own.sb
        for k in range(n):
            at, gat = (33 * k) // 4, (3 * k) // 2
            zi, yi = k // 2, k % 2
            sb[layer, zi, yi, 0:9] = vr[layer, at : at + 9, :]
            sb[layer, zi, yi, 9:11] = gr[layer, gat : gat + 2, :]
            sb[layer, zi, yi, 11:16] = jnp.zeros((5, CH), f32)
            h0, h1, h2 = (mg[3 * k + i] for i in range(3))
            left = jnp.concatenate([h0, h1[: HEAD // 2]], 0)
            right = jnp.concatenate([h1[HEAD // 2 :], h2], 0)
            sb[layer, zi, yi, 16:SMALL_OUT] = jnp.where(lanes(96) < HEAD, left, -right)
        smalls[layer].send_core()

    vr[...] = jnp.zeros(vr.shape, f32)
    gr[...] = jnp.zeros(gr.shape, f32)
    r1, r0 = reduces[1], reduces[0]
    s1, s0 = smalls[1], smalls[0]

    def run(*steps):
        def all_():
            for step in steps:
                step()

        return all_

    mlp_back(1, gbuf.at[0], {})
    load(0, v.o)
    load_w(0, U)
    load_w(0, O)
    for k in range(3):
        load_wd(0, k)
    loaded(v.n2, v.ob, v.a)
    for m in (DN, U, O):
        weight_grad(1, m, False)
    for m in (DN, U, O):
        weight_grad(1, m, True)
    load(0, v.gp, v.n2, v.ob)
    mix_back(1, {4: r1[DN].step_y})
    load_w(0, Q)
    load(0, v.r, v.inv, v.ph, v.u, v.pre)
    deliver(1)
    pack_small(1)
    weight_grad(1, Q, False)
    r1[U].step_y()
    weight_grad(1, Q, True)
    s1.step_d()
    load(0, v.qkv)
    load(0, v.a)

    mlp_back(
        0,
        gbuf.at[1],
        {2: r1[DN].step_z, 4: r1[O].step_y, 6: s1.step_y, 7: run(r1[DN].step_x)},
    )
    loaded(v.n2, v.ob, v.a)
    weight_grad(0, DN, False)
    r1[U].step_z()
    weight_grad(0, U, False)
    r1[O].step_z()
    weight_grad(0, O, False)
    r1[Q].step_y()
    s1.step_z()
    weight_grad(0, DN, True)
    weight_grad(0, U, True)
    weight_grad(0, O, True)
    mix_back(
        0,
        {
            0: run(r1[U].step_x, r1[O].step_x, s1.step_x),
            2: r1[Q].step_z,
            3: run(r1[Q].step_x, r0[DN].step_y),
        },
    )
    deliver(0)
    pack_small(0)
    weight_grad(0, Q, False)
    r0[U].step_y()
    weight_grad(0, Q, True)
    s0.step_d()
    r0[DN].step_z()
    r0[O].step_y()
    s0.step_y()
    r0[DN].step_x()
    r0[U].step_z()
    r0[Q].step_y()
    r0[O].step_z()
    s0.step_z()
    r0[U].step_x()
    r0[O].step_x()
    s0.step_x()
    r0[Q].step_z()
    r0[Q].step_x()

    for m in (Q, O, U, DN):
        r0[m].close()
        r1[m].end()
        r0[m].end()
    s1.close()
    s0.close()
    for layer in range(2):
        close_states(layer)

        @pl.when(p.x == layer)
        def _():
            for slot in range(8):
                finish(gin.at[0, slot // 2, slot % 2], own.d_recv.at[slot])

    for close in closing:
        close()


def backward_pass(n, cot, gains, bds, full, tokens, kept):
    t = cot.shape[0]
    nz = n // 2
    args = [cot, gains, bds] + list(full)
    for u, k in zip((tokens, kept[0].res), kept):
        read = Loaded(k.gp, k.r, k.o, k.inv, k.ph, k.qkv, k.n2, k.ob, k.a, u, k.pre)
        args += list(read)
    args += [k.hid for k in kept]
    widths = (3 * D // 2, D // 2, FF // 2, D // 2)
    rows = (D // n, D // n, D // n, FF // n)
    outs = [shape((1, 4, 2, CH, D), bf16)]
    outs += [shape((r, 2 * c), f32) for r, c in zip(rows, widths)]
    outs += [shape((SMALL_OUT, CH), f32)]
    for _ in range(2):
        for r, c in zip(rows, widths):
            outs += [
                shape((nz, 2, r, c), bf16),
                shape((nz, r, c), bf16),
                shape((nz - 1, r, c), bf16),
                shape((r, c), bf16),
            ]
    specs = [ANY] * 5 + [VMEM] + [ANY] * (len(outs) - 6)
    ins = [ANY, VMEM, VMEM] + [ANY] * (len(args) - 3)
    scratch = [pltpu.VMEM(a.shape, a.dtype) for a in read]

    def vmem(*dims, kind=f32):
        scratch.append(pltpu.VMEM(dims, kind))

    vmem(2, t, D, kind=bf16)
    vmem(t, D, kind=bf16)
    vmem(t, D, kind=bf16)
    vmem(t, D)
    vmem(8, D)
    vmem(2, STATE_ROWS, CH)
    vmem(2, n // 2 - 1, STATE_ROWS, CH)
    vmem(2 * H, HEAD, CH)
    vmem(2, VEC_ROWS, CH)
    vmem(2, GAIN_ROWS, CH)
    vmem(3, t, FF // n, kind=bf16)
    vmem(3, FF // n, D, kind=bf16)
    for w in full[:3]:
        vmem(*w.shape[1:], kind=bf16)
    for r, c in zip(rows, widths):
        vmem(nz, 2, r, c, kind=bf16)
    vmem(2, nz, 2, D // n, 384, kind=bf16)
    vmem(3, FF // n, D // 2, kind=bf16)
    for r, c in zip(rows, widths):
        vmem(r, c)
    vmem(nz, D // n, FF // 2, kind=bf16)
    vmem(nz, FF // n, D // 2, kind=bf16)
    vmem(2, nz, 2, SMALL_OUT, CH)
    vmem(2, nz, 2, SMALL_OUT, CH)
    vmem(2, nz, SMALL_OUT, CH)
    vmem(2, nz - 1, SMALL_OUT, CH)
    vmem(2, SMALL_OUT, CH)
    dma = pltpu.SemaphoreType.DMA
    scratch += [dma((2, 4, 7)), dma((2, 4, 7)), dma((8,)), dma((2, 7)), dma((2, 7))]
    scratch += [dma((2, n // 2 - 1)), dma((2, n // 2 - 1)), dma((2, 4)), dma((8,)), dma((4,))]
    scratch += [dma((len(read),)), dma((3,)), dma((5,)), dma((3,))]
    got = call(
        functools.partial(backward_kernel, n),
        outs,
        scratch,
        ins,
        args,
        8 * t * D * (4 * D + 2 * FF),
        specs,
        cid=1,
    )
    return got[:6]


def shards(inputs, cotangent, *weights):
    n = lax.axis_size("seq")
    d, j = lax.axis_index("dp"), lax.axis_index("seq")
    qkv_w, out_w, up_w, down_w, map_w, bias_w, gain_w = (w[0] for w in weights)

    def halved(w):
        width = w.shape[1] // 2
        return lax.dynamic_slice_in_dim(w, d * width, width, 1).astype(bf16)

    def placed(vector, offset, rows):
        flat = jnp.zeros((rows * CH,), f32)
        return lax.dynamic_update_slice(flat, vector, (offset,)).reshape(rows, CH)

    bias_at, gain_at = (j % 4) * 32, (j % 2) * 64
    small = jnp.concatenate(
        [
            placed(bias_w, bias_at, 9),
            placed(gain_w, gain_at, 2),
            jnp.zeros((5, CH), f32),
            jnp.concatenate([map_w, -map_w], 1),
        ]
    ).astype(bf16)
    full, layer_out, gains, bds, tokens, cot, kept = forward_pass(
        n, inputs, cotangent, small, halved(qkv_w), halved(out_w), halved(up_w), halved(down_w)
    )
    grads, g_qkv, g_out, g_up, g_down, g_small = backward_pass(n, cot, gains, bds, full, tokens, kept)
    maps = jnp.concatenate([g_small[16:, :HEAD], g_small[16:, HEAD:]])
    bias = lax.dynamic_slice_in_dim(g_small[:9].reshape(-1), bias_at, bias_w.shape[0])
    gain = lax.dynamic_slice_in_dim(g_small[9:11].reshape(-1), gain_at, gain_w.shape[0])
    return (
        layer_out,
        grads,
        g_qkv[None],
        g_out[None],
        g_up[None],
        g_down[None],
        maps[None],
        bias[None],
        gain[None],
    )


def solution(mesh):
    tokens = P("dp", None, "seq", None)
    matrix = P("section", "seq", None)
    vector = P("section", "seq")
    stacked = P("section", "dp", None, "seq", None)
    chosen = shards if mesh.shape["seq"] == 8 else plain_shards
    return jax.shard_map(
        chosen,
        mesh=mesh,
        in_specs=(tokens, tokens) + (matrix,) * 5 + (vector,) * 2,
        out_specs=(stacked, stacked) + (matrix,) * 5 + (vector,) * 2,
        check_vma=False,
    )
```

```python
import functools
from typing import Any, NamedTuple

import jax
import jax.numpy as jnp
from jax import lax
from jax.experimental import pallas as pl
from jax.experimental.pallas import tpu as pltpu
from jax.sharding import PartitionSpec as P


D = 768
FF = 3072
H = 12
HEAD = 64
BLOCK = 64


MAXIMUM_ACCURACY = lax.Precision.HIGHEST
NORM_EPSILON = 1e-05


def carried_in(part, axis, combine, identity, reverse):
    count = lax.axis_size(axis)
    place = lax.axis_index(axis)
    ahead = count - 1 - place if reverse else place
    gathered = jax.tree.map(lambda a: lax.all_gather(a, axis), part)
    state = jax.tree.map(lambda a, e: jnp.zeros_like(a) + jnp.asarray(e, a.dtype), part, identity)

    def one(lap, state):
        source = count - 1 - lap if reverse else lap
        return combine(
            state, jax.tree.map(lambda a: lax.dynamic_index_in_dim(a, source, 0, False), gathered)
        )

    return lax.fori_loop(0, ahead, one, state)


def shifted(value, axis, steps):
    count = lax.axis_size(axis)
    leading, last = (max(0, -steps), min(count, count - steps))
    return lax.ppermute(value, axis, [(source, source + steps) for source in range(leading, last)])


def normalize(values, gain_vector, shift_vector):
    average = jnp.mean(values, -1, keepdims=True)
    centred = values - average
    spread = jnp.mean(centred * centred, -1, keepdims=True)
    return centred * lax.rsqrt(spread + NORM_EPSILON) * gain_vector + shift_vector


def features(logits):
    return jnp.concatenate([jax.nn.softmax(logits, -1), jax.nn.softmax(-logits, -1)], -1)


def gelu_tanh(values):
    return jax.nn.gelu(values, approximate=True)


def adding(earlier, later_part):
    return jax.tree.map(jnp.add, earlier, later_part)


def across_rows(left_side, right_side):
    return lax.dot_general(
        left_side, right_side, (((0,), (0,)), ((), ())), preferred_element_type=jnp.float32
    )


def against_rows(left_side, right_side):
    return lax.dot_general(
        left_side, right_side, (((1,), (1,)), ((), ())), preferred_element_type=jnp.float32
    )


def precise(pattern, left_side, right_side):
    return jnp.einsum(pattern, left_side, right_side, precision=MAXIMUM_ACCURACY)


def causal_mask():
    places = lax.broadcasted_iota(jnp.int32, (BLOCK, BLOCK), 0)
    others = lax.broadcasted_iota(jnp.int32, (BLOCK, BLOCK), 1)
    return (others <= places).astype(jnp.float32)


def in_blocks(source_array, batch_rows):
    return source_array.reshape((batch_rows, -1, BLOCK) + source_array.shape[1:])


def prepare(gathered):
    qkv_full, out_full, up_full, down_full, map_full, bias_full, gain_full = [
        piece_array[0] for piece_array in gathered
    ]
    feature_maps = map_full.reshape(2, H, HEAD, HEAD)
    vectors = bias_full.astype(jnp.float32)
    scales = gain_full.astype(jnp.float32)
    pieces = (
        vectors[:D],
        vectors[D : 4 * D],
        vectors[4 * D : 5 * D],
        vectors[5 * D : 6 * D],
        vectors[6 * D : 6 * D + FF],
        vectors[6 * D + FF :],
        scales[:D],
        scales[D:],
    )
    return (qkv_full, out_full, up_full, down_full, feature_maps, pieces)


def block_sums(query_map, key_map, value_rows, batch_rows):
    query_blocks = in_blocks(query_map, batch_rows)
    key_blocks = in_blocks(key_map, batch_rows)
    value_blocks = in_blocks(value_rows, batch_rows).astype(jnp.float32)
    query_wide = query_blocks.astype(jnp.float32)
    key_wide = key_blocks.astype(jnp.float32)
    score_matrix = (
        jnp.einsum(
            "bcqhf,bckhf->bchqk", query_blocks, key_blocks, preferred_element_type=jnp.float32
        )
        * causal_mask()
    )
    block_state = precise("bckhf,bckhe->bchfe", key_wide, value_blocks)
    block_total = jnp.sum(key_wide, 2)
    return (query_wide, key_wide, value_blocks, score_matrix, block_state, block_total)


def attend(query_map, key_map, value_rows, initial, batch_rows):
    query_wide, key_wide, value_blocks, score_matrix, block_state, block_total = block_sums(
        query_map, key_map, value_rows, batch_rows
    )
    state_sum = jnp.sum(block_state, 1)
    total_sum = jnp.sum(block_total, 1)
    identity = (jnp.zeros_like(state_sum), jnp.zeros_like(total_sum))
    earlier = carried_in((state_sum, total_sum), "seq", adding, identity, False)
    overall = lax.psum((state_sum, total_sum), "seq")
    start_state = initial[0] + earlier[0]
    start_total = initial[1] + earlier[1]
    block_before = start_state[:, None] + jnp.cumsum(block_state, 1) - block_state
    total_before = start_total[:, None] + jnp.cumsum(block_total, 1) - block_total
    numerator = precise("bchqk,bckhe->bcqhe", score_matrix, value_blocks) + precise(
        "bcqhf,bchfe->bcqhe", query_wide, block_before
    )
    denominator = jnp.swapaxes(jnp.sum(score_matrix, -1), 2, 3) + precise(
        "bcqhf,bchf->bcqh", query_wide, total_before
    )
    mixture = numerator / denominator[..., None]
    handed = (initial[0] + overall[0], initial[1] + overall[1])
    return (mixture.reshape(value_rows.shape), denominator, (start_state, start_total), handed)


def attend_back(
    mixture_grad, query_map, key_map, value_rows, mixture, denominator, starts, future, batch_rows
):
    query_wide, key_wide, value_blocks, score_matrix, block_state, block_total = block_sums(
        query_map, key_map, value_rows, batch_rows
    )
    block_before = starts[0][:, None] + jnp.cumsum(block_state, 1) - block_state
    total_before = starts[1][:, None] + jnp.cumsum(block_total, 1) - block_total
    scaled = in_blocks(mixture_grad, batch_rows) / denominator[..., None]
    denominator_grad = -jnp.sum(scaled * in_blocks(mixture, batch_rows), -1)
    score_grad = (
        precise("bcqhe,bckhe->bchqk", scaled, value_blocks)
        + jnp.swapaxes(denominator_grad, 2, 3)[..., None]
    ) * causal_mask()
    query_grad = precise("bchqk,bckhf->bcqhf", score_grad, key_wide) + precise(
        "bcqhe,bchfe->bcqhf", scaled, block_before
    )
    query_grad = query_grad + denominator_grad[..., None] * total_before[:, :, None]
    state_grad = precise("bcqhf,bcqhe->bchfe", query_wide, scaled)
    total_grad = precise("bcqhf,bcqh->bchf", query_wide, denominator_grad)
    state_sum = jnp.sum(state_grad, 1)
    total_sum = jnp.sum(total_grad, 1)
    identity = (jnp.zeros_like(state_sum), jnp.zeros_like(total_sum))
    later_sums = carried_in((state_sum, total_sum), "seq", adding, identity, True)
    overall = lax.psum((state_sum, total_sum), "seq")
    ahead_state = future[0] + later_sums[0]
    ahead_total = future[1] + later_sums[1]
    rest_state = ahead_state[:, None] + state_sum[:, None] - jnp.cumsum(state_grad, 1)
    rest_total = ahead_total[:, None] + total_sum[:, None] - jnp.cumsum(total_grad, 1)
    key_grad = precise("bchqk,bcqhf->bckhf", score_grad, query_wide) + precise(
        "bckhe,bchfe->bckhf", value_blocks, rest_state
    )
    key_grad = key_grad + rest_total[:, :, None]
    value_grad = precise("bchqk,bcqhe->bckhe", score_matrix, scaled) + precise(
        "bckhf,bchfe->bckhe", key_wide, rest_state
    )
    return (
        query_grad.reshape(query_map.shape),
        key_grad.reshape(key_map.shape),
        value_grad.reshape(value_rows.shape),
        overall,
    )


def forward(tokens, params, initial):
    qkv_full, out_full, up_full, down_full, feature_maps, pieces = params
    shift_one, qkv_bias, out_bias, shift_two, up_bias, down_bias, gain_one, gain_two = pieces
    batch_rows = tokens.shape[0]
    flattened = tokens.reshape(-1, D)
    row_count = flattened.shape[0]
    normed = normalize(flattened, gain_one, shift_one).astype(jnp.bfloat16)
    projected = (jnp.dot(normed, qkv_full, preferred_element_type=jnp.float32) + qkv_bias).astype(
        jnp.bfloat16
    )
    query_rows = projected[:, :D].reshape(row_count, H, HEAD)
    key_rows = projected[:, D : 2 * D].reshape(row_count, H, HEAD)
    value_rows = projected[:, 2 * D :].reshape(row_count, H, HEAD)
    query_logits = jnp.einsum(
        "rhe,hef->rhf", query_rows, feature_maps[0], preferred_element_type=jnp.float32
    )
    key_logits = jnp.einsum(
        "rhe,hef->rhf", key_rows, feature_maps[1], preferred_element_type=jnp.float32
    )
    query_map = features(query_logits).astype(jnp.bfloat16)
    key_map = features(key_logits).astype(jnp.bfloat16)
    mixture, denominator, starts, handed = attend(
        query_map, key_map, value_rows, initial, batch_rows
    )
    mixture_low = mixture.reshape(row_count, D).astype(jnp.bfloat16)
    residual = (
        flattened + jnp.dot(mixture_low, out_full, preferred_element_type=jnp.float32) + out_bias
    )
    normed_two = normalize(residual, gain_two, shift_two).astype(jnp.bfloat16)
    before_act = jnp.dot(normed_two, up_full, preferred_element_type=jnp.float32) + up_bias
    hidden = gelu_tanh(before_act).astype(jnp.bfloat16)
    result = residual + jnp.dot(hidden, down_full, preferred_element_type=jnp.float32) + down_bias
    kept_values = (
        flattened,
        normed,
        projected,
        query_logits,
        key_logits,
        query_map,
        key_map,
        mixture,
        denominator,
        starts,
        residual,
        normed_two,
        before_act,
        hidden,
    )
    return (result.reshape(tokens.shape), handed, kept_values)


def backward(upstream, params, kept_values, future):
    qkv_full, out_full, up_full, down_full, feature_maps, pieces = params
    shift_one, qkv_bias, out_bias, shift_two, up_bias, down_bias, gain_one, gain_two = pieces
    (
        flattened,
        normed,
        projected,
        query_logits,
        key_logits,
        query_map,
        key_map,
        mixture,
        denominator,
        starts,
        residual,
        normed_two,
        before_act,
        hidden,
    ) = kept_values
    batch_rows = upstream.shape[0]
    row_count = flattened.shape[0]
    out_grad = upstream.reshape(row_count, D)
    down_bias_grad = jnp.sum(out_grad, 0)
    out_low = out_grad.astype(jnp.bfloat16)
    down_weight_grad = across_rows(hidden, out_low)
    hidden_grad = against_rows(out_low, down_full)
    _, gelu_back = jax.vjp(gelu_tanh, before_act)
    before_grad = gelu_back(hidden_grad)[0].astype(jnp.bfloat16)
    up_bias_grad = jnp.sum(before_grad.astype(jnp.float32), 0)
    up_weight_grad = across_rows(normed_two, before_grad)
    normed_two_grad = against_rows(before_grad, up_full)
    _, norm_back_two = jax.vjp(normalize, residual, gain_two, shift_two)
    residual_part, gain_two_grad, shift_two_grad = norm_back_two(normed_two_grad)
    residual_grad = out_grad + residual_part
    out_bias_grad = jnp.sum(residual_grad, 0)
    residual_low = residual_grad.astype(jnp.bfloat16)
    mixture_low = mixture.reshape(row_count, D).astype(jnp.bfloat16)
    out_weight_grad = across_rows(mixture_low, residual_low)
    mixture_grad = against_rows(residual_low, out_full).reshape(row_count, H, HEAD)
    query_rows = projected[:, :D].reshape(row_count, H, HEAD)
    key_rows = projected[:, D : 2 * D].reshape(row_count, H, HEAD)
    value_rows = projected[:, 2 * D :].reshape(row_count, H, HEAD)
    query_map_grad, key_map_grad, value_grad, handed = attend_back(
        mixture_grad,
        query_map,
        key_map,
        value_rows,
        mixture,
        denominator,
        starts,
        future,
        batch_rows,
    )
    _, query_back = jax.vjp(features, query_logits)
    query_logit_grad = query_back(query_map_grad)[0]
    _, key_back = jax.vjp(features, key_logits)
    key_logit_grad = key_back(key_map_grad)[0]
    maps_wide = feature_maps.astype(jnp.float32)
    query_grad = precise("rhf,hef->rhe", query_logit_grad, maps_wide[0])
    key_grad = precise("rhf,hef->rhe", key_logit_grad, maps_wide[1])
    map_weight_grad = jnp.stack(
        [
            precise("rhe,rhf->hef", query_rows.astype(jnp.float32), query_logit_grad),
            precise("rhe,rhf->hef", key_rows.astype(jnp.float32), key_logit_grad),
        ]
    ).reshape(2 * H * HEAD, HEAD)
    projected_grad = jnp.concatenate(
        [
            query_grad.reshape(row_count, D),
            key_grad.reshape(row_count, D),
            value_grad.reshape(row_count, D),
        ],
        1,
    ).astype(jnp.bfloat16)
    qkv_bias_grad = jnp.sum(projected_grad.astype(jnp.float32), 0)
    qkv_weight_grad = across_rows(normed, projected_grad)
    normed_grad = against_rows(projected_grad, qkv_full)
    _, norm_back_one = jax.vjp(normalize, flattened, gain_one, shift_one)
    input_part, gain_one_grad, shift_one_grad = norm_back_one(normed_grad)
    input_grad = residual_grad + input_part
    bias_grad = jnp.concatenate(
        [shift_one_grad, qkv_bias_grad, out_bias_grad, shift_two_grad, up_bias_grad, down_bias_grad]
    )
    gain_grad = jnp.concatenate([gain_one_grad, gain_two_grad])
    layer_grads = (
        qkv_weight_grad,
        out_weight_grad,
        up_weight_grad,
        down_weight_grad,
        map_weight_grad,
        bias_grad,
        gain_grad,
    )
    return (input_grad.reshape(upstream.shape), handed, layer_grads)


def reduce_grads(full_grads):
    g_qkv, g_out, g_up, g_down, g_map, g_bias, g_gain = full_grads
    s_qkv, s_out, s_up, s_down, s_map, s_bias, s_gain = (
        lax.psum_scatter(g_qkv, "seq", scatter_dimension=1, tiled=True),
        lax.psum_scatter(g_out, "seq", scatter_dimension=1, tiled=True),
        lax.psum_scatter(g_up, "seq", scatter_dimension=1, tiled=True),
        lax.psum_scatter(g_down, "seq", scatter_dimension=1, tiled=True),
        lax.psum_scatter(g_map, "seq", scatter_dimension=1, tiled=True),
        lax.psum_scatter(g_bias, "seq", scatter_dimension=1, tiled=True),
        lax.psum_scatter(g_gain, "seq", scatter_dimension=1, tiled=True),
    )
    return lax.psum((s_qkv, s_out, s_up, s_down, s_map, s_bias, s_gain), "dp")


def plain_shards(
    inputs, cotangent, qkv_weight, out_weight, up_weight, down_weight, map_weight, biases, gains
):
    section_index = lax.axis_index("section")
    batch_rows = inputs.shape[0]
    micro_count = inputs.shape[1]
    gathered = (
        lax.all_gather(qkv_weight.astype(jnp.bfloat16), "seq", axis=1, tiled=True),
        lax.all_gather(out_weight.astype(jnp.bfloat16), "seq", axis=1, tiled=True),
        lax.all_gather(up_weight.astype(jnp.bfloat16), "seq", axis=1, tiled=True),
        lax.all_gather(down_weight.astype(jnp.bfloat16), "seq", axis=1, tiled=True),
        lax.all_gather(map_weight.astype(jnp.bfloat16), "seq", axis=1, tiled=True),
        lax.all_gather(biases.astype(jnp.bfloat16), "seq", axis=1, tiled=True),
        lax.all_gather(gains.astype(jnp.bfloat16), "seq", axis=1, tiled=True),
    )
    params = prepare(gathered)
    empty_state = (
        jnp.zeros((batch_rows, H, 2 * HEAD, HEAD), jnp.float32),
        jnp.zeros((batch_rows, H, 2 * HEAD), jnp.float32),
    )
    blank_rows = jnp.zeros(inputs.shape[:1] + inputs.shape[2:], jnp.bfloat16)
    moments = jnp.arange(micro_count + 1, dtype=jnp.int32)

    def forward_moment(carry, moment):
        handed, arriving = carry
        own_tokens = lax.dynamic_index_in_dim(
            inputs, jnp.minimum(moment, micro_count - 1), 1, False
        )
        source = jnp.where(section_index == 0, own_tokens, arriving).astype(jnp.float32)
        carried = moment - section_index >= 1
        initial = (jnp.where(carried, handed[0], 0.0), jnp.where(carried, handed[1], 0.0))
        result, handed_next, kept_values = forward(source, params, initial)
        outgoing = result.astype(jnp.bfloat16)
        arriving_next = shifted(outgoing, "section", 1)
        return ((handed_next, arriving_next), (outgoing, kept_values))

    _, (result_stack, kept_stack) = lax.scan(forward_moment, (empty_state, blank_rows), moments)
    regathered = (
        lax.all_gather(qkv_weight.astype(jnp.bfloat16), "seq", axis=1, tiled=True),
        lax.all_gather(out_weight.astype(jnp.bfloat16), "seq", axis=1, tiled=True),
        lax.all_gather(up_weight.astype(jnp.bfloat16), "seq", axis=1, tiled=True),
        lax.all_gather(down_weight.astype(jnp.bfloat16), "seq", axis=1, tiled=True),
        lax.all_gather(map_weight.astype(jnp.bfloat16), "seq", axis=1, tiled=True),
        lax.all_gather(biases.astype(jnp.bfloat16), "seq", axis=1, tiled=True),
        lax.all_gather(gains.astype(jnp.bfloat16), "seq", axis=1, tiled=True),
    )
    back_params = prepare(regathered)
    zero_grads = (
        jnp.zeros((D, 3 * D), jnp.float32),
        jnp.zeros((D, D), jnp.float32),
        jnp.zeros((D, FF), jnp.float32),
        jnp.zeros((FF, D), jnp.float32),
        jnp.zeros((2 * H * HEAD, HEAD), jnp.float32),
        jnp.zeros((7 * D + FF,), jnp.float32),
        jnp.zeros((2 * D,), jnp.float32),
    )

    def backward_moment(carry, pieces):
        future, returning, grad_sums = carry
        slot, kept_values = pieces
        chosen = slot - section_index
        own_grad = lax.dynamic_index_in_dim(cotangent, jnp.maximum(slot - 1, 0), 1, False)
        live = (chosen >= 0) & (chosen < micro_count)
        upstream = jnp.where(section_index == 1, own_grad, returning).astype(jnp.float32)
        upstream = jnp.where(live, upstream, 0.0)
        later_micro = live & (chosen < micro_count - 1)
        ahead_part = (
            jnp.where(later_micro, future[0], 0.0),
            jnp.where(later_micro, future[1], 0.0),
        )
        input_grad, future_next, layer_grads = backward(
            upstream, back_params, kept_values, ahead_part
        )
        outgoing = input_grad.astype(jnp.bfloat16)
        grad_sums = tuple((previous + current for previous, current in zip(grad_sums, layer_grads)))
        returning_next = shifted(outgoing, "section", -1)
        return ((future_next, returning_next, grad_sums), outgoing)

    (_, _, grad_sums), grad_stack = lax.scan(
        backward_moment, (empty_state, blank_rows, zero_grads), (moments, kept_stack), reverse=True
    )
    layer_out = jnp.stack(
        [
            lax.dynamic_index_in_dim(result_stack, micro_index + section_index, 0, False)
            for micro_index in range(micro_count)
        ],
        1,
    )
    input_grads = jnp.stack(
        [
            lax.dynamic_index_in_dim(grad_stack, micro_index + section_index, 0, False)
            for micro_index in range(micro_count)
        ],
        1,
    )
    full_grads = tuple((grad_array[None] for grad_array in grad_sums))
    reduced = reduce_grads(full_grads)
    return (
        layer_out[None],
        input_grads[None],
        reduced[0],
        reduced[1],
        reduced[2],
        reduced[3],
        reduced[4],
        reduced[5],
        reduced[6],
    )


CH = 128
PAIRS = H // 2
QB = 2 * H * HEAD
STATE_ROWS = D + 16
EPS = 1e-05
TILE = 256
AXES = ("section", "dp", "seq")
MESH = pl.DeviceIdType.MESH
f32 = jnp.float32
bf16 = jnp.bfloat16
GELU_C = 0.7978845608028654
GELU_A = 0.044715
SMALL_ROWS = 208
VEC_ROWS = 72
GAIN_ROWS = 16
SHIFT1, QKV_BIAS, OUT_BIAS, SHIFT2, UP_BIAS, DOWN_BIAS = 0, 6, 24, 30, 36, 60


class Kept(NamedTuple):
    a: Any
    qkv: Any
    ph: Any
    o: Any
    inv: Any
    ob: Any
    r: Any
    n2: Any
    hid: Any
    gp: Any
    res: Any
    pre: Any


class ForwardRefs(NamedTuple):
    tokens: Any
    cot: Any
    small: Any
    wq: Any
    wo: Any
    wu: Any
    wd: Any
    gq: Any
    go: Any
    gu: Any
    gd: Any
    gv: Any
    bd: Any
    tok_out: Any
    cot_out: Any


class ForwardScratch(NamedTuple):
    tok: Any
    sm: Any
    vec: Any
    mt: Any
    st: Any
    stb: Any
    got: Any
    vq: Any
    vo: Any
    vu: Any
    vd: Any
    g_send: Any
    g_recv: Any
    g_local: Any
    c_send: Any
    c_recv: Any
    s_send: Any
    s_recv: Any
    w_sem: Any
    o_sem: Any
    m_sem: Any


class Weights(NamedTuple):
    q: Any
    o: Any
    u: Any
    d: Any = None


VMEM = pl.BlockSpec(memory_space=pltpu.VMEM)
SMEM = pl.BlockSpec(memory_space=pltpu.SMEM)
ANY = pl.BlockSpec(memory_space=pl.ANY)


def nn(a, b):
    return lax.dot_general(a, b, (((1,), (0,)), ((), ())), preferred_element_type=f32)


def nt(a, b):
    return lax.dot_general(a, b, (((1,), (1,)), ((), ())), preferred_element_type=f32)


def tn(a, b):
    return lax.dot_general(a, b, (((0,), (0,)), ((), ())), preferred_element_type=f32)


def loop(count, body, events=None):
    events = events or {}

    def step(i, c):
        body(i)
        for at, event in events.items():

            @pl.when(i == at)
            def _():
                event()

        return c

    lax.fori_loop(0, count, step, 0)


def span(i, size):
    return pl.ds(pl.multiple_of(i * size, size), size)


def wide(ref, layer, row, count):
    return jnp.concatenate([ref[layer, pl.ds(row + i, 1), :] for i in range(count)], 1)


def finish(dst, sem):
    pltpu.make_async_copy(dst, dst, sem).wait()


def arrived(dst, recv):
    finish(dst, recv)


def departed(src, send):
    finish(src, send)


def shape(dims, kind):
    return jax.ShapeDtypeStruct(dims, kind)


def call(kernel, outs, scratch, specs, args, flops, out_specs=None, vmem=60, cid=None):
    if out_specs is None:
        out_specs = [VMEM] * len(outs)
    moved = sum(a.size * a.dtype.itemsize for a in args if a.ndim > 0)
    moved += sum(o.size * o.dtype.itemsize for o in outs)
    params = dict(vmem_limit_bytes=vmem * 1024 * 1024)
    if cid is not None:
        params.update(collective_id=cid, has_side_effects=True)
    return pl.pallas_call(
        kernel,
        out_shape=outs,
        in_specs=specs,
        out_specs=out_specs,
        scratch_shapes=scratch,
        compiler_params=pltpu.CompilerParams(**params),
        cost_estimate=pl.CostEstimate(flops=flops, bytes_accessed=moved, transcendentals=0),
    )(*args)


def standardize(u):
    cen = u - jnp.mean(u, -1, keepdims=True)
    rstd = lax.rsqrt(jnp.mean(cen * cen, -1, keepdims=True) + EPS)
    return cen * rstd, rstd


def lanes(rows):
    return lax.broadcasted_iota(jnp.int32, (rows, CH), 1)


def half_sums(t, low):
    s1 = jnp.sum(jnp.where(low, t, 0.0), -1, keepdims=True)
    s2 = jnp.sum(jnp.where(low, 0.0, t), -1, keepdims=True)
    return jnp.where(low, s1, s2)


def half_softmax(l, low):
    m1 = jnp.max(jnp.where(low, l, -jnp.inf), -1, keepdims=True)
    m2 = jnp.max(jnp.where(low, -jnp.inf, l), -1, keepdims=True)
    p = jnp.exp(l - jnp.where(low, m1, m2))
    return p / half_sums(p, low)


def split_states(src, dst):
    hi = src[...].astype(bf16)
    dst[0:STATE_ROWS] = hi
    dst[STATE_ROWS:] = (src[D:] - hi[D:].astype(f32)).astype(bf16)


def add_states(dst, src):
    dst[...] += src[0:STATE_ROWS].astype(f32)
    dst[D:] += src[STATE_ROWS:].astype(f32)


class Place:
    def __init__(self, n):
        self.n, self.nz, self.group = n, n // 2, n // 4
        self.x = lax.axis_index("section")
        self.d = lax.axis_index("dp")
        self.j = lax.axis_index("seq")
        self.z, self.y = lax.div(self.j, 2), lax.rem(self.j, 2)
        self.i = lax.rem(self.z, 2) * 2 + self.y
        self.jj = lax.div(self.z, 2)
        self.r = self.x * self.group + self.jj

    def at(self, x=None, d=None, z=None, y=None, j=None):
        x = self.x if x is None else x
        d = self.d if d is None else d
        if j is None:
            j = (self.z if z is None else z) * 2 + (self.y if y is None else y)
        return (x, d, j)

    def zpos(self, o):
        return lax.rem(self.z + o + self.nz, self.nz)

    def member(self, r):
        z = lax.rem(r, self.group) * 2 + lax.rem(self.z, 2)
        return (lax.div(r, self.group), self.d, z * 2 + self.y)

    def meet(self):
        barrier = pltpu.get_barrier_semaphore()
        for dx in range(2):
            for o in range(self.n):
                if dx == 0 and o == 0:
                    continue
                other = (
                    lax.rem(self.x + dx, 2),
                    self.d,
                    lax.rem(self.j + o, self.n),
                )
                pl.semaphore_signal(barrier, inc=1, device_id=other, device_id_type=MESH)
        pl.semaphore_signal(
            barrier, inc=1, device_id=(self.x, 1 - self.d, self.j), device_id_type=MESH
        )
        pl.semaphore_wait(barrier, 2 * self.n)


def remote(src, dst, send, recv, to):
    return pltpu.make_async_remote_copy(
        src_ref=src, dst_ref=dst, send_sem=send, recv_sem=recv, device_id=to, device_id_type=MESH
    )


class Gather:
    def __init__(self, place, src, buf, send, recv, local, y_last, halves=True):
        self.p, self.src, self.buf = place, src, buf
        self.send, self.recv, self.local = send, recv, local
        self.y_last, self.halves = y_last, halves
        self.width = src.shape[1]
        self.sent = []

    def columns(self):
        if not self.halves:
            return slice(None)
        return pl.ds(pl.multiple_of(self.p.d * self.width, CH), self.width)

    def shard(self, x, o, y):
        return self.buf.at[x, self.p.zpos(-o), y, :, self.columns()]

    def column(self, x, y):
        return self.buf.at[x, :, y, :, self.columns()]

    def go(self, src, dst, slot, to):
        remote(src, dst, self.send.at[slot], self.recv.at[slot], to).start()
        self.sent.append(slot)

    def got(self, ref, slot):
        arrived(ref, self.recv.at[slot])

    def start(self):
        p = self.p
        own = self.shard(p.x, 0, p.y)
        pltpu.make_async_copy(self.src, own, self.local).start()
        for o in range(1, p.nz):
            self.go(self.src, own, o - 1, p.at(z=p.zpos(o)))
        self.first(0)

    def first(self, o):
        p = self.p
        here = self.shard(p.x, o, p.y)
        if o > 0:
            self.got(here, o - 1)
        src = self.src if o == 0 else here
        self.go(src, here, 3 + o, p.at(y=1 - p.y))
        self.go(src, here, 7 + o, p.at(x=1 - p.x))

    def firsts(self):
        for o in range(1, self.p.nz):
            self.first(o)
        finish(self.shard(self.p.x, 0, self.p.y), self.local)
        self.core(0)

    def seconds(self):
        p = self.p
        for o in range(p.nz):
            if self.y_last:
                here = self.shard(1 - p.x, o, p.y)
                self.got(here, 7 + o)
                self.go(here, here, 11 + o, p.at(y=1 - p.y))
            else:
                here = self.shard(p.x, o, 1 - p.y)
                self.got(here, 3 + o)
                self.go(here, here, 11 + o, p.at(x=1 - p.x))
        self.core(2 if self.y_last else 1)

    def thirds(self):
        q = 1 if self.y_last else 2
        self.wait_all(q)
        self.core(q)

    def last(self):
        self.wait_all(3)
        self.core(3)

    def kind(self, q):
        p = self.p
        return (p.x if q < 2 else 1 - p.x), (p.y if q % 2 == 0 else 1 - p.y)

    def wait_all(self, q):
        x, y = self.kind(q)
        for o in range(self.p.nz):
            self.got(self.shard(x, o, y), (0, 3, 7, 11)[q] + o)

    def core(self, q):
        if self.halves:
            part = self.column(*self.kind(q))
            self.go(part, part, 15 + q, self.p.at(d=1 - self.p.d))

    def done(self):
        if self.halves:
            p = self.p
            other = pl.ds(pl.multiple_of((1 - p.d) * self.width, CH), self.width)
            for q in range(4):
                x, y = self.kind(q)
                self.got(self.buf.at[x, :, y, :, other], 15 + q)

    def close(self):
        p = self.p
        for slot in self.sent:
            ref = self.column(p.x, p.y) if slot >= 15 else self.shard(p.x, 0, p.y)
            departed(ref, self.send.at[slot])


def forward_kernel(n, *refs):
    ref = ForwardRefs(*refs[:15])
    saved = [Kept(*refs[15:27]), Kept(*refs[27:39])]
    v = Kept(*refs[39:51])
    own = ForwardScratch(*refs[51:])
    p = Place(n)
    nz, group = p.nz, p.group
    t = v.a.shape[0]
    nc = t // CH
    p.meet()

    def gather(k, src, buf, y_last, halves=True):
        return Gather(
            p, src, buf, own.g_send.at[k], own.g_recv.at[k], own.g_local.at[k], y_last, halves
        )

    gs = gather(0, ref.small, own.sm, False, False)
    gq = gather(1, ref.wq, ref.gq, True)
    go = gather(2, ref.wo, ref.go, False)
    gu = gather(3, ref.wu, ref.gu, False)
    gd = gather(4, ref.wd, ref.gd, True)
    gathers = (gs, gq, go, gu, gd)

    def collect(which, s):
        i = lax.rem(p.j + s, 4)
        to = (lax.div(p.z, 2) * 2 + lax.div(i, 2)) * 2 + lax.rem(i, 2)
        slot = lax.rem(p.j, 4)
        src = (ref.cot if which else ref.tokens).at[i, p.x]
        dst = (ref.cot_out if which else own.tok).at[span(slot, CH), :]
        send, recv = own.c_send.at[which], own.c_recv.at[which]
        copy = remote(src, dst, send.at[s], recv.at[slot], p.at(j=to))

        @pl.when(to != p.j)
        def _():
            copy.start()

        @pl.when(to == p.j)
        def _():
            pltpu.make_async_copy(src, dst, recv.at[slot]).start()

        def close():
            @pl.when(to != p.j)
            def _():
                copy.wait_send()

        return close

    closing = [collect(0, s) for s in range(4)]
    for g in gathers:
        g.start()
    gs.firsts()
    gq.firsts()
    gs.seconds()
    go.firsts()
    gq.seconds()
    gs.thirds()
    gs.last()

    vec, gv, bd, sm, mt = own.vec, ref.gv, ref.bd, own.sm, own.mt
    vec[...] = jnp.zeros(vec.shape, f32)
    gv[...] = jnp.zeros(gv.shape, f32)
    bd[...] = jnp.zeros(bd.shape, bf16)
    for layer in range(2):
        for k in range(n):
            part = sm[layer, k // 2, k % 2, 0:16, :].astype(f32)
            row, grow = (33 * k) // 4, (3 * k) // 2
            vec[layer, row : row + 9, :] += part[0:9]
            gv[layer, grow : grow + 2, :] += part[9:11]
        for head in range(2 * H):
            k, at, odd = head // 3, 16 + (head % 3) * HEAD, head % 2
            both = sm[layer, k // 2, k % 2, at : at + HEAD, :].astype(f32)
            flip = pltpu.roll(both, HEAD, 1)
            rows = pl.ds(odd * HEAD, HEAD)
            signed = jnp.where(lanes(HEAD) < HEAD, both, -flip)
            bd[layer, head // 2, rows, odd * CH : (odd + 1) * CH] = signed.astype(bf16)
            if odd:
                turned = jnp.where(lanes(HEAD) < HEAD, 0.0, both)
            else:
                turned = jnp.where(lanes(HEAD) < HEAD, flip, 0.0)
            mt[layer, head // 2, rows, :] = turned.astype(bf16)

    for k in range(4):
        arrived(own.tok.at[pl.ds(k * CH, CH), :], own.c_recv.at[0, k])

    def load(g, dst, layer, k):
        pltpu.make_async_copy(g.buf.at[layer], dst, own.w_sem.at[k]).start()

    def loaded(dst, k):
        finish(dst, own.w_sem.at[k])

    def save(layer, *sources, part=None):
        for src in sources:
            k = [src is x for x in v].index(True)
            dst = saved[layer][k]
            if src is v.res:
                src = src.at[layer]
            if part is not None:
                cols = pl.ds(part * (FF // 2), FF // 2)
                src, dst = src.at[:, cols], dst.at[:, cols]
            pltpu.make_async_copy(src, dst, own.o_sem.at[layer, k]).start()

    def saved_all(layer, *sources):
        for src in sources:
            k = [src is x for x in v].index(True)
            finish(src.at[layer] if src is v.res else src, own.o_sem.at[layer, k])

    flat = Weights(
        own.vq.reshape(D, 3 * D),
        own.vo.reshape(D, D),
        own.vu.reshape(D, FF),
        own.vd.reshape(FF, D),
    )
    low = lanes(CH) < HEAD
    tril = lax.broadcasted_iota(jnp.int32, (CH, CH), 0) >= lanes(CH)
    eye = jnp.where(lax.broadcasted_iota(jnp.int32, (CH, CH), 0) == lanes(CH), 1.0, 0.0)
    eye = eye.astype(bf16)

    def norm_rows(layer, src, dst, which, shift):
        gain = wide(gv, layer, which * 6, 6)
        bias = wide(vec, layer, shift, 6)

        def body(i):
            xh, _ = standardize(src[span(i, CH), :].astype(f32))
            dst[span(i, CH), :] = (xh * gain + bias).astype(bf16)

        loop(nc, body)

    def bias_cols(layer, at, j):
        return wide(vec, layer, at + 2 * j, 2)

    def project(layer, u, events):
        a, qkv, ph, st = v.a, v.qkv, v.ph, own.st
        if layer == 1:
            saved_all(0, v.a, v.qkv, v.ph)
        norm_rows(layer, u, a, 0, SHIFT1)
        loaded(own.vq, 0)
        save(layer, v.a)

        def column(j):
            cols = span(j, TILE)
            qkv[:, cols] = (
                nn(a[...], flat.q[:, cols]) + bias_cols(layer, QKV_BIAS, j)
            ).astype(bf16)

        loop(3 * D // TILE, column, events[0])
        save(layer, v.qkv)

        def pair(k):
            logits = nt(mt[layer, k], qkv[:, span(k, CH)]).reshape(2, HEAD, t)
            up = jnp.exp(logits - jnp.max(logits, 1, keepdims=True))
            down = jnp.exp(jnp.min(logits, 1, keepdims=True) - logits)
            up = up * (1.0 / jnp.sum(up, 1, keepdims=True))
            down = down * (1.0 / jnp.sum(down, 1, keepdims=True))
            both = jnp.concatenate([up, down], 1).reshape(2 * CH, t).astype(bf16)
            for c in range(nc):
                ph[pl.ds(c * CH, CH), span(k, 2 * CH)] = nt(
                    eye, both[:, c * CH : (c + 1) * CH]
                ).astype(bf16)

        loop(PAIRS, lambda k: pair(k + PAIRS), events[1])

        def state(k):
            val = qkv[:, pl.ds(pl.multiple_of(2 * D + k * CH, CH), CH)]
            for hh in range(2):
                key = ph[:, pl.ds(pl.multiple_of((H + 2 * k + hh) * CH, CH), CH)]
                full = tn(val, key)
                st[layer, span(2 * k + hh, HEAD), :] = full[hh * HEAD : (hh + 1) * HEAD]
                st[layer, pl.ds(D + 2 * k + hh, 1), :] = jnp.sum(
                    key.astype(f32), 0, keepdims=True
                )

        loop(PAIRS, state)
        st[layer, D + H :, :] = jnp.zeros((STATE_ROWS - D - H, CH), f32)
        split_states(st.at[layer], own.stb.at[layer])
        send_states(layer, st, 1)
        loop(PAIRS, pair, events[2])
        save(layer, v.ph)

    members = 2 * group

    def send_states(layer, st, sign):
        for o in range(1, members):
            ok = (p.r + o < members) if sign > 0 else (p.r - o >= 0)

            @pl.when(ok)
            def _():
                remote(
                    own.stb.at[layer],
                    own.got.at[layer, o - 1],
                    own.s_send.at[layer, o - 1],
                    own.s_recv.at[layer, o - 1],
                    p.member(p.r + sign * o),
                ).start()

    def take_states(layer, sign):
        pre = v.pre
        pre[...] = jnp.zeros(pre.shape, f32)
        for o in range(1, members):
            ok = (p.r - o >= 0) if sign > 0 else (p.r + o < members)

            @pl.when(ok)
            def _():
                arrived(own.got.at[layer, o - 1], own.s_recv.at[layer, o - 1])
                add_states(pre, own.got.at[layer, o - 1])

    def close_states(layer, sign):
        for o in range(1, members):
            ok = (p.r + o < members) if sign > 0 else (p.r - o >= 0)

            @pl.when(ok)
            def _():
                departed(own.stb.at[layer], own.s_send.at[layer, o - 1])

    def mix(layer, u, events):
        qkv, ph, o_, inv, ob = v.qkv, v.ph, v.o, v.inv, v.ob
        r, n2, hid, gp = v.r, v.n2, v.hid, v.gp
        res = v.res.at[layer]
        if layer == 1:
            saved_all(0, v.pre, v.o, v.inv, v.ob, v.r, v.n2, v.hid, v.gp)
        take_states(layer, 1)
        if layer == 1:
            closing.extend([collect(1, s) for s in range(4)])
        save(layer, v.pre)
        s0 = v.pre

        def pair(k):
            cols = span(k, CH)
            s = s0[cols, :]
            tot = [s0[pl.ds(D + 2 * k + hh, 1), :] for hh in range(2)]
            for c in range(nc):
                rows = pl.ds(c * CH, CH)
                val = qkv[rows, pl.ds(pl.multiple_of(2 * D + k * CH, CH), CH)]
                sl = s.astype(bf16)
                sf = (s - sl.astype(f32)).astype(bf16)
                done = []
                new = []
                for hh in range(2):
                    qh = ph[rows, span(2 * k + hh, CH)]
                    kh = ph[rows, pl.ds(pl.multiple_of((H + 2 * k + hh) * CH, CH), CH)]
                    score = jnp.where(tril, nt(qh, kh), 0.0)
                    hi = score.astype(bf16)
                    lo = (score - hi.astype(f32)).astype(bf16)
                    num = nn(hi, val) + nn(lo, val) + nt(qh, sl) + nt(qh, sf)
                    den = jnp.sum(score + qh.astype(f32) * tot[hh], -1, keepdims=True)
                    rec = 1.0 / den
                    done.append((num * rec, rec))
                    new.append(tn(val, kh)[hh * HEAD : (hh + 1) * HEAD])
                    tot[hh] = tot[hh] + jnp.sum(kh.astype(f32), 0, keepdims=True)
                s = s + jnp.concatenate(new, 0)
                both = jnp.where(low, done[0][0], done[1][0])
                o_[rows, cols] = both
                ob[rows, cols] = both.astype(bf16)
                inv[rows, cols] = jnp.where(low, done[0][1], done[1][1])

        loop(PAIRS, pair, events[0])
        save(layer, v.o, v.inv, v.ob)
        events[1]()
        loaded(own.vo, 1)

        def out_col(j):
            cols = span(j, TILE)
            r[:, cols] = (
                u[:, cols].astype(f32)
                + nn(ob[...], flat.o[:, cols])
                + bias_cols(layer, OUT_BIAS, j)
            )

        loop(D // TILE, out_col)
        norm_rows(layer, r, n2, 1, SHIFT2)
        save(layer, v.r, v.n2)
        events[2]()
        loaded(own.vu, 2)

        def up_col(j):
            cols = span(j, TILE)
            zt = nn(n2[...], flat.u[:, cols]) + bias_cols(layer, UP_BIAS, j)
            z2 = zt * zt
            half = 0.5 + 0.5 * jnp.tanh(zt * (GELU_C + (GELU_C * GELU_A) * z2))
            act = zt * half
            hid[:, cols] = act.astype(bf16)
            slope = 2.0 * GELU_C + (6.0 * GELU_C * GELU_A) * z2
            gp[:, cols] = (half + act * ((1.0 - half) * slope)).astype(bf16)

        halfway = FF // TILE // 2 - 1
        loop(FF // TILE, up_col, {halfway: lambda: save(layer, v.hid, v.gp, part=0), **events[3]})
        save(layer, v.hid, v.gp, part=1)
        events[4]()
        loaded(own.vd, 3)

        def down_col(j):
            cols = span(j, TILE)
            res[:, cols] = (
                r[:, cols] + nn(hid[...], flat.d[:, cols]) + bias_cols(layer, DOWN_BIAS, j)
            ).astype(bf16)

        loop(D // TILE, down_col)
        save(layer, v.res)

    def run(*steps):
        def go_():
            for step in steps:
                step()

        return go_

    nothing = run()
    gu.firsts()
    go.seconds()
    gq.thirds()
    gq.last()
    gq.done()
    load(gq, own.vq, 0, 0)
    tok_out = pltpu.make_async_copy(own.tok, ref.tok_out, own.m_sem)
    tok_out.start()
    project(0, own.tok, [{}, {0: gd.firsts, 4: gu.seconds}, {1: go.thirds, 3: gd.seconds}])
    mix(
        0,
        own.tok,
        [
            {1: go.last, 2: gu.thirds},
            run(go.done, functools.partial(load, go, own.vo, 0, 1), gd.thirds),
            run(gu.last, gu.done, functools.partial(load, gu, own.vu, 0, 2)),
            {},
            run(
                functools.partial(load, gq, own.vq, 1, 0),
                functools.partial(load, go, own.vo, 1, 1),
                functools.partial(load, gu, own.vu, 1, 2),
                gd.last,
                gd.done,
                functools.partial(load, gd, own.vd, 0, 3),
            ),
        ],
    )
    load(gd, own.vd, 1, 3)
    project(1, v.res.at[0], [{}, {}, {}])
    mix(1, v.res.at[0], [{}, nothing, nothing, {}, nothing])

    for g in gathers:
        g.close()
    for close in closing:
        close()
    for k in range(4):
        arrived(ref.cot_out.at[pl.ds(k * CH, CH), :], own.c_recv.at[1, k])
    for layer in range(2):
        close_states(layer, 1)

    tok_out.wait()
    saved_all(0, v.res)
    saved_all(1, *v)


def forward_pass(n, tokens, cotangent, small, wq, wo, wu, wd):
    t = 4 * CH
    nz = n // 2
    full = [
        shape((2, nz, 2, w.shape[0], 2 * w.shape[1]), bf16) for w in (wq, wo, wu, wd)
    ]
    kept = [
        shape((t, D), bf16),
        shape((t, 3 * D), bf16),
        shape((t, 2 * QB), bf16),
        shape((t, D), f32),
        shape((t, D), f32),
        shape((t, D), bf16),
        shape((t, D), f32),
        shape((t, D), bf16),
        shape((t, FF), bf16),
        shape((t, FF), bf16),
        shape((t, D), bf16),
        shape((STATE_ROWS, CH), f32),
    ]
    outs = full + [shape((2, GAIN_ROWS, CH), f32), shape((2, 2 * PAIRS, CH, 2 * CH), bf16)]
    outs += [shape((t, D), bf16)] * 2 + kept * 2
    specs = [ANY] * 4 + [VMEM] * 2 + [ANY] * (len(outs) - 6)
    scratch = [pltpu.VMEM(k.shape, k.dtype) for k in kept]
    scratch[10] = pltpu.VMEM((2, t, D), bf16)
    scratch += [
        pltpu.VMEM((t, D), bf16),
        pltpu.VMEM((2, nz, 2, SMALL_ROWS, CH), bf16),
        pltpu.VMEM((2, VEC_ROWS, CH), f32),
        pltpu.VMEM((2, 2 * PAIRS, CH, CH), bf16),
        pltpu.VMEM((2, STATE_ROWS, CH), f32),
        pltpu.VMEM((2, STATE_ROWS + 16, CH), bf16),
        pltpu.VMEM((2, n // 2 - 1, STATE_ROWS + 16, CH), bf16),
    ]
    scratch += [pltpu.VMEM(w.shape[1:], bf16) for w in full]
    dma = pltpu.SemaphoreType.DMA
    scratch += [dma((5, 19)), dma((5, 19)), dma((5,)), dma((2, 4)), dma((2, 4))]
    scratch += [dma((2, n // 2 - 1)), dma((2, n // 2 - 1)), dma((4,))]
    scratch += [dma((2, 12)), dma]
    got = call(
        functools.partial(forward_kernel, n),
        outs,
        scratch,
        [ANY] * 7,
        [tokens, cotangent, small, wq, wo, wu, wd],
        4 * t * D * (4 * D + 2 * FF),
        specs,
        cid=0,
    )
    layers = [Kept(*got[8:20]), Kept(*got[20:32])]
    return got[:4], got[4], got[5], got[6], got[7], layers


def with_error(gv, swapped, lane, hh):
    first = HEAD * (1 - hh)
    hi = swapped.astype(bf16)
    lo = (swapped - hi.astype(f32)).astype(bf16)
    own = (lane < HEAD) if hh == 0 else (lane >= HEAD)
    spare = jnp.where(
        lane == first + 1,
        lo,
        jnp.where((lane == first) | (lane == first + 2), hi, jnp.zeros_like(gv)),
    )
    return jnp.where(own, gv, spare)


def with_ones(v, lane, hh):
    first = HEAD * (1 - hh)
    own = (lane < HEAD) if hh == 0 else (lane >= HEAD)
    spare = jnp.where((lane == first) | (lane == first + 1), jnp.ones_like(v), jnp.zeros_like(v))
    return jnp.where(own, v, spare)


def with_totals(s, tot, row, hh, again):
    first = HEAD * (1 - hh)
    hi = tot.astype(bf16).astype(f32)
    lo = tot - hi
    own = (row < HEAD) if hh == 0 else (row >= HEAD)
    if again:
        spare = jnp.where(
            (row == first) | (row == first + 1), hi, jnp.where(row == first + 2, lo, 0.0)
        )
    else:
        spare = jnp.where(row == first, hi, jnp.where(row == first + 1, lo, 0.0))
    return jnp.where(own, s, spare).astype(bf16)


def put_rows(ref, layer, row, val):
    for i in range(val.shape[1] // CH):
        ref[layer, pl.ds(row + i, 1), :] = val[:, i * CH : (i + 1) * CH]


class Reduce:
    def __init__(self, place, layer, buf, temp, land, out, fin, send, recv, local, last):
        self.p, self.layer, self.buf, self.temp = place, layer, buf, temp
        self.land_d, self.land_y, self.land_z, self.land_x = land
        self.out, self.fin, self.local, self.last = out, fin, local, last
        self.send, self.recv = send, recv
        self.r, self.c = buf.shape[2], buf.shape[3]

    def go(self, src, dst, slot, to):
        remote(src, dst, self.send.at[slot], self.recv.at[slot], to).start()

    def fetch(self, src, dst):
        copy = pltpu.make_async_copy(src, dst, self.local)
        copy.start()
        copy.wait()

    def send_core(self):
        self.go(self.buf, self.land_d, 0, self.p.at(d=1 - self.p.d))

    def got_core(self):
        departed(self.buf, self.send.at[0])
        arrived(self.land_d, self.recv.at[0])

    def send_y(self):
        p = self.p
        self.go(self.buf.at[:, 1 - p.y], self.land_y, 1, p.at(y=1 - p.y))

    def step_y(self):
        p = self.p
        arrived(self.land_y, self.recv.at[1])
        self.fetch(self.land_y, self.temp)
        for i in range(1, p.nz + 1):
            zi = p.zpos(i)
            self.buf[zi, p.y] = (
                self.buf[zi, p.y].astype(f32) + self.temp[zi].astype(f32)
            ).astype(bf16)
            if i < p.nz:
                self.go(self.buf.at[zi, p.y], self.land_z.at[i - 1], 1 + i, p.at(z=zi))

    def step_z(self):
        p = self.p
        for i in range(1, p.nz):
            arrived(self.land_z.at[i - 1], self.recv.at[1 + i])
        self.fetch(self.land_z, self.temp.at[pl.ds(0, p.nz - 1)])
        total = self.buf[p.z, p.y].astype(f32)
        for i in range(p.nz - 1):
            total = total + self.temp[i].astype(f32)

        @pl.when(p.x == self.layer)
        def _():
            self.fin[...] = total

        @pl.when(p.x != self.layer)
        def _():
            self.buf[p.z, p.y] = total.astype(bf16)
            self.go(self.buf.at[p.z, p.y], self.land_x, 5, p.at(x=1 - p.x))

    def half(self):
        return pl.ds(pl.multiple_of(self.p.d * self.c, CH), self.c)

    def other(self):
        return pl.ds(pl.multiple_of((1 - self.p.d) * self.c, CH), self.c)

    def step_x(self):
        p = self.p

        @pl.when(p.x == self.layer)
        def _():
            arrived(self.land_x, self.recv.at[5])
            self.fetch(self.land_x, self.temp.at[0])
            self.fin[...] += self.temp[0].astype(f32)
            own = self.out.at[:, self.half()]
            self.go(self.fin, own, 6, p.at(d=1 - p.d))
            pltpu.make_async_copy(self.fin, own, self.last).start()

    def close(self):
        p = self.p
        departed(self.buf.at[:, 0], self.send.at[1])
        for i in range(1, p.nz):
            departed(self.buf.at[0, 0], self.send.at[1 + i])

        @pl.when(p.x != self.layer)
        def _():
            departed(self.buf.at[0, 0], self.send.at[5])

    def end(self):
        @pl.when(self.p.x == self.layer)
        def _():
            departed(self.fin, self.send.at[6])
            arrived(self.out.at[:, self.other()], self.recv.at[6])
            finish(self.fin, self.last)


class SmallReduce:
    def __init__(self, place, layer, buf, land, out, send, recv):
        self.p, self.layer, self.buf, self.out = place, layer, buf, out
        self.land_d, self.land_y, self.land_z, self.land_x = land
        self.send, self.recv = send, recv

    def go(self, src, dst, slot, to):
        remote(src, dst, self.send.at[slot], self.recv.at[slot], to).start()

    def send_core(self):
        self.go(self.buf, self.land_d, 0, self.p.at(d=1 - self.p.d))

    def step_d(self):
        p = self.p
        departed(self.buf, self.send.at[0])
        arrived(self.land_d, self.recv.at[0])
        self.buf[...] += self.land_d[...]
        self.go(self.buf.at[:, 1 - p.y], self.land_y, 1, p.at(y=1 - p.y))

    def step_y(self):
        p = self.p
        arrived(self.land_y, self.recv.at[1])
        for i in range(1, p.nz + 1):
            zi = p.zpos(i)
            self.buf[zi, p.y] += self.land_y[zi]
            if i < p.nz:
                self.go(self.buf.at[zi, p.y], self.land_z.at[i - 1], 1 + i, p.at(z=zi))

    def step_z(self):
        p = self.p
        for i in range(1, p.nz):
            arrived(self.land_z.at[i - 1], self.recv.at[1 + i])
        total = self.buf[p.z, p.y]
        for i in range(p.nz - 1):
            total = total + self.land_z[i]
        self.buf[p.z, p.y] = total

        @pl.when(p.x != self.layer)
        def _():
            self.go(self.buf.at[p.z, p.y], self.land_x, 5, p.at(x=1 - p.x))

    def step_x(self):
        p = self.p

        @pl.when(p.x == self.layer)
        def _():
            arrived(self.land_x, self.recv.at[5])
            self.out[...] = self.buf[p.z, p.y] + self.land_x[...]

    def close(self):
        p = self.p
        departed(self.buf.at[:, 0], self.send.at[1])
        for i in range(1, p.nz):
            departed(self.buf.at[0, 0], self.send.at[1 + i])

        @pl.when(p.x != self.layer)
        def _():
            departed(self.buf.at[0, 0], self.send.at[5])


SMALL_OUT = 112


class Loaded(NamedTuple):
    gp: Any
    r: Any
    o: Any
    inv: Any
    ph: Any
    qkv: Any
    n2: Any
    ob: Any
    a: Any
    u: Any
    pre: Any


class BackwardRefs(NamedTuple):
    cot: Any
    res0: Any
    res1: Any
    gv: Any
    bd: Any
    wq: Any
    wo: Any
    wu: Any
    wd: Any


class BackwardScratch(NamedTuple):
    g: Any
    drb: Any
    gs: Any
    tmp: Any
    acc: Any
    st: Any
    stb: Any
    later: Any
    got: Any
    mg: Any
    vr: Any
    gr: Any
    hidr: Any
    wdr: Any
    vq: Any
    vo: Any
    vu: Any
    bq: Any
    bo: Any
    bu: Any
    bd_: Any
    tmp96: Any
    tmpd: Any
    fq: Any
    fo: Any
    fu: Any
    fd: Any
    ty96: Any
    tyd: Any
    sb: Any
    sd: Any
    sy: Any
    sz: Any
    sx: Any
    r_send: Any
    r_recv: Any
    r_local: Any
    q_send: Any
    q_recv: Any
    s_send: Any
    s_recv: Any
    d_send: Any
    d_recv: Any
    w_sem: Any
    l_sem: Any
    h_sem: Any
    t_sem: Any
    k_sem: Any


Q, O, U, DN = range(4)


def backward_kernel(n, *refs):
    ref = BackwardRefs(*refs[:9])
    source = [Loaded(*refs[9:20]), Loaded(*refs[20:31])]
    hidden = refs[31:33]
    lay, gin, small_out = refs[33], refs[34], refs[39]
    wgrads = refs[35:39]
    lands = refs[40:72]
    v = Loaded(*refs[72:83])
    own = BackwardScratch(*refs[83:])
    p = Place(n)
    nz, group = p.nz, p.group
    t = own.drb.shape[0]
    nc = t // CH
    members = 2 * group
    gains, gbuf, tmp, acc = ref.gv, own.g, own.tmp, own.acc
    vr, gr, mg = own.vr, own.gr, own.mg
    flat = Weights(own.vq.reshape(D, 3 * D), own.vo.reshape(D, D), own.vu.reshape(D, FF))
    stored = (own.vq, own.vo, own.vu)
    lane_t = lanes(t)
    lane = lanes(CH)
    low = lane < HEAD
    row = lax.broadcasted_iota(jnp.int32, (CH, CH), 0)
    tril, triu = row >= lane, row <= lane

    def load(layer, *wanted):
        for dst in wanted:
            k = [dst is x for x in v].index(True)
            pltpu.make_async_copy(source[layer][k], dst, own.l_sem.at[k]).start()

    def loaded(*wanted):
        for dst in wanted:
            k = [dst is x for x in v].index(True)
            finish(dst, own.l_sem.at[k])

    def load_w(layer, k):
        w = (ref.wq, ref.wo, ref.wu)[k]
        pltpu.make_async_copy(w.at[layer], stored[k], own.w_sem.at[k]).start()

    def loaded_w(k):
        finish(stored[k], own.w_sem.at[k])

    def load_wd(layer, k):
        pltpu.make_async_copy(
            ref.wd.at[layer, k // 2, k % 2], own.wdr.at[k % 3], own.k_sem.at[k % 3]
        ).start()

    pltpu.make_async_copy(ref.cot, gbuf.at[0], own.t_sem.at[4]).start()
    for k in range(3):
        load_wd(1, k)
    load(1, v.gp)
    load_w(1, U)
    load(1, v.r, v.o, v.inv, v.ph)
    load_w(1, O)
    load_w(1, Q)
    load(1, v.qkv, v.n2, v.ob, v.a, v.u, v.pre)
    p.meet()
    finish(gbuf.at[0], own.t_sem.at[4])

    width = (3 * D // 2, D // 2, FF // 2, D // 2)
    bufs = (own.bq, own.bo, own.bu, own.bd_)
    fins = (own.fq, own.fo, own.fu, own.fd)
    reduces = []
    for layer in range(2):
        line = []
        for m in (Q, O, U, DN):
            at = (layer * 4 + m) * 4
            line.append(
                Reduce(
                    p,
                    layer,
                    bufs[m],
                    own.tyd if m == DN else own.ty96.at[:, :, pl.ds(0, width[m])],
                    lands[at : at + 4],
                    wgrads[m],
                    fins[m],
                    own.r_send.at[layer, m],
                    own.r_recv.at[layer, m],
                    own.r_local.at[m],
                    own.r_local.at[4 + m],
                )
            )
        reduces.append(line)
    smalls = [
        SmallReduce(
            p,
            layer,
            own.sb.at[layer],
            [land.at[layer] for land in (own.sd, own.sy, own.sz, own.sx)],
            small_out,
            own.q_send.at[layer],
            own.q_recv.at[layer],
        )
        for layer in range(2)
    ]

    def states_ok(o, taking):
        return (p.r + o < members) if taking else (p.r - o >= 0)

    def send_states(layer):
        for o in range(1, members):
            @pl.when(states_ok(o, False))
            def _():
                remote(
                    own.stb.at[layer],
                    own.got.at[layer, o - 1],
                    own.s_send.at[layer, o - 1],
                    own.s_recv.at[layer, o - 1],
                    p.member(p.r - o),
                ).start()

    def take_states(layer):
        later = own.later
        later[...] = jnp.zeros(later.shape, f32)
        for o in range(1, members):

            @pl.when(states_ok(o, True))
            def _():
                arrived(own.got.at[layer, o - 1], own.s_recv.at[layer, o - 1])
                add_states(later, own.got.at[layer, o - 1])

        return later

    def close_states(layer):
        for o in range(1, members):

            @pl.when(states_ok(o, False))
            def _():
                departed(own.stb.at[layer], own.s_send.at[layer, o - 1])

    def norm_back(x_ref, which, layer, body):
        gain = wide(gains, layer, which * 6, 6)
        acc[...] = jnp.zeros(acc.shape, f32)

        def step(i):
            rows = span(i, CH)
            xh, rstd = standardize(x_ref[rows, :].astype(f32))
            dn = tmp[rows, :]
            acc[0:1, :] += jnp.sum(dn, 0, keepdims=True)
            acc[1:2, :] += jnp.sum(dn * xh, 0, keepdims=True)
            dx = dn * gain
            body(
                rows,
                rstd
                * (dx - jnp.mean(dx, -1, keepdims=True) - xh * jnp.mean(dx * xh, -1, keepdims=True)),
            )

        loop(nc, step)
        put_rows(vr, layer, SHIFT2 if which else SHIFT1, acc[0:1, :])
        put_rows(gr, layer, which * 6, acc[1:2, :])

    def mlp_back(layer, g, events):
        gp, r, o_, inv, ph = v.gp, v.r, v.o, v.inv, v.ph
        drb, gs, st = own.drb, own.gs, own.st
        loaded(v.gp)
        for k in range(2 * nz):
            finish(own.wdr.at[k % 3], own.k_sem.at[k % 3])
            cols = pl.ds(k * FF // n, FF // n)
            part = (nt(g[...], own.wdr[k % 3]) * gp[:, cols]).astype(bf16)
            gp[:, cols] = part
            put_rows(
                vr, layer, UP_BIAS + 3 * k, jnp.sum(part.astype(f32), 0, keepdims=True)
            )
            if k + 3 < 2 * nz:
                load_wd(layer, k + 3)
            if k in events:
                events[k]()
        loaded_w(U)

        def n2_col(j):
            cols = span(j, TILE)
            tmp[:, cols] = nt(gp[...], flat.u[cols, :])

        loop(D // TILE, n2_col)
        loaded(v.r)

        def body(rows, back):
            up = g[rows, :].astype(f32)
            total = up + back
            acc[2:3, :] += jnp.sum(up, 0, keepdims=True)
            acc[3:4, :] += jnp.sum(total, 0, keepdims=True)
            r[rows, :] = total
            drb[rows, :] = total.astype(bf16)

        norm_back(r, 1, layer, body)
        put_rows(vr, layer, DOWN_BIAS, acc[2:3, :])
        put_rows(vr, layer, OUT_BIAS, acc[3:4, :])
        loaded_w(O)
        loaded(v.inv, v.o, v.ph)

        def do_col(j):
            cols = span(j, TILE)
            gs[:, cols] = (nt(drb[...], flat.o[cols, :]) * inv[:, cols]).astype(bf16)

        loop(D // TILE, do_col)
        low_t = lane_t < HEAD

        def pair(k):
            cols = span(k, CH)
            gv = gs[:, cols]
            prod = gv.astype(f32) * o_[:, cols]
            e0 = -jnp.sum(jnp.where(low_t, prod, 0.0), -1, keepdims=True)
            e1 = -jnp.sum(jnp.where(low_t, 0.0, prod), -1, keepdims=True)
            swapped = jnp.where(low_t, e1, e0)
            inv[:, cols] = swapped
            for hh in range(2):
                ge = with_error(gv, swapped, lane_t, hh)
                full = tn(ge, ph[:, span(2 * k + hh, CH)])
                st[layer, span(2 * k + hh, HEAD), :] = full[hh * HEAD : (hh + 1) * HEAD]
                at = HEAD * (1 - hh)
                st[layer, pl.ds(D + 2 * k + hh, 1), :] = full[at : at + 1] + full[at + 1 : at + 2]

        loop(PAIRS, pair)
        st[layer, D + H :, :] = jnp.zeros((STATE_ROWS - D - H, CH), f32)
        split_states(st.at[layer], own.stb.at[layer])
        send_states(layer)

    def weight_grad(layer, m, keep):
        red = reduces[layer][m]
        buf, c = red.buf, red.c
        base = (p.d if keep else 1 - p.d) * c
        if keep:
            red.got_core()
        elif layer == 0:
            reduces[1][m].close()
        if m == DN:
            rhs = gbuf[1 - layer, :, pl.ds(pl.multiple_of(base, CH), c)]

            def fetch(k):
                pltpu.make_async_copy(
                    hidden[layer].at[:, pl.ds(k * FF // n, FF // n)],
                    own.hidr.at[k % 3],
                    own.h_sem.at[k % 3],
                ).start()
                if keep:
                    pltpu.make_async_copy(
                        red.land_d.at[k // 2, k % 2], own.tmpd.at[k % 3], own.t_sem.at[k % 3]
                    ).start()

            for k in range(3):
                fetch(k)
            for k in range(2 * nz):
                finish(own.hidr.at[k % 3], own.h_sem.at[k % 3])
                val = tn(own.hidr[k % 3], rhs)
                if keep:
                    finish(own.tmpd.at[k % 3], own.t_sem.at[k % 3])
                    val = val + own.tmpd[k % 3].astype(f32)
                buf[k // 2, k % 2] = val.astype(bf16)
                if k + 3 < 2 * nz:
                    fetch(k + 3)
        else:
            lhs = (v.a, v.ob, v.n2)[m]
            rhs = (v.qkv, own.drb, v.gp)[m]
            step = 384
            count = c // step

            def fetch(k):
                pltpu.make_async_copy(
                    red.land_d.at[:, :, :, pl.ds(k * step, step)],
                    own.tmp96.at[k % 2],
                    own.t_sem.at[k % 2],
                ).start()

            if keep:
                for k in range(min(2, count)):
                    fetch(k)
            for k in range(count):
                val = tn(lhs[...], rhs[:, pl.ds(pl.multiple_of(base + k * step, CH), step)])
                if keep:
                    finish(own.tmp96.at[k % 2], own.t_sem.at[k % 2])
                for zi in range(nz):
                    for yi in range(2):
                        at = (zi * 2 + yi) * red.r
                        part = val[at : at + red.r]
                        if keep:
                            part = part + own.tmp96[k % 2, zi, yi].astype(f32)
                        buf[zi, yi, :, pl.ds(k * step, step)] = part.astype(bf16)
                if keep and k + 2 < count:
                    fetch(k + 2)
        if keep:
            red.send_y()
        else:
            red.send_core()

    def mix_back(layer, events):
        qkv, ph, gs, es = v.qkv, v.ph, own.gs, v.inv
        bd = ref.bd.at[layer]
        s1 = take_states(layer)
        loaded(v.qkv, v.pre)
        s0 = v.pre

        def pair(k):
            cols = span(k, CH)
            vcols = pl.ds(pl.multiple_of(2 * D + k * CH, CH), CH)
            kcols = pl.ds(pl.multiple_of(D + k * CH, CH), CH)

            def keys(rows, hh):
                return ph[rows, pl.ds(pl.multiple_of((H + 2 * k + hh) * CH, CH), CH)]

            before, finer = [], []
            s = s0[cols, :]
            tot = [s0[pl.ds(D + 2 * k + hh, 1), :] for hh in range(2)]
            for c in range(nc):
                rows = pl.ds(c * CH, CH)
                fine = (s - s.astype(bf16).astype(f32)).astype(bf16)
                none = jnp.zeros_like(fine)
                before.append([with_totals(s, tot[hh], row, hh, True) for hh in range(2)])
                finer.append([jnp.where(row < HEAD, fine, none), jnp.where(row < HEAD, none, fine)])
                if c < nc - 1:
                    val = qkv[rows, vcols]
                    new = []
                    for hh in range(2):
                        kh = keys(rows, hh)
                        new.append(tn(val, kh)[hh * HEAD : (hh + 1) * HEAD])
                        tot[hh] = tot[hh] + jnp.sum(kh.astype(f32), 0, keepdims=True)
                    s = s + jnp.concatenate(new, 0)
            ds = s1[cols, :]
            dtot = [s1[pl.ds(D + 2 * k + hh, 1), :] for hh in range(2)]
            acc_q = jnp.zeros((CH, 2 * CH), f32)
            acc_k = jnp.zeros((CH, 2 * CH), f32)
            sums = [jnp.zeros((1, CH), f32) for _ in range(3)]
            for c in reversed(range(nc)):
                rows = pl.ds(c * CH, CH)
                val = qkv[rows, vcols]
                gv = gs[rows, cols]
                ev = es[rows, cols]
                dsl = ds.astype(bf16)
                dl_q, dl_k, dv, new = [], [], [], []
                for hh in range(2):
                    qh = ph[rows, span(2 * k + hh, CH)]
                    kh = keys(rows, hh)
                    ge = with_error(gv, ev, lane, hh)
                    v1 = with_ones(val, lane, hh)
                    after = with_totals(ds, dtot[hh], row, hh, False)
                    da = jnp.where(tril, nt(ge, v1), 0.0).astype(bf16)
                    dat = jnp.where(triu, nt(v1, ge), 0.0).astype(bf16)
                    at = jnp.where(triu, nt(kh, qh), 0.0).astype(bf16)
                    dq = nn(da, kh) + nn(ge, before[c][hh]) + nn(ge, finer[c][hh])
                    dk = nn(dat, qh) + nn(v1, after)
                    dv.append(nn(at, gv) + nt(kh, dsl))
                    for p_, d_, to in ((qh, dq, dl_q), (kh, dk, dl_k)):
                        pf = p_.astype(f32)
                        to.append((pf * (d_ - half_sums(pf * d_, low))).astype(bf16))
                    full = tn(ge, qh)
                    new.append(full[hh * HEAD : (hh + 1) * HEAD])
                    first = HEAD * (1 - hh)
                    dtot[hh] = dtot[hh] + full[first : first + 1] + full[first + 1 : first + 2]
                ds = ds + jnp.concatenate(new, 0)
                dl_q = jnp.concatenate(dl_q, 1)
                dl_k = jnp.concatenate(dl_k, 1)
                acc_q = acc_q + tn(qkv[rows, cols], dl_q)
                acc_k = acc_k + tn(qkv[rows, kcols], dl_k)
                parts = (
                    (cols, nt(dl_q, bd[k])),
                    (kcols, nt(dl_k, bd[PAIRS + k])),
                    (vcols, jnp.where(low, dv[0], dv[1])),
                )
                for i, (where, new_) in enumerate(parts):
                    new_ = new_.astype(bf16)
                    qkv[rows, where] = new_
                    sums[i] = sums[i] + jnp.sum(new_.astype(f32), 0, keepdims=True)
            for i in range(3):
                vr[layer, pl.ds(QKV_BIAS + i * PAIRS + k, 1), :] = sums[i]
            for which, total in enumerate((acc_q, acc_k)):
                for hh in range(2):
                    blk = total[hh * HEAD : (hh + 1) * HEAD, hh * CH : (hh + 1) * CH]
                    mg[which * H + 2 * k + hh] = blk - pltpu.roll(blk, HEAD, 1)

        loop(PAIRS, pair, events)
        loaded_w(Q)

        def n1_col(j):
            cols = span(j, TILE)
            tmp[:, cols] = nt(qkv[...], flat.q[cols, :])

        loop(D // TILE, n1_col)
        loaded(v.u)
        du = gbuf.at[layer]

        def body(rows, back):
            du[rows, :] = (v.r[rows, :] + back).astype(bf16)

        norm_back(v.u, 0, layer, body)

    closing = []

    def deliver(which, layer, rows):
        out = gin if which else lay
        send, recv = own.d_send.at[which, layer], own.d_recv.at[which]
        for k in range(4):
            to = p.jj * 4 + k
            src = rows.at[pl.ds(k * CH, CH), :]
            dst = out.at[0, p.i, p.x]
            slot = p.i * 2 + p.x
            mine = (to == p.j) & (p.x == layer)
            copy = remote(src, dst, send.at[k], recv.at[slot], p.at(x=layer, j=to))

            @pl.when(jnp.logical_not(mine))
            def _():
                copy.start()

            @pl.when(mine)
            def _():
                pltpu.make_async_copy(src, dst, recv.at[slot]).start()

            def close(copy=copy, mine=mine):
                @pl.when(jnp.logical_not(mine))
                def _():
                    copy.wait_send()

            closing.append(close)

    def pack_small(layer):
        sb = own.sb
        for k in range(n):
            at, gat = (33 * k) // 4, (3 * k) // 2
            zi, yi = k // 2, k % 2
            sb[layer, zi, yi, 0:9] = vr[layer, at : at + 9, :]
            sb[layer, zi, yi, 9:11] = gr[layer, gat : gat + 2, :]
            sb[layer, zi, yi, 11:16] = jnp.zeros((5, CH), f32)
            h0, h1, h2 = (mg[3 * k + i] for i in range(3))
            left = jnp.concatenate([h0, h1[: HEAD // 2]], 0)
            right = jnp.concatenate([h1[HEAD // 2 :], h2], 0)
            sb[layer, zi, yi, 16:SMALL_OUT] = jnp.where(lanes(96) < HEAD, left, -right)
        smalls[layer].send_core()

    vr[...] = jnp.zeros(vr.shape, f32)
    gr[...] = jnp.zeros(gr.shape, f32)
    r1, r0 = reduces[1], reduces[0]
    s1, s0 = smalls[1], smalls[0]

    def run(*steps):
        def all_():
            for step in steps:
                step()

        return all_

    deliver(0, 0, ref.res0)
    deliver(0, 1, ref.res1)
    mlp_back(1, gbuf.at[0], {})
    load(0, v.o)
    load_w(0, U)
    load_w(0, O)
    for k in range(3):
        load_wd(0, k)
    loaded(v.n2, v.ob, v.a)
    for m in (DN, U, O):
        weight_grad(1, m, False)
    for m in (DN, U, O):
        weight_grad(1, m, True)
    load(0, v.gp, v.n2, v.ob)
    mix_back(1, {4: r1[DN].step_y})
    load_w(0, Q)
    load(0, v.r, v.inv, v.ph, v.u, v.pre)
    deliver(1, 1, gbuf.at[1])
    pack_small(1)
    weight_grad(1, Q, False)
    r1[U].step_y()
    weight_grad(1, Q, True)
    s1.step_d()
    load(0, v.qkv)
    load(0, v.a)

    mlp_back(
        0,
        gbuf.at[1],
        {2: r1[DN].step_z, 4: r1[O].step_y, 6: s1.step_y, 7: run(r1[DN].step_x)},
    )
    loaded(v.n2, v.ob, v.a)
    weight_grad(0, DN, False)
    r1[U].step_z()
    weight_grad(0, U, False)
    r1[O].step_z()
    weight_grad(0, O, False)
    r1[Q].step_y()
    s1.step_z()
    weight_grad(0, DN, True)
    weight_grad(0, U, True)
    weight_grad(0, O, True)
    mix_back(
        0,
        {
            0: run(r1[U].step_x, r1[O].step_x, s1.step_x),
            2: r1[Q].step_z,
            3: run(r1[Q].step_x, r0[DN].step_y),
        },
    )
    deliver(1, 0, gbuf.at[0])
    pack_small(0)
    weight_grad(0, Q, False)
    r0[U].step_y()
    weight_grad(0, Q, True)
    s0.step_d()
    r0[DN].step_z()
    r0[O].step_y()
    s0.step_y()
    r0[DN].step_x()
    r0[U].step_z()
    r0[Q].step_y()
    r0[O].step_z()
    s0.step_z()
    r0[U].step_x()
    r0[O].step_x()
    s0.step_x()
    r0[Q].step_z()
    r0[Q].step_x()

    for m in (Q, O, U, DN):
        r0[m].close()
        r1[m].end()
        r0[m].end()
    s1.close()
    s0.close()
    for layer in range(2):
        close_states(layer)

        @pl.when(p.x == layer)
        def _():
            for which, out in enumerate((lay, gin)):
                for slot in range(8):
                    arrived(out.at[0, slot // 2, slot % 2], own.d_recv.at[which, slot])

    for close in closing:
        close()


def backward_pass(n, cot, gains, bds, full, tokens, kept):
    t = cot.shape[0]
    nz = n // 2
    args = [cot, kept[0].res, kept[1].res, gains, bds] + list(full)
    for u, k in zip((tokens, kept[0].res), kept):
        read = Loaded(k.gp, k.r, k.o, k.inv, k.ph, k.qkv, k.n2, k.ob, k.a, u, k.pre)
        args += list(read)
    args += [k.hid for k in kept]
    widths = (3 * D // 2, D // 2, FF // 2, D // 2)
    rows = (D // n, D // n, D // n, FF // n)
    outs = [shape((1, 4, 2, CH, D), bf16)] * 2
    outs += [shape((r, 2 * c), f32) for r, c in zip(rows, widths)]
    outs += [shape((SMALL_OUT, CH), f32)]
    for _ in range(2):
        for r, c in zip(rows, widths):
            outs += [
                shape((nz, 2, r, c), bf16),
                shape((nz, r, c), bf16),
                shape((nz - 1, r, c), bf16),
                shape((r, c), bf16),
            ]
    specs = [ANY] * 6 + [VMEM] + [ANY] * (len(outs) - 7)
    ins = [ANY] * 3 + [VMEM] * 2 + [ANY] * (len(args) - 5)
    scratch = [pltpu.VMEM(a.shape, a.dtype) for a in read]

    def vmem(*dims, kind=f32):
        scratch.append(pltpu.VMEM(dims, kind))

    vmem(2, t, D, kind=bf16)
    vmem(t, D, kind=bf16)
    vmem(t, D, kind=bf16)
    vmem(t, D)
    vmem(8, D)
    vmem(2, STATE_ROWS, CH)
    vmem(2, STATE_ROWS + 16, CH, kind=bf16)
    vmem(STATE_ROWS, CH)
    vmem(2, n // 2 - 1, STATE_ROWS + 16, CH, kind=bf16)
    vmem(2 * H, HEAD, CH)
    vmem(2, VEC_ROWS, CH)
    vmem(2, GAIN_ROWS, CH)
    vmem(3, t, FF // n, kind=bf16)
    vmem(3, FF // n, D, kind=bf16)
    for w in full[:3]:
        vmem(*w.shape[1:], kind=bf16)
    for r, c in zip(rows, widths):
        vmem(nz, 2, r, c, kind=bf16)
    vmem(2, nz, 2, D // n, 384, kind=bf16)
    vmem(3, FF // n, D // 2, kind=bf16)
    for r, c in zip(rows, widths):
        vmem(r, c)
    vmem(nz, D // n, FF // 2, kind=bf16)
    vmem(nz, FF // n, D // 2, kind=bf16)
    vmem(2, nz, 2, SMALL_OUT, CH)
    vmem(2, nz, 2, SMALL_OUT, CH)
    vmem(2, nz, SMALL_OUT, CH)
    vmem(2, nz - 1, SMALL_OUT, CH)
    vmem(2, SMALL_OUT, CH)
    dma = pltpu.SemaphoreType.DMA
    scratch += [dma((2, 4, 7)), dma((2, 4, 7)), dma((8,)), dma((2, 7)), dma((2, 7))]
    scratch += [dma((2, n // 2 - 1)), dma((2, n // 2 - 1)), dma((2, 2, 4)), dma((2, 8)), dma((4,))]
    scratch += [dma((len(read),)), dma((3,)), dma((5,)), dma((3,))]
    got = call(
        functools.partial(backward_kernel, n),
        outs,
        scratch,
        ins,
        args,
        8 * t * D * (4 * D + 2 * FF),
        specs,
        cid=1,
    )
    return got[:7]


def shards(inputs, cotangent, *weights):
    n = lax.axis_size("seq")
    d, j = lax.axis_index("dp"), lax.axis_index("seq")
    qkv_w, out_w, up_w, down_w, map_w, bias_w, gain_w = (w[0] for w in weights)

    def halved(w):
        width = w.shape[1] // 2
        return lax.dynamic_slice_in_dim(w, d * width, width, 1).astype(bf16)

    def placed(vector, offset, rows):
        flat = jnp.zeros((rows * CH,), f32)
        return lax.dynamic_update_slice(flat, vector, (offset,)).reshape(rows, CH)

    turned = jnp.swapaxes(map_w.reshape(-1, HEAD, HEAD), 1, 2).reshape(map_w.shape)
    bias_at, gain_at = (j % 4) * 32, (j % 2) * 64
    small = jnp.concatenate(
        [
            placed(bias_w, bias_at, 9),
            placed(gain_w, gain_at, 2),
            jnp.zeros((5, CH), f32),
            jnp.concatenate([map_w, turned], 1),
        ]
    ).astype(bf16)
    full, gains, bds, tokens, cot, kept = forward_pass(
        n, inputs, cotangent, small, halved(qkv_w), halved(out_w), halved(up_w), halved(down_w)
    )
    layer_out, grads, g_qkv, g_out, g_up, g_down, g_small = backward_pass(
        n, cot, gains, bds, full, tokens, kept
    )
    maps = jnp.concatenate([g_small[16:, :HEAD], g_small[16:, HEAD:]])
    bias = lax.dynamic_slice_in_dim(g_small[:9].reshape(-1), bias_at, bias_w.shape[0])
    gain = lax.dynamic_slice_in_dim(g_small[9:11].reshape(-1), gain_at, gain_w.shape[0])
    return (
        layer_out,
        grads,
        g_qkv[None],
        g_out[None],
        g_up[None],
        g_down[None],
        maps[None],
        bias[None],
        gain[None],
    )


def solution(mesh):
    tokens = P("dp", None, "seq", None)
    matrix = P("section", "seq", None)
    vector = P("section", "seq")
    stacked = P("section", "dp", None, "seq", None)
    chosen = shards if mesh.shape["seq"] == 8 else plain_shards
    return jax.shard_map(
        chosen,
        mesh=mesh,
        in_specs=(tokens, tokens) + (matrix,) * 5 + (vector,) * 2,
        out_specs=(stacked, stacked) + (matrix,) * 5 + (vector,) * 2,
        check_vma=False,
    )
```

```python
import functools
from typing import Any, NamedTuple

import jax
import jax.numpy as jnp
from jax import lax
from jax.experimental import pallas as pl
from jax.experimental.pallas import tpu as pltpu
from jax.sharding import PartitionSpec as P


D = 768
FF = 3072
H = 12
HEAD = 64
BLOCK = 64


MAXIMUM_ACCURACY = lax.Precision.HIGHEST
NORM_EPSILON = 1e-05


def carried_in(part, axis, combine, identity, reverse):
    count = lax.axis_size(axis)
    place = lax.axis_index(axis)
    ahead = count - 1 - place if reverse else place
    gathered = jax.tree.map(lambda a: lax.all_gather(a, axis), part)
    state = jax.tree.map(lambda a, e: jnp.zeros_like(a) + jnp.asarray(e, a.dtype), part, identity)

    def one(lap, state):
        source = count - 1 - lap if reverse else lap
        return combine(
            state, jax.tree.map(lambda a: lax.dynamic_index_in_dim(a, source, 0, False), gathered)
        )

    return lax.fori_loop(0, ahead, one, state)


def shifted(value, axis, steps):
    count = lax.axis_size(axis)
    leading, last = (max(0, -steps), min(count, count - steps))
    return lax.ppermute(value, axis, [(source, source + steps) for source in range(leading, last)])


def normalize(values, gain_vector, shift_vector):
    average = jnp.mean(values, -1, keepdims=True)
    centred = values - average
    spread = jnp.mean(centred * centred, -1, keepdims=True)
    return centred * lax.rsqrt(spread + NORM_EPSILON) * gain_vector + shift_vector


def features(logits):
    return jnp.concatenate([jax.nn.softmax(logits, -1), jax.nn.softmax(-logits, -1)], -1)


def gelu_tanh(values):
    return jax.nn.gelu(values, approximate=True)


def adding(earlier, later_part):
    return jax.tree.map(jnp.add, earlier, later_part)


def across_rows(left_side, right_side):
    return lax.dot_general(
        left_side, right_side, (((0,), (0,)), ((), ())), preferred_element_type=jnp.float32
    )


def against_rows(left_side, right_side):
    return lax.dot_general(
        left_side, right_side, (((1,), (1,)), ((), ())), preferred_element_type=jnp.float32
    )


def precise(pattern, left_side, right_side):
    return jnp.einsum(pattern, left_side, right_side, precision=MAXIMUM_ACCURACY)


def causal_mask():
    places = lax.broadcasted_iota(jnp.int32, (BLOCK, BLOCK), 0)
    others = lax.broadcasted_iota(jnp.int32, (BLOCK, BLOCK), 1)
    return (others <= places).astype(jnp.float32)


def in_blocks(source_array, batch_rows):
    return source_array.reshape((batch_rows, -1, BLOCK) + source_array.shape[1:])


def prepare(gathered):
    qkv_full, out_full, up_full, down_full, map_full, bias_full, gain_full = [
        piece_array[0] for piece_array in gathered
    ]
    feature_maps = map_full.reshape(2, H, HEAD, HEAD)
    vectors = bias_full.astype(jnp.float32)
    scales = gain_full.astype(jnp.float32)
    pieces = (
        vectors[:D],
        vectors[D : 4 * D],
        vectors[4 * D : 5 * D],
        vectors[5 * D : 6 * D],
        vectors[6 * D : 6 * D + FF],
        vectors[6 * D + FF :],
        scales[:D],
        scales[D:],
    )
    return (qkv_full, out_full, up_full, down_full, feature_maps, pieces)


def block_sums(query_map, key_map, value_rows, batch_rows):
    query_blocks = in_blocks(query_map, batch_rows)
    key_blocks = in_blocks(key_map, batch_rows)
    value_blocks = in_blocks(value_rows, batch_rows).astype(jnp.float32)
    query_wide = query_blocks.astype(jnp.float32)
    key_wide = key_blocks.astype(jnp.float32)
    score_matrix = (
        jnp.einsum(
            "bcqhf,bckhf->bchqk", query_blocks, key_blocks, preferred_element_type=jnp.float32
        )
        * causal_mask()
    )
    block_state = precise("bckhf,bckhe->bchfe", key_wide, value_blocks)
    block_total = jnp.sum(key_wide, 2)
    return (query_wide, key_wide, value_blocks, score_matrix, block_state, block_total)


def attend(query_map, key_map, value_rows, initial, batch_rows):
    query_wide, key_wide, value_blocks, score_matrix, block_state, block_total = block_sums(
        query_map, key_map, value_rows, batch_rows
    )
    state_sum = jnp.sum(block_state, 1)
    total_sum = jnp.sum(block_total, 1)
    identity = (jnp.zeros_like(state_sum), jnp.zeros_like(total_sum))
    earlier = carried_in((state_sum, total_sum), "seq", adding, identity, False)
    overall = lax.psum((state_sum, total_sum), "seq")
    start_state = initial[0] + earlier[0]
    start_total = initial[1] + earlier[1]
    block_before = start_state[:, None] + jnp.cumsum(block_state, 1) - block_state
    total_before = start_total[:, None] + jnp.cumsum(block_total, 1) - block_total
    numerator = precise("bchqk,bckhe->bcqhe", score_matrix, value_blocks) + precise(
        "bcqhf,bchfe->bcqhe", query_wide, block_before
    )
    denominator = jnp.swapaxes(jnp.sum(score_matrix, -1), 2, 3) + precise(
        "bcqhf,bchf->bcqh", query_wide, total_before
    )
    mixture = numerator / denominator[..., None]
    handed = (initial[0] + overall[0], initial[1] + overall[1])
    return (mixture.reshape(value_rows.shape), denominator, (start_state, start_total), handed)


def attend_back(
    mixture_grad, query_map, key_map, value_rows, mixture, denominator, starts, future, batch_rows
):
    query_wide, key_wide, value_blocks, score_matrix, block_state, block_total = block_sums(
        query_map, key_map, value_rows, batch_rows
    )
    block_before = starts[0][:, None] + jnp.cumsum(block_state, 1) - block_state
    total_before = starts[1][:, None] + jnp.cumsum(block_total, 1) - block_total
    scaled = in_blocks(mixture_grad, batch_rows) / denominator[..., None]
    denominator_grad = -jnp.sum(scaled * in_blocks(mixture, batch_rows), -1)
    score_grad = (
        precise("bcqhe,bckhe->bchqk", scaled, value_blocks)
        + jnp.swapaxes(denominator_grad, 2, 3)[..., None]
    ) * causal_mask()
    query_grad = precise("bchqk,bckhf->bcqhf", score_grad, key_wide) + precise(
        "bcqhe,bchfe->bcqhf", scaled, block_before
    )
    query_grad = query_grad + denominator_grad[..., None] * total_before[:, :, None]
    state_grad = precise("bcqhf,bcqhe->bchfe", query_wide, scaled)
    total_grad = precise("bcqhf,bcqh->bchf", query_wide, denominator_grad)
    state_sum = jnp.sum(state_grad, 1)
    total_sum = jnp.sum(total_grad, 1)
    identity = (jnp.zeros_like(state_sum), jnp.zeros_like(total_sum))
    later_sums = carried_in((state_sum, total_sum), "seq", adding, identity, True)
    overall = lax.psum((state_sum, total_sum), "seq")
    ahead_state = future[0] + later_sums[0]
    ahead_total = future[1] + later_sums[1]
    rest_state = ahead_state[:, None] + state_sum[:, None] - jnp.cumsum(state_grad, 1)
    rest_total = ahead_total[:, None] + total_sum[:, None] - jnp.cumsum(total_grad, 1)
    key_grad = precise("bchqk,bcqhf->bckhf", score_grad, query_wide) + precise(
        "bckhe,bchfe->bckhf", value_blocks, rest_state
    )
    key_grad = key_grad + rest_total[:, :, None]
    value_grad = precise("bchqk,bcqhe->bckhe", score_matrix, scaled) + precise(
        "bckhf,bchfe->bckhe", key_wide, rest_state
    )
    return (
        query_grad.reshape(query_map.shape),
        key_grad.reshape(key_map.shape),
        value_grad.reshape(value_rows.shape),
        overall,
    )


def forward(tokens, params, initial):
    qkv_full, out_full, up_full, down_full, feature_maps, pieces = params
    shift_one, qkv_bias, out_bias, shift_two, up_bias, down_bias, gain_one, gain_two = pieces
    batch_rows = tokens.shape[0]
    flattened = tokens.reshape(-1, D)
    row_count = flattened.shape[0]
    normed = normalize(flattened, gain_one, shift_one).astype(jnp.bfloat16)
    projected = (jnp.dot(normed, qkv_full, preferred_element_type=jnp.float32) + qkv_bias).astype(
        jnp.bfloat16
    )
    query_rows = projected[:, :D].reshape(row_count, H, HEAD)
    key_rows = projected[:, D : 2 * D].reshape(row_count, H, HEAD)
    value_rows = projected[:, 2 * D :].reshape(row_count, H, HEAD)
    query_logits = jnp.einsum(
        "rhe,hef->rhf", query_rows, feature_maps[0], preferred_element_type=jnp.float32
    )
    key_logits = jnp.einsum(
        "rhe,hef->rhf", key_rows, feature_maps[1], preferred_element_type=jnp.float32
    )
    query_map = features(query_logits).astype(jnp.bfloat16)
    key_map = features(key_logits).astype(jnp.bfloat16)
    mixture, denominator, starts, handed = attend(
        query_map, key_map, value_rows, initial, batch_rows
    )
    mixture_low = mixture.reshape(row_count, D).astype(jnp.bfloat16)
    residual = (
        flattened + jnp.dot(mixture_low, out_full, preferred_element_type=jnp.float32) + out_bias
    )
    normed_two = normalize(residual, gain_two, shift_two).astype(jnp.bfloat16)
    before_act = jnp.dot(normed_two, up_full, preferred_element_type=jnp.float32) + up_bias
    hidden = gelu_tanh(before_act).astype(jnp.bfloat16)
    result = residual + jnp.dot(hidden, down_full, preferred_element_type=jnp.float32) + down_bias
    kept_values = (
        flattened,
        normed,
        projected,
        query_logits,
        key_logits,
        query_map,
        key_map,
        mixture,
        denominator,
        starts,
        residual,
        normed_two,
        before_act,
        hidden,
    )
    return (result.reshape(tokens.shape), handed, kept_values)


def backward(upstream, params, kept_values, future):
    qkv_full, out_full, up_full, down_full, feature_maps, pieces = params
    shift_one, qkv_bias, out_bias, shift_two, up_bias, down_bias, gain_one, gain_two = pieces
    (
        flattened,
        normed,
        projected,
        query_logits,
        key_logits,
        query_map,
        key_map,
        mixture,
        denominator,
        starts,
        residual,
        normed_two,
        before_act,
        hidden,
    ) = kept_values
    batch_rows = upstream.shape[0]
    row_count = flattened.shape[0]
    out_grad = upstream.reshape(row_count, D)
    down_bias_grad = jnp.sum(out_grad, 0)
    out_low = out_grad.astype(jnp.bfloat16)
    down_weight_grad = across_rows(hidden, out_low)
    hidden_grad = against_rows(out_low, down_full)
    _, gelu_back = jax.vjp(gelu_tanh, before_act)
    before_grad = gelu_back(hidden_grad)[0].astype(jnp.bfloat16)
    up_bias_grad = jnp.sum(before_grad.astype(jnp.float32), 0)
    up_weight_grad = across_rows(normed_two, before_grad)
    normed_two_grad = against_rows(before_grad, up_full)
    _, norm_back_two = jax.vjp(normalize, residual, gain_two, shift_two)
    residual_part, gain_two_grad, shift_two_grad = norm_back_two(normed_two_grad)
    residual_grad = out_grad + residual_part
    out_bias_grad = jnp.sum(residual_grad, 0)
    residual_low = residual_grad.astype(jnp.bfloat16)
    mixture_low = mixture.reshape(row_count, D).astype(jnp.bfloat16)
    out_weight_grad = across_rows(mixture_low, residual_low)
    mixture_grad = against_rows(residual_low, out_full).reshape(row_count, H, HEAD)
    query_rows = projected[:, :D].reshape(row_count, H, HEAD)
    key_rows = projected[:, D : 2 * D].reshape(row_count, H, HEAD)
    value_rows = projected[:, 2 * D :].reshape(row_count, H, HEAD)
    query_map_grad, key_map_grad, value_grad, handed = attend_back(
        mixture_grad,
        query_map,
        key_map,
        value_rows,
        mixture,
        denominator,
        starts,
        future,
        batch_rows,
    )
    _, query_back = jax.vjp(features, query_logits)
    query_logit_grad = query_back(query_map_grad)[0]
    _, key_back = jax.vjp(features, key_logits)
    key_logit_grad = key_back(key_map_grad)[0]
    maps_wide = feature_maps.astype(jnp.float32)
    query_grad = precise("rhf,hef->rhe", query_logit_grad, maps_wide[0])
    key_grad = precise("rhf,hef->rhe", key_logit_grad, maps_wide[1])
    map_weight_grad = jnp.stack(
        [
            precise("rhe,rhf->hef", query_rows.astype(jnp.float32), query_logit_grad),
            precise("rhe,rhf->hef", key_rows.astype(jnp.float32), key_logit_grad),
        ]
    ).reshape(2 * H * HEAD, HEAD)
    projected_grad = jnp.concatenate(
        [
            query_grad.reshape(row_count, D),
            key_grad.reshape(row_count, D),
            value_grad.reshape(row_count, D),
        ],
        1,
    ).astype(jnp.bfloat16)
    qkv_bias_grad = jnp.sum(projected_grad.astype(jnp.float32), 0)
    qkv_weight_grad = across_rows(normed, projected_grad)
    normed_grad = against_rows(projected_grad, qkv_full)
    _, norm_back_one = jax.vjp(normalize, flattened, gain_one, shift_one)
    input_part, gain_one_grad, shift_one_grad = norm_back_one(normed_grad)
    input_grad = residual_grad + input_part
    bias_grad = jnp.concatenate(
        [shift_one_grad, qkv_bias_grad, out_bias_grad, shift_two_grad, up_bias_grad, down_bias_grad]
    )
    gain_grad = jnp.concatenate([gain_one_grad, gain_two_grad])
    layer_grads = (
        qkv_weight_grad,
        out_weight_grad,
        up_weight_grad,
        down_weight_grad,
        map_weight_grad,
        bias_grad,
        gain_grad,
    )
    return (input_grad.reshape(upstream.shape), handed, layer_grads)


def reduce_grads(full_grads):
    g_qkv, g_out, g_up, g_down, g_map, g_bias, g_gain = full_grads
    s_qkv, s_out, s_up, s_down, s_map, s_bias, s_gain = (
        lax.psum_scatter(g_qkv, "seq", scatter_dimension=1, tiled=True),
        lax.psum_scatter(g_out, "seq", scatter_dimension=1, tiled=True),
        lax.psum_scatter(g_up, "seq", scatter_dimension=1, tiled=True),
        lax.psum_scatter(g_down, "seq", scatter_dimension=1, tiled=True),
        lax.psum_scatter(g_map, "seq", scatter_dimension=1, tiled=True),
        lax.psum_scatter(g_bias, "seq", scatter_dimension=1, tiled=True),
        lax.psum_scatter(g_gain, "seq", scatter_dimension=1, tiled=True),
    )
    return lax.psum((s_qkv, s_out, s_up, s_down, s_map, s_bias, s_gain), "dp")


def plain_shards(
    inputs, cotangent, qkv_weight, out_weight, up_weight, down_weight, map_weight, biases, gains
):
    section_index = lax.axis_index("section")
    batch_rows = inputs.shape[0]
    micro_count = inputs.shape[1]
    gathered = (
        lax.all_gather(qkv_weight.astype(jnp.bfloat16), "seq", axis=1, tiled=True),
        lax.all_gather(out_weight.astype(jnp.bfloat16), "seq", axis=1, tiled=True),
        lax.all_gather(up_weight.astype(jnp.bfloat16), "seq", axis=1, tiled=True),
        lax.all_gather(down_weight.astype(jnp.bfloat16), "seq", axis=1, tiled=True),
        lax.all_gather(map_weight.astype(jnp.bfloat16), "seq", axis=1, tiled=True),
        lax.all_gather(biases.astype(jnp.bfloat16), "seq", axis=1, tiled=True),
        lax.all_gather(gains.astype(jnp.bfloat16), "seq", axis=1, tiled=True),
    )
    params = prepare(gathered)
    empty_state = (
        jnp.zeros((batch_rows, H, 2 * HEAD, HEAD), jnp.float32),
        jnp.zeros((batch_rows, H, 2 * HEAD), jnp.float32),
    )
    blank_rows = jnp.zeros(inputs.shape[:1] + inputs.shape[2:], jnp.bfloat16)
    moments = jnp.arange(micro_count + 1, dtype=jnp.int32)

    def forward_moment(carry, moment):
        handed, arriving = carry
        own_tokens = lax.dynamic_index_in_dim(
            inputs, jnp.minimum(moment, micro_count - 1), 1, False
        )
        source = jnp.where(section_index == 0, own_tokens, arriving).astype(jnp.float32)
        carried = moment - section_index >= 1
        initial = (jnp.where(carried, handed[0], 0.0), jnp.where(carried, handed[1], 0.0))
        result, handed_next, kept_values = forward(source, params, initial)
        outgoing = result.astype(jnp.bfloat16)
        arriving_next = shifted(outgoing, "section", 1)
        return ((handed_next, arriving_next), (outgoing, kept_values))

    _, (result_stack, kept_stack) = lax.scan(forward_moment, (empty_state, blank_rows), moments)
    regathered = (
        lax.all_gather(qkv_weight.astype(jnp.bfloat16), "seq", axis=1, tiled=True),
        lax.all_gather(out_weight.astype(jnp.bfloat16), "seq", axis=1, tiled=True),
        lax.all_gather(up_weight.astype(jnp.bfloat16), "seq", axis=1, tiled=True),
        lax.all_gather(down_weight.astype(jnp.bfloat16), "seq", axis=1, tiled=True),
        lax.all_gather(map_weight.astype(jnp.bfloat16), "seq", axis=1, tiled=True),
        lax.all_gather(biases.astype(jnp.bfloat16), "seq", axis=1, tiled=True),
        lax.all_gather(gains.astype(jnp.bfloat16), "seq", axis=1, tiled=True),
    )
    back_params = prepare(regathered)
    zero_grads = (
        jnp.zeros((D, 3 * D), jnp.float32),
        jnp.zeros((D, D), jnp.float32),
        jnp.zeros((D, FF), jnp.float32),
        jnp.zeros((FF, D), jnp.float32),
        jnp.zeros((2 * H * HEAD, HEAD), jnp.float32),
        jnp.zeros((7 * D + FF,), jnp.float32),
        jnp.zeros((2 * D,), jnp.float32),
    )

    def backward_moment(carry, pieces):
        future, returning, grad_sums = carry
        slot, kept_values = pieces
        chosen = slot - section_index
        own_grad = lax.dynamic_index_in_dim(cotangent, jnp.maximum(slot - 1, 0), 1, False)
        live = (chosen >= 0) & (chosen < micro_count)
        upstream = jnp.where(section_index == 1, own_grad, returning).astype(jnp.float32)
        upstream = jnp.where(live, upstream, 0.0)
        later_micro = live & (chosen < micro_count - 1)
        ahead_part = (
            jnp.where(later_micro, future[0], 0.0),
            jnp.where(later_micro, future[1], 0.0),
        )
        input_grad, future_next, layer_grads = backward(
            upstream, back_params, kept_values, ahead_part
        )
        outgoing = input_grad.astype(jnp.bfloat16)
        grad_sums = tuple((previous + current for previous, current in zip(grad_sums, layer_grads)))
        returning_next = shifted(outgoing, "section", -1)
        return ((future_next, returning_next, grad_sums), outgoing)

    (_, _, grad_sums), grad_stack = lax.scan(
        backward_moment, (empty_state, blank_rows, zero_grads), (moments, kept_stack), reverse=True
    )
    layer_out = jnp.stack(
        [
            lax.dynamic_index_in_dim(result_stack, micro_index + section_index, 0, False)
            for micro_index in range(micro_count)
        ],
        1,
    )
    input_grads = jnp.stack(
        [
            lax.dynamic_index_in_dim(grad_stack, micro_index + section_index, 0, False)
            for micro_index in range(micro_count)
        ],
        1,
    )
    full_grads = tuple((grad_array[None] for grad_array in grad_sums))
    reduced = reduce_grads(full_grads)
    return (
        layer_out[None],
        input_grads[None],
        reduced[0],
        reduced[1],
        reduced[2],
        reduced[3],
        reduced[4],
        reduced[5],
        reduced[6],
    )


CH = 128
PAIRS = H // 2
QB = 2 * H * HEAD
STATE_ROWS = D + 16
EPS = 1e-05
TILE = 256
AXES = ("section", "dp", "seq")
MESH = pl.DeviceIdType.MESH
f32 = jnp.float32
bf16 = jnp.bfloat16
GELU_C = 0.7978845608028654
GELU_A = 0.044715
SMALL_ROWS = 128
VEC_ROWS = 72
GAIN_ROWS = 16
SHIFT1, QKV_BIAS, OUT_BIAS, SHIFT2, UP_BIAS, DOWN_BIAS = 0, 6, 24, 30, 36, 60


class Kept(NamedTuple):
    a: Any
    qkv: Any
    ph: Any
    o: Any
    inv: Any
    ob: Any
    r: Any
    n2: Any
    hid: Any
    gp: Any
    res: Any
    pre: Any


class ForwardRefs(NamedTuple):
    tokens: Any
    cot: Any
    small: Any
    wq: Any
    wo: Any
    wu: Any
    wd: Any
    gq: Any
    go: Any
    gu: Any
    gd: Any
    gv: Any
    bd: Any
    tok_out: Any
    cot_out: Any
    lay: Any


class ForwardScratch(NamedTuple):
    wq: Any
    wo: Any
    wu: Any
    wd: Any
    hq: Any
    ho: Any
    hu: Any
    hd: Any
    tok: Any
    sm: Any
    vec: Any
    maps: Any
    st: Any
    stb: Any
    got: Any
    vq: Any
    vo: Any
    vu: Any
    vd: Any
    g_send: Any
    g_recv: Any
    g_local: Any
    c_send: Any
    c_recv: Any
    s_send: Any
    s_recv: Any
    d_send: Any
    d_recv: Any
    w_sem: Any
    o_sem: Any
    m_sem: Any


class Weights(NamedTuple):
    q: Any
    o: Any
    u: Any
    d: Any = None


VMEM = pl.BlockSpec(memory_space=pltpu.VMEM)
SMEM = pl.BlockSpec(memory_space=pltpu.SMEM)
ANY = pl.BlockSpec(memory_space=pl.ANY)


def nn(a, b):
    return lax.dot_general(a, b, (((1,), (0,)), ((), ())), preferred_element_type=f32)


def nt(a, b):
    return lax.dot_general(a, b, (((1,), (1,)), ((), ())), preferred_element_type=f32)


def tn(a, b):
    return lax.dot_general(a, b, (((0,), (0,)), ((), ())), preferred_element_type=f32)


def tt(a, b):
    return lax.dot_general(a, b, (((0,), (1,)), ((), ())), preferred_element_type=f32)


def loop(count, body, events=None):
    events = events or {}

    def step(i, c):
        body(i)
        for at, event in events.items():

            @pl.when(i == at)
            def _():
                event()

        return c

    lax.fori_loop(0, count, step, 0)


def span(i, size):
    return pl.ds(pl.multiple_of(i * size, size), size)


def wide(ref, layer, row, count):
    return jnp.concatenate([ref[layer, pl.ds(row + i, 1), :] for i in range(count)], 1)


def finish(dst, sem):
    pltpu.make_async_copy(dst, dst, sem).wait()


def arrived(dst, recv):
    finish(dst, recv)


def departed(src, send):
    finish(src, send)


def shape(dims, kind):
    return jax.ShapeDtypeStruct(dims, kind)


def call(kernel, outs, scratch, specs, args, flops, out_specs=None, vmem=60, cid=None):
    if out_specs is None:
        out_specs = [VMEM] * len(outs)
    moved = sum(a.size * a.dtype.itemsize for a in args if a.ndim > 0)
    moved += sum(o.size * o.dtype.itemsize for o in outs)
    params = dict(vmem_limit_bytes=vmem * 1024 * 1024)
    if cid is not None:
        params.update(collective_id=cid, has_side_effects=True)
    return pl.pallas_call(
        kernel,
        out_shape=outs,
        in_specs=specs,
        out_specs=out_specs,
        scratch_shapes=scratch,
        compiler_params=pltpu.CompilerParams(**params),
        cost_estimate=pl.CostEstimate(flops=flops, bytes_accessed=moved, transcendentals=0),
    )(*args)


def standardize(u):
    cen = u - jnp.mean(u, -1, keepdims=True)
    rstd = lax.rsqrt(jnp.mean(cen * cen, -1, keepdims=True) + EPS)
    return cen * rstd, rstd


def lanes(rows):
    return lax.broadcasted_iota(jnp.int32, (rows, CH), 1)


def half_sums(t, low):
    s1 = jnp.sum(jnp.where(low, t, 0.0), -1, keepdims=True)
    s2 = jnp.sum(jnp.where(low, 0.0, t), -1, keepdims=True)
    return jnp.where(low, s1, s2)


def half_softmax(l, low):
    m1 = jnp.max(jnp.where(low, l, -jnp.inf), -1, keepdims=True)
    m2 = jnp.max(jnp.where(low, -jnp.inf, l), -1, keepdims=True)
    p = jnp.exp(l - jnp.where(low, m1, m2))
    return p / half_sums(p, low)


def split_states(src, dst):
    hi = src[...].astype(bf16)
    dst[0:STATE_ROWS] = hi
    dst[STATE_ROWS:] = (src[D:] - hi[D:].astype(f32)).astype(bf16)


def add_states(dst, src):
    dst[...] += src[0:STATE_ROWS].astype(f32)
    dst[D:] += src[STATE_ROWS:].astype(f32)


class Place:
    def __init__(self, n):
        self.n, self.nz, self.group = n, n // 2, n // 4
        self.x = lax.axis_index("section")
        self.d = lax.axis_index("dp")
        self.j = lax.axis_index("seq")
        self.z, self.y = lax.div(self.j, 2), lax.rem(self.j, 2)
        self.zh, self.zl = lax.div(self.z, 2), lax.rem(self.z, 2)
        self.i = lax.rem(self.z, 2) * 2 + self.y
        self.jj = lax.div(self.z, 2)
        self.r = self.x * self.group + self.jj

    def at(self, x=None, d=None, z=None, y=None, j=None):
        x = self.x if x is None else x
        d = self.d if d is None else d
        if j is None:
            j = (self.z if z is None else z) * 2 + (self.y if y is None else y)
        return (x, d, j)

    def zpos(self, o):
        return lax.rem(self.z + o + self.nz, self.nz)

    def member(self, r):
        z = lax.rem(r, self.group) * 2 + lax.rem(self.z, 2)
        return (lax.div(r, self.group), self.d, z * 2 + self.y)

    def meet(self):
        barrier = pltpu.get_barrier_semaphore()
        for dx in range(2):
            for o in range(self.n):
                if dx == 0 and o == 0:
                    continue
                other = (
                    lax.rem(self.x + dx, 2),
                    self.d,
                    lax.rem(self.j + o, self.n),
                )
                pl.semaphore_signal(barrier, inc=1, device_id=other, device_id_type=MESH)
        pl.semaphore_signal(
            barrier, inc=1, device_id=(self.x, 1 - self.d, self.j), device_id_type=MESH
        )
        pl.semaphore_wait(barrier, 2 * self.n)


def remote(src, dst, send, recv, to):
    return pltpu.make_async_remote_copy(
        src_ref=src, dst_ref=dst, send_sem=send, recv_sem=recv, device_id=to, device_id_type=MESH
    )


def hand_over(p, layer, rows, out, send, recv):
    closing = []
    for k in range(4):
        to = p.jj * 4 + k
        src = rows.at[pl.ds(k * CH, CH), :]
        dst = out.at[0, p.i, p.x]
        slot = p.i * 2 + p.x
        mine = (to == p.j) & (p.x == layer)
        copy = remote(src, dst, send.at[k], recv.at[slot], p.at(x=layer, j=to))

        @pl.when(jnp.logical_not(mine))
        def _():
            copy.start()

        @pl.when(mine)
        def _():
            pltpu.make_async_copy(src, dst, recv.at[slot]).start()

        def close(copy=copy, mine=mine):
            @pl.when(jnp.logical_not(mine))
            def _():
                copy.wait_send()

        closing.append(close)
    return closing


def handed_over(p, layer, out, recv):
    @pl.when(p.x == layer)
    def _():
        for slot in range(8):
            arrived(out.at[0, slot // 2, slot % 2], recv.at[slot])


def signal(sem, to):
    pl.semaphore_signal(sem, inc=1, device_id=to, device_id_type=MESH)


class Gather:
    def __init__(self, place, src, buf, send, recv, local, y_last, eager=False, by_rows=False):
        self.p, self.src, self.buf = place, src, buf
        self.send, self.recv, self.local = send, recv, local
        self.y_last, self.eager, self.by_rows = y_last, eager, by_rows
        self.rows, self.width = src.shape
        self.sent = ([], [], [])

    def part(self, d):
        if self.by_rows:
            return pl.ds(pl.multiple_of(d * self.rows, 16), self.rows), slice(None)
        return slice(None), pl.ds(pl.multiple_of(d * self.width, CH), self.width)

    def shard(self, x, o, y):
        return self.buf.at[x, self.p.zpos(-o), y, *self.part(self.p.d)]

    def go(self, src, dst, out, slot, to, plane):
        remote(src, dst, self.send.at[out], self.recv.at[slot], to).start()
        self.sent[plane].append(out)

    def got(self, ref, slot):
        arrived(ref, self.recv.at[slot])

    def own(self, o):
        return self.src if o == 0 else self.shard(self.p.x, o, self.p.y)

    def send_y(self, o, plane):
        p = self.p
        self.go(self.own(o), self.shard(p.x, o, p.y), 3 + o, 3 + o, p.at(y=1 - p.y), plane)

    def send_x(self, o, plane):
        p = self.p
        self.go(self.own(o), self.shard(p.x, o, p.y), 7 + o, 7 + o, p.at(x=1 - p.x), plane)

    def core(self, q, plane):
        x, y = self.kind(q)
        part = self.buf.at[x, :, y, *self.part(self.p.d)]
        self.go(part, part, 15 + q, 15 + q, self.p.at(d=1 - self.p.d), plane)

    def kind(self, q):
        p = self.p
        return (p.x if q < 2 else 1 - p.x), (p.y if q % 2 == 0 else 1 - p.y)

    def wait_all(self, q):
        x, y = self.kind(q)
        for o in range(self.p.nz):
            self.got(self.shard(x, o, y), (0, 3, 7, 11)[q] + o)

    def begin(self):
        p = self.p
        own = self.shard(p.x, 0, p.y)
        pltpu.make_async_copy(self.src, own, self.local).start()
        for o in range(1, p.nz):
            self.go(self.src, own, o - 1, o - 1, p.at(z=p.zpos(o)), 2)
        self.send_x(0, 2)
        if self.eager:
            self.send_y(0, 2)
        else:

            @pl.when(p.x == 0)
            def _():
                self.send_y(0, 0)

    def early(self):
        @pl.when(self.p.x == 1)
        def _():
            for o in range(1, self.p.nz):
                self.got(self.shard(self.p.x, o, self.p.y), o - 1)
                self.send_x(o, 1)
                if self.eager:
                    self.send_y(o, 1)

    def spread(self, layer):
        p, nz = self.p, self.p.nz

        @pl.when(p.x == layer)
        def _():
            for o in range(nz):
                if layer == 0 and o > 0:
                    self.got(self.shard(p.x, o, p.y), o - 1)
                    self.send_x(o, layer)
                if o > 0 if layer == 0 else not self.eager:
                    self.send_y(o, layer)
            finish(self.shard(p.x, 0, p.y), self.local)
            self.core(0, layer)

        @pl.when(p.x != layer)
        def _():
            if self.y_last[layer]:
                for o in range(nz):
                    here = self.shard(1 - p.x, o, p.y)
                    self.got(here, 7 + o)
                    self.go(here, here, 11 + o, 11 + o, p.at(y=1 - p.y), 1 - layer)
            else:
                self.wait_all(2)
            self.core(2, 1 - layer)

    def hop(self, layer):
        p = self.p
        if not self.y_last[layer]:

            @pl.when(p.x == layer)
            def _():
                for o in range(p.nz):
                    here = self.shard(p.x, o, 1 - p.y)
                    self.got(here, 3 + o)
                    self.go(here, here, 19 + o, 11 + o, p.at(x=1 - p.x), layer)
                self.core(1, layer)

    def last(self, layer):
        p = self.p
        if self.y_last[layer]:

            @pl.when(p.x == layer)
            def _():
                self.wait_all(1)
                self.core(1, layer)

        @pl.when(p.x != layer)
        def _():
            self.wait_all(3)
            self.core(3, 1 - layer)

    def done(self, layer):
        p = self.p
        other = self.part(1 - p.d)
        for plane in range(2):

            @pl.when(p.x == plane)
            def _():
                for q in (0, 1) if plane == layer else (2, 3):
                    x, y = self.kind(q)
                    self.got(self.buf.at[x, :, y, *other], 15 + q)

    def close(self):
        p = self.p

        def leave(slots):
            for slot in slots:
                ref = self.shard(p.x, 0, p.y)
                if 15 <= slot < 19:
                    ref = self.buf.at[p.x, :, p.y, *self.part(p.d)]
                departed(ref, self.send.at[slot])

        leave(self.sent[2])
        for plane in range(2):

            @pl.when(p.x == plane)
            def _():
                leave(self.sent[plane])


def forward_kernel(n, *refs):
    ref = ForwardRefs(*refs[:16])
    saved = [Kept(*refs[16:28]), Kept(*refs[28:40])]
    v = Kept(*refs[40:52])
    own = ForwardScratch(*refs[52:])
    p = Place(n)
    nz, group = p.nz, p.group
    t = v.a.shape[0]
    nc = t // CH
    mine = ((ref.wq, own.wq, own.hq), (ref.wo, own.wo, own.ho))
    mine += ((ref.wu, own.wu, own.hu), (ref.wd, own.wd, own.hd))
    for k, (src, wide_, _) in enumerate(mine):
        width = wide_.shape[1]
        cols = pl.ds(pl.multiple_of(p.d * width, CH), width)
        pltpu.make_async_copy(src.at[:, cols], wide_, own.w_sem.at[k]).start()
    p.meet()
    for k, (_, wide_, half) in enumerate(mine):
        finish(wide_, own.w_sem.at[k])
        half[...] = wide_[...].astype(bf16)

    def gather(k, src, buf, y_last, eager=False, by_rows=False):
        sems = (own.g_send.at[k], own.g_recv.at[k], own.g_local.at[k])
        return Gather(p, src, buf, *sems, y_last, eager, by_rows)

    gs = gather(0, ref.small, own.sm, (True, True), True, True)
    gq = gather(1, own.hq, ref.gq, (True, True), True)
    go = gather(2, own.ho, ref.go, (True, False))
    gu = gather(3, own.hu, ref.gu, (True, False))
    gd = gather(4, own.hd, ref.gd, (False, True))
    gathers = (gs, gq, go, gu, gd)

    def collect(which, s):
        i = lax.rem(p.j + s, 4)
        to = (lax.div(p.z, 2) * 2 + lax.div(i, 2)) * 2 + lax.rem(i, 2)
        slot = lax.rem(p.j, 4)
        src = (ref.cot if which else ref.tokens).at[i, p.x]
        dst = (ref.cot_out if which else own.tok).at[span(slot, CH), :]
        send, recv = own.c_send.at[which], own.c_recv.at[which]
        copy = remote(src, dst, send.at[s], recv.at[slot], p.at(j=to))

        @pl.when(to != p.j)
        def _():
            copy.start()

        @pl.when(to == p.j)
        def _():
            pltpu.make_async_copy(src, dst, recv.at[slot]).start()

        def close():
            @pl.when(to != p.j)
            def _():
                copy.wait_send()

        return close

    gs.begin()
    gq.begin()
    closing = [collect(0, s) for s in range(4)]
    for g in (go, gu, gd):
        g.begin()
    gs.early()
    gs.spread(0)
    gq.early()
    gq.spread(0)
    gs.spread(1)
    gs.last(0)
    go.early()
    go.spread(0)
    gs.last(1)
    gs.done(0)
    gs.done(1)

    vec, gv, bd, sm, maps = own.vec, ref.gv, ref.bd, own.sm, own.maps
    vec[...] = jnp.zeros(vec.shape, f32)
    gv[...] = jnp.zeros(gv.shape, f32)
    bd[...] = jnp.zeros(bd.shape, bf16)
    for layer in range(2):
        for k in range(n):
            part = sm[layer, k // 2, k % 2, 0:16, :].astype(f32)
            row, grow = (33 * k) // 4, (3 * k) // 2
            vec[layer, row : row + 9, :] += part[0:9]
            gv[layer, grow : grow + 2, :] += part[9:11]
        first = lanes(HEAD) < HEAD
        for k in range(n):
            packed = sm[layer, k // 2, k % 2, 16:112, :].astype(f32)
            turned = pltpu.roll(packed, HEAD, 1)
            middle = jnp.concatenate([packed[HEAD:], turned[: HEAD // 2]], 0)
            for i, left in enumerate((packed[:HEAD], middle, turned[HEAD // 2 :])):
                right = pltpu.roll(left, HEAD, 1)
                pair, odd = (3 * k + i) // 2, (3 * k + i) % 2
                rows = pl.ds(odd * HEAD, HEAD)
                signed = jnp.where(first, left, -right)
                bd[layer, pair, rows, odd * CH : (odd + 1) * CH] = signed.astype(bf16)
                alone = jnp.where(first, 0.0, right) if odd else jnp.where(first, left, 0.0)
                maps[layer, pair, rows, :] = alone.astype(bf16)

    for k in range(4):
        arrived(own.tok.at[pl.ds(k * CH, CH), :], own.c_recv.at[0, k])

    def load(g, dst, layer, k):
        pltpu.make_async_copy(g.buf.at[layer], dst, own.w_sem.at[k]).start()

    def loaded(dst, k):
        finish(dst, own.w_sem.at[k])

    def save(layer, *sources, part=None):
        for src in sources:
            k = [src is x for x in v].index(True)
            dst = saved[layer][k]
            if src is v.res:
                src = src.at[layer]
            if part is not None:
                cols = pl.ds(part * (FF // 2), FF // 2)
                src, dst = src.at[:, cols], dst.at[:, cols]
            pltpu.make_async_copy(src, dst, own.o_sem.at[layer, k]).start()

    def saved_all(layer, *sources):
        for src in sources:
            k = [src is x for x in v].index(True)
            finish(src.at[layer] if src is v.res else src, own.o_sem.at[layer, k])

    flat = Weights(
        own.vq.reshape(D, 3 * D),
        own.vo.reshape(D, D),
        own.vu.reshape(D, FF),
        own.vd.reshape(FF, D),
    )
    low = lanes(CH) < HEAD
    tril = lax.broadcasted_iota(jnp.int32, (CH, CH), 0) >= lanes(CH)
    eye = jnp.where(lax.broadcasted_iota(jnp.int32, (CH, CH), 0) == lanes(CH), 1.0, 0.0)
    eye = eye.astype(bf16)

    def norm_rows(layer, src, dst, which, shift):
        gain = wide(gv, layer, which * 6, 6)
        bias = wide(vec, layer, shift, 6)

        def body(i):
            xh, _ = standardize(src[span(i, CH), :].astype(f32))
            dst[span(i, CH), :] = (xh * gain + bias).astype(bf16)

        loop(nc, body)

    def bias_cols(layer, at, j):
        return wide(vec, layer, at + 2 * j, 2)

    def project(layer, u, events):
        a, qkv, ph, st = v.a, v.qkv, v.ph, own.st
        if layer == 1:
            saved_all(0, v.a, v.qkv, v.ph)
        norm_rows(layer, u, a, 0, SHIFT1)
        loaded(own.vq, 0)
        save(layer, v.a)

        def column(j):
            cols = span(j, TILE)
            qkv[:, cols] = (
                nn(a[...], flat.q[:, cols]) + bias_cols(layer, QKV_BIAS, j)
            ).astype(bf16)

        loop(3 * D // TILE, column, events[0])
        save(layer, v.qkv)

        def pair(k):
            logits = tt(maps[layer, k], qkv[:, span(k, CH)]).reshape(2, HEAD, t)
            up = jnp.exp(logits - jnp.max(logits, 1, keepdims=True))
            down = jnp.exp(jnp.min(logits, 1, keepdims=True) - logits)
            up = up * (1.0 / jnp.sum(up, 1, keepdims=True))
            down = down * (1.0 / jnp.sum(down, 1, keepdims=True))
            both = jnp.concatenate([up, down], 1).reshape(2 * CH, t).astype(bf16)
            for c in range(nc):
                ph[pl.ds(c * CH, CH), span(k, 2 * CH)] = nt(
                    eye, both[:, c * CH : (c + 1) * CH]
                ).astype(bf16)

        loop(PAIRS, lambda k: pair(k + PAIRS), events[1])

        def state(k):
            val = qkv[:, pl.ds(pl.multiple_of(2 * D + k * CH, CH), CH)]
            for hh in range(2):
                key = ph[:, pl.ds(pl.multiple_of((H + 2 * k + hh) * CH, CH), CH)]
                full = tn(val, key)
                st[layer, span(2 * k + hh, HEAD), :] = full[hh * HEAD : (hh + 1) * HEAD]
                st[layer, pl.ds(D + 2 * k + hh, 1), :] = jnp.sum(
                    key.astype(f32), 0, keepdims=True
                )

        loop(PAIRS, state)
        st[layer, D + H :, :] = jnp.zeros((STATE_ROWS - D - H, CH), f32)
        split_states(st.at[layer], own.stb.at[layer])
        send_states(layer, st, 1)
        loop(PAIRS, pair, events[2])
        save(layer, v.ph)

    members = 2 * group

    def send_states(layer, st, sign):
        for o in range(1, members):
            ok = (p.r + o < members) if sign > 0 else (p.r - o >= 0)

            @pl.when(ok)
            def _():
                remote(
                    own.stb.at[layer],
                    own.got.at[layer, o - 1],
                    own.s_send.at[layer, o - 1],
                    own.s_recv.at[layer, o - 1],
                    p.member(p.r + sign * o),
                ).start()

    def take_states(layer, sign):
        pre = v.pre
        pre[...] = jnp.zeros(pre.shape, f32)
        for o in range(1, members):
            ok = (p.r - o >= 0) if sign > 0 else (p.r + o < members)

            @pl.when(ok)
            def _():
                arrived(own.got.at[layer, o - 1], own.s_recv.at[layer, o - 1])
                add_states(pre, own.got.at[layer, o - 1])

    def close_states(layer, sign):
        for o in range(1, members):
            ok = (p.r + o < members) if sign > 0 else (p.r - o >= 0)

            @pl.when(ok)
            def _():
                departed(own.stb.at[layer], own.s_send.at[layer, o - 1])

    def mix(layer, u, events):
        qkv, ph, o_, inv, ob = v.qkv, v.ph, v.o, v.inv, v.ob
        r, n2, hid, gp = v.r, v.n2, v.hid, v.gp
        res = v.res.at[layer]
        if layer == 1:
            saved_all(0, v.pre, v.o, v.inv, v.ob, v.r, v.n2, v.hid, v.gp)
        take_states(layer, 1)
        if layer == 1:
            closing.extend([collect(1, s) for s in range(4)])
            closing.extend(hand_over(p, 0, v.res.at[0], ref.lay, own.d_send, own.d_recv))
        save(layer, v.pre)
        s0 = v.pre

        def pair(k):
            cols = span(k, CH)
            s = s0[cols, :]
            tot = [s0[pl.ds(D + 2 * k + hh, 1), :] for hh in range(2)]
            for c in range(nc):
                rows = pl.ds(c * CH, CH)
                val = qkv[rows, pl.ds(pl.multiple_of(2 * D + k * CH, CH), CH)]
                sl = s.astype(bf16)
                sf = (s - sl.astype(f32)).astype(bf16)
                done = []
                new = []
                for hh in range(2):
                    qh = ph[rows, span(2 * k + hh, CH)]
                    kh = ph[rows, pl.ds(pl.multiple_of((H + 2 * k + hh) * CH, CH), CH)]
                    score = jnp.where(tril, nt(qh, kh), 0.0)
                    hi = score.astype(bf16)
                    lo = (score - hi.astype(f32)).astype(bf16)
                    num = nn(hi, val) + nn(lo, val) + nt(qh, sl) + nt(qh, sf)
                    den = jnp.sum(score + qh.astype(f32) * tot[hh], -1, keepdims=True)
                    rec = 1.0 / den
                    done.append((num * rec, rec))
                    new.append(tn(val, kh)[hh * HEAD : (hh + 1) * HEAD])
                    tot[hh] = tot[hh] + jnp.sum(kh.astype(f32), 0, keepdims=True)
                s = s + jnp.concatenate(new, 0)
                both = jnp.where(low, done[0][0], done[1][0])
                o_[rows, cols] = both
                ob[rows, cols] = both.astype(bf16)
                inv[rows, cols] = jnp.where(low, done[0][1], done[1][1])

        loop(PAIRS, pair, events[0])
        save(layer, v.o, v.inv, v.ob)
        events[1]()
        loaded(own.vo, 1)

        def out_col(j):
            cols = span(j, TILE)
            r[:, cols] = (
                u[:, cols].astype(f32)
                + nn(ob[...], flat.o[:, cols])
                + bias_cols(layer, OUT_BIAS, j)
            )

        loop(D // TILE, out_col)
        norm_rows(layer, r, n2, 1, SHIFT2)
        save(layer, v.r, v.n2)
        events[2]()
        loaded(own.vu, 2)

        def up_col(j):
            cols = span(j, TILE)
            zt = nn(n2[...], flat.u[:, cols]) + bias_cols(layer, UP_BIAS, j)
            z2 = zt * zt
            half = 0.5 + 0.5 * jnp.tanh(zt * (GELU_C + (GELU_C * GELU_A) * z2))
            act = zt * half
            hid[:, cols] = act.astype(bf16)
            slope = 2.0 * GELU_C + (6.0 * GELU_C * GELU_A) * z2
            gp[:, cols] = (half + act * ((1.0 - half) * slope)).astype(bf16)

        halfway = FF // TILE // 2 - 1
        loop(FF // TILE, up_col, {halfway: lambda: save(layer, v.hid, v.gp, part=0), **events[3]})
        save(layer, v.hid, v.gp, part=1)
        events[4]()
        loaded(own.vd, 3)

        def down_col(j):
            cols = span(j, TILE)
            res[:, cols] = (
                r[:, cols] + nn(hid[...], flat.d[:, cols]) + bias_cols(layer, DOWN_BIAS, j)
            ).astype(bf16)

        loop(D // TILE, down_col)
        save(layer, v.res)

    def run(*steps):
        def go_():
            for step in steps:
                step()

        return go_

    nothing = run()
    gu.early()
    go.spread(1)
    gu.spread(0)
    gq.last(0)
    gu.spread(1)
    gq.done(0)
    load(gq, own.vq, 0, 0)
    tok_out = pltpu.make_async_copy(own.tok, ref.tok_out, own.m_sem)
    tok_out.start()
    project(0, own.tok, [{}, {}, {}])
    gd.early()
    gd.spread(0)
    gq.spread(1)
    gd.spread(1)
    go.last(0)
    go.hop(1)
    mix(
        0,
        own.tok,
        [
            {
                1: run(
                    functools.partial(go.done, 0),
                    functools.partial(load, go, own.vo, 0, 1),
                    functools.partial(gd.hop, 0),
                ),
                3: run(
                    functools.partial(gu.last, 0),
                    functools.partial(gu.done, 0),
                    functools.partial(load, gu, own.vu, 0, 2),
                ),
            },
            functools.partial(gu.hop, 1),
            nothing,
            {},
            run(
                functools.partial(gq.last, 1),
                functools.partial(gq.done, 1),
                functools.partial(load, gq, own.vq, 1, 0),
                functools.partial(gd.last, 0),
                functools.partial(gd.done, 0),
                functools.partial(load, gd, own.vd, 0, 3),
            ),
        ],
    )
    project(1, v.res.at[0], [{}, {}, {}])
    mix(
        1,
        v.res.at[0],
        [
            {
                2: run(
                    functools.partial(go.last, 1),
                    functools.partial(go.done, 1),
                    functools.partial(load, go, own.vo, 1, 1),
                ),
                4: run(
                    functools.partial(gu.last, 1),
                    functools.partial(gu.done, 1),
                    functools.partial(load, gu, own.vu, 1, 2),
                ),
            },
            nothing,
            nothing,
            {
                1: run(
                    functools.partial(gd.last, 1),
                    functools.partial(gd.done, 1),
                    functools.partial(load, gd, own.vd, 1, 3),
                )
            },
            nothing,
        ],
    )

    for g in gathers:
        g.close()
    for close in closing:
        close()
    for k in range(4):
        arrived(ref.cot_out.at[pl.ds(k * CH, CH), :], own.c_recv.at[1, k])
    for layer in range(2):
        close_states(layer, 1)

    tok_out.wait()
    handed_over(p, 0, ref.lay, own.d_recv)
    saved_all(0, v.res)
    saved_all(1, *v)


def forward_pass(n, tokens, cotangent, small, wq, wo, wu, wd):
    t = 4 * CH
    nz = n // 2
    full = [
        shape((2, nz, 2) + w.shape, bf16) for w in (wq, wo, wu, wd)
    ]
    kept = [
        shape((t, D), bf16),
        shape((t, 3 * D), bf16),
        shape((t, 2 * QB), bf16),
        shape((t, D), f32),
        shape((t, D), f32),
        shape((t, D), bf16),
        shape((t, D), f32),
        shape((t, D), bf16),
        shape((t, FF), bf16),
        shape((t, FF), bf16),
        shape((t, D), bf16),
        shape((STATE_ROWS, CH), f32),
    ]
    outs = full + [shape((2, GAIN_ROWS, CH), f32), shape((2, 2 * PAIRS, CH, 2 * CH), bf16)]
    outs += [shape((t, D), bf16)] * 2 + [shape((1, 4, 2, CH, D), bf16)] + kept * 2
    specs = [ANY] * 4 + [VMEM] * 2 + [ANY] * (len(outs) - 6)
    scratch = [pltpu.VMEM(k.shape, k.dtype) for k in kept]
    scratch[10] = pltpu.VMEM((2, t, D), bf16)
    halves = [(w.shape[0], w.shape[1] // 2) for w in (wq, wo, wu, wd)]
    scratch += [pltpu.VMEM(half, f32) for half in halves]
    scratch += [pltpu.VMEM(half, bf16) for half in halves]
    scratch += [
        pltpu.VMEM((t, D), bf16),
        pltpu.VMEM((2, nz, 2, SMALL_ROWS, CH), bf16),
        pltpu.VMEM((2, VEC_ROWS, CH), f32),
        pltpu.VMEM((2, 2 * PAIRS, CH, CH), bf16),
        pltpu.VMEM((2, STATE_ROWS, CH), f32),
        pltpu.VMEM((2, STATE_ROWS + 16, CH), bf16),
        pltpu.VMEM((2, n // 2 - 1, STATE_ROWS + 16, CH), bf16),
    ]
    scratch += [pltpu.VMEM(w.shape[1:], bf16) for w in full]
    dma = pltpu.SemaphoreType.DMA
    scratch += [dma((5, 23)), dma((5, 19)), dma((5,)), dma((2, 4)), dma((2, 4))]
    scratch += [dma((2, n // 2 - 1)), dma((2, n // 2 - 1)), dma((4,)), dma((8,)), dma((4,))]
    scratch += [dma((2, 12)), dma]
    got = call(
        functools.partial(forward_kernel, n),
        outs,
        scratch,
        [ANY] * 7,
        [tokens, cotangent, small, wq, wo, wu, wd],
        4 * t * D * (4 * D + 2 * FF),
        specs,
        cid=0,
    )
    layers = [Kept(*got[9:21]), Kept(*got[21:33])]
    return got[:4], got[4], got[5], got[6], got[7], got[8], layers


def with_error(gv, swapped, lane, hh):
    first = HEAD * (1 - hh)
    hi = swapped.astype(bf16)
    lo = (swapped - hi.astype(f32)).astype(bf16)
    own = (lane < HEAD) if hh == 0 else (lane >= HEAD)
    spare = jnp.where(
        lane == first + 1,
        lo,
        jnp.where((lane == first) | (lane == first + 2), hi, jnp.zeros_like(gv)),
    )
    return jnp.where(own, gv, spare)


def with_ones(v, lane, hh):
    first = HEAD * (1 - hh)
    own = (lane < HEAD) if hh == 0 else (lane >= HEAD)
    spare = jnp.where((lane == first) | (lane == first + 1), jnp.ones_like(v), jnp.zeros_like(v))
    return jnp.where(own, v, spare)


def with_totals(s, tot, row, hh, again):
    first = HEAD * (1 - hh)
    hi = tot.astype(bf16).astype(f32)
    lo = tot - hi
    own = (row < HEAD) if hh == 0 else (row >= HEAD)
    if again:
        spare = jnp.where(
            (row == first) | (row == first + 1), hi, jnp.where(row == first + 2, lo, 0.0)
        )
    else:
        spare = jnp.where(row == first, hi, jnp.where(row == first + 1, lo, 0.0))
    return jnp.where(own, s, spare).astype(bf16)


def put_rows(ref, layer, row, val):
    for i in range(val.shape[1] // CH):
        ref[layer, pl.ds(row + i, 1), :] = val[:, i * CH : (i + 1) * CH]


class Reduce:
    def __init__(self, place, layer, buf, land, out, fin, sems, credit):
        self.p, self.layer, self.buf, self.fin = place, layer, buf, fin
        self.land_y, self.land_z, self.land_x, self.stage = land
        self.own, self.other = out
        self.send, self.recv, self.last = sems
        self.credit_y, self.credit_a, self.credit_b = credit

    def go(self, src, dst, slot, to):
        remote(src, dst, self.send.at[slot], self.recv.at[slot], to).start()

    def send_y(self):
        p = self.p
        if self.layer == 0:
            pl.semaphore_wait(self.credit_y, 1)
        self.go(self.buf.at[:, 1 - p.y], self.land_y, 0, p.at(y=1 - p.y))

    def add(self, zi, more):
        kept = self.buf.at[zi, self.p.y]
        kept[...] = (kept[...].astype(f32) + more.astype(f32)).astype(bf16)

    def step_y(self):
        p = self.p
        near = p.z + 1 - 2 * p.zl
        arrived(self.land_y, self.recv.at[0])
        if self.layer == 0:
            pl.semaphore_wait(self.credit_a, 1)
        for h in range(2):
            zi = 2 * h + 1 - p.zl
            self.add(zi, self.land_y[zi])
            self.go(self.buf.at[zi, p.y], self.land_z.at[h], 1 + h, p.at(z=near))
        for h in range(2):
            zi = 2 * h + p.zl
            self.add(zi, self.land_y[zi])
        if self.layer == 1:
            signal(self.credit_y, p.at(y=1 - p.y))

    def step_a(self):
        p = self.p
        near = p.z + 1 - 2 * p.zl
        far = p.z + 2 - 4 * p.zh
        if self.layer == 0:
            pl.semaphore_wait(self.credit_b, 1)
        for h in range(2):
            arrived(self.land_z.at[h], self.recv.at[1 + h])
        away = 2 * (1 - p.zh) + p.zl
        self.add(away, self.land_z[1 - p.zh])
        self.go(self.buf.at[away, p.y], self.land_z.at[2], 3, p.at(z=far))
        self.add(p.z, self.land_z[p.zh])
        if self.layer == 1:
            signal(self.credit_a, p.at(z=near))

    def step_z(self):
        p = self.p
        arrived(self.land_z.at[2], self.recv.at[3])
        total = self.buf[p.z, p.y].astype(f32) + self.land_z[2].astype(f32)
        if self.layer == 1:
            signal(self.credit_b, p.at(z=p.z + 2 - 4 * p.zh))

        @pl.when(p.x == self.layer)
        def _():
            self.fin[...] = total

        @pl.when(p.x != self.layer)
        def _():
            self.stage[...] = total.astype(bf16)
            self.go(self.stage, self.land_x, 4, p.at(x=1 - p.x))

    def step_x(self):
        p = self.p

        @pl.when(p.x == self.layer)
        def _():
            arrived(self.land_x, self.recv.at[4])
            self.fin[...] += self.land_x[...].astype(f32)
            self.go(self.fin, self.own, 5, p.at(d=1 - p.d))
            pltpu.make_async_copy(self.fin, self.own, self.last).start()

    def close(self):
        p = self.p
        departed(self.buf.at[:, 0], self.send.at[0])
        for i in range(1, p.nz):
            departed(self.buf.at[0, 0], self.send.at[i])

    def end(self):
        @pl.when(self.p.x == self.layer)
        def _():
            departed(self.fin, self.send.at[5])
            arrived(self.other, self.recv.at[5])
            finish(self.fin, self.last)

        @pl.when(self.p.x != self.layer)
        def _():
            departed(self.stage, self.send.at[4])


SMALL_OUT = 128
Q, O, U, DN, SM = range(5)
PARTS = (
    (Q, 0, 96, 0, 384),
    (Q, 0, 96, 384, 384),
    (Q, 0, 96, 768, 384),
    (O, 0, 96, 0, 384),
    (U, 0, 96, 0, 768),
    (U, 0, 96, 768, 768),
    (DN, 0, 192, 0, 384),
    (DN, 192, 192, 0, 384),
    (SM, 0, 64, 0, CH),
)


class Loaded(NamedTuple):
    gp: Any
    r: Any
    o: Any
    inv: Any
    ph: Any
    qkv: Any
    n2: Any
    ob: Any
    a: Any
    u: Any
    pre: Any


class BackwardRefs(NamedTuple):
    cot: Any
    res1: Any
    gv: Any
    bd: Any
    wq: Any
    wo: Any
    wu: Any
    wd: Any


class BackwardScratch(NamedTuple):
    g: Any
    drb: Any
    gs: Any
    tmp: Any
    acc: Any
    st: Any
    stb: Any
    later: Any
    got: Any
    mg: Any
    vr: Any
    gr: Any
    hidr: Any
    wdr: Any
    vq: Any
    vo: Any
    vu: Any
    bq: Any
    bo: Any
    bu: Any
    bd_: Any
    bs: Any
    yq: Any
    yo: Any
    yu: Any
    yd: Any
    ys: Any
    zq: Any
    zo: Any
    zu: Any
    zd: Any
    zs: Any
    xq: Any
    xo: Any
    xu: Any
    xd: Any
    xs: Any
    wq: Any
    wo: Any
    wu: Any
    wd: Any
    ws: Any
    fq: Any
    fo: Any
    fu: Any
    fd: Any
    fs: Any
    tmp96: Any
    tmpd: Any
    sb: Any
    sd: Any
    r_send: Any
    r_recv: Any
    r_last: Any
    credit_y: Any
    credit_a: Any
    credit_b: Any
    m_send: Any
    m_recv: Any
    s_send: Any
    s_recv: Any
    d_send: Any
    d_recv: Any
    w_sem: Any
    l_sem: Any
    h_sem: Any
    t_sem: Any
    k_sem: Any


def backward_kernel(n, *refs):
    ref = BackwardRefs(*refs[:8])
    source = [Loaded(*refs[8:19]), Loaded(*refs[19:30])]
    hidden = refs[30:32]
    lay, gin, small_out = refs[32], refs[33], refs[38]
    wgrads = refs[34:38]
    lands = refs[39:47]
    v = Loaded(*refs[47:58])
    own = BackwardScratch(*refs[58:])
    p = Place(n)
    nz, group = p.nz, p.group
    t = own.drb.shape[0]
    nc = t // CH
    members = 2 * group
    gains, gbuf, tmp, acc = ref.gv, own.g, own.tmp, own.acc
    vr, gr, mg = own.vr, own.gr, own.mg
    flat = Weights(own.vq.reshape(D, 3 * D), own.vo.reshape(D, D), own.vu.reshape(D, FF))
    stored = (own.vq, own.vo, own.vu)
    lane_t = lanes(t)
    lane = lanes(CH)
    low = lane < HEAD
    row = lax.broadcasted_iota(jnp.int32, (CH, CH), 0)
    tril, triu = row >= lane, row <= lane

    def load(layer, *wanted):
        for dst in wanted:
            k = [dst is x for x in v].index(True)
            pltpu.make_async_copy(source[layer][k], dst, own.l_sem.at[k]).start()

    def loaded(*wanted):
        for dst in wanted:
            k = [dst is x for x in v].index(True)
            finish(dst, own.l_sem.at[k])

    def load_w(layer, k):
        w = (ref.wq, ref.wo, ref.wu)[k]
        pltpu.make_async_copy(w.at[layer], stored[k], own.w_sem.at[k]).start()

    def loaded_w(k):
        finish(stored[k], own.w_sem.at[k])

    def load_wd(layer, k):
        pltpu.make_async_copy(
            ref.wd.at[layer, k // 2, k % 2], own.wdr.at[k % 3], own.k_sem.at[k % 3]
        ).start()

    pltpu.make_async_copy(ref.cot, gbuf.at[0], own.t_sem.at[4]).start()
    for k in range(3):
        load_wd(1, k)
    load(1, v.gp)
    load_w(1, U)
    load(1, v.r, v.o, v.inv, v.ph)
    load_w(1, O)
    load_w(1, Q)
    load(1, v.qkv, v.n2, v.ob, v.a, v.u, v.pre)
    p.meet()
    finish(gbuf.at[0], own.t_sem.at[4])

    width = (3 * D // 2, D // 2, FF // 2, D // 2)
    bufs = (own.bq, own.bo, own.bu, own.bd_, own.bs)
    spots = (
        (own.yq, own.yo, own.yu, own.yd, own.ys),
        (own.zq, own.zo, own.zu, own.zd, own.zs),
        (own.xq, own.xo, own.xu, own.xd, own.xs),
        (own.wq, own.wo, own.wu, own.wd, own.ws),
    )
    fins = (own.fq, own.fo, own.fu, own.fd, own.fs)
    reduces = []
    for layer in range(2):
        line = [[] for _ in range(5)]
        for k, (m, r0_, r_, c0_, c_) in enumerate(PARTS):
            rows, cols = pl.ds(r0_, r_), pl.ds(c0_, c_)
            out = []
            for side in (p.d, 1 - p.d):
                if m == SM:
                    out.append(small_out.at[pl.ds(pl.multiple_of(side * r_, r_), r_), :])
                else:
                    at = pl.ds(pl.multiple_of(side * width[m] + c0_, CH), c_)
                    out.append(wgrads[m].at[rows, at])
            line[m].append(
                Reduce(
                    p,
                    layer,
                    bufs[m].at[:, :, rows, cols],
                    (
                        spots[0][m].at[:, rows, cols],
                        spots[1][m].at[:, rows, cols],
                        spots[2][m].at[rows, cols],
                        spots[3][m].at[rows, cols],
                    ),
                    out,
                    fins[m].at[rows, cols],
                    (own.r_send.at[layer, k], own.r_recv.at[layer, k], own.r_last.at[layer, k]),
                    (own.credit_y.at[k], own.credit_a.at[k], own.credit_b.at[k]),
                )
            )
        reduces.append(line)

    def step(name, layer, *which):
        def all_():
            for m in which:
                for part in reduces[layer][m]:
                    name(part)

        return all_

    step_y = functools.partial(step, Reduce.step_y)
    step_a = functools.partial(step, Reduce.step_a)
    step_z = functools.partial(step, Reduce.step_z)
    step_x = functools.partial(step, Reduce.step_x)

    def states_ok(o, taking):
        return (p.r + o < members) if taking else (p.r - o >= 0)

    def send_states(layer):
        for o in range(1, members):
            @pl.when(states_ok(o, False))
            def _():
                remote(
                    own.stb.at[layer],
                    own.got.at[layer, o - 1],
                    own.s_send.at[layer, o - 1],
                    own.s_recv.at[layer, o - 1],
                    p.member(p.r - o),
                ).start()

    def take_states(layer):
        later = own.later
        later[...] = jnp.zeros(later.shape, f32)
        for o in range(1, members):

            @pl.when(states_ok(o, True))
            def _():
                arrived(own.got.at[layer, o - 1], own.s_recv.at[layer, o - 1])
                add_states(later, own.got.at[layer, o - 1])

        return later

    def close_states(layer):
        for o in range(1, members):

            @pl.when(states_ok(o, False))
            def _():
                departed(own.stb.at[layer], own.s_send.at[layer, o - 1])

    def norm_back(x_ref, which, layer, body):
        gain = wide(gains, layer, which * 6, 6)
        acc[...] = jnp.zeros(acc.shape, f32)

        def step(i):
            rows = span(i, CH)
            xh, rstd = standardize(x_ref[rows, :].astype(f32))
            dn = tmp[rows, :]
            acc[0:1, :] += jnp.sum(dn, 0, keepdims=True)
            acc[1:2, :] += jnp.sum(dn * xh, 0, keepdims=True)
            dx = dn * gain
            body(
                rows,
                rstd
                * (dx - jnp.mean(dx, -1, keepdims=True) - xh * jnp.mean(dx * xh, -1, keepdims=True)),
            )

        loop(nc, step)
        put_rows(vr, layer, SHIFT2 if which else SHIFT1, acc[0:1, :])
        put_rows(gr, layer, which * 6, acc[1:2, :])

    def mlp_back(layer, g, events):
        gp, r, o_, inv, ph = v.gp, v.r, v.o, v.inv, v.ph
        drb, gs, st = own.drb, own.gs, own.st
        loaded(v.gp)
        for k in range(2 * nz):
            finish(own.wdr.at[k % 3], own.k_sem.at[k % 3])
            cols = pl.ds(k * FF // n, FF // n)
            part = (nt(g[...], own.wdr[k % 3]) * gp[:, cols]).astype(bf16)
            gp[:, cols] = part
            put_rows(
                vr, layer, UP_BIAS + 3 * k, jnp.sum(part.astype(f32), 0, keepdims=True)
            )
            if k + 3 < 2 * nz:
                load_wd(layer, k + 3)
            if k in events:
                events[k]()
        loaded_w(U)

        def n2_col(j):
            cols = span(j, TILE)
            tmp[:, cols] = nt(gp[...], flat.u[cols, :])

        loop(D // TILE, n2_col)
        loaded(v.r)

        def body(rows, back):
            up = g[rows, :].astype(f32)
            total = up + back
            acc[2:3, :] += jnp.sum(up, 0, keepdims=True)
            acc[3:4, :] += jnp.sum(total, 0, keepdims=True)
            r[rows, :] = total
            drb[rows, :] = total.astype(bf16)

        norm_back(r, 1, layer, body)
        put_rows(vr, layer, DOWN_BIAS, acc[2:3, :])
        put_rows(vr, layer, OUT_BIAS, acc[3:4, :])
        loaded_w(O)
        loaded(v.inv, v.o, v.ph)

        def do_col(j):
            cols = span(j, TILE)
            gs[:, cols] = (nt(drb[...], flat.o[cols, :]) * inv[:, cols]).astype(bf16)

        loop(D // TILE, do_col)
        low_t = lane_t < HEAD

        def pair(k):
            cols = span(k, CH)
            gv = gs[:, cols]
            prod = gv.astype(f32) * o_[:, cols]
            e0 = -jnp.sum(jnp.where(low_t, prod, 0.0), -1, keepdims=True)
            e1 = -jnp.sum(jnp.where(low_t, 0.0, prod), -1, keepdims=True)
            swapped = jnp.where(low_t, e1, e0)
            inv[:, cols] = swapped
            for hh in range(2):
                ge = with_error(gv, swapped, lane_t, hh)
                full = tn(ge, ph[:, span(2 * k + hh, CH)])
                st[layer, span(2 * k + hh, HEAD), :] = full[hh * HEAD : (hh + 1) * HEAD]
                at = HEAD * (1 - hh)
                st[layer, pl.ds(D + 2 * k + hh, 1), :] = full[at : at + 1] + full[at + 1 : at + 2]

        loop(PAIRS, pair)
        st[layer, D + H :, :] = jnp.zeros((STATE_ROWS - D - H, CH), f32)
        split_states(st.at[layer], own.stb.at[layer])
        send_states(layer)

    def weight_grad(layer, m, keep):
        parts = reduces[layer][m]
        buf, c = bufs[m], width[m]
        r = buf.shape[2]
        land_d = lands[layer * 4 + m]
        send, recv = own.m_send.at[layer, m], own.m_recv.at[layer, m]
        base = (p.d if keep else 1 - p.d) * c
        if keep:
            departed(buf, send)
            arrived(land_d, recv)
        elif layer == 0:
            for part in reduces[1][m]:
                part.close()
        if m == DN:
            rhs = gbuf[1 - layer, :, pl.ds(pl.multiple_of(base, CH), c)]

            def fetch(k):
                pltpu.make_async_copy(
                    hidden[layer].at[:, pl.ds(k * FF // n, FF // n)],
                    own.hidr.at[k % 3],
                    own.h_sem.at[k % 3],
                ).start()
                if keep:
                    pltpu.make_async_copy(
                        land_d.at[k // 2, k % 2], own.tmpd.at[k % 3], own.t_sem.at[k % 3]
                    ).start()

            for k in range(3):
                fetch(k)
            for k in range(2 * nz):
                finish(own.hidr.at[k % 3], own.h_sem.at[k % 3])
                val = tn(own.hidr[k % 3], rhs)
                if keep:
                    finish(own.tmpd.at[k % 3], own.t_sem.at[k % 3])
                    val = val + own.tmpd[k % 3].astype(f32)
                buf[k // 2, k % 2] = val.astype(bf16)
                if k + 3 < 2 * nz:
                    fetch(k + 3)
        else:
            lhs = (v.a, v.ob, v.n2)[m]
            rhs = (v.qkv, own.drb, v.gp)[m]
            wide_ = 384
            count = c // wide_

            def fetch(k):
                pltpu.make_async_copy(
                    land_d.at[:, :, :, pl.ds(k * wide_, wide_)],
                    own.tmp96.at[k % 2],
                    own.t_sem.at[k % 2],
                ).start()

            if keep:
                for k in range(min(2, count)):
                    fetch(k)
            for k in range(count):
                val = tn(lhs[...], rhs[:, pl.ds(pl.multiple_of(base + k * wide_, CH), wide_)])
                if keep:
                    finish(own.tmp96.at[k % 2], own.t_sem.at[k % 2])
                for zi in range(nz):
                    for yi in range(2):
                        at = (zi * 2 + yi) * r
                        part = val[at : at + r]
                        if keep:
                            part = part + own.tmp96[k % 2, zi, yi].astype(f32)
                        buf[zi, yi, :, pl.ds(k * wide_, wide_)] = part.astype(bf16)
                if keep and k + 2 < count:
                    fetch(k + 2)
                each = count // len(parts)
                if keep and (k + 1) % each == 0:
                    parts[k // each].send_y()
        if keep and m == DN:
            for part in parts:
                part.send_y()
        if not keep:
            remote(buf, land_d, send, recv, p.at(d=1 - p.d)).start()

    def mix_back(layer, events):
        qkv, ph, gs, es = v.qkv, v.ph, own.gs, v.inv
        bd = ref.bd.at[layer]
        s1 = take_states(layer)
        loaded(v.qkv, v.pre)
        s0 = v.pre

        def pair(k):
            cols = span(k, CH)
            vcols = pl.ds(pl.multiple_of(2 * D + k * CH, CH), CH)
            kcols = pl.ds(pl.multiple_of(D + k * CH, CH), CH)

            def keys(rows, hh):
                return ph[rows, pl.ds(pl.multiple_of((H + 2 * k + hh) * CH, CH), CH)]

            before, finer = [], []
            s = s0[cols, :]
            tot = [s0[pl.ds(D + 2 * k + hh, 1), :] for hh in range(2)]
            for c in range(nc):
                rows = pl.ds(c * CH, CH)
                fine = (s - s.astype(bf16).astype(f32)).astype(bf16)
                none = jnp.zeros_like(fine)
                before.append([with_totals(s, tot[hh], row, hh, True) for hh in range(2)])
                finer.append([jnp.where(row < HEAD, fine, none), jnp.where(row < HEAD, none, fine)])
                if c < nc - 1:
                    val = qkv[rows, vcols]
                    new = []
                    for hh in range(2):
                        kh = keys(rows, hh)
                        new.append(tn(val, kh)[hh * HEAD : (hh + 1) * HEAD])
                        tot[hh] = tot[hh] + jnp.sum(kh.astype(f32), 0, keepdims=True)
                    s = s + jnp.concatenate(new, 0)
            ds = s1[cols, :]
            dtot = [s1[pl.ds(D + 2 * k + hh, 1), :] for hh in range(2)]
            acc_q = jnp.zeros((CH, 2 * CH), f32)
            acc_k = jnp.zeros((CH, 2 * CH), f32)
            sums = [jnp.zeros((1, CH), f32) for _ in range(3)]
            for c in reversed(range(nc)):
                rows = pl.ds(c * CH, CH)
                val = qkv[rows, vcols]
                gv = gs[rows, cols]
                ev = es[rows, cols]
                dsl = ds.astype(bf16)
                dl_q, dl_k, dv, new = [], [], [], []
                for hh in range(2):
                    qh = ph[rows, span(2 * k + hh, CH)]
                    kh = keys(rows, hh)
                    ge = with_error(gv, ev, lane, hh)
                    v1 = with_ones(val, lane, hh)
                    after = with_totals(ds, dtot[hh], row, hh, False)
                    da = jnp.where(tril, nt(ge, v1), 0.0).astype(bf16)
                    dat = jnp.where(triu, nt(v1, ge), 0.0).astype(bf16)
                    at = jnp.where(triu, nt(kh, qh), 0.0).astype(bf16)
                    dq = nn(da, kh) + nn(ge, before[c][hh]) + nn(ge, finer[c][hh])
                    dk = nn(dat, qh) + nn(v1, after)
                    dv.append(nn(at, gv) + nt(kh, dsl))
                    for p_, d_, to in ((qh, dq, dl_q), (kh, dk, dl_k)):
                        pf = p_.astype(f32)
                        to.append((pf * (d_ - half_sums(pf * d_, low))).astype(bf16))
                    full = tn(ge, qh)
                    new.append(full[hh * HEAD : (hh + 1) * HEAD])
                    first = HEAD * (1 - hh)
                    dtot[hh] = dtot[hh] + full[first : first + 1] + full[first + 1 : first + 2]
                ds = ds + jnp.concatenate(new, 0)
                dl_q = jnp.concatenate(dl_q, 1)
                dl_k = jnp.concatenate(dl_k, 1)
                acc_q = acc_q + tn(qkv[rows, cols], dl_q)
                acc_k = acc_k + tn(qkv[rows, kcols], dl_k)
                parts = (
                    (cols, nt(dl_q, bd[k])),
                    (kcols, nt(dl_k, bd[PAIRS + k])),
                    (vcols, jnp.where(low, dv[0], dv[1])),
                )
                for i, (where, new_) in enumerate(parts):
                    new_ = new_.astype(bf16)
                    qkv[rows, where] = new_
                    sums[i] = sums[i] + jnp.sum(new_.astype(f32), 0, keepdims=True)
            for i in range(3):
                vr[layer, pl.ds(QKV_BIAS + i * PAIRS + k, 1), :] = sums[i]
            for which, total in enumerate((acc_q, acc_k)):
                for hh in range(2):
                    blk = total[hh * HEAD : (hh + 1) * HEAD, hh * CH : (hh + 1) * CH]
                    mg[which * H + 2 * k + hh] = blk - pltpu.roll(blk, HEAD, 1)

        loop(PAIRS, pair, events)
        loaded_w(Q)

        def n1_col(j):
            cols = span(j, TILE)
            tmp[:, cols] = nt(qkv[...], flat.q[cols, :])

        loop(D // TILE, n1_col)
        loaded(v.u)
        du = gbuf.at[layer]

        def body(rows, back):
            du[rows, :] = (v.r[rows, :] + back).astype(bf16)

        norm_back(v.u, 0, layer, body)

    closing = []

    def deliver(which, layer, rows):
        sems = own.d_send.at[which, layer], own.d_recv.at[which]
        closing.extend(hand_over(p, layer, rows, gin if which else lay, *sems))

    def small_rows(side):
        return pl.ds(pl.multiple_of(side * 64, 64), 64)

    def pack_small(layer):
        sb = own.sb
        for k in range(n):
            at, gat = (33 * k) // 4, (3 * k) // 2
            zi, yi = k // 2, k % 2
            sb[zi, yi, 0:9] = vr[layer, at : at + 9, :]
            sb[zi, yi, 9:11] = gr[layer, gat : gat + 2, :]
            sb[zi, yi, 11:16] = jnp.zeros((5, CH), f32)
            h0, h1, h2 = (mg[3 * k + i] for i in range(3))
            left = jnp.concatenate([h0, h1[: HEAD // 2]], 0)
            right = jnp.concatenate([h1[HEAD // 2 :], h2], 0)
            sb[zi, yi, 16:112] = jnp.where(lanes(96) < HEAD, left, -right)
            sb[zi, yi, 112:] = jnp.zeros((16, CH), f32)
        remote(
            sb.at[:, :, small_rows(1 - p.d), :],
            own.sd.at[layer],
            own.m_send.at[layer, SM],
            own.m_recv.at[layer, SM],
            p.at(d=1 - p.d),
        ).start()

    def small_core(layer):
        part = reduces[layer][SM][0]
        departed(own.sd.at[layer], own.m_send.at[layer, SM])
        arrived(own.sd.at[layer], own.m_recv.at[layer, SM])
        if layer == 0:
            reduces[1][SM][0].close()
        part.buf[...] = (own.sb[:, :, small_rows(p.d), :] + own.sd[layer]).astype(bf16)
        part.send_y()

    vr[...] = jnp.zeros(vr.shape, f32)
    gr[...] = jnp.zeros(gr.shape, f32)
    def run(*steps):
        def all_():
            for step in steps:
                step()

        return all_

    deliver(0, 1, ref.res1)
    weight_grad(1, DN, False)
    mlp_back(1, gbuf.at[0], {4: functools.partial(weight_grad, 1, DN, True)})
    load(0, v.o)
    load_w(0, U)
    load_w(0, O)
    for k in range(3):
        load_wd(0, k)
    loaded(v.n2, v.ob, v.a)
    weight_grad(1, U, False)
    weight_grad(1, O, False)
    weight_grad(1, U, True)
    weight_grad(1, O, True)
    load(0, v.gp, v.n2, v.ob)
    mix_back(1, {1: step_y(1, DN), 5: step_a(1, DN)})
    load_w(0, Q)
    load(0, v.r, v.inv, v.ph, v.u, v.pre)
    pack_small(1)
    step_y(1, U)()
    weight_grad(1, Q, False)
    weight_grad(1, Q, True)
    small_core(1)
    load(0, v.qkv, v.a)

    step_z(1, DN)()
    weight_grad(0, DN, False)
    step_y(1, O)()
    mlp_back(
        0,
        gbuf.at[1],
        {4: functools.partial(weight_grad, 0, DN, True), 6: step_a(1, U), 7: step_x(1, DN)},
    )
    loaded(v.n2, v.ob, v.a)
    step_a(1, O)()
    step_z(1, U)()
    weight_grad(0, U, False)
    step_y(1, Q, SM)()
    weight_grad(0, U, True)
    step_z(1, O)()
    weight_grad(0, O, False)
    weight_grad(0, O, True)
    step_x(1, U)()
    mix_back(
        0,
        {
            0: step_x(1, O),
            1: step_a(1, Q, SM),
            3: step_y(0, DN),
            4: step_z(1, Q, SM),
        },
    )
    pack_small(0)
    weight_grad(0, Q, False)
    step_a(0, DN)()
    step_x(1, Q, SM)()
    weight_grad(0, Q, True)
    small_core(0)
    step_y(0, U)()
    step_y(0, O)()
    step_z(0, DN)()
    deliver(1, 1, gbuf.at[1])
    deliver(1, 0, gbuf.at[0])
    first, second, third = reduces[0][Q]
    step_x(0, DN)()
    first.step_y()
    step_a(0, U)()
    step_a(0, O)()
    second.step_y()
    first.step_a()
    step_z(0, U)()
    step_z(0, O)()
    third.step_y()
    second.step_a()
    step_x(0, U)()
    step_x(0, O)()
    step_y(0, SM)()
    first.step_z()
    third.step_a()
    step_a(0, SM)()
    second.step_z()
    first.step_x()
    third.step_z()
    step_z(0, SM)()
    second.step_x()
    third.step_x()
    step_x(0, SM)()

    for m in range(5):
        for part in reduces[0][m]:
            part.close()
        for layer in range(2):
            for part in reduces[layer][m]:
                part.end()
    for layer in range(2):
        close_states(layer)

        handed_over(p, layer, gin, own.d_recv.at[1])
    handed_over(p, 1, lay, own.d_recv.at[0])

    for close in closing:
        close()


def backward_pass(n, cot, gains, bds, full, tokens, kept):
    t = cot.shape[0]
    nz = n // 2
    args = [cot, kept[1].res, gains, bds] + list(full)
    for u, k in zip((tokens, kept[0].res), kept):
        read = Loaded(k.gp, k.r, k.o, k.inv, k.ph, k.qkv, k.n2, k.ob, k.a, u, k.pre)
        args += list(read)
    args += [k.hid for k in kept]
    widths = (3 * D // 2, D // 2, FF // 2, D // 2)
    rows = (D // n, D // n, D // n, FF // n)
    outs = [shape((1, 4, 2, CH, D), bf16)] * 2
    outs += [shape((r, 2 * c), f32) for r, c in zip(rows, widths)]
    outs += [shape((SMALL_OUT, CH), f32)]
    outs += [shape((nz, 2, r, c), bf16) for r, c in zip(rows, widths)] * 2
    specs = [ANY] * len(outs)
    ins = [ANY] * 2 + [VMEM] * 2 + [ANY] * (len(args) - 4)
    scratch = [pltpu.VMEM(a.shape, a.dtype) for a in read]

    def vmem(*dims, kind=f32):
        scratch.append(pltpu.VMEM(dims, kind))

    vmem(2, t, D, kind=bf16)
    vmem(t, D, kind=bf16)
    vmem(t, D, kind=bf16)
    vmem(t, D)
    vmem(8, D)
    vmem(2, STATE_ROWS, CH)
    vmem(2, STATE_ROWS + 16, CH, kind=bf16)
    vmem(STATE_ROWS, CH)
    vmem(2, n // 2 - 1, STATE_ROWS + 16, CH, kind=bf16)
    vmem(2 * H, HEAD, CH)
    vmem(2, VEC_ROWS, CH)
    vmem(2, GAIN_ROWS, CH)
    vmem(3, t, FF // n, kind=bf16)
    vmem(3, FF // n, D, kind=bf16)
    for w in full[:3]:
        vmem(*w.shape[1:], kind=bf16)
    sizes = list(zip(rows, widths)) + [(64, CH)]
    for lead in ((nz, 2), (nz,), (nz - 1,), (), ()):
        for size in sizes:
            vmem(*lead, *size, kind=bf16)
    for size in sizes:
        vmem(*size)
    vmem(2, nz, 2, D // n, 384, kind=bf16)
    vmem(3, FF // n, D // 2, kind=bf16)
    vmem(nz, 2, SMALL_OUT, CH)
    vmem(2, nz, 2, 64, CH)
    dma = pltpu.SemaphoreType.DMA
    regular = pltpu.SemaphoreType.REGULAR
    count = len(PARTS)
    scratch += [dma((2, count, 6)), dma((2, count, 6)), dma((2, count))]
    scratch += [regular((count,))] * 3 + [dma((2, 5)), dma((2, 5))]
    scratch += [dma((2, n // 2 - 1)), dma((2, n // 2 - 1)), dma((2, 2, 4)), dma((2, 8)), dma((4,))]
    scratch += [dma((len(read),)), dma((3,)), dma((5,)), dma((3,))]
    got = call(
        functools.partial(backward_kernel, n),
        outs,
        scratch,
        ins,
        args,
        8 * t * D * (4 * D + 2 * FF),
        specs,
        cid=1,
        vmem=63,
    )
    return got[:7]


def settle_kernel(lay0, lay1, *refs):
    rest, small, outs, held, sems = refs[:5], refs[5], refs[6:13], refs[13:19], refs[19]
    x = lax.axis_index("section")
    for plane, src in enumerate((lay0, lay1)):

        @pl.when(x == plane)
        def _():
            pltpu.make_async_copy(src, held[0], sems.at[0]).start()

    for i, src in enumerate(rest):
        pltpu.make_async_copy(src, held[1 + i], sems.at[1 + i]).start()
    both = small[16:112, :]
    outs[6][0:96, :] = both[:, :HEAD]
    outs[6][96:, :] = pltpu.roll(both, HEAD, 1)[:, :HEAD]
    copies = []
    for i, buf in enumerate(held):
        finish(buf, sems.at[i])
        copies.append(pltpu.make_async_copy(buf, outs[i], sems.at[6 + i]))
        copies[-1].start()
    for copy in copies:
        copy.wait()


def settle(lay0, lay1, rest, small):
    arrays = [lay0, lay1, *rest, small]
    outs = [shape(a.shape, a.dtype) for a in (lay0, *rest)]
    return call(
        settle_kernel,
        outs + [shape((192, HEAD), f32)],
        [pltpu.VMEM(o.shape, o.dtype) for o in outs] + [pltpu.SemaphoreType.DMA((12,))],
        [ANY] * 7 + [VMEM],
        arrays,
        1,
        [ANY] * 6 + [VMEM],
    )


def shards(inputs, cotangent, *weights):
    n = lax.axis_size("seq")
    d, j = lax.axis_index("dp"), lax.axis_index("seq")
    qkv_w, out_w, up_w, down_w, map_w, bias_w, gain_w = (w[0] for w in weights)

    def placed(vector, offset, rows):
        flat = jnp.zeros((rows * CH,), f32)
        return lax.dynamic_update_slice(flat, vector, (offset,)).reshape(rows, CH)

    bias_at, gain_at = (j % 4) * 32, (j % 2) * 64
    small = jnp.concatenate(
        [
            placed(bias_w, bias_at, 9),
            placed(gain_w, gain_at, 2),
            jnp.zeros((5, CH), f32),
            jnp.concatenate([map_w[:96], map_w[96:]], 1),
            jnp.zeros((16, CH), f32),
        ]
    ).astype(bf16)
    small = lax.dynamic_slice_in_dim(small, d * 64, 64, 0)
    full, gains, bds, tokens, cot, lay0, kept = forward_pass(
        n, inputs, cotangent, small, qkv_w, out_w, up_w, down_w
    )
    lay1, *rest, g_small = backward_pass(n, cot, gains, bds, full, tokens, kept)
    layer_out, grads, g_qkv, g_out, g_up, g_down, maps = settle(lay0, lay1, rest, g_small)
    bias = lax.dynamic_slice_in_dim(g_small[:9].reshape(-1), bias_at, bias_w.shape[0])
    gain = lax.dynamic_slice_in_dim(g_small[9:11].reshape(-1), gain_at, gain_w.shape[0])
    return (
        layer_out,
        grads,
        g_qkv[None],
        g_out[None],
        g_up[None],
        g_down[None],
        maps[None],
        bias[None],
        gain[None],
    )


def solution(mesh):
    tokens = P("dp", None, "seq", None)
    matrix = P("section", "seq", None)
    vector = P("section", "seq")
    stacked = P("section", "dp", None, "seq", None)
    chosen = shards if mesh.shape["seq"] == 8 else plain_shards
    return jax.shard_map(
        chosen,
        mesh=mesh,
        in_specs=(tokens, tokens) + (matrix,) * 5 + (vector,) * 2,
        out_specs=(stacked, stacked) + (matrix,) * 5 + (vector,) * 2,
        check_vma=False,
    )
```

```python
import functools
from typing import Any, NamedTuple

import jax
import jax.numpy as jnp
from jax import lax
from jax.experimental import pallas as pl
from jax.experimental.pallas import tpu as pltpu
from jax.sharding import PartitionSpec as P


D = 768
FF = 3072
H = 12
HEAD = 64
BLOCK = 64


MAXIMUM_ACCURACY = lax.Precision.HIGHEST
NORM_EPSILON = 1e-05


def carried_in(part, axis, combine, identity, reverse):
    count = lax.axis_size(axis)
    place = lax.axis_index(axis)
    ahead = count - 1 - place if reverse else place
    gathered = jax.tree.map(lambda a: lax.all_gather(a, axis), part)
    state = jax.tree.map(lambda a, e: jnp.zeros_like(a) + jnp.asarray(e, a.dtype), part, identity)

    def one(lap, state):
        source = count - 1 - lap if reverse else lap
        return combine(
            state, jax.tree.map(lambda a: lax.dynamic_index_in_dim(a, source, 0, False), gathered)
        )

    return lax.fori_loop(0, ahead, one, state)


def shifted(value, axis, steps):
    count = lax.axis_size(axis)
    leading, last = (max(0, -steps), min(count, count - steps))
    return lax.ppermute(value, axis, [(source, source + steps) for source in range(leading, last)])


def normalize(values, gain_vector, shift_vector):
    average = jnp.mean(values, -1, keepdims=True)
    centred = values - average
    spread = jnp.mean(centred * centred, -1, keepdims=True)
    return centred * lax.rsqrt(spread + NORM_EPSILON) * gain_vector + shift_vector


def features(logits):
    return jnp.concatenate([jax.nn.softmax(logits, -1), jax.nn.softmax(-logits, -1)], -1)


def gelu_tanh(values):
    return jax.nn.gelu(values, approximate=True)


def adding(earlier, later_part):
    return jax.tree.map(jnp.add, earlier, later_part)


def across_rows(left_side, right_side):
    return lax.dot_general(
        left_side, right_side, (((0,), (0,)), ((), ())), preferred_element_type=jnp.float32
    )


def against_rows(left_side, right_side):
    return lax.dot_general(
        left_side, right_side, (((1,), (1,)), ((), ())), preferred_element_type=jnp.float32
    )


def precise(pattern, left_side, right_side):
    return jnp.einsum(pattern, left_side, right_side, precision=MAXIMUM_ACCURACY)


def causal_mask():
    places = lax.broadcasted_iota(jnp.int32, (BLOCK, BLOCK), 0)
    others = lax.broadcasted_iota(jnp.int32, (BLOCK, BLOCK), 1)
    return (others <= places).astype(jnp.float32)


def in_blocks(source_array, batch_rows):
    return source_array.reshape((batch_rows, -1, BLOCK) + source_array.shape[1:])


def prepare(gathered):
    qkv_full, out_full, up_full, down_full, map_full, bias_full, gain_full = [
        piece_array[0] for piece_array in gathered
    ]
    feature_maps = map_full.reshape(2, H, HEAD, HEAD)
    vectors = bias_full.astype(jnp.float32)
    scales = gain_full.astype(jnp.float32)
    pieces = (
        vectors[:D],
        vectors[D : 4 * D],
        vectors[4 * D : 5 * D],
        vectors[5 * D : 6 * D],
        vectors[6 * D : 6 * D + FF],
        vectors[6 * D + FF :],
        scales[:D],
        scales[D:],
    )
    return (qkv_full, out_full, up_full, down_full, feature_maps, pieces)


def block_sums(query_map, key_map, value_rows, batch_rows):
    query_blocks = in_blocks(query_map, batch_rows)
    key_blocks = in_blocks(key_map, batch_rows)
    value_blocks = in_blocks(value_rows, batch_rows).astype(jnp.float32)
    query_wide = query_blocks.astype(jnp.float32)
    key_wide = key_blocks.astype(jnp.float32)
    score_matrix = (
        jnp.einsum(
            "bcqhf,bckhf->bchqk", query_blocks, key_blocks, preferred_element_type=jnp.float32
        )
        * causal_mask()
    )
    block_state = precise("bckhf,bckhe->bchfe", key_wide, value_blocks)
    block_total = jnp.sum(key_wide, 2)
    return (query_wide, key_wide, value_blocks, score_matrix, block_state, block_total)


def attend(query_map, key_map, value_rows, initial, batch_rows):
    query_wide, key_wide, value_blocks, score_matrix, block_state, block_total = block_sums(
        query_map, key_map, value_rows, batch_rows
    )
    state_sum = jnp.sum(block_state, 1)
    total_sum = jnp.sum(block_total, 1)
    identity = (jnp.zeros_like(state_sum), jnp.zeros_like(total_sum))
    earlier = carried_in((state_sum, total_sum), "seq", adding, identity, False)
    overall = lax.psum((state_sum, total_sum), "seq")
    start_state = initial[0] + earlier[0]
    start_total = initial[1] + earlier[1]
    block_before = start_state[:, None] + jnp.cumsum(block_state, 1) - block_state
    total_before = start_total[:, None] + jnp.cumsum(block_total, 1) - block_total
    numerator = precise("bchqk,bckhe->bcqhe", score_matrix, value_blocks) + precise(
        "bcqhf,bchfe->bcqhe", query_wide, block_before
    )
    denominator = jnp.swapaxes(jnp.sum(score_matrix, -1), 2, 3) + precise(
        "bcqhf,bchf->bcqh", query_wide, total_before
    )
    mixture = numerator / denominator[..., None]
    handed = (initial[0] + overall[0], initial[1] + overall[1])
    return (mixture.reshape(value_rows.shape), denominator, (start_state, start_total), handed)


def attend_back(
    mixture_grad, query_map, key_map, value_rows, mixture, denominator, starts, future, batch_rows
):
    query_wide, key_wide, value_blocks, score_matrix, block_state, block_total = block_sums(
        query_map, key_map, value_rows, batch_rows
    )
    block_before = starts[0][:, None] + jnp.cumsum(block_state, 1) - block_state
    total_before = starts[1][:, None] + jnp.cumsum(block_total, 1) - block_total
    scaled = in_blocks(mixture_grad, batch_rows) / denominator[..., None]
    denominator_grad = -jnp.sum(scaled * in_blocks(mixture, batch_rows), -1)
    score_grad = (
        precise("bcqhe,bckhe->bchqk", scaled, value_blocks)
        + jnp.swapaxes(denominator_grad, 2, 3)[..., None]
    ) * causal_mask()
    query_grad = precise("bchqk,bckhf->bcqhf", score_grad, key_wide) + precise(
        "bcqhe,bchfe->bcqhf", scaled, block_before
    )
    query_grad = query_grad + denominator_grad[..., None] * total_before[:, :, None]
    state_grad = precise("bcqhf,bcqhe->bchfe", query_wide, scaled)
    total_grad = precise("bcqhf,bcqh->bchf", query_wide, denominator_grad)
    state_sum = jnp.sum(state_grad, 1)
    total_sum = jnp.sum(total_grad, 1)
    identity = (jnp.zeros_like(state_sum), jnp.zeros_like(total_sum))
    later_sums = carried_in((state_sum, total_sum), "seq", adding, identity, True)
    overall = lax.psum((state_sum, total_sum), "seq")
    ahead_state = future[0] + later_sums[0]
    ahead_total = future[1] + later_sums[1]
    rest_state = ahead_state[:, None] + state_sum[:, None] - jnp.cumsum(state_grad, 1)
    rest_total = ahead_total[:, None] + total_sum[:, None] - jnp.cumsum(total_grad, 1)
    key_grad = precise("bchqk,bcqhf->bckhf", score_grad, query_wide) + precise(
        "bckhe,bchfe->bckhf", value_blocks, rest_state
    )
    key_grad = key_grad + rest_total[:, :, None]
    value_grad = precise("bchqk,bcqhe->bckhe", score_matrix, scaled) + precise(
        "bckhf,bchfe->bckhe", key_wide, rest_state
    )
    return (
        query_grad.reshape(query_map.shape),
        key_grad.reshape(key_map.shape),
        value_grad.reshape(value_rows.shape),
        overall,
    )


def forward(tokens, params, initial):
    qkv_full, out_full, up_full, down_full, feature_maps, pieces = params
    shift_one, qkv_bias, out_bias, shift_two, up_bias, down_bias, gain_one, gain_two = pieces
    batch_rows = tokens.shape[0]
    flattened = tokens.reshape(-1, D)
    row_count = flattened.shape[0]
    normed = normalize(flattened, gain_one, shift_one).astype(jnp.bfloat16)
    projected = (jnp.dot(normed, qkv_full, preferred_element_type=jnp.float32) + qkv_bias).astype(
        jnp.bfloat16
    )
    query_rows = projected[:, :D].reshape(row_count, H, HEAD)
    key_rows = projected[:, D : 2 * D].reshape(row_count, H, HEAD)
    value_rows = projected[:, 2 * D :].reshape(row_count, H, HEAD)
    query_logits = jnp.einsum(
        "rhe,hef->rhf", query_rows, feature_maps[0], preferred_element_type=jnp.float32
    )
    key_logits = jnp.einsum(
        "rhe,hef->rhf", key_rows, feature_maps[1], preferred_element_type=jnp.float32
    )
    query_map = features(query_logits).astype(jnp.bfloat16)
    key_map = features(key_logits).astype(jnp.bfloat16)
    mixture, denominator, starts, handed = attend(
        query_map, key_map, value_rows, initial, batch_rows
    )
    mixture_low = mixture.reshape(row_count, D).astype(jnp.bfloat16)
    residual = (
        flattened + jnp.dot(mixture_low, out_full, preferred_element_type=jnp.float32) + out_bias
    )
    normed_two = normalize(residual, gain_two, shift_two).astype(jnp.bfloat16)
    before_act = jnp.dot(normed_two, up_full, preferred_element_type=jnp.float32) + up_bias
    hidden = gelu_tanh(before_act).astype(jnp.bfloat16)
    result = residual + jnp.dot(hidden, down_full, preferred_element_type=jnp.float32) + down_bias
    kept_values = (
        flattened,
        normed,
        projected,
        query_logits,
        key_logits,
        query_map,
        key_map,
        mixture,
        denominator,
        starts,
        residual,
        normed_two,
        before_act,
        hidden,
    )
    return (result.reshape(tokens.shape), handed, kept_values)


def backward(upstream, params, kept_values, future):
    qkv_full, out_full, up_full, down_full, feature_maps, pieces = params
    shift_one, qkv_bias, out_bias, shift_two, up_bias, down_bias, gain_one, gain_two = pieces
    (
        flattened,
        normed,
        projected,
        query_logits,
        key_logits,
        query_map,
        key_map,
        mixture,
        denominator,
        starts,
        residual,
        normed_two,
        before_act,
        hidden,
    ) = kept_values
    batch_rows = upstream.shape[0]
    row_count = flattened.shape[0]
    out_grad = upstream.reshape(row_count, D)
    down_bias_grad = jnp.sum(out_grad, 0)
    out_low = out_grad.astype(jnp.bfloat16)
    down_weight_grad = across_rows(hidden, out_low)
    hidden_grad = against_rows(out_low, down_full)
    _, gelu_back = jax.vjp(gelu_tanh, before_act)
    before_grad = gelu_back(hidden_grad)[0].astype(jnp.bfloat16)
    up_bias_grad = jnp.sum(before_grad.astype(jnp.float32), 0)
    up_weight_grad = across_rows(normed_two, before_grad)
    normed_two_grad = against_rows(before_grad, up_full)
    _, norm_back_two = jax.vjp(normalize, residual, gain_two, shift_two)
    residual_part, gain_two_grad, shift_two_grad = norm_back_two(normed_two_grad)
    residual_grad = out_grad + residual_part
    out_bias_grad = jnp.sum(residual_grad, 0)
    residual_low = residual_grad.astype(jnp.bfloat16)
    mixture_low = mixture.reshape(row_count, D).astype(jnp.bfloat16)
    out_weight_grad = across_rows(mixture_low, residual_low)
    mixture_grad = against_rows(residual_low, out_full).reshape(row_count, H, HEAD)
    query_rows = projected[:, :D].reshape(row_count, H, HEAD)
    key_rows = projected[:, D : 2 * D].reshape(row_count, H, HEAD)
    value_rows = projected[:, 2 * D :].reshape(row_count, H, HEAD)
    query_map_grad, key_map_grad, value_grad, handed = attend_back(
        mixture_grad,
        query_map,
        key_map,
        value_rows,
        mixture,
        denominator,
        starts,
        future,
        batch_rows,
    )
    _, query_back = jax.vjp(features, query_logits)
    query_logit_grad = query_back(query_map_grad)[0]
    _, key_back = jax.vjp(features, key_logits)
    key_logit_grad = key_back(key_map_grad)[0]
    maps_wide = feature_maps.astype(jnp.float32)
    query_grad = precise("rhf,hef->rhe", query_logit_grad, maps_wide[0])
    key_grad = precise("rhf,hef->rhe", key_logit_grad, maps_wide[1])
    map_weight_grad = jnp.stack(
        [
            precise("rhe,rhf->hef", query_rows.astype(jnp.float32), query_logit_grad),
            precise("rhe,rhf->hef", key_rows.astype(jnp.float32), key_logit_grad),
        ]
    ).reshape(2 * H * HEAD, HEAD)
    projected_grad = jnp.concatenate(
        [
            query_grad.reshape(row_count, D),
            key_grad.reshape(row_count, D),
            value_grad.reshape(row_count, D),
        ],
        1,
    ).astype(jnp.bfloat16)
    qkv_bias_grad = jnp.sum(projected_grad.astype(jnp.float32), 0)
    qkv_weight_grad = across_rows(normed, projected_grad)
    normed_grad = against_rows(projected_grad, qkv_full)
    _, norm_back_one = jax.vjp(normalize, flattened, gain_one, shift_one)
    input_part, gain_one_grad, shift_one_grad = norm_back_one(normed_grad)
    input_grad = residual_grad + input_part
    bias_grad = jnp.concatenate(
        [shift_one_grad, qkv_bias_grad, out_bias_grad, shift_two_grad, up_bias_grad, down_bias_grad]
    )
    gain_grad = jnp.concatenate([gain_one_grad, gain_two_grad])
    layer_grads = (
        qkv_weight_grad,
        out_weight_grad,
        up_weight_grad,
        down_weight_grad,
        map_weight_grad,
        bias_grad,
        gain_grad,
    )
    return (input_grad.reshape(upstream.shape), handed, layer_grads)


def reduce_grads(full_grads):
    g_qkv, g_out, g_up, g_down, g_map, g_bias, g_gain = full_grads
    s_qkv, s_out, s_up, s_down, s_map, s_bias, s_gain = (
        lax.psum_scatter(g_qkv, "seq", scatter_dimension=1, tiled=True),
        lax.psum_scatter(g_out, "seq", scatter_dimension=1, tiled=True),
        lax.psum_scatter(g_up, "seq", scatter_dimension=1, tiled=True),
        lax.psum_scatter(g_down, "seq", scatter_dimension=1, tiled=True),
        lax.psum_scatter(g_map, "seq", scatter_dimension=1, tiled=True),
        lax.psum_scatter(g_bias, "seq", scatter_dimension=1, tiled=True),
        lax.psum_scatter(g_gain, "seq", scatter_dimension=1, tiled=True),
    )
    return lax.psum((s_qkv, s_out, s_up, s_down, s_map, s_bias, s_gain), "dp")


def plain_shards(
    inputs, cotangent, qkv_weight, out_weight, up_weight, down_weight, map_weight, biases, gains
):
    section_index = lax.axis_index("section")
    batch_rows = inputs.shape[0]
    micro_count = inputs.shape[1]
    gathered = (
        lax.all_gather(qkv_weight.astype(jnp.bfloat16), "seq", axis=1, tiled=True),
        lax.all_gather(out_weight.astype(jnp.bfloat16), "seq", axis=1, tiled=True),
        lax.all_gather(up_weight.astype(jnp.bfloat16), "seq", axis=1, tiled=True),
        lax.all_gather(down_weight.astype(jnp.bfloat16), "seq", axis=1, tiled=True),
        lax.all_gather(map_weight.astype(jnp.bfloat16), "seq", axis=1, tiled=True),
        lax.all_gather(biases.astype(jnp.bfloat16), "seq", axis=1, tiled=True),
        lax.all_gather(gains.astype(jnp.bfloat16), "seq", axis=1, tiled=True),
    )
    params = prepare(gathered)
    empty_state = (
        jnp.zeros((batch_rows, H, 2 * HEAD, HEAD), jnp.float32),
        jnp.zeros((batch_rows, H, 2 * HEAD), jnp.float32),
    )
    blank_rows = jnp.zeros(inputs.shape[:1] + inputs.shape[2:], jnp.bfloat16)
    moments = jnp.arange(micro_count + 1, dtype=jnp.int32)

    def forward_moment(carry, moment):
        handed, arriving = carry
        own_tokens = lax.dynamic_index_in_dim(
            inputs, jnp.minimum(moment, micro_count - 1), 1, False
        )
        source = jnp.where(section_index == 0, own_tokens, arriving).astype(jnp.float32)
        carried = moment - section_index >= 1
        initial = (jnp.where(carried, handed[0], 0.0), jnp.where(carried, handed[1], 0.0))
        result, handed_next, kept_values = forward(source, params, initial)
        outgoing = result.astype(jnp.bfloat16)
        arriving_next = shifted(outgoing, "section", 1)
        return ((handed_next, arriving_next), (outgoing, kept_values))

    _, (result_stack, kept_stack) = lax.scan(forward_moment, (empty_state, blank_rows), moments)
    regathered = (
        lax.all_gather(qkv_weight.astype(jnp.bfloat16), "seq", axis=1, tiled=True),
        lax.all_gather(out_weight.astype(jnp.bfloat16), "seq", axis=1, tiled=True),
        lax.all_gather(up_weight.astype(jnp.bfloat16), "seq", axis=1, tiled=True),
        lax.all_gather(down_weight.astype(jnp.bfloat16), "seq", axis=1, tiled=True),
        lax.all_gather(map_weight.astype(jnp.bfloat16), "seq", axis=1, tiled=True),
        lax.all_gather(biases.astype(jnp.bfloat16), "seq", axis=1, tiled=True),
        lax.all_gather(gains.astype(jnp.bfloat16), "seq", axis=1, tiled=True),
    )
    back_params = prepare(regathered)
    zero_grads = (
        jnp.zeros((D, 3 * D), jnp.float32),
        jnp.zeros((D, D), jnp.float32),
        jnp.zeros((D, FF), jnp.float32),
        jnp.zeros((FF, D), jnp.float32),
        jnp.zeros((2 * H * HEAD, HEAD), jnp.float32),
        jnp.zeros((7 * D + FF,), jnp.float32),
        jnp.zeros((2 * D,), jnp.float32),
    )

    def backward_moment(carry, pieces):
        future, returning, grad_sums = carry
        slot, kept_values = pieces
        chosen = slot - section_index
        own_grad = lax.dynamic_index_in_dim(cotangent, jnp.maximum(slot - 1, 0), 1, False)
        live = (chosen >= 0) & (chosen < micro_count)
        upstream = jnp.where(section_index == 1, own_grad, returning).astype(jnp.float32)
        upstream = jnp.where(live, upstream, 0.0)
        later_micro = live & (chosen < micro_count - 1)
        ahead_part = (
            jnp.where(later_micro, future[0], 0.0),
            jnp.where(later_micro, future[1], 0.0),
        )
        input_grad, future_next, layer_grads = backward(
            upstream, back_params, kept_values, ahead_part
        )
        outgoing = input_grad.astype(jnp.bfloat16)
        grad_sums = tuple((previous + current for previous, current in zip(grad_sums, layer_grads)))
        returning_next = shifted(outgoing, "section", -1)
        return ((future_next, returning_next, grad_sums), outgoing)

    (_, _, grad_sums), grad_stack = lax.scan(
        backward_moment, (empty_state, blank_rows, zero_grads), (moments, kept_stack), reverse=True
    )
    layer_out = jnp.stack(
        [
            lax.dynamic_index_in_dim(result_stack, micro_index + section_index, 0, False)
            for micro_index in range(micro_count)
        ],
        1,
    )
    input_grads = jnp.stack(
        [
            lax.dynamic_index_in_dim(grad_stack, micro_index + section_index, 0, False)
            for micro_index in range(micro_count)
        ],
        1,
    )
    full_grads = tuple((grad_array[None] for grad_array in grad_sums))
    reduced = reduce_grads(full_grads)
    return (
        layer_out[None],
        input_grads[None],
        reduced[0],
        reduced[1],
        reduced[2],
        reduced[3],
        reduced[4],
        reduced[5],
        reduced[6],
    )


CH = 128
PAIRS = H // 2
QB = 2 * H * HEAD
STATE_ROWS = D + 16
EPS = 1e-05
TILE = 256
AXES = ("section", "dp", "seq")
MESH = pl.DeviceIdType.MESH
f32 = jnp.float32
bf16 = jnp.bfloat16
GELU_C = 0.7978845608028654
GELU_A = 0.044715
SMALL_ROWS = 128
VEC_ROWS = 72
GAIN_ROWS = 16
SHIFT1, QKV_BIAS, OUT_BIAS, SHIFT2, UP_BIAS, DOWN_BIAS = 0, 6, 24, 30, 36, 60


class Kept(NamedTuple):
    a: Any
    qkv: Any
    ph: Any
    o: Any
    inv: Any
    ob: Any
    r: Any
    n2: Any
    hid: Any
    gp: Any
    res: Any
    pre: Any


class ForwardRefs(NamedTuple):
    tokens: Any
    cot: Any
    small: Any
    wq: Any
    wo: Any
    wu: Any
    wd: Any
    gq: Any
    go: Any
    gu: Any
    gd: Any
    gv: Any
    bd: Any
    tok_out: Any
    cot_out: Any
    lay: Any


class ForwardScratch(NamedTuple):
    wq: Any
    wo: Any
    wu: Any
    wd: Any
    hq: Any
    ho: Any
    hu: Any
    hd: Any
    tok: Any
    sm: Any
    vec: Any
    maps: Any
    st: Any
    stb: Any
    got: Any
    vq: Any
    vo: Any
    vu: Any
    vd: Any
    g_send: Any
    g_recv: Any
    g_local: Any
    c_send: Any
    c_recv: Any
    s_send: Any
    s_recv: Any
    d_send: Any
    d_recv: Any
    w_sem: Any
    o_sem: Any
    m_sem: Any


class Weights(NamedTuple):
    q: Any
    o: Any
    u: Any
    d: Any = None


VMEM = pl.BlockSpec(memory_space=pltpu.VMEM)
SMEM = pl.BlockSpec(memory_space=pltpu.SMEM)
ANY = pl.BlockSpec(memory_space=pl.ANY)


def nn(a, b):
    return lax.dot_general(a, b, (((1,), (0,)), ((), ())), preferred_element_type=f32)


def nt(a, b):
    return lax.dot_general(a, b, (((1,), (1,)), ((), ())), preferred_element_type=f32)


def tn(a, b):
    return lax.dot_general(a, b, (((0,), (0,)), ((), ())), preferred_element_type=f32)


def tt(a, b):
    return lax.dot_general(a, b, (((0,), (1,)), ((), ())), preferred_element_type=f32)


def loop(count, body, events=None):
    events = events or {}

    def step(i, c):
        body(i)
        for at, event in events.items():

            @pl.when(i == at)
            def _():
                event()

        return c

    lax.fori_loop(0, count, step, 0)


def span(i, size):
    return pl.ds(pl.multiple_of(i * size, size), size)


def wide(ref, layer, row, count):
    return jnp.concatenate([ref[layer, pl.ds(row + i, 1), :] for i in range(count)], 1)


def finish(dst, sem):
    pltpu.make_async_copy(dst, dst, sem).wait()


def arrived(dst, recv):
    finish(dst, recv)


def departed(src, send):
    finish(src, send)


def shape(dims, kind):
    return jax.ShapeDtypeStruct(dims, kind)


def call(kernel, outs, scratch, specs, args, flops, out_specs=None, vmem=60, cid=None):
    if out_specs is None:
        out_specs = [VMEM] * len(outs)
    moved = sum(a.size * a.dtype.itemsize for a in args if a.ndim > 0)
    moved += sum(o.size * o.dtype.itemsize for o in outs)
    params = dict(vmem_limit_bytes=vmem * 1024 * 1024)
    if cid is not None:
        params.update(collective_id=cid, has_side_effects=True)
    return pl.pallas_call(
        kernel,
        out_shape=outs,
        in_specs=specs,
        out_specs=out_specs,
        scratch_shapes=scratch,
        compiler_params=pltpu.CompilerParams(**params),
        cost_estimate=pl.CostEstimate(flops=flops, bytes_accessed=moved, transcendentals=0),
    )(*args)


def standardize(u):
    cen = u - jnp.mean(u, -1, keepdims=True)
    rstd = lax.rsqrt(jnp.mean(cen * cen, -1, keepdims=True) + EPS)
    return cen * rstd, rstd


def lanes(rows):
    return lax.broadcasted_iota(jnp.int32, (rows, CH), 1)


def half_sums(t, low):
    s1 = jnp.sum(jnp.where(low, t, 0.0), -1, keepdims=True)
    s2 = jnp.sum(jnp.where(low, 0.0, t), -1, keepdims=True)
    return jnp.where(low, s1, s2)


def half_softmax(l, low):
    m1 = jnp.max(jnp.where(low, l, -jnp.inf), -1, keepdims=True)
    m2 = jnp.max(jnp.where(low, -jnp.inf, l), -1, keepdims=True)
    p = jnp.exp(l - jnp.where(low, m1, m2))
    return p / half_sums(p, low)


def split_states(src, dst):
    hi = src[...].astype(bf16)
    dst[0:STATE_ROWS] = hi
    dst[STATE_ROWS:] = (src[D:] - hi[D:].astype(f32)).astype(bf16)


def add_states(dst, src):
    dst[...] += src[0:STATE_ROWS].astype(f32)
    dst[D:] += src[STATE_ROWS:].astype(f32)


class Place:
    def __init__(self, n):
        self.n, self.nz, self.group = n, n // 2, n // 4
        self.x = lax.axis_index("section")
        self.d = lax.axis_index("dp")
        self.j = lax.axis_index("seq")
        self.z, self.y = lax.div(self.j, 2), lax.rem(self.j, 2)
        self.zh, self.zl = lax.div(self.z, 2), lax.rem(self.z, 2)
        self.i = lax.rem(self.z, 2) * 2 + self.y
        self.jj = lax.div(self.z, 2)
        self.r = self.x * self.group + self.jj

    def at(self, x=None, d=None, z=None, y=None, j=None):
        x = self.x if x is None else x
        d = self.d if d is None else d
        if j is None:
            j = (self.z if z is None else z) * 2 + (self.y if y is None else y)
        return (x, d, j)

    def zpos(self, o):
        return lax.rem(self.z + o + self.nz, self.nz)

    def member(self, r):
        z = lax.rem(r, self.group) * 2 + lax.rem(self.z, 2)
        return (lax.div(r, self.group), self.d, z * 2 + self.y)

    def meet(self):
        barrier = pltpu.get_barrier_semaphore()
        for dx in range(2):
            for o in range(self.n):
                if dx == 0 and o == 0:
                    continue
                other = (
                    lax.rem(self.x + dx, 2),
                    self.d,
                    lax.rem(self.j + o, self.n),
                )
                pl.semaphore_signal(barrier, inc=1, device_id=other, device_id_type=MESH)
        pl.semaphore_signal(
            barrier, inc=1, device_id=(self.x, 1 - self.d, self.j), device_id_type=MESH
        )
        pl.semaphore_wait(barrier, 2 * self.n)


def remote(src, dst, send, recv, to):
    return pltpu.make_async_remote_copy(
        src_ref=src, dst_ref=dst, send_sem=send, recv_sem=recv, device_id=to, device_id_type=MESH
    )


def hand_over(p, layer, rows, out, send, recv):
    closing = []
    for k in range(4):
        to = p.jj * 4 + k
        src = rows.at[pl.ds(k * CH, CH), :]
        dst = out.at[0, p.i, p.x]
        slot = p.i * 2 + p.x
        mine = (to == p.j) & (p.x == layer)
        copy = remote(src, dst, send.at[k], recv.at[slot], p.at(x=layer, j=to))

        @pl.when(jnp.logical_not(mine))
        def _():
            copy.start()

        @pl.when(mine)
        def _():
            pltpu.make_async_copy(src, dst, recv.at[slot]).start()

        def close(copy=copy, mine=mine):
            @pl.when(jnp.logical_not(mine))
            def _():
                copy.wait_send()

        closing.append(close)
    return closing


def handed_over(p, layer, out, recv):
    @pl.when(p.x == layer)
    def _():
        for slot in range(8):
            arrived(out.at[0, slot // 2, slot % 2], recv.at[slot])


def signal(sem, to):
    pl.semaphore_signal(sem, inc=1, device_id=to, device_id_type=MESH)


class Gather:
    def __init__(self, place, src, buf, send, recv, local, y_last, eager=False, by_rows=False):
        self.p, self.src, self.buf = place, src, buf
        self.send, self.recv, self.local = send, recv, local
        self.y_last, self.eager, self.by_rows = y_last, eager, by_rows
        self.rows, self.width = src.shape
        self.sent = ([], [], [])

    def part(self, d):
        if self.by_rows:
            return pl.ds(pl.multiple_of(d * self.rows, 16), self.rows), slice(None)
        return slice(None), pl.ds(pl.multiple_of(d * self.width, CH), self.width)

    def shard(self, x, o, y):
        return self.buf.at[x, self.p.zpos(-o), y, *self.part(self.p.d)]

    def go(self, src, dst, out, slot, to, plane):
        remote(src, dst, self.send.at[out], self.recv.at[slot], to).start()
        self.sent[plane].append(out)

    def got(self, ref, slot):
        arrived(ref, self.recv.at[slot])

    def own(self, o):
        return self.src if o == 0 else self.shard(self.p.x, o, self.p.y)

    def send_y(self, o, plane):
        p = self.p
        self.go(self.own(o), self.shard(p.x, o, p.y), 3 + o, 3 + o, p.at(y=1 - p.y), plane)

    def send_x(self, o, plane):
        p = self.p
        self.go(self.own(o), self.shard(p.x, o, p.y), 7 + o, 7 + o, p.at(x=1 - p.x), plane)

    def core(self, q, plane):
        x, y = self.kind(q)
        part = self.buf.at[x, :, y, *self.part(self.p.d)]
        self.go(part, part, 15 + q, 15 + q, self.p.at(d=1 - self.p.d), plane)

    def kind(self, q):
        p = self.p
        return (p.x if q < 2 else 1 - p.x), (p.y if q % 2 == 0 else 1 - p.y)

    def wait_all(self, q):
        x, y = self.kind(q)
        for o in range(self.p.nz):
            self.got(self.shard(x, o, y), (0, 3, 7, 11)[q] + o)

    def begin(self):
        p = self.p
        own = self.shard(p.x, 0, p.y)
        pltpu.make_async_copy(self.src, own, self.local).start()
        for o in range(1, p.nz):
            self.go(self.src, own, o - 1, o - 1, p.at(z=p.zpos(o)), 2)
        self.send_x(0, 2)
        if self.eager:
            self.send_y(0, 2)
        else:

            @pl.when(p.x == 0)
            def _():
                self.send_y(0, 0)

    def early(self):
        @pl.when(self.p.x == 1)
        def _():
            for o in range(1, self.p.nz):
                self.got(self.shard(self.p.x, o, self.p.y), o - 1)
                self.send_x(o, 1)
                if self.eager:
                    self.send_y(o, 1)

    def spread(self, layer):
        p, nz = self.p, self.p.nz

        @pl.when(p.x == layer)
        def _():
            for o in range(nz):
                if layer == 0 and o > 0:
                    self.got(self.shard(p.x, o, p.y), o - 1)
                    self.send_x(o, layer)
                if o > 0 if layer == 0 else not self.eager:
                    self.send_y(o, layer)
            finish(self.shard(p.x, 0, p.y), self.local)
            self.core(0, layer)

        @pl.when(p.x != layer)
        def _():
            if self.y_last[layer]:
                for o in range(nz):
                    here = self.shard(1 - p.x, o, p.y)
                    self.got(here, 7 + o)
                    self.go(here, here, 11 + o, 11 + o, p.at(y=1 - p.y), 1 - layer)
            else:
                self.wait_all(2)
            self.core(2, 1 - layer)

    def hop(self, layer):
        p = self.p
        if not self.y_last[layer]:

            @pl.when(p.x == layer)
            def _():
                for o in range(p.nz):
                    here = self.shard(p.x, o, 1 - p.y)
                    self.got(here, 3 + o)
                    self.go(here, here, 19 + o, 11 + o, p.at(x=1 - p.x), layer)
                self.core(1, layer)

    def last(self, layer):
        p = self.p
        if self.y_last[layer]:

            @pl.when(p.x == layer)
            def _():
                self.wait_all(1)
                self.core(1, layer)

        @pl.when(p.x != layer)
        def _():
            self.wait_all(3)
            self.core(3, 1 - layer)

    def done(self, layer):
        p = self.p
        other = self.part(1 - p.d)
        for plane in range(2):

            @pl.when(p.x == plane)
            def _():
                for q in (0, 1) if plane == layer else (2, 3):
                    x, y = self.kind(q)
                    self.got(self.buf.at[x, :, y, *other], 15 + q)

    def close(self):
        p = self.p

        def leave(slots):
            for slot in slots:
                ref = self.shard(p.x, 0, p.y)
                if 15 <= slot < 19:
                    ref = self.buf.at[p.x, :, p.y, *self.part(p.d)]
                departed(ref, self.send.at[slot])

        leave(self.sent[2])
        for plane in range(2):

            @pl.when(p.x == plane)
            def _():
                leave(self.sent[plane])


def forward_kernel(n, *refs):
    ref = ForwardRefs(*refs[:16])
    saved = [Kept(*refs[16:28]), Kept(*refs[28:40])]
    v = Kept(*refs[40:52])
    own = ForwardScratch(*refs[52:])
    p = Place(n)
    nz, group = p.nz, p.group
    t = v.a.shape[0]
    nc = t // CH
    mine = ((ref.wq, own.wq, own.hq), (ref.wo, own.wo, own.ho))
    mine += ((ref.wu, own.wu, own.hu), (ref.wd, own.wd, own.hd))
    for k, (src, wide_, _) in enumerate(mine):
        width = wide_.shape[1]
        cols = pl.ds(pl.multiple_of(p.d * width, CH), width)
        pltpu.make_async_copy(src.at[:, cols], wide_, own.w_sem.at[k]).start()
    p.meet()
    for k, (_, wide_, half) in enumerate(mine):
        finish(wide_, own.w_sem.at[k])
        half[...] = wide_[...].astype(bf16)

    def gather(k, src, buf, y_last, eager=False, by_rows=False):
        sems = (own.g_send.at[k], own.g_recv.at[k], own.g_local.at[k])
        return Gather(p, src, buf, *sems, y_last, eager, by_rows)

    gs = gather(0, ref.small, own.sm, (True, True), True, True)
    gq = gather(1, own.hq, ref.gq, (True, True), True)
    go = gather(2, own.ho, ref.go, (True, False))
    gu = gather(3, own.hu, ref.gu, (True, False))
    gd = gather(4, own.hd, ref.gd, (False, True))
    gathers = (gs, gq, go, gu, gd)

    def collect(which, s):
        i = lax.rem(p.j + s, 4)
        to = (lax.div(p.z, 2) * 2 + lax.div(i, 2)) * 2 + lax.rem(i, 2)
        slot = lax.rem(p.j, 4)
        src = (ref.cot if which else ref.tokens).at[i, p.x]
        dst = (ref.cot_out if which else own.tok).at[span(slot, CH), :]
        send, recv = own.c_send.at[which], own.c_recv.at[which]
        copy = remote(src, dst, send.at[s], recv.at[slot], p.at(j=to))

        @pl.when(to != p.j)
        def _():
            copy.start()

        @pl.when(to == p.j)
        def _():
            pltpu.make_async_copy(src, dst, recv.at[slot]).start()

        def close():
            @pl.when(to != p.j)
            def _():
                copy.wait_send()

        return close

    gs.begin()
    gq.begin()
    closing = [collect(0, s) for s in range(4)]
    for g in (go, gu, gd):
        g.begin()
    gs.early()
    gs.spread(0)
    gq.early()
    gq.spread(0)
    gs.spread(1)
    gs.last(0)
    go.early()
    go.spread(0)
    gs.last(1)
    gs.done(0)
    gs.done(1)

    vec, gv, bd, sm, maps = own.vec, ref.gv, ref.bd, own.sm, own.maps
    vec[...] = jnp.zeros(vec.shape, f32)
    gv[...] = jnp.zeros(gv.shape, f32)
    bd[...] = jnp.zeros(bd.shape, bf16)
    for layer in range(2):
        for k in range(n):
            part = sm[layer, k // 2, k % 2, 0:16, :].astype(f32)
            row, grow = (33 * k) // 4, (3 * k) // 2
            vec[layer, row : row + 9, :] += part[0:9]
            gv[layer, grow : grow + 2, :] += part[9:11]
        first = lanes(HEAD) < HEAD
        for k in range(n):
            packed = sm[layer, k // 2, k % 2, 16:112, :].astype(f32)
            turned = pltpu.roll(packed, HEAD, 1)
            middle = jnp.concatenate([packed[HEAD:], turned[: HEAD // 2]], 0)
            for i, left in enumerate((packed[:HEAD], middle, turned[HEAD // 2 :])):
                right = pltpu.roll(left, HEAD, 1)
                pair, odd = (3 * k + i) // 2, (3 * k + i) % 2
                rows = pl.ds(odd * HEAD, HEAD)
                signed = jnp.where(first, left, -right)
                bd[layer, pair, rows, odd * CH : (odd + 1) * CH] = signed.astype(bf16)
                alone = jnp.where(first, 0.0, right) if odd else jnp.where(first, left, 0.0)
                maps[layer, pair, rows, :] = alone.astype(bf16)

    for k in range(4):
        arrived(own.tok.at[pl.ds(k * CH, CH), :], own.c_recv.at[0, k])

    def load(g, dst, layer, k):
        pltpu.make_async_copy(g.buf.at[layer], dst, own.w_sem.at[k]).start()

    def loaded(dst, k):
        finish(dst, own.w_sem.at[k])

    def save(layer, *sources, part=None):
        for src in sources:
            k = [src is x for x in v].index(True)
            dst = saved[layer][k]
            if src is v.res:
                src = src.at[layer]
            if part is not None:
                cols = pl.ds(part * (FF // 2), FF // 2)
                src, dst = src.at[:, cols], dst.at[:, cols]
            pltpu.make_async_copy(src, dst, own.o_sem.at[layer, k]).start()

    def saved_all(layer, *sources):
        for src in sources:
            k = [src is x for x in v].index(True)
            finish(src.at[layer] if src is v.res else src, own.o_sem.at[layer, k])

    flat = Weights(
        own.vq.reshape(D, 3 * D),
        own.vo.reshape(D, D),
        own.vu.reshape(D, FF),
        own.vd.reshape(FF, D),
    )
    low = lanes(CH) < HEAD
    tril = lax.broadcasted_iota(jnp.int32, (CH, CH), 0) >= lanes(CH)
    eye = jnp.where(lax.broadcasted_iota(jnp.int32, (CH, CH), 0) == lanes(CH), 1.0, 0.0)
    eye = eye.astype(bf16)

    def norm_rows(layer, src, dst, which, shift):
        gain = wide(gv, layer, which * 6, 6)
        bias = wide(vec, layer, shift, 6)

        def body(i):
            xh, _ = standardize(src[span(i, CH), :].astype(f32))
            dst[span(i, CH), :] = (xh * gain + bias).astype(bf16)

        loop(nc, body)

    def bias_cols(layer, at, j):
        return wide(vec, layer, at + 2 * j, 2)

    def project(layer, u, events):
        a, qkv, ph, st = v.a, v.qkv, v.ph, own.st
        if layer == 1:
            saved_all(0, v.a, v.qkv, v.ph)
        norm_rows(layer, u, a, 0, SHIFT1)
        loaded(own.vq, 0)
        save(layer, v.a)

        def column(j):
            cols = span(j, TILE)
            qkv[:, cols] = (
                nn(a[...], flat.q[:, cols]) + bias_cols(layer, QKV_BIAS, j)
            ).astype(bf16)

        loop(3 * D // TILE, column, events[0])
        save(layer, v.qkv)

        def pair(k):
            logits = tt(maps[layer, k], qkv[:, span(k, CH)]).reshape(2, HEAD, t)
            up = jnp.exp(logits - jnp.max(logits, 1, keepdims=True))
            down = jnp.exp(jnp.min(logits, 1, keepdims=True) - logits)
            up = up * (1.0 / jnp.sum(up, 1, keepdims=True))
            down = down * (1.0 / jnp.sum(down, 1, keepdims=True))
            both = jnp.concatenate([up, down], 1).reshape(2 * CH, t).astype(bf16)
            for c in range(nc):
                ph[pl.ds(c * CH, CH), span(k, 2 * CH)] = nt(
                    eye, both[:, c * CH : (c + 1) * CH]
                ).astype(bf16)

        loop(PAIRS, lambda k: pair(k + PAIRS), events[1])

        def state(k):
            val = qkv[:, pl.ds(pl.multiple_of(2 * D + k * CH, CH), CH)]
            for hh in range(2):
                key = ph[:, pl.ds(pl.multiple_of((H + 2 * k + hh) * CH, CH), CH)]
                full = tn(val, key)
                st[layer, span(2 * k + hh, HEAD), :] = full[hh * HEAD : (hh + 1) * HEAD]
                st[layer, pl.ds(D + 2 * k + hh, 1), :] = jnp.sum(
                    key.astype(f32), 0, keepdims=True
                )

        loop(PAIRS, state)
        st[layer, D + H :, :] = jnp.zeros((STATE_ROWS - D - H, CH), f32)
        split_states(st.at[layer], own.stb.at[layer])
        send_states(layer, st, 1)
        loop(PAIRS, pair, events[2])
        save(layer, v.ph)

    members = 2 * group

    def send_states(layer, st, sign):
        for o in range(1, members):
            ok = (p.r + o < members) if sign > 0 else (p.r - o >= 0)

            @pl.when(ok)
            def _():
                remote(
                    own.stb.at[layer],
                    own.got.at[layer, o - 1],
                    own.s_send.at[layer, o - 1],
                    own.s_recv.at[layer, o - 1],
                    p.member(p.r + sign * o),
                ).start()

    def take_states(layer, sign):
        pre = v.pre
        pre[...] = jnp.zeros(pre.shape, f32)
        for o in range(1, members):
            ok = (p.r - o >= 0) if sign > 0 else (p.r + o < members)

            @pl.when(ok)
            def _():
                arrived(own.got.at[layer, o - 1], own.s_recv.at[layer, o - 1])
                add_states(pre, own.got.at[layer, o - 1])

    def close_states(layer, sign):
        for o in range(1, members):
            ok = (p.r + o < members) if sign > 0 else (p.r - o >= 0)

            @pl.when(ok)
            def _():
                departed(own.stb.at[layer], own.s_send.at[layer, o - 1])

    def mix(layer, u, events):
        qkv, ph, o_, inv, ob = v.qkv, v.ph, v.o, v.inv, v.ob
        r, n2, hid, gp = v.r, v.n2, v.hid, v.gp
        res = v.res.at[layer]
        if layer == 1:
            saved_all(0, v.pre, v.o, v.inv, v.ob, v.r, v.n2, v.hid, v.gp)
        take_states(layer, 1)
        if layer == 1:
            closing.extend([collect(1, s) for s in range(4)])
            closing.extend(hand_over(p, 0, v.res.at[0], ref.lay, own.d_send, own.d_recv))
        save(layer, v.pre)
        s0 = v.pre

        def pair(k):
            cols = span(k, CH)
            s = s0[cols, :]
            tot = [s0[pl.ds(D + 2 * k + hh, 1), :] for hh in range(2)]
            for c in range(nc):
                rows = pl.ds(c * CH, CH)
                val = qkv[rows, pl.ds(pl.multiple_of(2 * D + k * CH, CH), CH)]
                sl = s.astype(bf16)
                sf = (s - sl.astype(f32)).astype(bf16)
                done = []
                new = []
                for hh in range(2):
                    qh = ph[rows, span(2 * k + hh, CH)]
                    kh = ph[rows, pl.ds(pl.multiple_of((H + 2 * k + hh) * CH, CH), CH)]
                    score = jnp.where(tril, nt(qh, kh), 0.0)
                    hi = score.astype(bf16)
                    lo = (score - hi.astype(f32)).astype(bf16)
                    num = nn(hi, val) + nn(lo, val) + nt(qh, sl) + nt(qh, sf)
                    den = jnp.sum(score + qh.astype(f32) * tot[hh], -1, keepdims=True)
                    rec = 1.0 / den
                    done.append((num * rec, rec))
                    new.append(tn(val, kh)[hh * HEAD : (hh + 1) * HEAD])
                    tot[hh] = tot[hh] + jnp.sum(kh.astype(f32), 0, keepdims=True)
                s = s + jnp.concatenate(new, 0)
                both = jnp.where(low, done[0][0], done[1][0])
                o_[rows, cols] = both
                ob[rows, cols] = both.astype(bf16)
                inv[rows, cols] = jnp.where(low, done[0][1], done[1][1])

        loop(PAIRS, pair, events[0])
        save(layer, v.o, v.inv, v.ob)
        events[1]()
        loaded(own.vo, 1)

        def out_col(j):
            cols = span(j, TILE)
            r[:, cols] = (
                u[:, cols].astype(f32)
                + nn(ob[...], flat.o[:, cols])
                + bias_cols(layer, OUT_BIAS, j)
            )

        loop(D // TILE, out_col)
        norm_rows(layer, r, n2, 1, SHIFT2)
        save(layer, v.r, v.n2)
        events[2]()
        loaded(own.vu, 2)

        def up_col(j):
            cols = span(j, TILE)
            zt = nn(n2[...], flat.u[:, cols]) + bias_cols(layer, UP_BIAS, j)
            z2 = zt * zt
            half = 0.5 + 0.5 * jnp.tanh(zt * (GELU_C + (GELU_C * GELU_A) * z2))
            act = zt * half
            hid[:, cols] = act.astype(bf16)
            slope = 2.0 * GELU_C + (6.0 * GELU_C * GELU_A) * z2
            gp[:, cols] = (half + act * ((1.0 - half) * slope)).astype(bf16)

        halfway = FF // TILE // 2 - 1
        loop(FF // TILE, up_col, {halfway: lambda: save(layer, v.hid, v.gp, part=0), **events[3]})
        save(layer, v.hid, v.gp, part=1)
        events[4]()
        loaded(own.vd, 3)

        def down_col(j):
            cols = span(j, TILE)
            res[:, cols] = (
                r[:, cols] + nn(hid[...], flat.d[:, cols]) + bias_cols(layer, DOWN_BIAS, j)
            ).astype(bf16)

        loop(D // TILE, down_col)
        save(layer, v.res)

    def run(*steps):
        def go_():
            for step in steps:
                step()

        return go_

    nothing = run()
    gu.early()
    go.spread(1)
    gu.spread(0)
    gq.last(0)
    gu.spread(1)
    gq.done(0)
    load(gq, own.vq, 0, 0)
    tok_out = pltpu.make_async_copy(own.tok, ref.tok_out, own.m_sem)
    tok_out.start()
    project(0, own.tok, [{}, {}, {}])
    gd.early()
    gd.spread(0)
    gq.spread(1)
    gd.spread(1)
    go.last(0)
    go.hop(1)
    mix(
        0,
        own.tok,
        [
            {
                1: run(
                    functools.partial(go.done, 0),
                    functools.partial(load, go, own.vo, 0, 1),
                    functools.partial(gd.hop, 0),
                ),
                3: run(
                    functools.partial(gu.last, 0),
                    functools.partial(gu.done, 0),
                    functools.partial(load, gu, own.vu, 0, 2),
                ),
            },
            functools.partial(gu.hop, 1),
            nothing,
            {},
            run(
                functools.partial(gq.last, 1),
                functools.partial(gq.done, 1),
                functools.partial(load, gq, own.vq, 1, 0),
                functools.partial(gd.last, 0),
                functools.partial(gd.done, 0),
                functools.partial(load, gd, own.vd, 0, 3),
            ),
        ],
    )
    project(1, v.res.at[0], [{}, {}, {}])
    mix(
        1,
        v.res.at[0],
        [
            {
                2: run(
                    functools.partial(go.last, 1),
                    functools.partial(go.done, 1),
                    functools.partial(load, go, own.vo, 1, 1),
                ),
                4: run(
                    functools.partial(gu.last, 1),
                    functools.partial(gu.done, 1),
                    functools.partial(load, gu, own.vu, 1, 2),
                ),
            },
            nothing,
            nothing,
            {
                1: run(
                    functools.partial(gd.last, 1),
                    functools.partial(gd.done, 1),
                    functools.partial(load, gd, own.vd, 1, 3),
                )
            },
            nothing,
        ],
    )

    for g in gathers:
        g.close()
    for close in closing:
        close()
    for k in range(4):
        arrived(ref.cot_out.at[pl.ds(k * CH, CH), :], own.c_recv.at[1, k])
    for layer in range(2):
        close_states(layer, 1)

    tok_out.wait()
    handed_over(p, 0, ref.lay, own.d_recv)
    saved_all(0, v.res)
    saved_all(1, *v)


def forward_pass(n, tokens, cotangent, small, wq, wo, wu, wd):
    t = 4 * CH
    nz = n // 2
    full = [
        shape((2, nz, 2) + w.shape, bf16) for w in (wq, wo, wu, wd)
    ]
    kept = [
        shape((t, D), bf16),
        shape((t, 3 * D), bf16),
        shape((t, 2 * QB), bf16),
        shape((t, D), f32),
        shape((t, D), f32),
        shape((t, D), bf16),
        shape((t, D), f32),
        shape((t, D), bf16),
        shape((t, FF), bf16),
        shape((t, FF), bf16),
        shape((t, D), bf16),
        shape((STATE_ROWS, CH), f32),
    ]
    outs = full + [shape((2, GAIN_ROWS, CH), f32), shape((2, 2 * PAIRS, CH, 2 * CH), bf16)]
    outs += [shape((t, D), bf16)] * 2 + [shape((1, 4, 2, CH, D), bf16)] + kept * 2
    specs = [ANY] * 4 + [VMEM] * 2 + [ANY] * (len(outs) - 6)
    scratch = [pltpu.VMEM(k.shape, k.dtype) for k in kept]
    scratch[10] = pltpu.VMEM((2, t, D), bf16)
    halves = [(w.shape[0], w.shape[1] // 2) for w in (wq, wo, wu, wd)]
    scratch += [pltpu.VMEM(half, f32) for half in halves]
    scratch += [pltpu.VMEM(half, bf16) for half in halves]
    scratch += [
        pltpu.VMEM((t, D), bf16),
        pltpu.VMEM((2, nz, 2, SMALL_ROWS, CH), bf16),
        pltpu.VMEM((2, VEC_ROWS, CH), f32),
        pltpu.VMEM((2, 2 * PAIRS, CH, CH), bf16),
        pltpu.VMEM((2, STATE_ROWS, CH), f32),
        pltpu.VMEM((2, STATE_ROWS + 16, CH), bf16),
        pltpu.VMEM((2, n // 2 - 1, STATE_ROWS + 16, CH), bf16),
    ]
    scratch += [pltpu.VMEM(w.shape[1:], bf16) for w in full]
    dma = pltpu.SemaphoreType.DMA
    scratch += [dma((5, 23)), dma((5, 19)), dma((5,)), dma((2, 4)), dma((2, 4))]
    scratch += [dma((2, n // 2 - 1)), dma((2, n // 2 - 1)), dma((4,)), dma((8,)), dma((4,))]
    scratch += [dma((2, 12)), dma]
    got = call(
        functools.partial(forward_kernel, n),
        outs,
        scratch,
        [ANY] * 7,
        [tokens, cotangent, small, wq, wo, wu, wd],
        4 * t * D * (4 * D + 2 * FF),
        specs,
        cid=0,
    )
    layers = [Kept(*got[9:21]), Kept(*got[21:33])]
    return got[:4], got[4], got[5], got[6], got[7], got[8], layers


def with_error(gv, swapped, lane, hh):
    first = HEAD * (1 - hh)
    hi = swapped.astype(bf16)
    lo = (swapped - hi.astype(f32)).astype(bf16)
    own = (lane < HEAD) if hh == 0 else (lane >= HEAD)
    spare = jnp.where(
        lane == first + 1,
        lo,
        jnp.where((lane == first) | (lane == first + 2), hi, jnp.zeros_like(gv)),
    )
    return jnp.where(own, gv, spare)


def with_ones(v, lane, hh):
    first = HEAD * (1 - hh)
    own = (lane < HEAD) if hh == 0 else (lane >= HEAD)
    spare = jnp.where((lane == first) | (lane == first + 1), jnp.ones_like(v), jnp.zeros_like(v))
    return jnp.where(own, v, spare)


def with_totals(s, tot, row, hh, again):
    first = HEAD * (1 - hh)
    hi = tot.astype(bf16).astype(f32)
    lo = tot - hi
    own = (row < HEAD) if hh == 0 else (row >= HEAD)
    if again:
        spare = jnp.where(
            (row == first) | (row == first + 1), hi, jnp.where(row == first + 2, lo, 0.0)
        )
    else:
        spare = jnp.where(row == first, hi, jnp.where(row == first + 1, lo, 0.0))
    return jnp.where(own, s, spare).astype(bf16)


def put_rows(ref, layer, row, val):
    for i in range(val.shape[1] // CH):
        ref[layer, pl.ds(row + i, 1), :] = val[:, i * CH : (i + 1) * CH]


class Reduce:
    def __init__(self, place, layer, buf, land, out, fin, sems, credit):
        self.p, self.layer, self.buf, self.fin = place, layer, buf, fin
        self.land_y, self.land_z, self.land_x, self.stage = land
        self.own, self.other = out
        self.send, self.recv, self.last = sems
        self.credit_y, self.credit_a, self.credit_b = credit

    def go(self, src, dst, slot, to):
        remote(src, dst, self.send.at[slot], self.recv.at[slot], to).start()

    def send_y(self):
        p = self.p
        if self.layer == 0:
            pl.semaphore_wait(self.credit_y, 1)
        self.go(self.buf.at[:, 1 - p.y], self.land_y, 0, p.at(y=1 - p.y))

    def add(self, zi, more):
        kept = self.buf.at[zi, self.p.y]
        kept[...] = (kept[...].astype(f32) + more.astype(f32)).astype(bf16)

    def step_y(self):
        p = self.p
        near = p.z + 1 - 2 * p.zl
        arrived(self.land_y, self.recv.at[0])
        if self.layer == 0:
            pl.semaphore_wait(self.credit_a, 1)
        for h in range(2):
            zi = 2 * h + 1 - p.zl
            self.add(zi, self.land_y[zi])
            self.go(self.buf.at[zi, p.y], self.land_z.at[h], 1 + h, p.at(z=near))
        for h in range(2):
            zi = 2 * h + p.zl
            self.add(zi, self.land_y[zi])
        if self.layer == 1:
            signal(self.credit_y, p.at(y=1 - p.y))

    def step_a(self):
        p = self.p
        near = p.z + 1 - 2 * p.zl
        far = p.z + 2 - 4 * p.zh
        if self.layer == 0:
            pl.semaphore_wait(self.credit_b, 1)
        for h in range(2):
            arrived(self.land_z.at[h], self.recv.at[1 + h])
        away = 2 * (1 - p.zh) + p.zl
        self.add(away, self.land_z[1 - p.zh])
        self.go(self.buf.at[away, p.y], self.land_z.at[2], 3, p.at(z=far))
        self.add(p.z, self.land_z[p.zh])
        if self.layer == 1:
            signal(self.credit_a, p.at(z=near))

    def step_z(self):
        p = self.p
        arrived(self.land_z.at[2], self.recv.at[3])
        total = self.buf[p.z, p.y].astype(f32) + self.land_z[2].astype(f32)
        if self.layer == 1:
            signal(self.credit_b, p.at(z=p.z + 2 - 4 * p.zh))

        @pl.when(p.x == self.layer)
        def _():
            self.fin[...] = total

        @pl.when(p.x != self.layer)
        def _():
            self.stage[...] = total.astype(bf16)
            self.go(self.stage, self.land_x, 4, p.at(x=1 - p.x))

    def step_x(self):
        p = self.p

        @pl.when(p.x == self.layer)
        def _():
            arrived(self.land_x, self.recv.at[4])
            self.fin[...] += self.land_x[...].astype(f32)
            self.go(self.fin, self.own, 5, p.at(d=1 - p.d))
            pltpu.make_async_copy(self.fin, self.own, self.last).start()

    def close(self):
        p = self.p
        departed(self.buf.at[:, 0], self.send.at[0])
        for i in range(1, p.nz):
            departed(self.buf.at[0, 0], self.send.at[i])

    def end(self):
        @pl.when(self.p.x == self.layer)
        def _():
            departed(self.fin, self.send.at[5])
            arrived(self.other, self.recv.at[5])
            finish(self.fin, self.last)

        @pl.when(self.p.x != self.layer)
        def _():
            departed(self.stage, self.send.at[4])


SMALL_OUT = 128
Q, O, U, DN, SM = range(5)
PARTS = (
    (Q, 0, 96, 0, 384),
    (Q, 0, 96, 384, 384),
    (Q, 0, 96, 768, 384),
    (O, 0, 96, 0, 384),
    (U, 0, 96, 0, 768),
    (U, 0, 96, 768, 768),
    (DN, 0, 192, 0, 384),
    (DN, 192, 192, 0, 384),
    (SM, 0, 64, 0, CH),
)


class Loaded(NamedTuple):
    gp: Any
    r: Any
    o: Any
    inv: Any
    ph: Any
    qkv: Any
    n2: Any
    ob: Any
    a: Any
    u: Any
    pre: Any


class BackwardRefs(NamedTuple):
    cot: Any
    res1: Any
    gv: Any
    bd: Any
    wq: Any
    wo: Any
    wu: Any
    wd: Any


class BackwardScratch(NamedTuple):
    g: Any
    drb: Any
    gs: Any
    tmp: Any
    acc: Any
    st: Any
    stb: Any
    later: Any
    got: Any
    mg: Any
    vr: Any
    gr: Any
    hidr: Any
    wdr: Any
    vq: Any
    vo: Any
    vu: Any
    bq: Any
    bo: Any
    bu: Any
    bd_: Any
    bs: Any
    yq: Any
    yo: Any
    yu: Any
    yd: Any
    ys: Any
    zq: Any
    zo: Any
    zu: Any
    zd: Any
    zs: Any
    xq: Any
    xo: Any
    xu: Any
    xd: Any
    xs: Any
    wq: Any
    wo: Any
    wu: Any
    wd: Any
    ws: Any
    fq: Any
    fo: Any
    fu: Any
    fd: Any
    fs: Any
    tmp96: Any
    tmpd: Any
    sb: Any
    sd: Any
    r_send: Any
    r_recv: Any
    r_last: Any
    credit_y: Any
    credit_a: Any
    credit_b: Any
    m_send: Any
    m_recv: Any
    s_send: Any
    s_recv: Any
    d_send: Any
    d_recv: Any
    w_sem: Any
    l_sem: Any
    h_sem: Any
    t_sem: Any
    k_sem: Any


def backward_kernel(n, *refs):
    ref = BackwardRefs(*refs[:8])
    source = [Loaded(*refs[8:19]), Loaded(*refs[19:30])]
    hidden = refs[30:32]
    lay, gin, small_out = refs[32], refs[33], refs[38]
    wgrads = refs[34:38]
    lands = refs[39:47]
    v = Loaded(*refs[47:58])
    own = BackwardScratch(*refs[58:])
    p = Place(n)
    nz, group = p.nz, p.group
    t = own.drb.shape[0]
    nc = t // CH
    members = 2 * group
    gains, gbuf, tmp, acc = ref.gv, own.g, own.tmp, own.acc
    vr, gr, mg = own.vr, own.gr, own.mg
    flat = Weights(own.vq.reshape(D, 3 * D), own.vo.reshape(D, D), own.vu.reshape(D, FF))
    stored = (own.vq, own.vo, own.vu)
    lane_t = lanes(t)
    lane = lanes(CH)
    low = lane < HEAD
    row = lax.broadcasted_iota(jnp.int32, (CH, CH), 0)
    tril, triu = row >= lane, row <= lane

    def load(layer, *wanted):
        for dst in wanted:
            k = [dst is x for x in v].index(True)
            pltpu.make_async_copy(source[layer][k], dst, own.l_sem.at[k]).start()

    def loaded(*wanted):
        for dst in wanted:
            k = [dst is x for x in v].index(True)
            finish(dst, own.l_sem.at[k])

    def load_w(layer, k):
        w = (ref.wq, ref.wo, ref.wu)[k]
        pltpu.make_async_copy(w.at[layer], stored[k], own.w_sem.at[k]).start()

    def loaded_w(k):
        finish(stored[k], own.w_sem.at[k])

    def load_wd(layer, k):
        pltpu.make_async_copy(
            ref.wd.at[layer, k // 2, k % 2], own.wdr.at[k % 3], own.k_sem.at[k % 3]
        ).start()

    pltpu.make_async_copy(ref.cot, gbuf.at[0], own.t_sem.at[4]).start()
    for k in range(3):
        load_wd(1, k)
    load(1, v.gp)
    load_w(1, U)
    load(1, v.r, v.o, v.inv, v.ph)
    load_w(1, O)
    load_w(1, Q)
    load(1, v.qkv, v.n2, v.ob, v.a, v.u, v.pre)
    p.meet()
    finish(gbuf.at[0], own.t_sem.at[4])

    width = (3 * D // 2, D // 2, FF // 2, D // 2)
    bufs = (own.bq, own.bo, own.bu, own.bd_, own.bs)
    spots = (
        (own.yq, own.yo, own.yu, own.yd, own.ys),
        (own.zq, own.zo, own.zu, own.zd, own.zs),
        (own.xq, own.xo, own.xu, own.xd, own.xs),
        (own.wq, own.wo, own.wu, own.wd, own.ws),
    )
    fins = (own.fq, own.fo, own.fu, own.fd, own.fs)
    reduces = []
    for layer in range(2):
        line = [[] for _ in range(5)]
        for k, (m, r0_, r_, c0_, c_) in enumerate(PARTS):
            rows, cols = pl.ds(r0_, r_), pl.ds(c0_, c_)
            out = []
            for side in (p.d, 1 - p.d):
                if m == SM:
                    out.append(small_out.at[pl.ds(pl.multiple_of(side * r_, r_), r_), :])
                else:
                    at = pl.ds(pl.multiple_of(side * width[m] + c0_, CH), c_)
                    out.append(wgrads[m].at[rows, at])
            line[m].append(
                Reduce(
                    p,
                    layer,
                    bufs[m].at[:, :, rows, cols],
                    (
                        spots[0][m].at[:, rows, cols],
                        spots[1][m].at[:, rows, cols],
                        spots[2][m].at[rows, cols],
                        spots[3][m].at[rows, cols],
                    ),
                    out,
                    fins[m].at[rows, cols],
                    (own.r_send.at[layer, k], own.r_recv.at[layer, k], own.r_last.at[layer, k]),
                    (own.credit_y.at[k], own.credit_a.at[k], own.credit_b.at[k]),
                )
            )
        reduces.append(line)

    def step(name, layer, *which):
        def all_():
            for m in which:
                for part in reduces[layer][m]:
                    name(part)

        return all_

    step_y = functools.partial(step, Reduce.step_y)
    step_a = functools.partial(step, Reduce.step_a)
    step_z = functools.partial(step, Reduce.step_z)
    step_x = functools.partial(step, Reduce.step_x)

    def states_ok(o, taking):
        return (p.r + o < members) if taking else (p.r - o >= 0)

    def send_states(layer):
        for o in range(1, members):
            @pl.when(states_ok(o, False))
            def _():
                remote(
                    own.stb.at[layer],
                    own.got.at[layer, o - 1],
                    own.s_send.at[layer, o - 1],
                    own.s_recv.at[layer, o - 1],
                    p.member(p.r - o),
                ).start()

    def take_states(layer):
        later = own.later
        later[...] = jnp.zeros(later.shape, f32)
        for o in range(1, members):

            @pl.when(states_ok(o, True))
            def _():
                arrived(own.got.at[layer, o - 1], own.s_recv.at[layer, o - 1])
                add_states(later, own.got.at[layer, o - 1])

        return later

    def close_states(layer):
        for o in range(1, members):

            @pl.when(states_ok(o, False))
            def _():
                departed(own.stb.at[layer], own.s_send.at[layer, o - 1])

    def norm_back(x_ref, which, layer, body):
        gain = wide(gains, layer, which * 6, 6)
        acc[...] = jnp.zeros(acc.shape, f32)

        def step(i):
            rows = span(i, CH)
            xh, rstd = standardize(x_ref[rows, :].astype(f32))
            dn = tmp[rows, :]
            acc[0:1, :] += jnp.sum(dn, 0, keepdims=True)
            acc[1:2, :] += jnp.sum(dn * xh, 0, keepdims=True)
            dx = dn * gain
            body(
                rows,
                rstd
                * (dx - jnp.mean(dx, -1, keepdims=True) - xh * jnp.mean(dx * xh, -1, keepdims=True)),
            )

        loop(nc, step)
        put_rows(vr, layer, SHIFT2 if which else SHIFT1, acc[0:1, :])
        put_rows(gr, layer, which * 6, acc[1:2, :])

    def mlp_back(layer, g, events, hooks):
        gp, r, o_, inv, ph = v.gp, v.r, v.o, v.inv, v.ph
        drb, gs, st = own.drb, own.gs, own.st
        loaded(v.gp)
        for k in range(2 * nz):
            finish(own.wdr.at[k % 3], own.k_sem.at[k % 3])
            cols = pl.ds(k * FF // n, FF // n)
            part = (nt(g[...], own.wdr[k % 3]) * gp[:, cols]).astype(bf16)
            gp[:, cols] = part
            put_rows(
                vr, layer, UP_BIAS + 3 * k, jnp.sum(part.astype(f32), 0, keepdims=True)
            )
            if k + 3 < 2 * nz:
                load_wd(layer, k + 3)
            if k in events:
                events[k]()
        hooks[0]()
        loaded_w(U)

        def n2_col(j):
            cols = span(j, TILE)
            tmp[:, cols] = nt(gp[...], flat.u[cols, :])

        loop(D // TILE, n2_col)
        hooks[1]()
        loaded(v.r)

        def body(rows, back):
            up = g[rows, :].astype(f32)
            total = up + back
            acc[2:3, :] += jnp.sum(up, 0, keepdims=True)
            acc[3:4, :] += jnp.sum(total, 0, keepdims=True)
            r[rows, :] = total
            drb[rows, :] = total.astype(bf16)

        norm_back(r, 1, layer, body)
        put_rows(vr, layer, DOWN_BIAS, acc[2:3, :])
        put_rows(vr, layer, OUT_BIAS, acc[3:4, :])
        hooks[2]()
        loaded_w(O)
        loaded(v.inv, v.o, v.ph)

        def do_col(j):
            cols = span(j, TILE)
            gs[:, cols] = (nt(drb[...], flat.o[cols, :]) * inv[:, cols]).astype(bf16)

        loop(D // TILE, do_col)
        low_t = lane_t < HEAD

        def pair(k):
            cols = span(k, CH)
            gv = gs[:, cols]
            prod = gv.astype(f32) * o_[:, cols]
            e0 = -jnp.sum(jnp.where(low_t, prod, 0.0), -1, keepdims=True)
            e1 = -jnp.sum(jnp.where(low_t, 0.0, prod), -1, keepdims=True)
            swapped = jnp.where(low_t, e1, e0)
            inv[:, cols] = swapped
            for hh in range(2):
                ge = with_error(gv, swapped, lane_t, hh)
                full = tn(ge, ph[:, span(2 * k + hh, CH)])
                st[layer, span(2 * k + hh, HEAD), :] = full[hh * HEAD : (hh + 1) * HEAD]
                at = HEAD * (1 - hh)
                st[layer, pl.ds(D + 2 * k + hh, 1), :] = full[at : at + 1] + full[at + 1 : at + 2]

        loop(PAIRS, pair)
        st[layer, D + H :, :] = jnp.zeros((STATE_ROWS - D - H, CH), f32)
        split_states(st.at[layer], own.stb.at[layer])
        send_states(layer)

    def weight_grad(layer, m, keep):
        parts = reduces[layer][m]
        buf, c = bufs[m], width[m]
        r = buf.shape[2]
        land_d = lands[layer * 4 + m]
        send, recv = own.m_send.at[layer, m], own.m_recv.at[layer, m]
        base = (p.d if keep else 1 - p.d) * c
        if keep:
            departed(buf, send)
            arrived(land_d, recv)
        elif layer == 0:
            for part in reduces[1][m]:
                part.close()
        if m == DN:
            rhs = gbuf[1 - layer, :, pl.ds(pl.multiple_of(base, CH), c)]

            def fetch(k):
                pltpu.make_async_copy(
                    hidden[layer].at[:, pl.ds(k * FF // n, FF // n)],
                    own.hidr.at[k % 3],
                    own.h_sem.at[k % 3],
                ).start()
                if keep:
                    pltpu.make_async_copy(
                        land_d.at[k // 2, k % 2], own.tmpd.at[k % 3], own.t_sem.at[k % 3]
                    ).start()

            for k in range(3):
                fetch(k)
            for k in range(2 * nz):
                finish(own.hidr.at[k % 3], own.h_sem.at[k % 3])
                val = tn(own.hidr[k % 3], rhs)
                if keep:
                    finish(own.tmpd.at[k % 3], own.t_sem.at[k % 3])
                    val = val + own.tmpd[k % 3].astype(f32)
                buf[k // 2, k % 2] = val.astype(bf16)
                if k + 3 < 2 * nz:
                    fetch(k + 3)
        else:
            lhs = (v.a, v.ob, v.n2)[m]
            rhs = (v.qkv, own.drb, v.gp)[m]
            wide_ = 384
            count = c // wide_

            def fetch(k):
                pltpu.make_async_copy(
                    land_d.at[:, :, :, pl.ds(k * wide_, wide_)],
                    own.tmp96.at[k % 2],
                    own.t_sem.at[k % 2],
                ).start()

            if keep:
                for k in range(min(2, count)):
                    fetch(k)
            for k in range(count):
                val = tn(lhs[...], rhs[:, pl.ds(pl.multiple_of(base + k * wide_, CH), wide_)])
                if keep:
                    finish(own.tmp96.at[k % 2], own.t_sem.at[k % 2])
                for zi in range(nz):
                    for yi in range(2):
                        at = (zi * 2 + yi) * r
                        part = val[at : at + r]
                        if keep:
                            part = part + own.tmp96[k % 2, zi, yi].astype(f32)
                        buf[zi, yi, :, pl.ds(k * wide_, wide_)] = part.astype(bf16)
                if keep and k + 2 < count:
                    fetch(k + 2)
                each = count // len(parts)
                if keep and (k + 1) % each == 0:
                    parts[k // each].send_y()
        if keep and m == DN:
            for part in parts:
                part.send_y()
        if not keep:
            remote(buf, land_d, send, recv, p.at(d=1 - p.d)).start()

    def mix_back(layer, events):
        qkv, ph, gs, es = v.qkv, v.ph, own.gs, v.inv
        bd = ref.bd.at[layer]
        s1 = take_states(layer)
        loaded(v.qkv, v.pre)
        s0 = v.pre

        def pair(k):
            cols = span(k, CH)
            vcols = pl.ds(pl.multiple_of(2 * D + k * CH, CH), CH)
            kcols = pl.ds(pl.multiple_of(D + k * CH, CH), CH)

            def keys(rows, hh):
                return ph[rows, pl.ds(pl.multiple_of((H + 2 * k + hh) * CH, CH), CH)]

            before, finer = [], []
            s = s0[cols, :]
            tot = [s0[pl.ds(D + 2 * k + hh, 1), :] for hh in range(2)]
            for c in range(nc):
                rows = pl.ds(c * CH, CH)
                fine = (s - s.astype(bf16).astype(f32)).astype(bf16)
                none = jnp.zeros_like(fine)
                before.append([with_totals(s, tot[hh], row, hh, True) for hh in range(2)])
                finer.append([jnp.where(row < HEAD, fine, none), jnp.where(row < HEAD, none, fine)])
                if c < nc - 1:
                    val = qkv[rows, vcols]
                    new = []
                    for hh in range(2):
                        kh = keys(rows, hh)
                        new.append(tn(val, kh)[hh * HEAD : (hh + 1) * HEAD])
                        tot[hh] = tot[hh] + jnp.sum(kh.astype(f32), 0, keepdims=True)
                    s = s + jnp.concatenate(new, 0)
            ds = s1[cols, :]
            dtot = [s1[pl.ds(D + 2 * k + hh, 1), :] for hh in range(2)]
            acc_q = jnp.zeros((CH, 2 * CH), f32)
            acc_k = jnp.zeros((CH, 2 * CH), f32)
            sums = [jnp.zeros((1, CH), f32) for _ in range(3)]
            for c in reversed(range(nc)):
                rows = pl.ds(c * CH, CH)
                val = qkv[rows, vcols]
                gv = gs[rows, cols]
                ev = es[rows, cols]
                dsl = ds.astype(bf16)
                dl_q, dl_k, dv, new = [], [], [], []
                for hh in range(2):
                    qh = ph[rows, span(2 * k + hh, CH)]
                    kh = keys(rows, hh)
                    ge = with_error(gv, ev, lane, hh)
                    v1 = with_ones(val, lane, hh)
                    after = with_totals(ds, dtot[hh], row, hh, False)
                    da = jnp.where(tril, nt(ge, v1), 0.0).astype(bf16)
                    dat = jnp.where(triu, nt(v1, ge), 0.0).astype(bf16)
                    at = jnp.where(triu, nt(kh, qh), 0.0).astype(bf16)
                    dq = nn(da, kh) + nn(ge, before[c][hh]) + nn(ge, finer[c][hh])
                    dk = nn(dat, qh) + nn(v1, after)
                    dv.append(nn(at, gv) + nt(kh, dsl))
                    for p_, d_, to in ((qh, dq, dl_q), (kh, dk, dl_k)):
                        pf = p_.astype(f32)
                        to.append((pf * (d_ - half_sums(pf * d_, low))).astype(bf16))
                    full = tn(ge, qh)
                    new.append(full[hh * HEAD : (hh + 1) * HEAD])
                    first = HEAD * (1 - hh)
                    dtot[hh] = dtot[hh] + full[first : first + 1] + full[first + 1 : first + 2]
                ds = ds + jnp.concatenate(new, 0)
                dl_q = jnp.concatenate(dl_q, 1)
                dl_k = jnp.concatenate(dl_k, 1)
                acc_q = acc_q + tn(qkv[rows, cols], dl_q)
                acc_k = acc_k + tn(qkv[rows, kcols], dl_k)
                parts = (
                    (cols, nt(dl_q, bd[k])),
                    (kcols, nt(dl_k, bd[PAIRS + k])),
                    (vcols, jnp.where(low, dv[0], dv[1])),
                )
                for i, (where, new_) in enumerate(parts):
                    new_ = new_.astype(bf16)
                    qkv[rows, where] = new_
                    sums[i] = sums[i] + jnp.sum(new_.astype(f32), 0, keepdims=True)
            for i in range(3):
                vr[layer, pl.ds(QKV_BIAS + i * PAIRS + k, 1), :] = sums[i]
            for which, total in enumerate((acc_q, acc_k)):
                for hh in range(2):
                    blk = total[hh * HEAD : (hh + 1) * HEAD, hh * CH : (hh + 1) * CH]
                    mg[which * H + 2 * k + hh] = blk - pltpu.roll(blk, HEAD, 1)

        loop(PAIRS, pair, events)

    def input_back(layer):
        loaded_w(Q)

        def n1_col(j):
            cols = span(j, TILE)
            tmp[:, cols] = nt(v.qkv[...], flat.q[cols, :])

        loop(D // TILE, n1_col)
        loaded(v.u)
        du = gbuf.at[layer]

        def body(rows, back):
            du[rows, :] = (v.r[rows, :] + back).astype(bf16)

        norm_back(v.u, 0, layer, body)

    closing = []

    def deliver(which, layer, rows):
        sems = own.d_send.at[which, layer], own.d_recv.at[which]
        closing.extend(hand_over(p, layer, rows, gin if which else lay, *sems))

    def small_rows(side):
        return pl.ds(pl.multiple_of(side * 64, 64), 64)

    def pack_small(layer):
        sb = own.sb
        for k in range(n):
            at, gat = (33 * k) // 4, (3 * k) // 2
            zi, yi = k // 2, k % 2
            sb[zi, yi, 0:9] = vr[layer, at : at + 9, :]
            sb[zi, yi, 9:11] = gr[layer, gat : gat + 2, :]
            sb[zi, yi, 11:16] = jnp.zeros((5, CH), f32)
            h0, h1, h2 = (mg[3 * k + i] for i in range(3))
            left = jnp.concatenate([h0, h1[: HEAD // 2]], 0)
            right = jnp.concatenate([h1[HEAD // 2 :], h2], 0)
            sb[zi, yi, 16:112] = jnp.where(lanes(96) < HEAD, left, -right)
            sb[zi, yi, 112:] = jnp.zeros((16, CH), f32)
        remote(
            sb.at[:, :, small_rows(1 - p.d), :],
            own.sd.at[layer],
            own.m_send.at[layer, SM],
            own.m_recv.at[layer, SM],
            p.at(d=1 - p.d),
        ).start()

    def small_core(layer):
        part = reduces[layer][SM][0]
        departed(own.sd.at[layer], own.m_send.at[layer, SM])
        arrived(own.sd.at[layer], own.m_recv.at[layer, SM])
        if layer == 0:
            reduces[1][SM][0].close()
        part.buf[...] = (own.sb[:, :, small_rows(p.d), :] + own.sd[layer]).astype(bf16)
        part.send_y()

    vr[...] = jnp.zeros(vr.shape, f32)
    gr[...] = jnp.zeros(gr.shape, f32)
    def run(*steps):
        def all_():
            for step in steps:
                step()

        return all_

    deliver(0, 1, ref.res1)
    weight_grad(1, DN, False)
    mlp_back(
        1,
        gbuf.at[0],
        {},
        (
            run(functools.partial(loaded, v.n2), functools.partial(weight_grad, 1, U, False)),
            functools.partial(weight_grad, 1, DN, True),
            run(functools.partial(loaded, v.ob), functools.partial(weight_grad, 1, O, False)),
        ),
    )
    load(0, v.o)
    load_w(0, U)
    load_w(0, O)
    for k in range(3):
        load_wd(0, k)
    loaded(v.a)
    weight_grad(1, U, True)
    weight_grad(1, O, True)
    load(0, v.gp, v.n2, v.ob)
    mix_back(1, {1: step_y(1, DN), 5: step_a(1, DN)})
    input_back(1)
    deliver(1, 1, gbuf.at[1])
    load_w(0, Q)
    load(0, v.r, v.inv, v.ph, v.u, v.pre)
    pack_small(1)
    step_y(1, U)()
    weight_grad(1, Q, False)
    weight_grad(1, Q, True)
    small_core(1)
    load(0, v.qkv, v.a)

    step_z(1, DN)()
    weight_grad(0, DN, False)
    step_y(1, O)()
    mlp_back(
        0,
        gbuf.at[1],
        {5: step_x(1, DN), 6: step_a(1, U)},
        (
            step_a(1, O),
            functools.partial(weight_grad, 0, DN, True),
            run(
                step_z(1, U),
                functools.partial(loaded, v.n2),
                functools.partial(weight_grad, 0, U, False),
            ),
        ),
    )
    loaded(v.ob, v.a)
    step_z(1, O)()
    weight_grad(0, O, False)
    weight_grad(0, U, True)
    step_y(1, Q, SM)()
    weight_grad(0, O, True)
    step_x(1, U)()
    mix_back(
        0,
        {
            0: step_x(1, O),
            1: step_a(1, Q, SM),
            3: step_y(0, DN),
            4: step_z(1, Q, SM),
        },
    )
    weight_grad(0, Q, False)
    step_a(0, DN)()
    step_x(1, Q, SM)()
    weight_grad(0, Q, True)
    step_y(0, U)()
    input_back(0)
    pack_small(0)
    step_z(0, DN)()
    step_y(0, O)()
    step_a(0, U)()
    small_core(0)
    deliver(1, 0, gbuf.at[0])
    step_x(0, DN)()
    first, second, third = reduces[0][Q]
    first.step_y()
    step_a(0, O)()
    second.step_y()
    first.step_a()
    step_z(0, U)()
    step_z(0, O)()
    third.step_y()
    second.step_a()
    step_x(0, U)()
    step_x(0, O)()
    step_y(0, SM)()
    first.step_z()
    third.step_a()
    step_a(0, SM)()
    second.step_z()
    first.step_x()
    third.step_z()
    step_z(0, SM)()
    second.step_x()
    third.step_x()
    step_x(0, SM)()

    for m in range(5):
        for part in reduces[0][m]:
            part.close()
        for layer in range(2):
            for part in reduces[layer][m]:
                part.end()
    for layer in range(2):
        close_states(layer)

        handed_over(p, layer, gin, own.d_recv.at[1])
    handed_over(p, 1, lay, own.d_recv.at[0])

    for close in closing:
        close()


def backward_pass(n, cot, gains, bds, full, tokens, kept):
    t = cot.shape[0]
    nz = n // 2
    args = [cot, kept[1].res, gains, bds] + list(full)
    for u, k in zip((tokens, kept[0].res), kept):
        read = Loaded(k.gp, k.r, k.o, k.inv, k.ph, k.qkv, k.n2, k.ob, k.a, u, k.pre)
        args += list(read)
    args += [k.hid for k in kept]
    widths = (3 * D // 2, D // 2, FF // 2, D // 2)
    rows = (D // n, D // n, D // n, FF // n)
    outs = [shape((1, 4, 2, CH, D), bf16)] * 2
    outs += [shape((r, 2 * c), f32) for r, c in zip(rows, widths)]
    outs += [shape((SMALL_OUT, CH), f32)]
    outs += [shape((nz, 2, r, c), bf16) for r, c in zip(rows, widths)] * 2
    specs = [ANY] * len(outs)
    ins = [ANY] * 2 + [VMEM] * 2 + [ANY] * (len(args) - 4)
    scratch = [pltpu.VMEM(a.shape, a.dtype) for a in read]

    def vmem(*dims, kind=f32):
        scratch.append(pltpu.VMEM(dims, kind))

    vmem(2, t, D, kind=bf16)
    vmem(t, D, kind=bf16)
    vmem(t, D, kind=bf16)
    vmem(t, D)
    vmem(8, D)
    vmem(2, STATE_ROWS, CH)
    vmem(2, STATE_ROWS + 16, CH, kind=bf16)
    vmem(STATE_ROWS, CH)
    vmem(2, n // 2 - 1, STATE_ROWS + 16, CH, kind=bf16)
    vmem(2 * H, HEAD, CH)
    vmem(2, VEC_ROWS, CH)
    vmem(2, GAIN_ROWS, CH)
    vmem(3, t, FF // n, kind=bf16)
    vmem(3, FF // n, D, kind=bf16)
    for w in full[:3]:
        vmem(*w.shape[1:], kind=bf16)
    sizes = list(zip(rows, widths)) + [(64, CH)]
    for lead in ((nz, 2), (nz,), (nz - 1,), (), ()):
        for size in sizes:
            vmem(*lead, *size, kind=bf16)
    for size in sizes:
        vmem(*size)
    vmem(2, nz, 2, D // n, 384, kind=bf16)
    vmem(3, FF // n, D // 2, kind=bf16)
    vmem(nz, 2, SMALL_OUT, CH)
    vmem(2, nz, 2, 64, CH)
    dma = pltpu.SemaphoreType.DMA
    regular = pltpu.SemaphoreType.REGULAR
    count = len(PARTS)
    scratch += [dma((2, count, 6)), dma((2, count, 6)), dma((2, count))]
    scratch += [regular((count,))] * 3 + [dma((2, 5)), dma((2, 5))]
    scratch += [dma((2, n // 2 - 1)), dma((2, n // 2 - 1)), dma((2, 2, 4)), dma((2, 8)), dma((4,))]
    scratch += [dma((len(read),)), dma((3,)), dma((5,)), dma((3,))]
    got = call(
        functools.partial(backward_kernel, n),
        outs,
        scratch,
        ins,
        args,
        8 * t * D * (4 * D + 2 * FF),
        specs,
        cid=1,
        vmem=63,
    )
    return got[:7]


def settle_kernel(lay0, lay1, *refs):
    rest, small, outs, held, sems = refs[:5], refs[5], refs[6:13], refs[13:19], refs[19]
    x = lax.axis_index("section")
    for plane, src in enumerate((lay0, lay1)):

        @pl.when(x == plane)
        def _():
            pltpu.make_async_copy(src, held[0], sems.at[0]).start()

    for i, src in enumerate(rest):
        pltpu.make_async_copy(src, held[1 + i], sems.at[1 + i]).start()
    both = small[16:112, :]
    outs[6][0:96, :] = both[:, :HEAD]
    outs[6][96:, :] = pltpu.roll(both, HEAD, 1)[:, :HEAD]
    copies = []
    for i, buf in enumerate(held):
        finish(buf, sems.at[i])
        copies.append(pltpu.make_async_copy(buf, outs[i], sems.at[6 + i]))
        copies[-1].start()
    for copy in copies:
        copy.wait()


def settle(lay0, lay1, rest, small):
    arrays = [lay0, lay1, *rest, small]
    outs = [shape(a.shape, a.dtype) for a in (lay0, *rest)]
    return call(
        settle_kernel,
        outs + [shape((192, HEAD), f32)],
        [pltpu.VMEM(o.shape, o.dtype) for o in outs] + [pltpu.SemaphoreType.DMA((12,))],
        [ANY] * 7 + [VMEM],
        arrays,
        1,
        [ANY] * 6 + [VMEM],
    )


def shards(inputs, cotangent, *weights):
    n = lax.axis_size("seq")
    d, j = lax.axis_index("dp"), lax.axis_index("seq")
    qkv_w, out_w, up_w, down_w, map_w, bias_w, gain_w = (w[0] for w in weights)

    def placed(vector, offset, rows):
        flat = jnp.zeros((rows * CH,), f32)
        return lax.dynamic_update_slice(flat, vector, (offset,)).reshape(rows, CH)

    bias_at, gain_at = (j % 4) * 32, (j % 2) * 64
    small = jnp.concatenate(
        [
            placed(bias_w, bias_at, 9),
            placed(gain_w, gain_at, 2),
            jnp.zeros((5, CH), f32),
            jnp.concatenate([map_w[:96], map_w[96:]], 1),
            jnp.zeros((16, CH), f32),
        ]
    ).astype(bf16)
    small = lax.dynamic_slice_in_dim(small, d * 64, 64, 0)
    full, gains, bds, tokens, cot, lay0, kept = forward_pass(
        n, inputs, cotangent, small, qkv_w, out_w, up_w, down_w
    )
    lay1, *rest, g_small = backward_pass(n, cot, gains, bds, full, tokens, kept)
    layer_out, grads, g_qkv, g_out, g_up, g_down, maps = settle(lay0, lay1, rest, g_small)
    bias = lax.dynamic_slice_in_dim(g_small[:9].reshape(-1), bias_at, bias_w.shape[0])
    gain = lax.dynamic_slice_in_dim(g_small[9:11].reshape(-1), gain_at, gain_w.shape[0])
    return (
        layer_out,
        grads,
        g_qkv[None],
        g_out[None],
        g_up[None],
        g_down[None],
        maps[None],
        bias[None],
        gain[None],
    )


def solution(mesh):
    tokens = P("dp", None, "seq", None)
    matrix = P("section", "seq", None)
    vector = P("section", "seq")
    stacked = P("section", "dp", None, "seq", None)
    chosen = shards if mesh.shape["seq"] == 8 else plain_shards
    return jax.shard_map(
        chosen,
        mesh=mesh,
        in_specs=(tokens, tokens) + (matrix,) * 5 + (vector,) * 2,
        out_specs=(stacked, stacked) + (matrix,) * 5 + (vector,) * 2,
        check_vma=False,
    )
```

```python
import functools
from typing import Any, NamedTuple

import jax
import jax.numpy as jnp
from jax import lax
from jax.experimental import pallas as pl
from jax.experimental.pallas import tpu as pltpu
from jax.sharding import PartitionSpec as P


D = 768
FF = 3072
H = 12
HEAD = 64
BLOCK = 64


MAXIMUM_ACCURACY = lax.Precision.HIGHEST
NORM_EPSILON = 1e-05


def carried_in(part, axis, combine, identity, reverse):
    count = lax.axis_size(axis)
    place = lax.axis_index(axis)
    ahead = count - 1 - place if reverse else place
    gathered = jax.tree.map(lambda a: lax.all_gather(a, axis), part)
    state = jax.tree.map(lambda a, e: jnp.zeros_like(a) + jnp.asarray(e, a.dtype), part, identity)

    def one(lap, state):
        source = count - 1 - lap if reverse else lap
        return combine(
            state, jax.tree.map(lambda a: lax.dynamic_index_in_dim(a, source, 0, False), gathered)
        )

    return lax.fori_loop(0, ahead, one, state)


def shifted(value, axis, steps):
    count = lax.axis_size(axis)
    leading, last = (max(0, -steps), min(count, count - steps))
    return lax.ppermute(value, axis, [(source, source + steps) for source in range(leading, last)])


def normalize(values, gain_vector, shift_vector):
    average = jnp.mean(values, -1, keepdims=True)
    centred = values - average
    spread = jnp.mean(centred * centred, -1, keepdims=True)
    return centred * lax.rsqrt(spread + NORM_EPSILON) * gain_vector + shift_vector


def features(logits):
    return jnp.concatenate([jax.nn.softmax(logits, -1), jax.nn.softmax(-logits, -1)], -1)


def gelu_tanh(values):
    return jax.nn.gelu(values, approximate=True)


def adding(earlier, later_part):
    return jax.tree.map(jnp.add, earlier, later_part)


def across_rows(left_side, right_side):
    return lax.dot_general(
        left_side, right_side, (((0,), (0,)), ((), ())), preferred_element_type=jnp.float32
    )


def against_rows(left_side, right_side):
    return lax.dot_general(
        left_side, right_side, (((1,), (1,)), ((), ())), preferred_element_type=jnp.float32
    )


def precise(pattern, left_side, right_side):
    return jnp.einsum(pattern, left_side, right_side, precision=MAXIMUM_ACCURACY)


def causal_mask():
    places = lax.broadcasted_iota(jnp.int32, (BLOCK, BLOCK), 0)
    others = lax.broadcasted_iota(jnp.int32, (BLOCK, BLOCK), 1)
    return (others <= places).astype(jnp.float32)


def in_blocks(source_array, batch_rows):
    return source_array.reshape((batch_rows, -1, BLOCK) + source_array.shape[1:])


def prepare(gathered):
    qkv_full, out_full, up_full, down_full, map_full, bias_full, gain_full = [
        piece_array[0] for piece_array in gathered
    ]
    feature_maps = map_full.reshape(2, H, HEAD, HEAD)
    vectors = bias_full.astype(jnp.float32)
    scales = gain_full.astype(jnp.float32)
    pieces = (
        vectors[:D],
        vectors[D : 4 * D],
        vectors[4 * D : 5 * D],
        vectors[5 * D : 6 * D],
        vectors[6 * D : 6 * D + FF],
        vectors[6 * D + FF :],
        scales[:D],
        scales[D:],
    )
    return (qkv_full, out_full, up_full, down_full, feature_maps, pieces)


def block_sums(query_map, key_map, value_rows, batch_rows):
    query_blocks = in_blocks(query_map, batch_rows)
    key_blocks = in_blocks(key_map, batch_rows)
    value_blocks = in_blocks(value_rows, batch_rows).astype(jnp.float32)
    query_wide = query_blocks.astype(jnp.float32)
    key_wide = key_blocks.astype(jnp.float32)
    score_matrix = (
        jnp.einsum(
            "bcqhf,bckhf->bchqk", query_blocks, key_blocks, preferred_element_type=jnp.float32
        )
        * causal_mask()
    )
    block_state = precise("bckhf,bckhe->bchfe", key_wide, value_blocks)
    block_total = jnp.sum(key_wide, 2)
    return (query_wide, key_wide, value_blocks, score_matrix, block_state, block_total)


def attend(query_map, key_map, value_rows, initial, batch_rows):
    query_wide, key_wide, value_blocks, score_matrix, block_state, block_total = block_sums(
        query_map, key_map, value_rows, batch_rows
    )
    state_sum = jnp.sum(block_state, 1)
    total_sum = jnp.sum(block_total, 1)
    identity = (jnp.zeros_like(state_sum), jnp.zeros_like(total_sum))
    earlier = carried_in((state_sum, total_sum), "seq", adding, identity, False)
    overall = lax.psum((state_sum, total_sum), "seq")
    start_state = initial[0] + earlier[0]
    start_total = initial[1] + earlier[1]
    block_before = start_state[:, None] + jnp.cumsum(block_state, 1) - block_state
    total_before = start_total[:, None] + jnp.cumsum(block_total, 1) - block_total
    numerator = precise("bchqk,bckhe->bcqhe", score_matrix, value_blocks) + precise(
        "bcqhf,bchfe->bcqhe", query_wide, block_before
    )
    denominator = jnp.swapaxes(jnp.sum(score_matrix, -1), 2, 3) + precise(
        "bcqhf,bchf->bcqh", query_wide, total_before
    )
    mixture = numerator / denominator[..., None]
    handed = (initial[0] + overall[0], initial[1] + overall[1])
    return (mixture.reshape(value_rows.shape), denominator, (start_state, start_total), handed)


def attend_back(
    mixture_grad, query_map, key_map, value_rows, mixture, denominator, starts, future, batch_rows
):
    query_wide, key_wide, value_blocks, score_matrix, block_state, block_total = block_sums(
        query_map, key_map, value_rows, batch_rows
    )
    block_before = starts[0][:, None] + jnp.cumsum(block_state, 1) - block_state
    total_before = starts[1][:, None] + jnp.cumsum(block_total, 1) - block_total
    scaled = in_blocks(mixture_grad, batch_rows) / denominator[..., None]
    denominator_grad = -jnp.sum(scaled * in_blocks(mixture, batch_rows), -1)
    score_grad = (
        precise("bcqhe,bckhe->bchqk", scaled, value_blocks)
        + jnp.swapaxes(denominator_grad, 2, 3)[..., None]
    ) * causal_mask()
    query_grad = precise("bchqk,bckhf->bcqhf", score_grad, key_wide) + precise(
        "bcqhe,bchfe->bcqhf", scaled, block_before
    )
    query_grad = query_grad + denominator_grad[..., None] * total_before[:, :, None]
    state_grad = precise("bcqhf,bcqhe->bchfe", query_wide, scaled)
    total_grad = precise("bcqhf,bcqh->bchf", query_wide, denominator_grad)
    state_sum = jnp.sum(state_grad, 1)
    total_sum = jnp.sum(total_grad, 1)
    identity = (jnp.zeros_like(state_sum), jnp.zeros_like(total_sum))
    later_sums = carried_in((state_sum, total_sum), "seq", adding, identity, True)
    overall = lax.psum((state_sum, total_sum), "seq")
    ahead_state = future[0] + later_sums[0]
    ahead_total = future[1] + later_sums[1]
    rest_state = ahead_state[:, None] + state_sum[:, None] - jnp.cumsum(state_grad, 1)
    rest_total = ahead_total[:, None] + total_sum[:, None] - jnp.cumsum(total_grad, 1)
    key_grad = precise("bchqk,bcqhf->bckhf", score_grad, query_wide) + precise(
        "bckhe,bchfe->bckhf", value_blocks, rest_state
    )
    key_grad = key_grad + rest_total[:, :, None]
    value_grad = precise("bchqk,bcqhe->bckhe", score_matrix, scaled) + precise(
        "bckhf,bchfe->bckhe", key_wide, rest_state
    )
    return (
        query_grad.reshape(query_map.shape),
        key_grad.reshape(key_map.shape),
        value_grad.reshape(value_rows.shape),
        overall,
    )


def forward(tokens, params, initial):
    qkv_full, out_full, up_full, down_full, feature_maps, pieces = params
    shift_one, qkv_bias, out_bias, shift_two, up_bias, down_bias, gain_one, gain_two = pieces
    batch_rows = tokens.shape[0]
    flattened = tokens.reshape(-1, D)
    row_count = flattened.shape[0]
    normed = normalize(flattened, gain_one, shift_one).astype(jnp.bfloat16)
    projected = (jnp.dot(normed, qkv_full, preferred_element_type=jnp.float32) + qkv_bias).astype(
        jnp.bfloat16
    )
    query_rows = projected[:, :D].reshape(row_count, H, HEAD)
    key_rows = projected[:, D : 2 * D].reshape(row_count, H, HEAD)
    value_rows = projected[:, 2 * D :].reshape(row_count, H, HEAD)
    query_logits = jnp.einsum(
        "rhe,hef->rhf", query_rows, feature_maps[0], preferred_element_type=jnp.float32
    )
    key_logits = jnp.einsum(
        "rhe,hef->rhf", key_rows, feature_maps[1], preferred_element_type=jnp.float32
    )
    query_map = features(query_logits).astype(jnp.bfloat16)
    key_map = features(key_logits).astype(jnp.bfloat16)
    mixture, denominator, starts, handed = attend(
        query_map, key_map, value_rows, initial, batch_rows
    )
    mixture_low = mixture.reshape(row_count, D).astype(jnp.bfloat16)
    residual = (
        flattened + jnp.dot(mixture_low, out_full, preferred_element_type=jnp.float32) + out_bias
    )
    normed_two = normalize(residual, gain_two, shift_two).astype(jnp.bfloat16)
    before_act = jnp.dot(normed_two, up_full, preferred_element_type=jnp.float32) + up_bias
    hidden = gelu_tanh(before_act).astype(jnp.bfloat16)
    result = residual + jnp.dot(hidden, down_full, preferred_element_type=jnp.float32) + down_bias
    kept_values = (
        flattened,
        normed,
        projected,
        query_logits,
        key_logits,
        query_map,
        key_map,
        mixture,
        denominator,
        starts,
        residual,
        normed_two,
        before_act,
        hidden,
    )
    return (result.reshape(tokens.shape), handed, kept_values)


def backward(upstream, params, kept_values, future):
    qkv_full, out_full, up_full, down_full, feature_maps, pieces = params
    shift_one, qkv_bias, out_bias, shift_two, up_bias, down_bias, gain_one, gain_two = pieces
    (
        flattened,
        normed,
        projected,
        query_logits,
        key_logits,
        query_map,
        key_map,
        mixture,
        denominator,
        starts,
        residual,
        normed_two,
        before_act,
        hidden,
    ) = kept_values
    batch_rows = upstream.shape[0]
    row_count = flattened.shape[0]
    out_grad = upstream.reshape(row_count, D)
    down_bias_grad = jnp.sum(out_grad, 0)
    out_low = out_grad.astype(jnp.bfloat16)
    down_weight_grad = across_rows(hidden, out_low)
    hidden_grad = against_rows(out_low, down_full)
    _, gelu_back = jax.vjp(gelu_tanh, before_act)
    before_grad = gelu_back(hidden_grad)[0].astype(jnp.bfloat16)
    up_bias_grad = jnp.sum(before_grad.astype(jnp.float32), 0)
    up_weight_grad = across_rows(normed_two, before_grad)
    normed_two_grad = against_rows(before_grad, up_full)
    _, norm_back_two = jax.vjp(normalize, residual, gain_two, shift_two)
    residual_part, gain_two_grad, shift_two_grad = norm_back_two(normed_two_grad)
    residual_grad = out_grad + residual_part
    out_bias_grad = jnp.sum(residual_grad, 0)
    residual_low = residual_grad.astype(jnp.bfloat16)
    mixture_low = mixture.reshape(row_count, D).astype(jnp.bfloat16)
    out_weight_grad = across_rows(mixture_low, residual_low)
    mixture_grad = against_rows(residual_low, out_full).reshape(row_count, H, HEAD)
    query_rows = projected[:, :D].reshape(row_count, H, HEAD)
    key_rows = projected[:, D : 2 * D].reshape(row_count, H, HEAD)
    value_rows = projected[:, 2 * D :].reshape(row_count, H, HEAD)
    query_map_grad, key_map_grad, value_grad, handed = attend_back(
        mixture_grad,
        query_map,
        key_map,
        value_rows,
        mixture,
        denominator,
        starts,
        future,
        batch_rows,
    )
    _, query_back = jax.vjp(features, query_logits)
    query_logit_grad = query_back(query_map_grad)[0]
    _, key_back = jax.vjp(features, key_logits)
    key_logit_grad = key_back(key_map_grad)[0]
    maps_wide = feature_maps.astype(jnp.float32)
    query_grad = precise("rhf,hef->rhe", query_logit_grad, maps_wide[0])
    key_grad = precise("rhf,hef->rhe", key_logit_grad, maps_wide[1])
    map_weight_grad = jnp.stack(
        [
            precise("rhe,rhf->hef", query_rows.astype(jnp.float32), query_logit_grad),
            precise("rhe,rhf->hef", key_rows.astype(jnp.float32), key_logit_grad),
        ]
    ).reshape(2 * H * HEAD, HEAD)
    projected_grad = jnp.concatenate(
        [
            query_grad.reshape(row_count, D),
            key_grad.reshape(row_count, D),
            value_grad.reshape(row_count, D),
        ],
        1,
    ).astype(jnp.bfloat16)
    qkv_bias_grad = jnp.sum(projected_grad.astype(jnp.float32), 0)
    qkv_weight_grad = across_rows(normed, projected_grad)
    normed_grad = against_rows(projected_grad, qkv_full)
    _, norm_back_one = jax.vjp(normalize, flattened, gain_one, shift_one)
    input_part, gain_one_grad, shift_one_grad = norm_back_one(normed_grad)
    input_grad = residual_grad + input_part
    bias_grad = jnp.concatenate(
        [shift_one_grad, qkv_bias_grad, out_bias_grad, shift_two_grad, up_bias_grad, down_bias_grad]
    )
    gain_grad = jnp.concatenate([gain_one_grad, gain_two_grad])
    layer_grads = (
        qkv_weight_grad,
        out_weight_grad,
        up_weight_grad,
        down_weight_grad,
        map_weight_grad,
        bias_grad,
        gain_grad,
    )
    return (input_grad.reshape(upstream.shape), handed, layer_grads)


def reduce_grads(full_grads):
    g_qkv, g_out, g_up, g_down, g_map, g_bias, g_gain = full_grads
    s_qkv, s_out, s_up, s_down, s_map, s_bias, s_gain = (
        lax.psum_scatter(g_qkv, "seq", scatter_dimension=1, tiled=True),
        lax.psum_scatter(g_out, "seq", scatter_dimension=1, tiled=True),
        lax.psum_scatter(g_up, "seq", scatter_dimension=1, tiled=True),
        lax.psum_scatter(g_down, "seq", scatter_dimension=1, tiled=True),
        lax.psum_scatter(g_map, "seq", scatter_dimension=1, tiled=True),
        lax.psum_scatter(g_bias, "seq", scatter_dimension=1, tiled=True),
        lax.psum_scatter(g_gain, "seq", scatter_dimension=1, tiled=True),
    )
    return lax.psum((s_qkv, s_out, s_up, s_down, s_map, s_bias, s_gain), "dp")


def plain_shards(
    inputs, cotangent, qkv_weight, out_weight, up_weight, down_weight, map_weight, biases, gains
):
    section_index = lax.axis_index("section")
    batch_rows = inputs.shape[0]
    micro_count = inputs.shape[1]
    gathered = (
        lax.all_gather(qkv_weight.astype(jnp.bfloat16), "seq", axis=1, tiled=True),
        lax.all_gather(out_weight.astype(jnp.bfloat16), "seq", axis=1, tiled=True),
        lax.all_gather(up_weight.astype(jnp.bfloat16), "seq", axis=1, tiled=True),
        lax.all_gather(down_weight.astype(jnp.bfloat16), "seq", axis=1, tiled=True),
        lax.all_gather(map_weight.astype(jnp.bfloat16), "seq", axis=1, tiled=True),
        lax.all_gather(biases.astype(jnp.bfloat16), "seq", axis=1, tiled=True),
        lax.all_gather(gains.astype(jnp.bfloat16), "seq", axis=1, tiled=True),
    )
    params = prepare(gathered)
    empty_state = (
        jnp.zeros((batch_rows, H, 2 * HEAD, HEAD), jnp.float32),
        jnp.zeros((batch_rows, H, 2 * HEAD), jnp.float32),
    )
    blank_rows = jnp.zeros(inputs.shape[:1] + inputs.shape[2:], jnp.bfloat16)
    moments = jnp.arange(micro_count + 1, dtype=jnp.int32)

    def forward_moment(carry, moment):
        handed, arriving = carry
        own_tokens = lax.dynamic_index_in_dim(
            inputs, jnp.minimum(moment, micro_count - 1), 1, False
        )
        source = jnp.where(section_index == 0, own_tokens, arriving).astype(jnp.float32)
        carried = moment - section_index >= 1
        initial = (jnp.where(carried, handed[0], 0.0), jnp.where(carried, handed[1], 0.0))
        result, handed_next, kept_values = forward(source, params, initial)
        outgoing = result.astype(jnp.bfloat16)
        arriving_next = shifted(outgoing, "section", 1)
        return ((handed_next, arriving_next), (outgoing, kept_values))

    _, (result_stack, kept_stack) = lax.scan(forward_moment, (empty_state, blank_rows), moments)
    regathered = (
        lax.all_gather(qkv_weight.astype(jnp.bfloat16), "seq", axis=1, tiled=True),
        lax.all_gather(out_weight.astype(jnp.bfloat16), "seq", axis=1, tiled=True),
        lax.all_gather(up_weight.astype(jnp.bfloat16), "seq", axis=1, tiled=True),
        lax.all_gather(down_weight.astype(jnp.bfloat16), "seq", axis=1, tiled=True),
        lax.all_gather(map_weight.astype(jnp.bfloat16), "seq", axis=1, tiled=True),
        lax.all_gather(biases.astype(jnp.bfloat16), "seq", axis=1, tiled=True),
        lax.all_gather(gains.astype(jnp.bfloat16), "seq", axis=1, tiled=True),
    )
    back_params = prepare(regathered)
    zero_grads = (
        jnp.zeros((D, 3 * D), jnp.float32),
        jnp.zeros((D, D), jnp.float32),
        jnp.zeros((D, FF), jnp.float32),
        jnp.zeros((FF, D), jnp.float32),
        jnp.zeros((2 * H * HEAD, HEAD), jnp.float32),
        jnp.zeros((7 * D + FF,), jnp.float32),
        jnp.zeros((2 * D,), jnp.float32),
    )

    def backward_moment(carry, pieces):
        future, returning, grad_sums = carry
        slot, kept_values = pieces
        chosen = slot - section_index
        own_grad = lax.dynamic_index_in_dim(cotangent, jnp.maximum(slot - 1, 0), 1, False)
        live = (chosen >= 0) & (chosen < micro_count)
        upstream = jnp.where(section_index == 1, own_grad, returning).astype(jnp.float32)
        upstream = jnp.where(live, upstream, 0.0)
        later_micro = live & (chosen < micro_count - 1)
        ahead_part = (
            jnp.where(later_micro, future[0], 0.0),
            jnp.where(later_micro, future[1], 0.0),
        )
        input_grad, future_next, layer_grads = backward(
            upstream, back_params, kept_values, ahead_part
        )
        outgoing = input_grad.astype(jnp.bfloat16)
        grad_sums = tuple((previous + current for previous, current in zip(grad_sums, layer_grads)))
        returning_next = shifted(outgoing, "section", -1)
        return ((future_next, returning_next, grad_sums), outgoing)

    (_, _, grad_sums), grad_stack = lax.scan(
        backward_moment, (empty_state, blank_rows, zero_grads), (moments, kept_stack), reverse=True
    )
    layer_out = jnp.stack(
        [
            lax.dynamic_index_in_dim(result_stack, micro_index + section_index, 0, False)
            for micro_index in range(micro_count)
        ],
        1,
    )
    input_grads = jnp.stack(
        [
            lax.dynamic_index_in_dim(grad_stack, micro_index + section_index, 0, False)
            for micro_index in range(micro_count)
        ],
        1,
    )
    full_grads = tuple((grad_array[None] for grad_array in grad_sums))
    reduced = reduce_grads(full_grads)
    return (
        layer_out[None],
        input_grads[None],
        reduced[0],
        reduced[1],
        reduced[2],
        reduced[3],
        reduced[4],
        reduced[5],
        reduced[6],
    )


CH = 128
PAIRS = H // 2
QB = 2 * H * HEAD
STATE_ROWS = D + 16
EPS = 1e-05
TILE = 256
AXES = ("section", "dp", "seq")
MESH = pl.DeviceIdType.MESH
f32 = jnp.float32
bf16 = jnp.bfloat16
GELU_C = 0.7978845608028654
GELU_A = 0.044715
SMALL_ROWS = 128
VEC_ROWS = 72
GAIN_ROWS = 16
SHIFT1, QKV_BIAS, OUT_BIAS, SHIFT2, UP_BIAS, DOWN_BIAS = 0, 6, 24, 30, 36, 60


class Kept(NamedTuple):
    a: Any
    qkv: Any
    ph: Any
    o: Any
    inv: Any
    ob: Any
    r: Any
    n2: Any
    hid: Any
    gp: Any
    res: Any
    pre: Any


class ForwardRefs(NamedTuple):
    tokens: Any
    cot: Any
    small: Any
    wq: Any
    wo: Any
    wu: Any
    wd: Any
    gq: Any
    go: Any
    gu: Any
    gd: Any
    gv: Any
    bd: Any
    tok_out: Any
    cot_out: Any
    lay: Any


class ForwardScratch(NamedTuple):
    wq: Any
    wo: Any
    wu: Any
    wd: Any
    hq: Any
    ho: Any
    hu: Any
    hd: Any
    tok: Any
    sm: Any
    vec: Any
    maps: Any
    st: Any
    stb: Any
    got: Any
    vq: Any
    vo: Any
    vu: Any
    vd: Any
    g_send: Any
    g_recv: Any
    g_local: Any
    c_send: Any
    c_recv: Any
    s_send: Any
    s_recv: Any
    d_send: Any
    d_recv: Any
    w_sem: Any
    o_sem: Any
    m_sem: Any


class Weights(NamedTuple):
    q: Any
    o: Any
    u: Any
    d: Any = None


VMEM = pl.BlockSpec(memory_space=pltpu.VMEM)
SMEM = pl.BlockSpec(memory_space=pltpu.SMEM)
ANY = pl.BlockSpec(memory_space=pl.ANY)


def nn(a, b):
    return lax.dot_general(a, b, (((1,), (0,)), ((), ())), preferred_element_type=f32)


def nt(a, b):
    return lax.dot_general(a, b, (((1,), (1,)), ((), ())), preferred_element_type=f32)


def tn(a, b):
    return lax.dot_general(a, b, (((0,), (0,)), ((), ())), preferred_element_type=f32)


def tt(a, b):
    return lax.dot_general(a, b, (((0,), (1,)), ((), ())), preferred_element_type=f32)


def loop(count, body, events=None):
    events = events or {}

    def step(i, c):
        body(i)
        for at, event in events.items():

            @pl.when(i == at)
            def _():
                event()

        return c

    lax.fori_loop(0, count, step, 0)


def span(i, size):
    return pl.ds(pl.multiple_of(i * size, size), size)


def wide(ref, layer, row, count):
    return jnp.concatenate([ref[layer, pl.ds(row + i, 1), :] for i in range(count)], 1)


def finish(dst, sem):
    pltpu.make_async_copy(dst, dst, sem).wait()


def arrived(dst, recv):
    finish(dst, recv)


def departed(src, send):
    finish(src, send)


def shape(dims, kind):
    return jax.ShapeDtypeStruct(dims, kind)


def call(kernel, outs, scratch, specs, args, flops, out_specs=None, vmem=60, cid=None):
    if out_specs is None:
        out_specs = [VMEM] * len(outs)
    moved = sum(a.size * a.dtype.itemsize for a in args if a.ndim > 0)
    moved += sum(o.size * o.dtype.itemsize for o in outs)
    params = dict(vmem_limit_bytes=vmem * 1024 * 1024)
    if cid is not None:
        params.update(collective_id=cid, has_side_effects=True)
    return pl.pallas_call(
        kernel,
        out_shape=outs,
        in_specs=specs,
        out_specs=out_specs,
        scratch_shapes=scratch,
        compiler_params=pltpu.CompilerParams(**params),
        cost_estimate=pl.CostEstimate(flops=flops, bytes_accessed=moved, transcendentals=0),
    )(*args)


def standardize(u):
    cen = u - jnp.mean(u, -1, keepdims=True)
    rstd = lax.rsqrt(jnp.mean(cen * cen, -1, keepdims=True) + EPS)
    return cen * rstd, rstd


def lanes(rows):
    return lax.broadcasted_iota(jnp.int32, (rows, CH), 1)


def half_sums(t, low):
    s1 = jnp.sum(jnp.where(low, t, 0.0), -1, keepdims=True)
    s2 = jnp.sum(jnp.where(low, 0.0, t), -1, keepdims=True)
    return jnp.where(low, s1, s2)


def half_softmax(l, low):
    m1 = jnp.max(jnp.where(low, l, -jnp.inf), -1, keepdims=True)
    m2 = jnp.max(jnp.where(low, -jnp.inf, l), -1, keepdims=True)
    p = jnp.exp(l - jnp.where(low, m1, m2))
    return p / half_sums(p, low)


def split_states(src, dst):
    hi = src[...].astype(bf16)
    dst[0:STATE_ROWS] = hi
    dst[STATE_ROWS:] = (src[D:] - hi[D:].astype(f32)).astype(bf16)


def add_states(dst, src):
    dst[...] += src[0:STATE_ROWS].astype(f32)
    dst[D:] += src[STATE_ROWS:].astype(f32)


class Place:
    def __init__(self, n):
        self.n, self.nz, self.group = n, n // 2, n // 4
        self.x = lax.axis_index("section")
        self.d = lax.axis_index("dp")
        self.j = lax.axis_index("seq")
        self.z, self.y = lax.div(self.j, 2), lax.rem(self.j, 2)
        self.zh, self.zl = lax.div(self.z, 2), lax.rem(self.z, 2)
        self.i = lax.rem(self.z, 2) * 2 + self.y
        self.jj = lax.div(self.z, 2)
        self.r = self.x * self.group + self.jj

    def at(self, x=None, d=None, z=None, y=None, j=None):
        x = self.x if x is None else x
        d = self.d if d is None else d
        if j is None:
            j = (self.z if z is None else z) * 2 + (self.y if y is None else y)
        return (x, d, j)

    def zpos(self, o):
        return lax.rem(self.z + o + self.nz, self.nz)

    def member(self, r):
        z = lax.rem(r, self.group) * 2 + lax.rem(self.z, 2)
        return (lax.div(r, self.group), self.d, z * 2 + self.y)

    def meet(self):
        barrier = pltpu.get_barrier_semaphore()
        for dx in range(2):
            for o in range(self.n):
                if dx == 0 and o == 0:
                    continue
                other = (
                    lax.rem(self.x + dx, 2),
                    self.d,
                    lax.rem(self.j + o, self.n),
                )
                pl.semaphore_signal(barrier, inc=1, device_id=other, device_id_type=MESH)
        pl.semaphore_signal(
            barrier, inc=1, device_id=(self.x, 1 - self.d, self.j), device_id_type=MESH
        )
        pl.semaphore_wait(barrier, 2 * self.n)


def remote(src, dst, send, recv, to):
    return pltpu.make_async_remote_copy(
        src_ref=src, dst_ref=dst, send_sem=send, recv_sem=recv, device_id=to, device_id_type=MESH
    )


def hand_over(p, layer, rows, out, send, recv):
    closing = []
    for k in range(4):
        to = p.jj * 4 + k
        src = rows.at[pl.ds(k * CH, CH), :]
        dst = out.at[0, p.i, p.x]
        slot = p.i * 2 + p.x
        mine = (to == p.j) & (p.x == layer)
        copy = remote(src, dst, send.at[k], recv.at[slot], p.at(x=layer, j=to))

        @pl.when(jnp.logical_not(mine))
        def _():
            copy.start()

        @pl.when(mine)
        def _():
            pltpu.make_async_copy(src, dst, recv.at[slot]).start()

        def close(copy=copy, mine=mine):
            @pl.when(jnp.logical_not(mine))
            def _():
                copy.wait_send()

        closing.append(close)
    return closing


def handed_over(p, layer, out, recv):
    @pl.when(p.x == layer)
    def _():
        for slot in range(8):
            arrived(out.at[0, slot // 2, slot % 2], recv.at[slot])


def signal(sem, to):
    pl.semaphore_signal(sem, inc=1, device_id=to, device_id_type=MESH)


class Gather:
    def __init__(self, place, src, buf, send, recv, local, y_last, eager=False, by_rows=False):
        self.p, self.src, self.buf = place, src, buf
        self.send, self.recv, self.local = send, recv, local
        self.y_last, self.eager, self.by_rows = y_last, eager, by_rows
        self.rows, self.width = src.shape
        self.sent = ([], [], [])

    def part(self, d):
        if self.by_rows:
            return pl.ds(pl.multiple_of(d * self.rows, 16), self.rows), slice(None)
        return slice(None), pl.ds(pl.multiple_of(d * self.width, CH), self.width)

    def shard(self, x, o, y):
        return self.buf.at[x, self.p.zpos(-o), y, *self.part(self.p.d)]

    def go(self, src, dst, out, slot, to, plane):
        remote(src, dst, self.send.at[out], self.recv.at[slot], to).start()
        self.sent[plane].append(out)

    def got(self, ref, slot):
        arrived(ref, self.recv.at[slot])

    def own(self, o):
        return self.src if o == 0 else self.shard(self.p.x, o, self.p.y)

    def send_y(self, o, plane):
        p = self.p
        self.go(self.own(o), self.shard(p.x, o, p.y), 3 + o, 3 + o, p.at(y=1 - p.y), plane)

    def send_x(self, o, plane):
        p = self.p
        self.go(self.own(o), self.shard(p.x, o, p.y), 7 + o, 7 + o, p.at(x=1 - p.x), plane)

    def core(self, q, plane):
        x, y = self.kind(q)
        part = self.buf.at[x, :, y, *self.part(self.p.d)]
        self.go(part, part, 15 + q, 15 + q, self.p.at(d=1 - self.p.d), plane)

    def kind(self, q):
        p = self.p
        return (p.x if q < 2 else 1 - p.x), (p.y if q % 2 == 0 else 1 - p.y)

    def wait_all(self, q):
        x, y = self.kind(q)
        for o in range(self.p.nz):
            self.got(self.shard(x, o, y), (0, 3, 7, 11)[q] + o)

    def begin(self):
        p = self.p
        own = self.shard(p.x, 0, p.y)
        pltpu.make_async_copy(self.src, own, self.local).start()
        for o in range(1, p.nz):
            self.go(self.src, own, o - 1, o - 1, p.at(z=p.zpos(o)), 2)
        self.send_x(0, 2)
        if self.eager:
            self.send_y(0, 2)
        else:

            @pl.when(p.x == 0)
            def _():
                self.send_y(0, 0)

    def early(self):
        @pl.when(self.p.x == 1)
        def _():
            for o in range(1, self.p.nz):
                self.got(self.shard(self.p.x, o, self.p.y), o - 1)
                self.send_x(o, 1)
                if self.eager:
                    self.send_y(o, 1)

    def spread(self, layer):
        p, nz = self.p, self.p.nz

        @pl.when(p.x == layer)
        def _():
            for o in range(nz):
                if layer == 0 and o > 0:
                    self.got(self.shard(p.x, o, p.y), o - 1)
                    self.send_x(o, layer)
                if o > 0 if layer == 0 else not self.eager:
                    self.send_y(o, layer)
            finish(self.shard(p.x, 0, p.y), self.local)
            self.core(0, layer)

        @pl.when(p.x != layer)
        def _():
            if self.y_last[layer]:
                for o in range(nz):
                    here = self.shard(1 - p.x, o, p.y)
                    self.got(here, 7 + o)
                    self.go(here, here, 11 + o, 11 + o, p.at(y=1 - p.y), 1 - layer)
            else:
                self.wait_all(2)
            self.core(2, 1 - layer)

    def hop(self, layer):
        p = self.p
        if not self.y_last[layer]:

            @pl.when(p.x == layer)
            def _():
                for o in range(p.nz):
                    here = self.shard(p.x, o, 1 - p.y)
                    self.got(here, 3 + o)
                    self.go(here, here, 19 + o, 11 + o, p.at(x=1 - p.x), layer)
                self.core(1, layer)

    def last(self, layer):
        p = self.p
        if self.y_last[layer]:

            @pl.when(p.x == layer)
            def _():
                self.wait_all(1)
                self.core(1, layer)

        @pl.when(p.x != layer)
        def _():
            self.wait_all(3)
            self.core(3, 1 - layer)

    def done(self, layer):
        p = self.p
        other = self.part(1 - p.d)
        for plane in range(2):

            @pl.when(p.x == plane)
            def _():
                for q in (0, 1) if plane == layer else (2, 3):
                    x, y = self.kind(q)
                    self.got(self.buf.at[x, :, y, *other], 15 + q)

    def close(self):
        p = self.p

        def leave(slots):
            for slot in slots:
                ref = self.shard(p.x, 0, p.y)
                if 15 <= slot < 19:
                    ref = self.buf.at[p.x, :, p.y, *self.part(p.d)]
                departed(ref, self.send.at[slot])

        leave(self.sent[2])
        for plane in range(2):

            @pl.when(p.x == plane)
            def _():
                leave(self.sent[plane])


def forward_kernel(n, *refs):
    ref = ForwardRefs(*refs[:16])
    saved = [Kept(*refs[16:28]), Kept(*refs[28:40])]
    v = Kept(*refs[40:52])
    own = ForwardScratch(*refs[52:])
    p = Place(n)
    nz, group = p.nz, p.group
    t = v.a.shape[0]
    nc = t // CH
    mine = ((ref.wq, own.wq, own.hq), (ref.wo, own.wo, own.ho))
    mine += ((ref.wu, own.wu, own.hu), (ref.wd, own.wd, own.hd))
    for k, (src, wide_, _) in enumerate(mine):
        width = wide_.shape[1]
        cols = pl.ds(pl.multiple_of(p.d * width, CH), width)
        pltpu.make_async_copy(src.at[:, cols], wide_, own.w_sem.at[k]).start()
    p.meet()
    for k, (_, wide_, half) in enumerate(mine):
        finish(wide_, own.w_sem.at[k])
        half[...] = wide_[...].astype(bf16)

    def gather(k, src, buf, y_last, eager=False, by_rows=False):
        sems = (own.g_send.at[k], own.g_recv.at[k], own.g_local.at[k])
        return Gather(p, src, buf, *sems, y_last, eager, by_rows)

    gs = gather(0, ref.small, own.sm, (True, True), True, True)
    gq = gather(1, own.hq, ref.gq, (True, True), True)
    go = gather(2, own.ho, ref.go, (True, False))
    gu = gather(3, own.hu, ref.gu, (True, False))
    gd = gather(4, own.hd, ref.gd, (False, True))
    gathers = (gs, gq, go, gu, gd)

    def collect(which, s):
        i = lax.rem(p.j + s, 4)
        to = (lax.div(p.z, 2) * 2 + lax.div(i, 2)) * 2 + lax.rem(i, 2)
        slot = lax.rem(p.j, 4)
        src = (ref.cot if which else ref.tokens).at[i, p.x]
        dst = (ref.cot_out if which else own.tok).at[span(slot, CH), :]
        send, recv = own.c_send.at[which], own.c_recv.at[which]
        copy = remote(src, dst, send.at[s], recv.at[slot], p.at(j=to))

        @pl.when(to != p.j)
        def _():
            copy.start()

        @pl.when(to == p.j)
        def _():
            pltpu.make_async_copy(src, dst, recv.at[slot]).start()

        def close():
            @pl.when(to != p.j)
            def _():
                copy.wait_send()

        return close

    gs.begin()
    gq.begin()
    closing = [collect(0, s) for s in range(4)]
    for g in (go, gu, gd):
        g.begin()
    gs.early()
    gs.spread(0)
    gq.early()
    gq.spread(0)
    gs.spread(1)
    gs.last(0)
    go.early()
    go.spread(0)
    gs.last(1)
    gs.done(0)
    gs.done(1)

    vec, gv, bd, sm, maps = own.vec, ref.gv, ref.bd, own.sm, own.maps
    vec[...] = jnp.zeros(vec.shape, f32)
    gv[...] = jnp.zeros(gv.shape, f32)
    bd[...] = jnp.zeros(bd.shape, bf16)
    for layer in range(2):
        for k in range(n):
            part = sm[layer, k // 2, k % 2, 0:16, :].astype(f32)
            row, grow = (33 * k) // 4, (3 * k) // 2
            vec[layer, row : row + 9, :] += part[0:9]
            gv[layer, grow : grow + 2, :] += part[9:11]
        first = lanes(HEAD) < HEAD
        for k in range(n):
            packed = sm[layer, k // 2, k % 2, 16:112, :].astype(f32)
            turned = pltpu.roll(packed, HEAD, 1)
            middle = jnp.concatenate([packed[HEAD:], turned[: HEAD // 2]], 0)
            for i, left in enumerate((packed[:HEAD], middle, turned[HEAD // 2 :])):
                right = pltpu.roll(left, HEAD, 1)
                pair, odd = (3 * k + i) // 2, (3 * k + i) % 2
                rows = pl.ds(odd * HEAD, HEAD)
                signed = jnp.where(first, left, -right)
                bd[layer, pair, rows, odd * CH : (odd + 1) * CH] = signed.astype(bf16)
                alone = jnp.where(first, 0.0, right) if odd else jnp.where(first, left, 0.0)
                maps[layer, pair, rows, :] = alone.astype(bf16)

    for k in range(4):
        arrived(own.tok.at[pl.ds(k * CH, CH), :], own.c_recv.at[0, k])

    def load(g, dst, layer, k):
        pltpu.make_async_copy(g.buf.at[layer], dst, own.w_sem.at[k]).start()

    def loaded(dst, k):
        finish(dst, own.w_sem.at[k])

    def save(layer, *sources, part=None):
        for src in sources:
            k = [src is x for x in v].index(True)
            dst = saved[layer][k]
            if src is v.res:
                src = src.at[layer]
            if part is not None:
                cols = pl.ds(part * (FF // 2), FF // 2)
                src, dst = src.at[:, cols], dst.at[:, cols]
            pltpu.make_async_copy(src, dst, own.o_sem.at[layer, k]).start()

    def saved_all(layer, *sources):
        for src in sources:
            k = [src is x for x in v].index(True)
            finish(src.at[layer] if src is v.res else src, own.o_sem.at[layer, k])

    flat = Weights(
        own.vq.reshape(D, 3 * D),
        own.vo.reshape(D, D),
        own.vu.reshape(D, FF),
        own.vd.reshape(FF, D),
    )
    low = lanes(CH) < HEAD
    tril = lax.broadcasted_iota(jnp.int32, (CH, CH), 0) >= lanes(CH)
    eye = jnp.where(lax.broadcasted_iota(jnp.int32, (CH, CH), 0) == lanes(CH), 1.0, 0.0)
    eye = eye.astype(bf16)

    def norm_rows(layer, src, dst, which, shift):
        gain = wide(gv, layer, which * 6, 6)
        bias = wide(vec, layer, shift, 6)

        def body(i):
            xh, _ = standardize(src[span(i, CH), :].astype(f32))
            dst[span(i, CH), :] = (xh * gain + bias).astype(bf16)

        loop(nc, body)

    def bias_cols(layer, at, j):
        return wide(vec, layer, at + 2 * j, 2)

    def project(layer, u, events):
        a, qkv, ph, st = v.a, v.qkv, v.ph, own.st
        if layer == 1:
            saved_all(0, v.a, v.qkv, v.ph)
        norm_rows(layer, u, a, 0, SHIFT1)
        loaded(own.vq, 0)
        save(layer, v.a)

        def column(j):
            cols = span(j, TILE)
            qkv[:, cols] = (
                nn(a[...], flat.q[:, cols]) + bias_cols(layer, QKV_BIAS, j)
            ).astype(bf16)

        loop(3 * D // TILE, column, events[0])
        save(layer, v.qkv)

        def pair(k):
            logits = tt(maps[layer, k], qkv[:, span(k, CH)]).reshape(2, HEAD, t)
            up = jnp.exp(logits - jnp.max(logits, 1, keepdims=True))
            down = jnp.exp(jnp.min(logits, 1, keepdims=True) - logits)
            up = up * (1.0 / jnp.sum(up, 1, keepdims=True))
            down = down * (1.0 / jnp.sum(down, 1, keepdims=True))
            both = jnp.concatenate([up, down], 1).reshape(2 * CH, t).astype(bf16)
            for c in range(nc):
                ph[pl.ds(c * CH, CH), span(k, 2 * CH)] = nt(
                    eye, both[:, c * CH : (c + 1) * CH]
                ).astype(bf16)

        loop(PAIRS, lambda k: pair(k + PAIRS), events[1])

        def state(k):
            val = qkv[:, pl.ds(pl.multiple_of(2 * D + k * CH, CH), CH)]
            for hh in range(2):
                key = ph[:, pl.ds(pl.multiple_of((H + 2 * k + hh) * CH, CH), CH)]
                full = tn(val, key)
                st[layer, span(2 * k + hh, HEAD), :] = full[hh * HEAD : (hh + 1) * HEAD]
                st[layer, pl.ds(D + 2 * k + hh, 1), :] = jnp.sum(
                    key.astype(f32), 0, keepdims=True
                )

        loop(PAIRS, state)
        st[layer, D + H :, :] = jnp.zeros((STATE_ROWS - D - H, CH), f32)
        split_states(st.at[layer], own.stb.at[layer])
        send_states(layer, st, 1)
        loop(PAIRS, pair, events[2])
        save(layer, v.ph)

    members = 2 * group

    def send_states(layer, st, sign):
        for o in range(1, members):
            ok = (p.r + o < members) if sign > 0 else (p.r - o >= 0)

            @pl.when(ok)
            def _():
                remote(
                    own.stb.at[layer],
                    own.got.at[layer, o - 1],
                    own.s_send.at[layer, o - 1],
                    own.s_recv.at[layer, o - 1],
                    p.member(p.r + sign * o),
                ).start()

    def take_states(layer, sign):
        pre = v.pre
        pre[...] = jnp.zeros(pre.shape, f32)
        for o in range(1, members):
            ok = (p.r - o >= 0) if sign > 0 else (p.r + o < members)

            @pl.when(ok)
            def _():
                arrived(own.got.at[layer, o - 1], own.s_recv.at[layer, o - 1])
                add_states(pre, own.got.at[layer, o - 1])

    def close_states(layer, sign):
        for o in range(1, members):
            ok = (p.r + o < members) if sign > 0 else (p.r - o >= 0)

            @pl.when(ok)
            def _():
                departed(own.stb.at[layer], own.s_send.at[layer, o - 1])

    def mix(layer, u, events):
        qkv, ph, o_, inv, ob = v.qkv, v.ph, v.o, v.inv, v.ob
        r, n2, hid, gp = v.r, v.n2, v.hid, v.gp
        res = v.res.at[layer]
        if layer == 1:
            saved_all(0, v.pre, v.o, v.inv, v.ob, v.r, v.n2, v.hid, v.gp)
        take_states(layer, 1)
        if layer == 1:
            closing.extend([collect(1, s) for s in range(4)])
            closing.extend(hand_over(p, 0, v.res.at[0], ref.lay, own.d_send, own.d_recv))
        save(layer, v.pre)
        s0 = v.pre

        def pair(k):
            cols = span(k, CH)
            s = s0[cols, :]
            tot = [s0[pl.ds(D + 2 * k + hh, 1), :] for hh in range(2)]
            for c in range(nc):
                rows = pl.ds(c * CH, CH)
                val = qkv[rows, pl.ds(pl.multiple_of(2 * D + k * CH, CH), CH)]
                sl = s.astype(bf16)
                sf = (s - sl.astype(f32)).astype(bf16)
                done = []
                new = []
                for hh in range(2):
                    qh = ph[rows, span(2 * k + hh, CH)]
                    kh = ph[rows, pl.ds(pl.multiple_of((H + 2 * k + hh) * CH, CH), CH)]
                    score = jnp.where(tril, nt(qh, kh), 0.0)
                    hi = score.astype(bf16)
                    lo = (score - hi.astype(f32)).astype(bf16)
                    num = nn(hi, val) + nn(lo, val) + nt(qh, sl) + nt(qh, sf)
                    den = jnp.sum(score + qh.astype(f32) * tot[hh], -1, keepdims=True)
                    rec = 1.0 / den
                    done.append((num * rec, rec))
                    new.append(tn(val, kh)[hh * HEAD : (hh + 1) * HEAD])
                    tot[hh] = tot[hh] + jnp.sum(kh.astype(f32), 0, keepdims=True)
                s = s + jnp.concatenate(new, 0)
                both = jnp.where(low, done[0][0], done[1][0])
                o_[rows, cols] = both
                ob[rows, cols] = both.astype(bf16)
                inv[rows, cols] = jnp.where(low, done[0][1], done[1][1])

        loop(PAIRS, pair, events[0])
        save(layer, v.o, v.inv, v.ob)
        events[1]()
        loaded(own.vo, 1)

        def out_col(j):
            cols = span(j, TILE)
            r[:, cols] = (
                u[:, cols].astype(f32)
                + nn(ob[...], flat.o[:, cols])
                + bias_cols(layer, OUT_BIAS, j)
            )

        loop(D // TILE, out_col)
        norm_rows(layer, r, n2, 1, SHIFT2)
        save(layer, v.r, v.n2)
        events[2]()
        loaded(own.vu, 2)

        def up_col(j):
            cols = span(j, TILE)
            zt = nn(n2[...], flat.u[:, cols]) + bias_cols(layer, UP_BIAS, j)
            z2 = zt * zt
            half = 0.5 + 0.5 * jnp.tanh(zt * (GELU_C + (GELU_C * GELU_A) * z2))
            act = zt * half
            hid[:, cols] = act.astype(bf16)
            slope = 2.0 * GELU_C + (6.0 * GELU_C * GELU_A) * z2
            gp[:, cols] = (half + act * ((1.0 - half) * slope)).astype(bf16)

        halfway = FF // TILE // 2 - 1
        loop(FF // TILE, up_col, {halfway: lambda: save(layer, v.hid, v.gp, part=0), **events[3]})
        save(layer, v.hid, v.gp, part=1)
        events[4]()
        loaded(own.vd, 3)

        def down_col(j):
            cols = span(j, TILE)
            res[:, cols] = (
                r[:, cols] + nn(hid[...], flat.d[:, cols]) + bias_cols(layer, DOWN_BIAS, j)
            ).astype(bf16)

        loop(D // TILE, down_col)
        save(layer, v.res)

    def run(*steps):
        def go_():
            for step in steps:
                step()

        return go_

    nothing = run()
    gu.early()
    go.spread(1)
    gu.spread(0)
    gq.last(0)
    gu.spread(1)
    gq.done(0)
    load(gq, own.vq, 0, 0)
    tok_out = pltpu.make_async_copy(own.tok, ref.tok_out, own.m_sem)
    tok_out.start()
    project(0, own.tok, [{}, {}, {}])
    gd.early()
    gd.spread(0)
    gq.spread(1)
    gd.spread(1)
    go.last(0)
    go.hop(1)
    mix(
        0,
        own.tok,
        [
            {
                1: run(
                    functools.partial(go.done, 0),
                    functools.partial(load, go, own.vo, 0, 1),
                    functools.partial(gd.hop, 0),
                ),
                3: run(
                    functools.partial(gu.last, 0),
                    functools.partial(gu.done, 0),
                    functools.partial(load, gu, own.vu, 0, 2),
                ),
            },
            functools.partial(gu.hop, 1),
            nothing,
            {},
            run(
                functools.partial(gq.last, 1),
                functools.partial(gq.done, 1),
                functools.partial(load, gq, own.vq, 1, 0),
                functools.partial(gd.last, 0),
                functools.partial(gd.done, 0),
                functools.partial(load, gd, own.vd, 0, 3),
            ),
        ],
    )
    project(1, v.res.at[0], [{}, {}, {}])
    mix(
        1,
        v.res.at[0],
        [
            {
                2: run(
                    functools.partial(go.last, 1),
                    functools.partial(go.done, 1),
                    functools.partial(load, go, own.vo, 1, 1),
                ),
                4: run(
                    functools.partial(gu.last, 1),
                    functools.partial(gu.done, 1),
                    functools.partial(load, gu, own.vu, 1, 2),
                ),
            },
            nothing,
            nothing,
            {
                1: run(
                    functools.partial(gd.last, 1),
                    functools.partial(gd.done, 1),
                    functools.partial(load, gd, own.vd, 1, 3),
                )
            },
            nothing,
        ],
    )

    for g in gathers:
        g.close()
    for close in closing:
        close()
    for k in range(4):
        arrived(ref.cot_out.at[pl.ds(k * CH, CH), :], own.c_recv.at[1, k])
    for layer in range(2):
        close_states(layer, 1)

    tok_out.wait()
    handed_over(p, 0, ref.lay, own.d_recv)
    saved_all(0, v.res)
    saved_all(1, *v)


def forward_pass(n, tokens, cotangent, small, wq, wo, wu, wd):
    t = 4 * CH
    nz = n // 2
    full = [
        shape((2, nz, 2) + w.shape, bf16) for w in (wq, wo, wu, wd)
    ]
    kept = [
        shape((t, D), bf16),
        shape((t, 3 * D), bf16),
        shape((t, 2 * QB), bf16),
        shape((t, D), f32),
        shape((t, D), f32),
        shape((t, D), bf16),
        shape((t, D), f32),
        shape((t, D), bf16),
        shape((t, FF), bf16),
        shape((t, FF), bf16),
        shape((t, D), bf16),
        shape((STATE_ROWS, CH), f32),
    ]
    outs = full + [shape((2, GAIN_ROWS, CH), f32), shape((2, 2 * PAIRS, CH, 2 * CH), bf16)]
    outs += [shape((t, D), bf16)] * 2 + [shape((1, 4, 2, CH, D), bf16)] + kept * 2
    specs = [ANY] * 4 + [VMEM] * 2 + [ANY] * (len(outs) - 6)
    scratch = [pltpu.VMEM(k.shape, k.dtype) for k in kept]
    scratch[10] = pltpu.VMEM((2, t, D), bf16)
    halves = [(w.shape[0], w.shape[1] // 2) for w in (wq, wo, wu, wd)]
    scratch += [pltpu.VMEM(half, f32) for half in halves]
    scratch += [pltpu.VMEM(half, bf16) for half in halves]
    scratch += [
        pltpu.VMEM((t, D), bf16),
        pltpu.VMEM((2, nz, 2, SMALL_ROWS, CH), bf16),
        pltpu.VMEM((2, VEC_ROWS, CH), f32),
        pltpu.VMEM((2, 2 * PAIRS, CH, CH), bf16),
        pltpu.VMEM((2, STATE_ROWS, CH), f32),
        pltpu.VMEM((2, STATE_ROWS + 16, CH), bf16),
        pltpu.VMEM((2, n // 2 - 1, STATE_ROWS + 16, CH), bf16),
    ]
    scratch += [pltpu.VMEM(w.shape[1:], bf16) for w in full]
    dma = pltpu.SemaphoreType.DMA
    scratch += [dma((5, 23)), dma((5, 19)), dma((5,)), dma((2, 4)), dma((2, 4))]
    scratch += [dma((2, n // 2 - 1)), dma((2, n // 2 - 1)), dma((4,)), dma((8,)), dma((4,))]
    scratch += [dma((2, 12)), dma]
    got = call(
        functools.partial(forward_kernel, n),
        outs,
        scratch,
        [ANY] * 7,
        [tokens, cotangent, small, wq, wo, wu, wd],
        4 * t * D * (4 * D + 2 * FF),
        specs,
        cid=0,
    )
    layers = [Kept(*got[9:21]), Kept(*got[21:33])]
    return got[:4], got[4], got[5], got[6], got[7], got[8], layers


def with_error(gv, swapped, lane, hh):
    first = HEAD * (1 - hh)
    hi = swapped.astype(bf16)
    lo = (swapped - hi.astype(f32)).astype(bf16)
    own = (lane < HEAD) if hh == 0 else (lane >= HEAD)
    spare = jnp.where(
        lane == first + 1,
        lo,
        jnp.where((lane == first) | (lane == first + 2), hi, jnp.zeros_like(gv)),
    )
    return jnp.where(own, gv, spare)


def with_ones(v, lane, hh):
    first = HEAD * (1 - hh)
    own = (lane < HEAD) if hh == 0 else (lane >= HEAD)
    spare = jnp.where((lane == first) | (lane == first + 1), jnp.ones_like(v), jnp.zeros_like(v))
    return jnp.where(own, v, spare)


def with_totals(s, tot, row, hh, again):
    first = HEAD * (1 - hh)
    hi = tot.astype(bf16).astype(f32)
    lo = tot - hi
    own = (row < HEAD) if hh == 0 else (row >= HEAD)
    if again:
        spare = jnp.where(
            (row == first) | (row == first + 1), hi, jnp.where(row == first + 2, lo, 0.0)
        )
    else:
        spare = jnp.where(row == first, hi, jnp.where(row == first + 1, lo, 0.0))
    return jnp.where(own, s, spare).astype(bf16)


def put_rows(ref, layer, row, val):
    for i in range(val.shape[1] // CH):
        ref[layer, pl.ds(row + i, 1), :] = val[:, i * CH : (i + 1) * CH]


class Reduce:
    def __init__(self, place, layer, buf, land, out, fin, sems, credit):
        self.p, self.layer, self.buf, self.fin = place, layer, buf, fin
        self.land_y, self.land_z, self.land_x, self.stage = land
        self.own, self.other = out
        self.send, self.recv, self.last = sems
        self.credit_y, self.credit_a, self.credit_b = credit

    def go(self, src, dst, slot, to):
        remote(src, dst, self.send.at[slot], self.recv.at[slot], to).start()

    def send_y(self):
        p = self.p
        if self.layer == 0:
            pl.semaphore_wait(self.credit_y, 1)
        self.go(self.buf.at[:, 1 - p.y], self.land_y, 0, p.at(y=1 - p.y))

    def add(self, zi, more):
        kept = self.buf.at[zi, self.p.y]
        kept[...] = (kept[...].astype(f32) + more.astype(f32)).astype(bf16)

    def step_y(self):
        p = self.p
        near = p.z + 1 - 2 * p.zl
        arrived(self.land_y, self.recv.at[0])
        if self.layer == 0:
            pl.semaphore_wait(self.credit_a, 1)
        for h in range(2):
            zi = 2 * h + 1 - p.zl
            self.add(zi, self.land_y[zi])
            self.go(self.buf.at[zi, p.y], self.land_z.at[h], 1 + h, p.at(z=near))
        for h in range(2):
            zi = 2 * h + p.zl
            self.add(zi, self.land_y[zi])
        if self.layer == 1:
            signal(self.credit_y, p.at(y=1 - p.y))

    def step_a(self):
        p = self.p
        near = p.z + 1 - 2 * p.zl
        far = p.z + 2 - 4 * p.zh
        if self.layer == 0:
            pl.semaphore_wait(self.credit_b, 1)
        for h in range(2):
            arrived(self.land_z.at[h], self.recv.at[1 + h])
        away = 2 * (1 - p.zh) + p.zl
        self.add(away, self.land_z[1 - p.zh])
        self.go(self.buf.at[away, p.y], self.land_z.at[2], 3, p.at(z=far))
        self.add(p.z, self.land_z[p.zh])
        if self.layer == 1:
            signal(self.credit_a, p.at(z=near))

    def step_z(self):
        p = self.p
        arrived(self.land_z.at[2], self.recv.at[3])
        total = self.buf[p.z, p.y].astype(f32) + self.land_z[2].astype(f32)
        if self.layer == 1:
            signal(self.credit_b, p.at(z=p.z + 2 - 4 * p.zh))

        @pl.when(p.x == self.layer)
        def _():
            self.fin[...] = total

        @pl.when(p.x != self.layer)
        def _():
            self.stage[...] = total.astype(bf16)
            self.go(self.stage, self.land_x, 4, p.at(x=1 - p.x))

    def step_x(self):
        p = self.p

        @pl.when(p.x == self.layer)
        def _():
            arrived(self.land_x, self.recv.at[4])
            self.fin[...] += self.land_x[...].astype(f32)
            self.go(self.fin, self.own, 5, p.at(d=1 - p.d))
            pltpu.make_async_copy(self.fin, self.own, self.last).start()

    def close(self):
        p = self.p
        departed(self.buf.at[:, 0], self.send.at[0])
        for i in range(1, p.nz):
            departed(self.buf.at[0, 0], self.send.at[i])

    def end(self):
        @pl.when(self.p.x == self.layer)
        def _():
            departed(self.fin, self.send.at[5])
            arrived(self.other, self.recv.at[5])
            finish(self.fin, self.last)

        @pl.when(self.p.x != self.layer)
        def _():
            departed(self.stage, self.send.at[4])


SMALL_OUT = 128
Q, O, U, DN, SM = range(5)
PARTS = (
    (Q, 0, 96, 0, 384),
    (Q, 0, 96, 384, 384),
    (Q, 0, 96, 768, 384),
    (O, 0, 96, 0, 384),
    (U, 0, 96, 0, 768),
    (U, 0, 96, 768, 768),
    (DN, 0, 192, 0, 384),
    (DN, 192, 192, 0, 384),
    (SM, 0, 64, 0, CH),
)


class Loaded(NamedTuple):
    gp: Any
    r: Any
    o: Any
    inv: Any
    ph: Any
    qkv: Any
    n2: Any
    ob: Any
    a: Any
    u: Any
    pre: Any


class BackwardRefs(NamedTuple):
    cot: Any
    res1: Any
    gv: Any
    bd: Any
    wq: Any
    wo: Any
    wu: Any
    wd: Any


class BackwardScratch(NamedTuple):
    g: Any
    drb: Any
    gs: Any
    tmp: Any
    acc: Any
    st: Any
    stb: Any
    later: Any
    got: Any
    mg: Any
    vr: Any
    gr: Any
    hidr: Any
    wdr: Any
    vq: Any
    vo: Any
    vu: Any
    bq: Any
    bo: Any
    bu: Any
    bd_: Any
    bs: Any
    yq: Any
    yo: Any
    yu: Any
    yd: Any
    ys: Any
    zq: Any
    zo: Any
    zu: Any
    zd: Any
    zs: Any
    xq: Any
    xo: Any
    xu: Any
    xd: Any
    xs: Any
    wq: Any
    wo: Any
    wu: Any
    wd: Any
    ws: Any
    fq: Any
    fo: Any
    fu: Any
    fd: Any
    fs: Any
    tmp96: Any
    tmpd: Any
    sb: Any
    sd: Any
    r_send: Any
    r_recv: Any
    r_last: Any
    credit_y: Any
    credit_a: Any
    credit_b: Any
    m_send: Any
    m_recv: Any
    s_send: Any
    s_recv: Any
    d_send: Any
    d_recv: Any
    w_sem: Any
    l_sem: Any
    h_sem: Any
    t_sem: Any
    k_sem: Any


def backward_kernel(n, *refs):
    ref = BackwardRefs(*refs[:8])
    source = [Loaded(*refs[8:19]), Loaded(*refs[19:30])]
    hidden = refs[30:32]
    lay, gin, small_out = refs[32], refs[33], refs[38]
    wgrads = refs[34:38]
    lands = refs[39:47]
    v = Loaded(*refs[47:58])
    own = BackwardScratch(*refs[58:])
    p = Place(n)
    nz, group = p.nz, p.group
    t = own.drb.shape[0]
    nc = t // CH
    members = 2 * group
    gains, gbuf, tmp, acc = ref.gv, own.g, own.tmp, own.acc
    vr, gr, mg = own.vr, own.gr, own.mg
    flat = Weights(own.vq.reshape(D, 3 * D), own.vo.reshape(D, D), own.vu.reshape(D, FF))
    stored = (own.vq, own.vo, own.vu)
    lane_t = lanes(t)
    lane = lanes(CH)
    low = lane < HEAD
    row = lax.broadcasted_iota(jnp.int32, (CH, CH), 0)
    tril, triu = row >= lane, row <= lane

    def load(layer, *wanted):
        for dst in wanted:
            k = [dst is x for x in v].index(True)
            pltpu.make_async_copy(source[layer][k], dst, own.l_sem.at[k]).start()

    def loaded(*wanted):
        for dst in wanted:
            k = [dst is x for x in v].index(True)
            finish(dst, own.l_sem.at[k])

    def load_w(layer, k):
        w = (ref.wq, ref.wo, ref.wu)[k]
        pltpu.make_async_copy(w.at[layer], stored[k], own.w_sem.at[k]).start()

    def loaded_w(k):
        finish(stored[k], own.w_sem.at[k])

    def load_wd(layer, k):
        pltpu.make_async_copy(
            ref.wd.at[layer, k // 2, k % 2], own.wdr.at[k % 3], own.k_sem.at[k % 3]
        ).start()

    pltpu.make_async_copy(ref.cot, gbuf.at[0], own.t_sem.at[4]).start()
    for k in range(3):
        load_wd(1, k)
    load(1, v.gp)
    load_w(1, U)
    load(1, v.r, v.o, v.inv, v.ph)
    load_w(1, O)
    load_w(1, Q)
    load(1, v.qkv, v.n2, v.ob, v.a, v.u, v.pre)
    p.meet()
    finish(gbuf.at[0], own.t_sem.at[4])

    width = (3 * D // 2, D // 2, FF // 2, D // 2)
    bufs = (own.bq, own.bo, own.bu, own.bd_, own.bs)
    spots = (
        (own.yq, own.yo, own.yu, own.yd, own.ys),
        (own.zq, own.zo, own.zu, own.zd, own.zs),
        (own.xq, own.xo, own.xu, own.xd, own.xs),
        (own.wq, own.wo, own.wu, own.wd, own.ws),
    )
    fins = (own.fq, own.fo, own.fu, own.fd, own.fs)
    reduces = []
    for layer in range(2):
        line = [[] for _ in range(5)]
        for k, (m, r0_, r_, c0_, c_) in enumerate(PARTS):
            rows, cols = pl.ds(r0_, r_), pl.ds(c0_, c_)
            out = []
            for side in (p.d, 1 - p.d):
                if m == SM:
                    out.append(small_out.at[pl.ds(pl.multiple_of(side * r_, r_), r_), :])
                else:
                    at = pl.ds(pl.multiple_of(side * width[m] + c0_, CH), c_)
                    out.append(wgrads[m].at[rows, at])
            line[m].append(
                Reduce(
                    p,
                    layer,
                    bufs[m].at[:, :, rows, cols],
                    (
                        spots[0][m].at[:, rows, cols],
                        spots[1][m].at[:, rows, cols],
                        spots[2][m].at[rows, cols],
                        spots[3][m].at[rows, cols],
                    ),
                    out,
                    fins[m].at[rows, cols],
                    (own.r_send.at[layer, k], own.r_recv.at[layer, k], own.r_last.at[layer, k]),
                    (own.credit_y.at[k], own.credit_a.at[k], own.credit_b.at[k]),
                )
            )
        reduces.append(line)

    def step(name, layer, *which):
        def all_():
            for m in which:
                for part in reduces[layer][m]:
                    name(part)

        return all_

    step_y = functools.partial(step, Reduce.step_y)
    step_a = functools.partial(step, Reduce.step_a)
    step_z = functools.partial(step, Reduce.step_z)
    step_x = functools.partial(step, Reduce.step_x)

    def states_ok(o, taking):
        return (p.r + o < members) if taking else (p.r - o >= 0)

    def send_states(layer):
        for o in range(1, members):
            @pl.when(states_ok(o, False))
            def _():
                remote(
                    own.stb.at[layer],
                    own.got.at[layer, o - 1],
                    own.s_send.at[layer, o - 1],
                    own.s_recv.at[layer, o - 1],
                    p.member(p.r - o),
                ).start()

    def take_states(layer):
        later = own.later
        later[...] = jnp.zeros(later.shape, f32)
        for o in range(1, members):

            @pl.when(states_ok(o, True))
            def _():
                arrived(own.got.at[layer, o - 1], own.s_recv.at[layer, o - 1])
                add_states(later, own.got.at[layer, o - 1])

        return later

    def close_states(layer):
        for o in range(1, members):

            @pl.when(states_ok(o, False))
            def _():
                departed(own.stb.at[layer], own.s_send.at[layer, o - 1])

    def norm_back(x_ref, which, layer, body):
        gain = wide(gains, layer, which * 6, 6)
        acc[...] = jnp.zeros(acc.shape, f32)

        def step(i):
            rows = span(i, CH)
            xh, rstd = standardize(x_ref[rows, :].astype(f32))
            dn = tmp[rows, :]
            acc[0:1, :] += jnp.sum(dn, 0, keepdims=True)
            acc[1:2, :] += jnp.sum(dn * xh, 0, keepdims=True)
            dx = dn * gain
            body(
                rows,
                rstd
                * (dx - jnp.mean(dx, -1, keepdims=True) - xh * jnp.mean(dx * xh, -1, keepdims=True)),
            )

        loop(nc, step)
        put_rows(vr, layer, SHIFT2 if which else SHIFT1, acc[0:1, :])
        put_rows(gr, layer, which * 6, acc[1:2, :])

    def mlp_back(layer, g, events, hooks):
        gp, r, o_, inv, ph = v.gp, v.r, v.o, v.inv, v.ph
        drb, gs, st = own.drb, own.gs, own.st
        loaded(v.gp)
        for k in range(2 * nz):
            finish(own.wdr.at[k % 3], own.k_sem.at[k % 3])
            cols = pl.ds(k * FF // n, FF // n)
            part = (nt(g[...], own.wdr[k % 3]) * gp[:, cols]).astype(bf16)
            gp[:, cols] = part
            put_rows(
                vr, layer, UP_BIAS + 3 * k, jnp.sum(part.astype(f32), 0, keepdims=True)
            )
            if k + 3 < 2 * nz:
                load_wd(layer, k + 3)
            if k in events:
                events[k]()
        hooks[0]()
        loaded_w(U)

        def n2_col(j):
            cols = span(j, TILE)
            tmp[:, cols] = nt(gp[...], flat.u[cols, :])

        loop(D // TILE, n2_col)
        hooks[1]()
        loaded(v.r)

        def body(rows, back):
            up = g[rows, :].astype(f32)
            total = up + back
            acc[2:3, :] += jnp.sum(up, 0, keepdims=True)
            acc[3:4, :] += jnp.sum(total, 0, keepdims=True)
            r[rows, :] = total
            drb[rows, :] = total.astype(bf16)

        norm_back(r, 1, layer, body)
        put_rows(vr, layer, DOWN_BIAS, acc[2:3, :])
        put_rows(vr, layer, OUT_BIAS, acc[3:4, :])
        hooks[2]()
        loaded_w(O)
        loaded(v.inv, v.o, v.ph)

        def do_col(j):
            cols = span(j, TILE)
            gs[:, cols] = (nt(drb[...], flat.o[cols, :]) * inv[:, cols]).astype(bf16)

        loop(D // TILE, do_col)
        low_t = lane_t < HEAD

        def pair(k):
            cols = span(k, CH)
            gv = gs[:, cols]
            prod = gv.astype(f32) * o_[:, cols]
            e0 = -jnp.sum(jnp.where(low_t, prod, 0.0), -1, keepdims=True)
            e1 = -jnp.sum(jnp.where(low_t, 0.0, prod), -1, keepdims=True)
            swapped = jnp.where(low_t, e1, e0)
            inv[:, cols] = swapped
            for hh in range(2):
                ge = with_error(gv, swapped, lane_t, hh)
                full = tn(ge, ph[:, span(2 * k + hh, CH)])
                st[layer, span(2 * k + hh, HEAD), :] = full[hh * HEAD : (hh + 1) * HEAD]
                at = HEAD * (1 - hh)
                st[layer, pl.ds(D + 2 * k + hh, 1), :] = full[at : at + 1] + full[at + 1 : at + 2]

        loop(PAIRS, pair)
        st[layer, D + H :, :] = jnp.zeros((STATE_ROWS - D - H, CH), f32)
        split_states(st.at[layer], own.stb.at[layer])
        send_states(layer)

    def weight_grad(layer, m, keep):
        parts = reduces[layer][m]
        buf, c = bufs[m], width[m]
        r = buf.shape[2]
        land_d = lands[layer * 4 + m]
        send, recv = own.m_send.at[layer, m], own.m_recv.at[layer, m]
        base = (p.d if keep else 1 - p.d) * c
        if keep:
            departed(buf, send)
            arrived(land_d, recv)
        elif layer == 0:
            for part in reduces[1][m]:
                part.close()
        if m == DN:
            rhs = gbuf[1 - layer, :, pl.ds(pl.multiple_of(base, CH), c)]

            def fetch(k):
                pltpu.make_async_copy(
                    hidden[layer].at[:, pl.ds(k * FF // n, FF // n)],
                    own.hidr.at[k % 3],
                    own.h_sem.at[k % 3],
                ).start()
                if keep:
                    pltpu.make_async_copy(
                        land_d.at[k // 2, k % 2], own.tmpd.at[k % 3], own.t_sem.at[k % 3]
                    ).start()

            for k in range(3):
                fetch(k)
            for k in range(2 * nz):
                finish(own.hidr.at[k % 3], own.h_sem.at[k % 3])
                val = tn(own.hidr[k % 3], rhs)
                if keep:
                    finish(own.tmpd.at[k % 3], own.t_sem.at[k % 3])
                    val = val + own.tmpd[k % 3].astype(f32)
                buf[k // 2, k % 2] = val.astype(bf16)
                if k + 3 < 2 * nz:
                    fetch(k + 3)
        else:
            lhs = (v.a, v.ob, v.n2)[m]
            rhs = (v.qkv, own.drb, v.gp)[m]
            wide_ = 384
            count = c // wide_

            def fetch(k):
                pltpu.make_async_copy(
                    land_d.at[:, :, :, pl.ds(k * wide_, wide_)],
                    own.tmp96.at[k % 2],
                    own.t_sem.at[k % 2],
                ).start()

            if keep:
                for k in range(min(2, count)):
                    fetch(k)
            for k in range(count):
                val = tn(lhs[...], rhs[:, pl.ds(pl.multiple_of(base + k * wide_, CH), wide_)])
                if keep:
                    finish(own.tmp96.at[k % 2], own.t_sem.at[k % 2])
                for zi in range(nz):
                    for yi in range(2):
                        at = (zi * 2 + yi) * r
                        part = val[at : at + r]
                        if keep:
                            part = part + own.tmp96[k % 2, zi, yi].astype(f32)
                        buf[zi, yi, :, pl.ds(k * wide_, wide_)] = part.astype(bf16)
                if keep and k + 2 < count:
                    fetch(k + 2)
                each = count // len(parts)
                if keep and (k + 1) % each == 0:
                    parts[k // each].send_y()
        if keep and m == DN:
            for part in parts:
                part.send_y()
        if not keep:
            remote(buf, land_d, send, recv, p.at(d=1 - p.d)).start()

    def mix_back(layer, events):
        qkv, ph, gs, es = v.qkv, v.ph, own.gs, v.inv
        bd = ref.bd.at[layer]
        s1 = take_states(layer)
        loaded(v.qkv, v.pre)
        s0 = v.pre

        def pair(k):
            cols = span(k, CH)
            vcols = pl.ds(pl.multiple_of(2 * D + k * CH, CH), CH)
            kcols = pl.ds(pl.multiple_of(D + k * CH, CH), CH)

            def keys(rows, hh):
                return ph[rows, pl.ds(pl.multiple_of((H + 2 * k + hh) * CH, CH), CH)]

            before, finer = [], []
            s = s0[cols, :]
            tot = [s0[pl.ds(D + 2 * k + hh, 1), :] for hh in range(2)]
            for c in range(nc):
                rows = pl.ds(c * CH, CH)
                fine = (s - s.astype(bf16).astype(f32)).astype(bf16)
                none = jnp.zeros_like(fine)
                before.append([with_totals(s, tot[hh], row, hh, True) for hh in range(2)])
                finer.append([jnp.where(row < HEAD, fine, none), jnp.where(row < HEAD, none, fine)])
                if c < nc - 1:
                    val = qkv[rows, vcols]
                    new = []
                    for hh in range(2):
                        kh = keys(rows, hh)
                        new.append(tn(val, kh)[hh * HEAD : (hh + 1) * HEAD])
                        tot[hh] = tot[hh] + jnp.sum(kh.astype(f32), 0, keepdims=True)
                    s = s + jnp.concatenate(new, 0)
            ds = s1[cols, :]
            dtot = [s1[pl.ds(D + 2 * k + hh, 1), :] for hh in range(2)]
            acc_q = jnp.zeros((CH, 2 * CH), f32)
            acc_k = jnp.zeros((CH, 2 * CH), f32)
            sums = [jnp.zeros((1, CH), f32) for _ in range(3)]
            for c in reversed(range(nc)):
                rows = pl.ds(c * CH, CH)
                val = qkv[rows, vcols]
                gv = gs[rows, cols]
                ev = es[rows, cols]
                dsl = ds.astype(bf16)
                dl_q, dl_k, dv, new = [], [], [], []
                for hh in range(2):
                    qh = ph[rows, span(2 * k + hh, CH)]
                    kh = keys(rows, hh)
                    ge = with_error(gv, ev, lane, hh)
                    v1 = with_ones(val, lane, hh)
                    after = with_totals(ds, dtot[hh], row, hh, False)
                    da = jnp.where(tril, nt(ge, v1), 0.0).astype(bf16)
                    dat = jnp.where(triu, nt(v1, ge), 0.0).astype(bf16)
                    at = jnp.where(triu, nt(kh, qh), 0.0).astype(bf16)
                    dq = nn(da, kh) + nn(ge, before[c][hh]) + nn(ge, finer[c][hh])
                    dk = nn(dat, qh) + nn(v1, after)
                    dv.append(nn(at, gv) + nt(kh, dsl))
                    for p_, d_, to in ((qh, dq, dl_q), (kh, dk, dl_k)):
                        pf = p_.astype(f32)
                        to.append((pf * (d_ - half_sums(pf * d_, low))).astype(bf16))
                    full = tn(ge, qh)
                    new.append(full[hh * HEAD : (hh + 1) * HEAD])
                    first = HEAD * (1 - hh)
                    dtot[hh] = dtot[hh] + full[first : first + 1] + full[first + 1 : first + 2]
                ds = ds + jnp.concatenate(new, 0)
                dl_q = jnp.concatenate(dl_q, 1)
                dl_k = jnp.concatenate(dl_k, 1)
                acc_q = acc_q + tn(qkv[rows, cols], dl_q)
                acc_k = acc_k + tn(qkv[rows, kcols], dl_k)
                parts = (
                    (cols, nt(dl_q, bd[k])),
                    (kcols, nt(dl_k, bd[PAIRS + k])),
                    (vcols, jnp.where(low, dv[0], dv[1])),
                )
                for i, (where, new_) in enumerate(parts):
                    new_ = new_.astype(bf16)
                    qkv[rows, where] = new_
                    sums[i] = sums[i] + jnp.sum(new_.astype(f32), 0, keepdims=True)
            for i in range(3):
                vr[layer, pl.ds(QKV_BIAS + i * PAIRS + k, 1), :] = sums[i]
            for which, total in enumerate((acc_q, acc_k)):
                for hh in range(2):
                    blk = total[hh * HEAD : (hh + 1) * HEAD, hh * CH : (hh + 1) * CH]
                    mg[which * H + 2 * k + hh] = blk - pltpu.roll(blk, HEAD, 1)

        loop(PAIRS, pair, events)

    def input_back(layer):
        loaded_w(Q)

        def n1_col(j):
            cols = span(j, TILE)
            tmp[:, cols] = nt(v.qkv[...], flat.q[cols, :])

        loop(D // TILE, n1_col)
        loaded(v.u)
        du = gbuf.at[layer]

        def body(rows, back):
            du[rows, :] = (v.r[rows, :] + back).astype(bf16)

        norm_back(v.u, 0, layer, body)

    closing = []

    def deliver(which, layer, rows):
        sems = own.d_send.at[which, layer], own.d_recv.at[which]
        closing.extend(hand_over(p, layer, rows, gin if which else lay, *sems))

    def small_rows(side):
        return pl.ds(pl.multiple_of(side * 64, 64), 64)

    def pack_small(layer):
        sb = own.sb
        for k in range(n):
            at, gat = (33 * k) // 4, (3 * k) // 2
            zi, yi = k // 2, k % 2
            sb[zi, yi, 0:9] = vr[layer, at : at + 9, :]
            sb[zi, yi, 9:11] = gr[layer, gat : gat + 2, :]
            sb[zi, yi, 11:16] = jnp.zeros((5, CH), f32)
            h0, h1, h2 = (mg[3 * k + i] for i in range(3))
            left = jnp.concatenate([h0, h1[: HEAD // 2]], 0)
            right = jnp.concatenate([h1[HEAD // 2 :], h2], 0)
            sb[zi, yi, 16:112] = jnp.where(lanes(96) < HEAD, left, -right)
            sb[zi, yi, 112:] = jnp.zeros((16, CH), f32)
        remote(
            sb.at[:, :, small_rows(1 - p.d), :],
            own.sd.at[layer],
            own.m_send.at[layer, SM],
            own.m_recv.at[layer, SM],
            p.at(d=1 - p.d),
        ).start()

    def small_core(layer):
        part = reduces[layer][SM][0]
        departed(own.sd.at[layer], own.m_send.at[layer, SM])
        arrived(own.sd.at[layer], own.m_recv.at[layer, SM])
        if layer == 0:
            reduces[1][SM][0].close()
        part.buf[...] = (own.sb[:, :, small_rows(p.d), :] + own.sd[layer]).astype(bf16)
        part.send_y()

    vr[...] = jnp.zeros(vr.shape, f32)
    gr[...] = jnp.zeros(gr.shape, f32)
    def run(*steps):
        def all_():
            for step in steps:
                step()

        return all_

    deliver(0, 1, ref.res1)
    weight_grad(1, DN, False)
    mlp_back(
        1,
        gbuf.at[0],
        {},
        (
            run(functools.partial(loaded, v.n2), functools.partial(weight_grad, 1, U, False)),
            functools.partial(weight_grad, 1, DN, True),
            run(functools.partial(loaded, v.ob), functools.partial(weight_grad, 1, O, False)),
        ),
    )
    load(0, v.o)
    load_w(0, U)
    load_w(0, O)
    for k in range(3):
        load_wd(0, k)
    loaded(v.a)
    weight_grad(1, U, True)
    weight_grad(1, O, True)
    load(0, v.gp, v.n2, v.ob)
    mix_back(1, {1: step_y(1, DN), 5: step_a(1, DN)})
    input_back(1)
    deliver(1, 1, gbuf.at[1])
    load_w(0, Q)
    load(0, v.r, v.inv, v.ph, v.u, v.pre)
    pack_small(1)
    step_y(1, U)()
    weight_grad(1, Q, False)
    weight_grad(1, Q, True)
    small_core(1)
    load(0, v.qkv, v.a)

    step_z(1, DN)()
    weight_grad(0, DN, False)
    step_y(1, O)()
    mlp_back(
        0,
        gbuf.at[1],
        {5: step_x(1, DN), 6: step_a(1, U)},
        (
            step_a(1, O),
            functools.partial(weight_grad, 0, DN, True),
            run(
                step_z(1, U),
                functools.partial(loaded, v.n2),
                functools.partial(weight_grad, 0, U, False),
            ),
        ),
    )
    loaded(v.ob, v.a)
    step_z(1, O)()
    weight_grad(0, O, False)
    weight_grad(0, U, True)
    step_y(1, Q, SM)()
    weight_grad(0, O, True)
    step_x(1, U)()
    mix_back(
        0,
        {
            0: step_x(1, O),
            1: step_a(1, Q, SM),
            2: step_y(0, DN),
            4: step_z(1, Q, SM),
        },
    )
    weight_grad(0, Q, False)
    step_a(0, DN)()
    step_x(1, Q, SM)()
    weight_grad(0, Q, True)
    input_back(0)
    deliver(1, 0, gbuf.at[0])
    step_y(0, U)()
    pack_small(0)
    step_z(0, DN)()
    step_y(0, O)()
    step_a(0, U)()
    small_core(0)
    step_x(0, DN)()
    first, second, third = reduces[0][Q]
    first.step_y()
    step_a(0, O)()
    second.step_y()
    first.step_a()
    step_z(0, U)()
    step_z(0, O)()
    third.step_y()
    second.step_a()
    step_x(0, U)()
    step_x(0, O)()
    step_y(0, SM)()
    first.step_z()
    third.step_a()
    step_a(0, SM)()
    second.step_z()
    first.step_x()
    third.step_z()
    step_z(0, SM)()
    second.step_x()
    third.step_x()
    step_x(0, SM)()

    for m in range(5):
        for part in reduces[0][m]:
            part.close()
        for layer in range(2):
            for part in reduces[layer][m]:
                part.end()
    for layer in range(2):
        close_states(layer)

        handed_over(p, layer, gin, own.d_recv.at[1])
    handed_over(p, 1, lay, own.d_recv.at[0])

    for close in closing:
        close()


def backward_pass(n, cot, gains, bds, full, tokens, kept):
    t = cot.shape[0]
    nz = n // 2
    args = [cot, kept[1].res, gains, bds] + list(full)
    for u, k in zip((tokens, kept[0].res), kept):
        read = Loaded(k.gp, k.r, k.o, k.inv, k.ph, k.qkv, k.n2, k.ob, k.a, u, k.pre)
        args += list(read)
    args += [k.hid for k in kept]
    widths = (3 * D // 2, D // 2, FF // 2, D // 2)
    rows = (D // n, D // n, D // n, FF // n)
    outs = [shape((1, 4, 2, CH, D), bf16)] * 2
    outs += [shape((r, 2 * c), f32) for r, c in zip(rows, widths)]
    outs += [shape((SMALL_OUT, CH), f32)]
    outs += [shape((nz, 2, r, c), bf16) for r, c in zip(rows, widths)] * 2
    specs = [ANY] * len(outs)
    ins = [ANY] * 2 + [VMEM] * 2 + [ANY] * (len(args) - 4)
    scratch = [pltpu.VMEM(a.shape, a.dtype) for a in read]

    def vmem(*dims, kind=f32):
        scratch.append(pltpu.VMEM(dims, kind))

    vmem(2, t, D, kind=bf16)
    vmem(t, D, kind=bf16)
    vmem(t, D, kind=bf16)
    vmem(t, D)
    vmem(8, D)
    vmem(2, STATE_ROWS, CH)
    vmem(2, STATE_ROWS + 16, CH, kind=bf16)
    vmem(STATE_ROWS, CH)
    vmem(2, n // 2 - 1, STATE_ROWS + 16, CH, kind=bf16)
    vmem(2 * H, HEAD, CH)
    vmem(2, VEC_ROWS, CH)
    vmem(2, GAIN_ROWS, CH)
    vmem(3, t, FF // n, kind=bf16)
    vmem(3, FF // n, D, kind=bf16)
    for w in full[:3]:
        vmem(*w.shape[1:], kind=bf16)
    sizes = list(zip(rows, widths)) + [(64, CH)]
    for lead in ((nz, 2), (nz,), (nz - 1,), (), ()):
        for size in sizes:
            vmem(*lead, *size, kind=bf16)
    for size in sizes:
        vmem(*size)
    vmem(2, nz, 2, D // n, 384, kind=bf16)
    vmem(3, FF // n, D // 2, kind=bf16)
    vmem(nz, 2, SMALL_OUT, CH)
    vmem(2, nz, 2, 64, CH)
    dma = pltpu.SemaphoreType.DMA
    regular = pltpu.SemaphoreType.REGULAR
    count = len(PARTS)
    scratch += [dma((2, count, 6)), dma((2, count, 6)), dma((2, count))]
    scratch += [regular((count,))] * 3 + [dma((2, 5)), dma((2, 5))]
    scratch += [dma((2, n // 2 - 1)), dma((2, n // 2 - 1)), dma((2, 2, 4)), dma((2, 8)), dma((4,))]
    scratch += [dma((len(read),)), dma((3,)), dma((5,)), dma((3,))]
    got = call(
        functools.partial(backward_kernel, n),
        outs,
        scratch,
        ins,
        args,
        8 * t * D * (4 * D + 2 * FF),
        specs,
        cid=1,
        vmem=63,
    )
    return got[:7]


def settle_kernel(lay0, lay1, *refs):
    rest, small, outs, held, sems = refs[:5], refs[5], refs[6:13], refs[13:19], refs[19]
    x = lax.axis_index("section")
    for plane, src in enumerate((lay0, lay1)):

        @pl.when(x == plane)
        def _():
            pltpu.make_async_copy(src, held[0], sems.at[0]).start()

    for i, src in enumerate(rest):
        pltpu.make_async_copy(src, held[1 + i], sems.at[1 + i]).start()
    both = small[16:112, :]
    outs[6][0:96, :] = both[:, :HEAD]
    outs[6][96:, :] = pltpu.roll(both, HEAD, 1)[:, :HEAD]
    copies = []
    for i, buf in enumerate(held):
        finish(buf, sems.at[i])
        copies.append(pltpu.make_async_copy(buf, outs[i], sems.at[6 + i]))
        copies[-1].start()
    for copy in copies:
        copy.wait()


def settle(lay0, lay1, rest, small):
    arrays = [lay0, lay1, *rest, small]
    outs = [shape(a.shape, a.dtype) for a in (lay0, *rest)]
    return call(
        settle_kernel,
        outs + [shape((192, HEAD), f32)],
        [pltpu.VMEM(o.shape, o.dtype) for o in outs] + [pltpu.SemaphoreType.DMA((12,))],
        [ANY] * 7 + [VMEM],
        arrays,
        1,
        [ANY] * 6 + [VMEM],
    )


def shards(inputs, cotangent, *weights):
    n = lax.axis_size("seq")
    d, j = lax.axis_index("dp"), lax.axis_index("seq")
    qkv_w, out_w, up_w, down_w, map_w, bias_w, gain_w = (w[0] for w in weights)

    def placed(vector, offset, rows):
        flat = jnp.zeros((rows * CH,), f32)
        return lax.dynamic_update_slice(flat, vector, (offset,)).reshape(rows, CH)

    bias_at, gain_at = (j % 4) * 32, (j % 2) * 64
    small = jnp.concatenate(
        [
            placed(bias_w, bias_at, 9),
            placed(gain_w, gain_at, 2),
            jnp.zeros((5, CH), f32),
            jnp.concatenate([map_w[:96], map_w[96:]], 1),
            jnp.zeros((16, CH), f32),
        ]
    ).astype(bf16)
    small = lax.dynamic_slice_in_dim(small, d * 64, 64, 0)
    full, gains, bds, tokens, cot, lay0, kept = forward_pass(
        n, inputs, cotangent, small, qkv_w, out_w, up_w, down_w
    )
    lay1, *rest, g_small = backward_pass(n, cot, gains, bds, full, tokens, kept)
    layer_out, grads, g_qkv, g_out, g_up, g_down, maps = settle(lay0, lay1, rest, g_small)
    bias = lax.dynamic_slice_in_dim(g_small[:9].reshape(-1), bias_at, bias_w.shape[0])
    gain = lax.dynamic_slice_in_dim(g_small[9:11].reshape(-1), gain_at, gain_w.shape[0])
    return (
        layer_out,
        grads,
        g_qkv[None],
        g_out[None],
        g_up[None],
        g_down[None],
        maps[None],
        bias[None],
        gain[None],
    )


def solution(mesh):
    tokens = P("dp", None, "seq", None)
    matrix = P("section", "seq", None)
    vector = P("section", "seq")
    stacked = P("section", "dp", None, "seq", None)
    chosen = shards if mesh.shape["seq"] == 8 else plain_shards
    return jax.shard_map(
        chosen,
        mesh=mesh,
        in_specs=(tokens, tokens) + (matrix,) * 5 + (vector,) * 2,
        out_specs=(stacked, stacked) + (matrix,) * 5 + (vector,) * 2,
        check_vma=False,
    )
```
